32 devices in a mesh: bins: 8 (over z, y), scans: 4 (over x, core).
Axes of the slice: x: 2, y: 2, z: 4, core: 2. Of those that a mesh axis runs over, the one named last changes fastest.
Arguments:
- profiles: float32 [4, 262144], P('scans', 'bins'), may hold values from -150 to 150
- band_edges: int32 [6], replicated, may hold values from 0 to 256, as said below
- owner_counts: int32 [8], replicated, may hold values from 1 to 64, 256 in all
- dynamics: float32 [5, 64, 64], replicated, may hold values from -0.6 to 0.6
- prev_state: float32 [512, 4, 128], P('bins', 'scans'), may hold values from -6 to 6
Outputs:
- new_state: float32 [512, 4, 128], P('bins', 'scans')
The draws below stay inside these ranges and needn't reach their ends.
Inputs may be any that keep to these rules, and one draw needn't show every extreme that they name: Strictly increasing, band_edges[0] = 0 and band_edges[5] = 256. `owner_counts`: the counts sum to 256, and some owner holds exactly 64 tiles.
All inputs are finite; a program needn't handle non-finite values.
Results may differ from the reference program's by a relative error of at most 0.0001.
Values sent between devices are 32-bit elements; how exact they have to be, the bound alone decides.
No kernel may reach another device: no remote copies, remote signals or barrier semaphores. Data moves between devices by JAX's collectives and lax.ppermute only.
A program may use at most 64 MiB of HBM per device.

```python
import math
import jax
import jax.numpy as jnp
import numpy as np
from jax import lax

NBINS = 262144
PROFILES = 4
TILE = 512
STATES = 64
NCLASS = 5
NT = 256
CAP = 64
SLOTS = 512
N_BINS = 8


def draw_profiles(key, part):
    key_scale = jax.random.fold_in(key, 11)
    key_noise = jax.random.fold_in(key, 12)
    row_index = jnp.arange(PROFILES, dtype=jnp.float32)
    trend_scale = jnp.exp(jnp.log(3.0) * row_index / max(PROFILES - 1, 1))
    jitter = jnp.exp(jax.random.uniform(key_scale, (PROFILES,), jnp.float32, 0.0, jnp.log(10.0)))
    scaling = trend_scale * jitter
    values = jnp.clip(jax.random.normal(key_noise, (PROFILES, NBINS), jnp.float32), -5.0, 5.0)
    return (scaling[:, None] * values).astype(jnp.float32)


def draw_band_edges(key, part):
    interior = jax.random.permutation(jax.random.fold_in(key, 21), NT - 1)[:NCLASS - 1] + 1
    interior = jnp.sort(interior.astype(jnp.int32))
    return jnp.concatenate([jnp.zeros((1,), jnp.int32), interior, jnp.full((1,), NT, jnp.int32)])


def shard_levels(own_key, dims, cuts, smallest, largest):
    factor_of = 1.0
    for axis_at, blocks in cuts:
        heights = jax.random.uniform(jax.random.fold_in(jax.random.fold_in(own_key, 6), axis_at), (blocks,), jnp.float32, smallest / len(cuts), largest / len(cuts))
        factor_of = factor_of * jnp.repeat(jnp.exp(heights), dims[axis_at] // blocks).reshape((-1,) + (1,) * (len(dims) - 1 - axis_at))
    return factor_of


def profile(number_of, total, reach, lean):
    loads = [(1 << 20) // math.isqrt(standing ** lean) + 1 for standing in range(2, number_of + 1)]
    spare, given = total - reach - (number_of - 1), [1] * (number_of - 1)
    while spare > 0:
        free = [i for i in range(number_of - 1) if given[i] < reach]
        mass, budget = sum([loads[i] for i in free]), spare
        for i in free:
            addition = min(reach - given[i], max(1, budget * loads[i] // mass), spare)
            given[i] = given[i] + addition
            spare = spare - addition
    return np.array([reach] + given)


def ragged_sizes(rng, count, total, reach, lean):
    if count == 2:
        one = jax.random.randint(rng, (), max(1, total - reach), min(reach, total - 1) + 1)
        return jnp.stack([one, total - one])
    sizes = jnp.asarray(profile(count, total, reach, lean), jnp.int32)
    twos = (count - 1) // 2
    donor, taker = sizes[1:1 + 2 * twos:2], sizes[2:2 + 2 * twos:2]
    slack = jnp.minimum(donor - 1, reach - taker)
    passed = jax.random.randint(jax.random.fold_in(rng, 1), (twos,), 0, 1 << 20) % (slack + 1)
    sizes = sizes.at[1:1 + 2 * twos:2].set(donor - passed).at[2:2 + 2 * twos:2].set(taker + passed)
    return sizes[jax.random.permutation(jax.random.fold_in(rng, 2), count)]


def scatter_about(stream_key, shape, spread, most, split=(), kind=jnp.bfloat16):
    values = spread * jax.random.normal(stream_key, shape, jnp.float32)
    if split:
        values = values * shard_levels(stream_key, shape, split, -0.22, 0.18)
    return jnp.clip(values, -most, most).astype(kind)


def setup_inputs(seed: int = 0) -> dict:
    streams_of = jax.random.split(jax.random.key(seed), 6)
    profiles = draw_profiles(jax.random.fold_in(streams_of[5], 71), 0)
    band_edges = draw_band_edges(jax.random.fold_in(streams_of[5], 71), 0)
    owner_counts = ragged_sizes(streams_of[2], N_BINS, NT, CAP, 2).astype(jnp.int32)
    dynamics = scatter_about(streams_of[3], (NCLASS, STATES, STATES), 0.15, 0.6, (), jnp.float32)
    prev_state = scatter_about(streams_of[4], (SLOTS, PROFILES, 2 * STATES), 1.0, 6.0, ((0, 8), (1, 4)), jnp.float32)
    return dict(profiles=profiles, band_edges=band_edges, owner_counts=owner_counts, dynamics=dynamics, prev_state=prev_state)


EPSILON = 1e-05
HIGHEST = lax.Precision.HIGHEST

def tile_sums(profile_row):
    spectrum = jnp.fft.rfft(profile_row)[:NBINS // 2]
    real_part = jnp.real(spectrum).reshape(NT, STATES, TILE // STATES)
    imag_part = jnp.imag(spectrum).reshape(NT, STATES, TILE // STATES)
    bin_power = lax.optimization_barrier(jnp.sum(real_part * real_part + imag_part * imag_part, axis=(1, 2)))
    return (lax.optimization_barrier(jnp.sum(real_part, axis=2)), lax.optimization_barrier(jnp.sum(imag_part, axis=2)), bin_power)

def measure(fine_sums, mean_power, band_index):
    measured = jnp.zeros_like(fine_sums)
    for class_index in range(NCLASS):
        group_span = 2 ** class_index
        state_count = STATES // group_span
        coarse = lax.optimization_barrier(jnp.sum(fine_sums.reshape(fine_sums.shape[:-1] + (state_count, group_span)), axis=-1))
        coarse = jnp.pad(coarse, [(0, 0)] * (coarse.ndim - 1) + [(0, STATES - state_count)])
        scaling = 1.0 / jnp.sqrt(TILE // state_count * (mean_power + EPSILON))
        chosen = band_index == class_index
        measured = measured + jnp.where(chosen[:, None, None, None], coarse * scaling[:, None, None, None], 0.0)
    return measured

def update(dynamics, band_index, previous, measured, occupied):
    state_index = jnp.arange(STATES)
    blocks = []
    for class_index in range(NCLASS):
        state_count = STATES // 2 ** class_index
        inside = state_index < state_count
        blocks.append(jnp.where(inside[:, None] & inside[None, :], dynamics[class_index], 0.0))
    masked = jnp.stack(blocks)
    selection = (band_index[:, None] == jnp.arange(NCLASS)[None, :]).astype(masked.dtype)
    picked = jnp.einsum('rk,kij->rij', selection, masked, precision=HIGHEST)
    updated = jnp.einsum('rij,rpcj->rpci', picked, previous, precision=HIGHEST) + measured
    return jnp.where(occupied[:, None, None, None], updated, 0.0)

def reference(profiles, band_edges, owner_counts, dynamics, prev_state):
    fine_real, fine_imag, bin_power = lax.map(tile_sums, profiles)
    mean_power = lax.optimization_barrier(jnp.sum(bin_power, axis=0)) / (PROFILES * TILE)
    stacked = jnp.stack([fine_real, fine_imag], axis=2)
    fine_all = jnp.transpose(stacked, (1, 0, 2, 3))
    tile_numbers = jnp.arange(NT, dtype=jnp.int32)
    band_all = lax.optimization_barrier(jnp.sum((tile_numbers[:, None] >= band_edges[None, 1:NCLASS]).astype(jnp.int32), axis=1))
    measured_all = measure(fine_all, mean_power, band_all)
    starts = jnp.cumsum(owner_counts) - owner_counts
    slot_index = jnp.arange(CAP, dtype=jnp.int32)
    wanted = (starts[:, None] + slot_index[None, :]).reshape(SLOTS)
    occupied = (slot_index[None, :] < owner_counts[:, None]).reshape(SLOTS)
    slot_tiles = jnp.clip(wanted, 0, NT - 1).astype(jnp.int32)
    measured = measured_all[slot_tiles]
    band_index = band_all[slot_tiles]
    previous = prev_state.reshape(SLOTS, PROFILES, 2, STATES)
    updated = update(dynamics, band_index, previous, measured, occupied)
    return updated.reshape(SLOTS, PROFILES, 2 * STATES)
```

```python
import functools
import math

import jax
import jax.numpy as jnp
import numpy as np
from jax import lax
from jax.experimental import pallas as pl
from jax.experimental.pallas import tpu as pltpu
from jax.sharding import PartitionSpec as P

TILE = 512
STATES = 64
NCLASS = 5
LANES = 128

EPSILON = 1e-05
HIGHEST = lax.Precision.HIGHEST
BF16 = jnp.bfloat16
F32 = jnp.float32


def unit_root(order, exponents):
    angles = 2.0 * np.pi * (np.asarray(exponents, dtype=np.int64) % order) / order
    return np.cos(angles), -np.sin(angles)


def two_terms(values):
    high = np.asarray(values, np.float32).astype(BF16)
    low = (np.asarray(values, np.float64) - high.astype(np.float64)).astype(BF16)
    return high, low


def three_terms(values):
    high, low = two_terms(values)
    rest = np.asarray(values, np.float64) - high.astype(np.float64) - low.astype(np.float64)
    return high, low, rest.astype(BF16)


def split_two(values):
    high = values.astype(BF16)
    return high, (values - high.astype(F32)).astype(BF16)


def split_three(values):
    high = values.astype(BF16)
    rest = values - high.astype(F32)
    middle = rest.astype(BF16)
    return high, middle, (rest - middle.astype(F32)).astype(BF16)


def dot(left, right):
    return jnp.dot(left, right, preferred_element_type=F32)


VMEM = pl.BlockSpec(memory_space=pltpu.VMEM)
SMEM = pl.BlockSpec(memory_space=pltpu.SMEM)


def coarse_tables(coarse, groups):
    total = coarse * groups * LANES
    k_index = np.arange(coarse)
    real, imag = unit_root(coarse, k_index[:, None] * np.arange(coarse)[None, :])
    dft = np.stack(two_terms(np.concatenate([real, imag])))
    turn = np.stack(unit_root(total, k_index[:, None] * np.arange(LANES)[None, :]))
    real, imag = unit_root(total // LANES, k_index[:, None] * np.arange(groups)[None, :])
    row_turn = np.concatenate(three_terms(np.concatenate([real, imag])), axis=1)
    return dft, turn.astype(np.float32), row_turn


def coarse_kernel(coarse, groups, shares, x_ref, dft_ref, turn_ref, row_ref, out_ref):
    own = lax.axis_index("bins")
    high, low = split_two(x_ref[...])
    both = dot(dft_ref[0], jnp.concatenate([high, low], axis=1))
    spectrum = both[:, :LANES] + both[:, LANES:] + dot(dft_ref[1], high)
    picked = lax.broadcasted_iota(jnp.int32, (3 * groups, LANES), 0) % groups == own
    row_turn = dot(row_ref[...], jnp.where(picked, 1.0, 0.0).astype(BF16))
    row_real, row_imag = row_turn[:coarse], row_turn[coarse:]
    turn_real = turn_ref[0] * row_real - turn_ref[1] * row_imag
    turn_imag = turn_ref[0] * row_imag + turn_ref[1] * row_real
    real, imag = spectrum[:coarse], spectrum[coarse:]
    rows = coarse // shares
    out_ref[:, :rows, :] = (real * turn_real - imag * turn_imag).reshape(shares, rows, LANES)
    out_ref[:, rows:, :] = (real * turn_imag + imag * turn_real).reshape(shares, rows, LANES)


def coarse_step(columns, groups, shares):
    coarse = columns.shape[0]
    dft, turn, row_turn = coarse_tables(coarse, groups)
    return pl.pallas_call(
        functools.partial(coarse_kernel, coarse, groups, shares),
        out_shape=jax.ShapeDtypeStruct((shares, 2 * coarse // shares, LANES), F32),
        in_specs=[VMEM] * 4,
        out_specs=VMEM,
        compiler_params=pltpu.CompilerParams(vmem_limit_bytes=32 << 20),
        name="coarse_dft",
    )(columns, jnp.asarray(dft), jnp.asarray(turn), jnp.asarray(row_turn))


def fine_tables(groups):
    turn = np.stack(
        unit_root(groups * LANES, np.arange(groups)[:, None] * np.arange(LANES)[None, :])
    )
    real, imag = unit_root(LANES, np.arange(LANES)[:, None] * np.arange(LANES // 2)[None, :])
    matrix = np.block([[real, imag], [-imag, real]])
    return turn.astype(np.float32), np.concatenate(two_terms(matrix), axis=1)


def eight_point(values):
    half = math.sqrt(0.5)

    def add(p, q):
        return (p[0] + q[0], p[1] + q[1])

    def sub(p, q):
        return (p[0] - q[0], p[1] - q[1])

    def down(p):
        return (p[1], -p[0])

    def four(a, b, c, d):
        s0, s1, s2, s3 = add(a, c), sub(a, c), add(b, d), down(sub(b, d))
        return add(s0, s2), add(s1, s3), sub(s0, s2), sub(s1, s3)

    even = four(values[0], values[2], values[4], values[6])
    odd = four(values[1], values[3], values[5], values[7])
    turned = [
        odd[0],
        ((odd[1][0] + odd[1][1]) * half, (odd[1][1] - odd[1][0]) * half),
        down(odd[2]),
        ((odd[3][1] - odd[3][0]) * half, -(odd[3][0] + odd[3][1]) * half),
    ]
    return [add(e, t) for e, t in zip(even, turned)] + [sub(e, t) for e, t in zip(even, turned)]


def fine_kernel(profiles, capacity, counts_ref, x_ref, turn_ref, matrix_ref, out_ref):
    groups = 8
    blocks = {}
    for p in range(profiles):
        pieces = [
            (x_ref[c * profiles + p, :8, :], x_ref[c * profiles + p, 8:, :]) for c in range(groups)
        ]
        for u, (real, imag) in enumerate(eight_point(pieces)):
            if u:
                turn_real, turn_imag = turn_ref[0, u : u + 1, :], turn_ref[1, u : u + 1, :]
                real, imag = (
                    real * turn_real - imag * turn_imag,
                    real * turn_imag + imag * turn_real,
                )
            blocks[u, p] = (real, imag)
    order = [(u, p) for u in range(groups) for p in range(profiles)]
    left = jnp.concatenate(
        [
            jnp.concatenate([blocks[at][0] for at in order], axis=0),
            jnp.concatenate([blocks[at][1] for at in order], axis=0),
        ],
        axis=1,
    )
    high, low = split_two(left)
    both = dot(high, matrix_ref[...])
    spectrum = both[:, :LANES] + both[:, LANES:] + dot(low, matrix_ref[:, :LANES])
    by_block = spectrum.reshape(groups * profiles, 8, LANES)
    fine = jnp.sum(by_block, axis=1, keepdims=True)
    power = jnp.sum(
        (spectrum * spectrum).reshape(groups // 2, 2 * profiles * 8, LANES), axis=1, keepdims=True
    )
    power = power + pltpu.roll(power.reshape(groups // 2, LANES), LANES // 2, 1).reshape(
        groups // 2, 1, LANES
    )
    row_kind = lax.broadcasted_iota(jnp.int32, (4 * profiles, LANES), 0)
    halves = []
    for pair in range(groups // 2):
        block = jnp.where(row_kind % 4 == 2, jnp.broadcast_to(power[pair], row_kind.shape), 0.0)
        for h in range(2):
            for p in range(profiles):
                piece = jnp.broadcast_to(fine[(2 * pair + h) * profiles + p], row_kind.shape)
                block = jnp.where(row_kind == 4 * p + h, piece, block)
        halves.append(block)
    half = LANES // 2
    left = jnp.concatenate(
        [
            jnp.concatenate([block[:, :half] for block in halves], axis=1),
            jnp.concatenate([block[:, half:] for block in halves], axis=1),
        ],
        axis=0,
    )
    owner_of = lax.broadcasted_iota(jnp.int32, (1, groups * capacity), 1)
    rank_of, owner_of = owner_of % capacity, owner_of // capacity
    wanted = jnp.full((1, groups * capacity), -1, jnp.int32)
    start = jnp.int32(0)
    for owner in range(groups):
        count = counts_ref[owner]
        wanted = jnp.where((owner_of == owner) & (rank_of < count), start + rank_of, wanted)
        start = start + count
    tile_of = lax.broadcasted_iota(jnp.int32, (groups // 2 * half, groups * capacity), 0)
    tile_of = tile_of // half + (groups // 2) * (tile_of % half)
    chosen = jnp.where(tile_of == wanted, 1.0, 0.0).astype(BF16)
    rows = left.shape[0]
    routed = dot(jnp.concatenate(split_three(left), axis=0), chosen)
    routed = routed[:rows] + routed[rows : 2 * rows] + routed[2 * rows :]
    for owner in range(groups):
        piece = routed[:, owner * capacity : (owner + 1) * capacity]
        block = jnp.concatenate([piece[: rows // 2], piece[rows // 2 :]], axis=1)
        out_ref[owner] = block


def fine_step(arrived, owner_counts, groups, profiles, capacity):
    turn, matrix = fine_tables(groups)
    out = pl.pallas_call(
        functools.partial(fine_kernel, profiles, capacity),
        out_shape=jax.ShapeDtypeStruct((groups, 4 * profiles, LANES), F32),
        in_specs=[SMEM] + [VMEM] * 3,
        out_specs=VMEM,
        compiler_params=pltpu.CompilerParams(vmem_limit_bytes=32 << 20),
        name="fine_dft",
    )(owner_counts, arrived, jnp.asarray(turn), jnp.asarray(matrix))
    return out.reshape(groups * profiles, 4, LANES)


def fine_step_general(arrived, owner_counts, groups, capacity):
    rows = arrived.shape[1] // 2
    real, imag = arrived[:, :rows], arrived[:, rows:]

    def turned(pattern, root, parts):
        cosine, sine = (jnp.asarray(part.astype(np.float32)) for part in root)
        mul = functools.partial(jnp.einsum, pattern, precision=HIGHEST)
        return (
            mul(cosine, parts[0]) - mul(sine, parts[1]),
            mul(cosine, parts[1]) + mul(sine, parts[0]),
        )

    group_index, lane_index = np.arange(groups), np.arange(LANES)
    parts = turned(
        "cu,crj->urj", unit_root(groups, group_index[:, None] * group_index), (real, imag)
    )
    parts = turned(
        "uj,urj->urj", unit_root(groups * LANES, group_index[:, None] * lane_index), parts
    )
    real, imag = turned(
        "jv,urj->vur", unit_root(LANES, lane_index[:, None] * lane_index[: LANES // 2]), parts
    )
    tiles = groups * LANES // 4
    power = jnp.sum((real * real + imag * imag).reshape(tiles, 2 * rows), axis=1)
    fine_real = jnp.sum(real.reshape(tiles, 2, rows), axis=2)
    fine_imag = jnp.sum(imag.reshape(tiles, 2, rows), axis=2)
    starts = jnp.cumsum(owner_counts) - owner_counts
    slot_index = jnp.arange(capacity, dtype=jnp.int32)
    filled = slot_index[None, :] < owner_counts[:, None]
    chosen = jnp.clip(starts[:, None] + slot_index[None, :], 0, tiles - 1)

    def routed(values):
        return jnp.where(filled, values[chosen], 0.0)

    empty = jnp.zeros((groups, capacity), F32)
    payload = [
        [routed(fine_real[:, 0]), routed(fine_imag[:, 0])],
        [routed(fine_real[:, 1]), routed(fine_imag[:, 1])],
        [routed(power), routed(power)],
        [empty, empty],
    ]
    return jnp.stack([jnp.concatenate(row, axis=1) for row in payload], axis=1)


def pool_table(shares):
    pool = np.zeros((shares, 4, 6, STATES), np.float32)
    for share in range(shares):
        for h in range(2):
            for band in range(NCLASS):
                pool[share, h, band, (share + shares * h) >> band] = 1.0
        pool[share, 2, NCLASS, :] = 1.0
    return np.tile(pool.reshape(shares * 4, 6 * STATES), (3, 1)).astype(BF16)


def update_kernel(count, edges_ref, counts_ref, x_ref, pool_ref, dynamics_ref, state_ref, out_ref):
    own = lax.axis_index("bins")
    groups = counts_ref.shape[0]
    capacity = state_ref.shape[0]
    wide = NCLASS * STATES

    def before(owner, start):
        return start + jnp.where(owner < own, counts_ref[owner], 0)

    start = lax.fori_loop(0, groups, before, jnp.int32(0))
    own_count = counts_ref[own]
    state = state_ref[...]
    state = jnp.concatenate([state[:, :STATES], state[:, STATES:]], axis=0)
    row = lax.broadcasted_iota(jnp.int32, (wide, STATES), 0)
    column = lax.broadcasted_iota(jnp.int32, (wide, STATES), 1)
    limit = STATES >> (row // STATES)
    inside = (row % STATES < limit) & (column < limit)
    dynamics = jnp.where(inside, dynamics_ref[...], 0.0)
    moved = lax.dot_general(
        state, dynamics, (((1,), (1,)), ((), ())), precision=HIGHEST, preferred_element_type=F32
    )
    moved = jnp.concatenate([moved, jnp.zeros((2 * capacity, STATES), F32)], axis=1)
    sums = lax.dot_general(
        jnp.concatenate(split_three(x_ref[...]), axis=0),
        pool_ref[...],
        (((0,), (0,)), ((), ())),
        preferred_element_type=F32,
    )
    slot = lax.broadcasted_iota(jnp.int32, (2 * capacity, 6 * STATES), 0) % capacity
    lane_band = lax.broadcasted_iota(jnp.int32, (2 * capacity, 6 * STATES), 1) // STATES
    band = jnp.zeros_like(slot)
    for edge in range(1, NCLASS):
        band = band + jnp.where(slot + start >= edges_ref[edge], 1, 0)
    wanted = lane_band == band

    def of_band(values):
        values = jnp.where(wanted, values, 0.0)
        folded = values[:, :LANES] + values[:, LANES : 2 * LANES] + values[:, 2 * LANES :]
        return folded[:, :STATES] + folded[:, STATES:]

    power = sums[:, wide:] * (1.0 / count)
    span = jnp.left_shift(TILE // STATES, band[:, :STATES]).astype(F32)
    scaling = 1.0 / jnp.sqrt(span * (power + EPSILON))
    result = of_band(moved) + of_band(sums) * scaling
    result = jnp.where(slot[:, :STATES] < own_count, result, 0.0)
    out_ref[...] = jnp.concatenate([result[:capacity], result[capacity:]], axis=1)


def update_step(arrived, band_edges, owner_counts, dynamics, state, count):
    shares = arrived.shape[0]
    return pl.pallas_call(
        functools.partial(update_kernel, count),
        out_shape=jax.ShapeDtypeStruct(state.shape, F32),
        in_specs=[SMEM, SMEM] + [VMEM] * 4,
        out_specs=VMEM,
        compiler_params=pltpu.CompilerParams(vmem_limit_bytes=32 << 20),
        name="state_update",
    )(
        band_edges,
        owner_counts,
        arrived.reshape(shares * 4, LANES),
        jnp.asarray(pool_table(shares)),
        dynamics.reshape(NCLASS * STATES, STATES),
        state,
    )


def exchanged(values, axes):
    return lax.all_to_all(values, axes, split_axis=0, concat_axis=0, tiled=True)


def body(profiles, band_edges, owner_counts, dynamics, prev_state):
    groups, scans = lax.axis_size("bins"), lax.axis_size("scans")
    prof_rows, length = profiles.shape
    capacity = prev_state.shape[0]
    coarse = length // LANES
    shares = TILE // 16
    count = prof_rows * scans * TILE
    columns = profiles.reshape(coarse // groups, groups, LANES).transpose(1, 0, 2)
    columns = exchanged(columns, "bins").reshape(coarse, LANES)
    if groups * scans == shares and groups == 8:
        blocks = coarse_step(columns, groups, shares)
        blocks = exchanged(blocks, ("bins", "scans"))
        payload = fine_step(blocks, owner_counts, groups, scans, capacity)
        arrived = exchanged(payload, ("bins", "scans"))
    else:
        blocks = coarse_step(columns, groups, groups)
        blocks = exchanged(blocks, "bins")
        payload = fine_step_general(blocks, owner_counts, groups, capacity)
        arrived = exchanged(payload, "bins")
        arrived = jnp.sum(arrived.reshape(shares, groups // shares, 4, LANES), axis=1)
        power = lax.psum(arrived[:, 2], "scans")
        arrived = jnp.concatenate([arrived[:, :2], power[:, None], arrived[:, 3:]], axis=1)
    state = prev_state.reshape(capacity, 2 * STATES)
    updated = update_step(arrived, band_edges, owner_counts, dynamics, state, count)
    return updated.reshape(prev_state.shape)


def solution(mesh):
    return jax.shard_map(
        body,
        mesh=mesh,
        in_specs=(P("scans", "bins"), P(), P(), P(), P("bins", "scans", None)),
        out_specs=P("bins", "scans", None),
        check_vma=False,
    )
```

```python
import functools
import math

import jax
import jax.numpy as jnp
import numpy as np
from jax import lax
from jax.experimental import pallas as pl
from jax.experimental.pallas import tpu as pltpu
from jax.sharding import PartitionSpec as P

TILE = 512
STATES = 64
NCLASS = 5
LANES = 128

EPSILON = 1e-05
HIGHEST = lax.Precision.HIGHEST
BF16 = jnp.bfloat16
F32 = jnp.float32


def unit_root(order, exponents):
    angles = 2.0 * np.pi * (np.asarray(exponents, dtype=np.int64) % order) / order
    return np.cos(angles), -np.sin(angles)


def two_terms(values):
    high = np.asarray(values, np.float32).astype(BF16)
    low = (np.asarray(values, np.float64) - high.astype(np.float64)).astype(BF16)
    return high, low


def three_terms(values):
    high, low = two_terms(values)
    rest = np.asarray(values, np.float64) - high.astype(np.float64) - low.astype(np.float64)
    return high, low, rest.astype(BF16)


def split_two(values):
    high = values.astype(BF16)
    return high, (values - high.astype(F32)).astype(BF16)


def split_three(values):
    high = values.astype(BF16)
    rest = values - high.astype(F32)
    middle = rest.astype(BF16)
    return high, middle, (rest - middle.astype(F32)).astype(BF16)


def dot(left, right):
    return jnp.dot(left, right, preferred_element_type=F32)


VMEM = pl.BlockSpec(memory_space=pltpu.VMEM)
SMEM = pl.BlockSpec(memory_space=pltpu.SMEM)


def coarse_table(coarse, groups):
    total = coarse * groups * LANES
    k_index = np.arange(coarse)

    def stacked(order, others):
        return np.concatenate(unit_root(order, k_index[:, None] * others[None, :]))

    columns = two_terms(stacked(coarse, np.arange(coarse)))
    columns += three_terms(stacked(total, np.arange(LANES)))
    columns += three_terms(stacked(total // LANES, np.arange(groups)))
    table = np.concatenate(columns, axis=1)
    return np.pad(table, [(0, 0), (0, -table.shape[1] % LANES)])


def coarse_kernel(coarse, groups, shares, x_ref, table_ref, out_ref):
    own = lax.axis_index("bins")
    high, low = split_two(x_ref[...])
    both = dot(table_ref[:, :coarse], jnp.concatenate([high, low], axis=1))
    spectrum = both[:, :LANES] + both[:, LANES:] + dot(table_ref[:, coarse : 2 * coarse], high)
    at = 2 * coarse
    turn = sum(table_ref[:, at + i * LANES : at + (i + 1) * LANES].astype(F32) for i in range(3))
    at += 3 * LANES
    entries = table_ref.shape[1] - at
    entry = lax.broadcasted_iota(jnp.int32, (entries, LANES), 0)
    picked = (entry % groups == own) & (entry < 3 * groups)
    row_turn = dot(table_ref[:, at:], jnp.where(picked, 1.0, 0.0).astype(BF16))
    row_real, row_imag = row_turn[:coarse], row_turn[coarse:]
    turn_real = turn[:coarse] * row_real - turn[coarse:] * row_imag
    turn_imag = turn[:coarse] * row_imag + turn[coarse:] * row_real
    real, imag = spectrum[:coarse], spectrum[coarse:]
    rows = coarse // shares
    out_ref[:, :rows, :] = (real * turn_real - imag * turn_imag).reshape(shares, rows, LANES)
    out_ref[:, rows:, :] = (real * turn_imag + imag * turn_real).reshape(shares, rows, LANES)


def coarse_step(columns, groups, shares):
    coarse = columns.shape[0]
    return pl.pallas_call(
        functools.partial(coarse_kernel, coarse, groups, shares),
        out_shape=jax.ShapeDtypeStruct((shares, 2 * coarse // shares, LANES), F32),
        in_specs=[VMEM] * 2,
        out_specs=VMEM,
        compiler_params=pltpu.CompilerParams(vmem_limit_bytes=32 << 20),
        name="coarse_dft",
    )(columns, jnp.asarray(coarse_table(coarse, groups)))


def fine_tables(groups):
    turn = np.stack(
        unit_root(groups * LANES, np.arange(groups)[:, None] * np.arange(LANES)[None, :])
    )
    real, imag = unit_root(LANES, np.arange(LANES)[:, None] * np.arange(LANES // 2)[None, :])
    matrix = np.block([[real, imag], [-imag, real]])
    return turn.astype(np.float32), np.concatenate(two_terms(matrix), axis=1)


def eight_point(values):
    half = math.sqrt(0.5)

    def add(p, q):
        return (p[0] + q[0], p[1] + q[1])

    def sub(p, q):
        return (p[0] - q[0], p[1] - q[1])

    def down(p):
        return (p[1], -p[0])

    def four(a, b, c, d):
        s0, s1, s2, s3 = add(a, c), sub(a, c), add(b, d), down(sub(b, d))
        return add(s0, s2), add(s1, s3), sub(s0, s2), sub(s1, s3)

    even = four(values[0], values[2], values[4], values[6])
    odd = four(values[1], values[3], values[5], values[7])
    turned = [
        odd[0],
        ((odd[1][0] + odd[1][1]) * half, (odd[1][1] - odd[1][0]) * half),
        down(odd[2]),
        ((odd[3][1] - odd[3][0]) * half, -(odd[3][0] + odd[3][1]) * half),
    ]
    return [add(e, t) for e, t in zip(even, turned)] + [sub(e, t) for e, t in zip(even, turned)]


def fine_kernel(profiles, capacity, counts_ref, x_ref, turn_ref, matrix_ref, out_ref):
    groups = 8
    blocks = {}
    for p in range(profiles):
        pieces = [
            (x_ref[c * profiles + p, :8, :], x_ref[c * profiles + p, 8:, :]) for c in range(groups)
        ]
        for u, (real, imag) in enumerate(eight_point(pieces)):
            if u:
                turn_real, turn_imag = turn_ref[0, u : u + 1, :], turn_ref[1, u : u + 1, :]
                real, imag = (
                    real * turn_real - imag * turn_imag,
                    real * turn_imag + imag * turn_real,
                )
            blocks[u, p] = (real, imag)
    order = [(u, p) for u in range(groups) for p in range(profiles)]
    left = jnp.concatenate(
        [
            jnp.concatenate([blocks[at][0] for at in order], axis=0),
            jnp.concatenate([blocks[at][1] for at in order], axis=0),
        ],
        axis=1,
    )
    high, low = split_two(left)
    both = dot(high, matrix_ref[...])
    spectrum = both[:, :LANES] + both[:, LANES:] + dot(low, matrix_ref[:, :LANES])
    by_block = spectrum.reshape(groups * profiles, 8, LANES)
    fine = jnp.sum(by_block, axis=1, keepdims=True)
    power = jnp.sum(
        (spectrum * spectrum).reshape(groups // 2, 2 * profiles * 8, LANES), axis=1, keepdims=True
    )
    power = power + pltpu.roll(power.reshape(groups // 2, LANES), LANES // 2, 1).reshape(
        groups // 2, 1, LANES
    )
    row_kind = lax.broadcasted_iota(jnp.int32, (4 * profiles, LANES), 0)
    halves = []
    for pair in range(groups // 2):
        block = jnp.where(row_kind % 4 == 2, jnp.broadcast_to(power[pair], row_kind.shape), 0.0)
        for h in range(2):
            for p in range(profiles):
                piece = jnp.broadcast_to(fine[(2 * pair + h) * profiles + p], row_kind.shape)
                block = jnp.where(row_kind == 4 * p + h, piece, block)
        halves.append(block)
    half = LANES // 2
    left = jnp.concatenate(
        [
            jnp.concatenate([block[:, :half] for block in halves], axis=1),
            jnp.concatenate([block[:, half:] for block in halves], axis=1),
        ],
        axis=0,
    )
    owner_of = lax.broadcasted_iota(jnp.int32, (1, groups * capacity), 1)
    rank_of, owner_of = owner_of % capacity, owner_of // capacity
    wanted = jnp.full((1, groups * capacity), -1, jnp.int32)
    start = jnp.int32(0)
    for owner in range(groups):
        count = counts_ref[owner]
        wanted = jnp.where((owner_of == owner) & (rank_of < count), start + rank_of, wanted)
        start = start + count
    tile_of = lax.broadcasted_iota(jnp.int32, (groups // 2 * half, groups * capacity), 0)
    tile_of = tile_of // half + (groups // 2) * (tile_of % half)
    chosen = jnp.where(tile_of == wanted, 1.0, 0.0).astype(BF16)
    rows = left.shape[0]
    routed = dot(jnp.concatenate(split_three(left), axis=0), chosen)
    routed = routed[:rows] + routed[rows : 2 * rows] + routed[2 * rows :]
    for owner in range(groups):
        piece = routed[:, owner * capacity : (owner + 1) * capacity]
        block = jnp.concatenate([piece[: rows // 2], piece[rows // 2 :]], axis=1)
        out_ref[owner] = block


def fine_step(arrived, owner_counts, groups, profiles, capacity):
    turn, matrix = fine_tables(groups)
    out = pl.pallas_call(
        functools.partial(fine_kernel, profiles, capacity),
        out_shape=jax.ShapeDtypeStruct((groups, 4 * profiles, LANES), F32),
        in_specs=[SMEM] + [VMEM] * 3,
        out_specs=VMEM,
        compiler_params=pltpu.CompilerParams(vmem_limit_bytes=32 << 20),
        name="fine_dft",
    )(owner_counts, arrived, jnp.asarray(turn), jnp.asarray(matrix))
    return out.reshape(groups * profiles, 4, LANES)


def fine_step_general(arrived, owner_counts, groups, capacity):
    rows = arrived.shape[1] // 2
    real, imag = arrived[:, :rows], arrived[:, rows:]

    def turned(pattern, root, parts):
        cosine, sine = (jnp.asarray(part.astype(np.float32)) for part in root)
        mul = functools.partial(jnp.einsum, pattern, precision=HIGHEST)
        return (
            mul(cosine, parts[0]) - mul(sine, parts[1]),
            mul(cosine, parts[1]) + mul(sine, parts[0]),
        )

    group_index, lane_index = np.arange(groups), np.arange(LANES)
    parts = turned(
        "cu,crj->urj", unit_root(groups, group_index[:, None] * group_index), (real, imag)
    )
    parts = turned(
        "uj,urj->urj", unit_root(groups * LANES, group_index[:, None] * lane_index), parts
    )
    real, imag = turned(
        "jv,urj->vur", unit_root(LANES, lane_index[:, None] * lane_index[: LANES // 2]), parts
    )
    tiles = groups * LANES // 4
    power = jnp.sum((real * real + imag * imag).reshape(tiles, 2 * rows), axis=1)
    fine_real = jnp.sum(real.reshape(tiles, 2, rows), axis=2)
    fine_imag = jnp.sum(imag.reshape(tiles, 2, rows), axis=2)
    starts = jnp.cumsum(owner_counts) - owner_counts
    slot_index = jnp.arange(capacity, dtype=jnp.int32)
    filled = slot_index[None, :] < owner_counts[:, None]
    chosen = jnp.clip(starts[:, None] + slot_index[None, :], 0, tiles - 1)

    def routed(values):
        return jnp.where(filled, values[chosen], 0.0)

    empty = jnp.zeros((groups, capacity), F32)
    payload = [
        [routed(fine_real[:, 0]), routed(fine_imag[:, 0])],
        [routed(fine_real[:, 1]), routed(fine_imag[:, 1])],
        [routed(power), routed(power)],
        [empty, empty],
    ]
    return jnp.stack([jnp.concatenate(row, axis=1) for row in payload], axis=1)


def pool_table(shares):
    pool = np.zeros((shares, 4, 6, STATES), np.float32)
    for share in range(shares):
        for h in range(2):
            for band in range(NCLASS):
                pool[share, h, band, (share + shares * h) >> band] = 1.0
        pool[share, 2, NCLASS, :] = 1.0
    return np.tile(pool.reshape(shares * 4, 6 * STATES), (3, 1)).astype(BF16)


def state_kernel(edges_ref, counts_ref, dynamics_ref, state_ref, moved_ref, band_ref):
    own = lax.axis_index("bins")
    groups = counts_ref.shape[0]
    capacity = state_ref.shape[0]
    wide = NCLASS * STATES

    def before(owner, start):
        return start + jnp.where(owner < own, counts_ref[owner], 0)

    start = lax.fori_loop(0, groups, before, jnp.int32(0))
    slot = lax.broadcasted_iota(jnp.int32, (2 * capacity, LANES), 0) % capacity
    band = jnp.zeros_like(slot)
    for edge in range(1, NCLASS):
        band = band + jnp.where(slot + start >= edges_ref[edge], 1, 0)
    band = jnp.where(slot < counts_ref[own], band, -1)
    band_ref[...] = band
    state = state_ref[...]
    state = jnp.concatenate([state[:, :STATES], state[:, STATES:]], axis=0)
    row = lax.broadcasted_iota(jnp.int32, (wide, STATES), 0)
    column = lax.broadcasted_iota(jnp.int32, (wide, STATES), 1)
    limit = STATES >> (row // STATES)
    inside = (row % STATES < limit) & (column < limit)
    dynamics = jnp.where(inside, dynamics_ref[...], 0.0)
    moved = lax.dot_general(
        state, dynamics, (((1,), (1,)), ((), ())), precision=HIGHEST, preferred_element_type=F32
    )
    moved = jnp.concatenate([moved, jnp.zeros((2 * capacity, STATES), F32)], axis=1)
    moved_ref[...] = of_band(moved, band)


def of_band(values, band):
    lane = lax.broadcasted_iota(jnp.int32, band.shape, 1) // STATES
    folded = jnp.zeros(band.shape, F32)
    for pair in range((NCLASS + 1) // 2):
        piece = values[:, pair * LANES : (pair + 1) * LANES]
        folded = folded + jnp.where(lane + 2 * pair == band, piece, 0.0)
    return folded[:, :STATES] + folded[:, STATES:]


def update_kernel(count, x_ref, pool_ref, moved_ref, band_ref, out_ref):
    capacity = out_ref.shape[0]
    band = band_ref[...]
    sums = lax.dot_general(
        jnp.concatenate(split_three(x_ref[...]), axis=0),
        pool_ref[...],
        (((0,), (0,)), ((), ())),
        preferred_element_type=F32,
    )
    power = sums[:, NCLASS * STATES :] * (1.0 / count)
    span = jnp.left_shift(TILE // STATES, jnp.maximum(band[:, :STATES], 0)).astype(F32)
    scaling = 1.0 / jnp.sqrt(span * (power + EPSILON))
    result = moved_ref[...] + of_band(sums, band) * scaling
    out_ref[...] = jnp.concatenate([result[:capacity], result[capacity:]], axis=1)


def state_step(band_edges, owner_counts, dynamics, state):
    rows = 2 * state.shape[0]
    return pl.pallas_call(
        state_kernel,
        out_shape=(
            jax.ShapeDtypeStruct((rows, STATES), F32),
            jax.ShapeDtypeStruct((rows, LANES), jnp.int32),
        ),
        in_specs=[SMEM, SMEM, VMEM, VMEM],
        out_specs=(VMEM, VMEM),
        compiler_params=pltpu.CompilerParams(vmem_limit_bytes=32 << 20),
        cost_estimate=pl.CostEstimate(flops=1 << 25, bytes_accessed=1 << 19, transcendentals=0),
        name="state_step",
    )(band_edges, owner_counts, dynamics.reshape(NCLASS * STATES, STATES), state)


def update_step(arrived, moved, band, count):
    shares = arrived.shape[0]
    return pl.pallas_call(
        functools.partial(update_kernel, count),
        out_shape=jax.ShapeDtypeStruct((moved.shape[0] // 2, 2 * STATES), F32),
        in_specs=[VMEM] * 4,
        out_specs=VMEM,
        compiler_params=pltpu.CompilerParams(vmem_limit_bytes=32 << 20),
        name="state_update",
    )(arrived.reshape(shares * 4, LANES), jnp.asarray(pool_table(shares)), moved, band)


def exchanged(values, axes):
    return lax.all_to_all(values, axes, split_axis=0, concat_axis=0, tiled=True)


def body(profiles, band_edges, owner_counts, dynamics, prev_state):
    groups, scans = lax.axis_size("bins"), lax.axis_size("scans")
    prof_rows, length = profiles.shape
    capacity = prev_state.shape[0]
    coarse = length // LANES
    shares = TILE // 16
    count = prof_rows * scans * TILE
    state = prev_state.reshape(capacity, 2 * STATES)
    moved, band = state_step(band_edges, owner_counts, dynamics, state)
    columns = profiles.reshape(coarse // groups, groups, LANES).transpose(1, 0, 2)
    columns = exchanged(columns, "bins").reshape(coarse, LANES)
    if groups * scans == shares and groups == 8:
        blocks = coarse_step(columns, groups, shares)
        blocks = exchanged(blocks, ("bins", "scans"))
        payload = fine_step(blocks, owner_counts, groups, scans, capacity)
        arrived = exchanged(payload, ("bins", "scans"))
    else:
        blocks = coarse_step(columns, groups, groups)
        blocks = exchanged(blocks, "bins")
        payload = fine_step_general(blocks, owner_counts, groups, capacity)
        arrived = exchanged(payload, "bins")
        arrived = jnp.sum(arrived.reshape(shares, groups // shares, 4, LANES), axis=1)
        power = lax.psum(arrived[:, 2], "scans")
        arrived = jnp.concatenate([arrived[:, :2], power[:, None], arrived[:, 3:]], axis=1)
    updated = update_step(arrived, moved, band, count)
    return updated.reshape(prev_state.shape)


def solution(mesh):
    return jax.shard_map(
        body,
        mesh=mesh,
        in_specs=(P("scans", "bins"), P(), P(), P(), P("bins", "scans", None)),
        out_specs=P("bins", "scans", None),
        check_vma=False,
    )
```

```python
import functools
import math

import jax
import jax.numpy as jnp
import numpy as np
from jax import lax
from jax.experimental import pallas as pl
from jax.experimental.pallas import tpu as pltpu
from jax.sharding import PartitionSpec as P

TILE = 512
STATES = 64
NCLASS = 5
LANES = 128

EPSILON = 1e-05
HIGHEST = lax.Precision.HIGHEST
BF16 = jnp.bfloat16
F32 = jnp.float32


def unit_root(order, exponents):
    angles = 2.0 * np.pi * (np.asarray(exponents, dtype=np.int64) % order) / order
    return np.cos(angles), -np.sin(angles)


def two_terms(values):
    high = np.asarray(values, np.float32).astype(BF16)
    low = (np.asarray(values, np.float64) - high.astype(np.float64)).astype(BF16)
    return high, low


def split_two(values):
    high = values.astype(BF16)
    return high, (values - high.astype(F32)).astype(BF16)


def dot(left, right):
    return jnp.dot(left, right, preferred_element_type=F32)


VMEM = pl.BlockSpec(memory_space=pltpu.VMEM)
SMEM = pl.BlockSpec(memory_space=pltpu.SMEM)


KINDS = 8


def doubled(values):
    return jnp.concatenate([values, values], axis=0)


def coarse_table(coarse, shares):
    half = coarse // 2
    real, imag = unit_root(coarse, np.arange(half)[:, None] * np.arange(coarse)[None, :])
    imag[0] = 1 - 2 * (np.arange(coarse) % 2)
    rows = half // shares
    parts = [part.reshape(shares, 1, rows, coarse) for part in (real, imag)]
    return np.concatenate(two_terms(np.concatenate(parts, axis=1).reshape(coarse, coarse)), axis=1)


def coarse_kernel(x_ref, table_ref, out_ref):
    coarse = x_ref.shape[0]
    high, low = split_two(x_ref[...])
    both = dot(table_ref[:, :coarse], jnp.concatenate([high, low], axis=1))
    out_ref[...] = both[:, :LANES] + both[:, LANES:] + dot(table_ref[:, coarse:], high)


def coarse_step(columns, shares):
    coarse = columns.shape[0]
    out = pl.pallas_call(
        coarse_kernel,
        out_shape=jax.ShapeDtypeStruct(columns.shape, F32),
        in_specs=[VMEM] * 2,
        out_specs=VMEM,
        compiler_params=pltpu.CompilerParams(vmem_limit_bytes=32 << 20),
        name="coarse_dft",
    )(columns, jnp.asarray(coarse_table(coarse, shares)))
    return out.reshape(shares, coarse // shares, LANES)


def fine_tables(groups, profiles, coarse):
    total = coarse * groups * LANES
    turn = unit_root(groups * LANES, np.arange(groups)[:, None] * np.arange(LANES)[None, :])
    extra = unit_root(total, np.arange(groups * LANES) * (coarse // 2))
    extra = [np.repeat(part.reshape(groups, 1, LANES), profiles, axis=1) for part in extra]
    lanes = np.arange(LANES)
    order = np.where(lanes < LANES // 2, lanes, LANES - 1 - (lanes - LANES // 2))
    high, low = two_terms(np.concatenate(unit_root(LANES, lanes[:, None] * order[None, :]), axis=1))
    turns = np.concatenate([np.concatenate(turn), np.concatenate(extra, axis=1).reshape(-1, LANES)])
    return turns.astype(np.float32), np.concatenate([high, low], axis=1)


def sum_table(profiles):
    table = np.zeros((2, 2, profiles, KINDS, 96), np.float32)
    for part in range(2):
        for p in range(profiles):
            for h in range(2):
                first = (h * profiles + p) * 8 + part * 4
                sign = 1 - 2 * part
                table[0, part, p, h, first : first + 4] = 1
                table[1, part, p, 2 + h, first + 1 : first + 4] = sign
                table[1, part, p, 4 + h, first] = sign
                table[0, part, p, 4 + h, 16 * profiles + h * 8 + part * 4 + p] = 1
            table[:, part, p, 6, 80:88] = 1
    return np.tile(table.reshape(-1, 96), (1, 2)).astype(BF16)


def unit_turn(phase, order):
    shifted = phase + order // 8
    quadrant = (shifted >> (order.bit_length() - 3)) & 3
    x = ((shifted & (order // 4 - 1)) - order // 8).astype(F32) * (2.0 * math.pi / order)
    y = x * x
    cosine = 1.0 + y * (-1 / 2 + y * (1 / 24 + y * (-1 / 720 + y * (1 / 40320))))
    sine = x * (1.0 + y * (-1 / 6 + y * (1 / 120 + y * (-1 / 5040 + y * (1 / 362880)))))
    odd = (quadrant & 1) == 1
    real, imag = jnp.where(odd, sine, cosine), jnp.where(odd, cosine, sine)
    real = jnp.where((quadrant == 1) | (quadrant == 2), -real, real)
    return real, jnp.where(quadrant >= 2, -imag, imag)


def eight_point(values, down):
    half = math.sqrt(0.5)

    def four(a, b, c, d):
        s0, s1, s2, s3 = a + c, a - c, b + d, down(b - d)
        return s0 + s2, s1 + s3, s0 - s2, s1 - s3

    even = four(values[0], values[2], values[4], values[6])
    odd = four(values[1], values[3], values[5], values[7])
    turned = [
        odd[0],
        (odd[1] + down(odd[1])) * half,
        down(odd[2]),
        (down(odd[3]) - odd[3]) * half,
    ]
    return [e + t for e, t in zip(even, turned)] + [e - t for e, t in zip(even, turned)]


def fine_kernel(
    profiles,
    order,
    edges_ref,
    counts_ref,
    x_ref,
    turns_ref,
    matrix_ref,
    sums_ref,
    dynamics_ref,
    state_ref,
    out_ref,
    moved_ref,
    band_ref,
):
    groups = counts_ref.shape[0]
    capacity = state_ref.shape[0]
    own = lax.axis_index("bins") * profiles + lax.axis_index("scans")
    row = lax.broadcasted_iota(jnp.int32, (8, LANES), 0)
    lane = lax.broadcasted_iota(jnp.int32, (8, LANES), 1)
    low_side = lane < LANES // 2
    first = own == 0
    side = jnp.where(row < 4, -1.0, 1.0)

    def swapped(values):
        return pltpu.roll(values, 4, 0)

    def down(values):
        return swapped(values) * -side

    columns = [[] for _ in range(profiles + 1)]
    for c in range(groups):
        cosine, sine = unit_turn(((c * LANES + lane) * (4 * own + (row & 3))) & (order - 1), order)
        sine = sine * -side
        real_only = []
        for p in range(profiles):
            block = x_ref[c * profiles + p]
            real_only.append(block[4:5])
            block = jnp.where(first & (row == 4), 0.0, block)
            columns[p].append(block * cosine + swapped(block) * sine)
        block = doubled(jnp.concatenate(real_only, axis=0))
        turn = turns_ref[2 * groups + 8 * c : 2 * groups + 8 * (c + 1), :]
        columns[profiles].append(jnp.where(first, block * turn, 0.0))
    transformed = [eight_point(column, down) for column in columns]
    blocks = []
    for u in range(groups):
        cosine, sine = turns_ref[u : u + 1, :], turns_ref[groups + u : groups + u + 1, :] * side
        for column in transformed:
            block = column[u]
            blocks.append(block * cosine + swapped(block) * sine if u else block)
    high, low = split_two(jnp.concatenate(blocks, axis=0))
    wide = 2 * LANES
    product = dot(high, matrix_ref[...])
    product = product[:, :wide] + product[:, wide:] + dot(low, matrix_ref[:, :wide])
    spectrum = []
    for at in range(len(blocks)):
        piece = product[8 * at : 8 * (at + 1)]
        block = piece[:, :LANES] + swapped(piece[:, LANES:]) * side
        if at % (profiles + 1) < profiles:
            block = jnp.where(first & ~low_side & ((row & 3) == 0), 0.0, block)
        else:
            block = jnp.where(low_side, block, 0.0)
        spectrum.append(block)
    spectrum = [
        spectrum[u * (profiles + 1) : (u + 1) * (profiles + 1)] for u in range(groups)
    ]
    pairs = groups // 2
    power = [
        sum(block * block for block in spectrum[2 * q] + spectrum[2 * q + 1]) for q in range(pairs)
    ]
    summands = []
    for q in range(pairs):
        rows = []
        for h in range(2):
            for p in range(profiles):
                high_block = spectrum[groups - 1 - 2 * q - h][p]
                rows.append(jnp.where(low_side, spectrum[2 * q + h][p], high_block))
        rows += [spectrum[2 * q + h][profiles] for h in range(2)]
        rows.append(jnp.where(low_side, power[q], power[pairs - 1 - q]))
        rows.append(jnp.zeros((8, LANES), F32))
        summands.append(jnp.concatenate(rows, axis=0))
    summed = dot(
        sums_ref[...],
        jnp.concatenate(split_two(jnp.concatenate(summands, axis=1)), axis=0),
    )
    rows, half = summed.shape[0] // 2, LANES // 2
    left = jnp.concatenate(
        [
            summed[:rows, q * LANES : q * LANES + half]
            + summed[rows:, q * LANES + half : (q + 1) * LANES]
            for q in range(pairs)
        ],
        axis=1,
    )
    owner_of = lax.broadcasted_iota(jnp.int32, (1, groups * capacity), 1)
    rank_of, owner_of = owner_of & (capacity - 1), owner_of >> (capacity.bit_length() - 1)
    wanted = jnp.full((1, groups * capacity), -1, jnp.int32)
    start = jnp.int32(0)
    for owner in range(groups):
        count = counts_ref[owner]
        wanted = jnp.where((owner_of == owner) & (rank_of < count), start + rank_of, wanted)
        start = start + count
    tile_of = lax.broadcasted_iota(jnp.int32, (pairs * half, groups * capacity), 0)
    tile_of = (tile_of >> (half.bit_length() - 1)) + pairs * (tile_of & (half - 1))
    chosen = jnp.where(tile_of == wanted, 1.0, 0.0).astype(BF16)
    routed = dot(jnp.concatenate(split_two(left), axis=0), chosen)
    routed = routed[:rows] + routed[rows:]
    for owner in range(groups):
        piece = routed[:, owner * capacity : (owner + 1) * capacity]
        out_ref[owner] = jnp.concatenate([piece[: rows // 2], piece[rows // 2 :]], axis=1)
    state_kernel(edges_ref, counts_ref, dynamics_ref, state_ref, moved_ref, band_ref)


def fine_step(arrived, band_edges, owner_counts, dynamics, state, profiles, coarse):
    groups, capacity = owner_counts.shape[0], state.shape[0]
    turns, matrix = fine_tables(groups, profiles, coarse)
    out, moved, band = pl.pallas_call(
        functools.partial(fine_kernel, profiles, coarse * groups * LANES),
        out_shape=(
            jax.ShapeDtypeStruct((groups, profiles * KINDS, LANES), F32),
            jax.ShapeDtypeStruct((2 * capacity, STATES), F32),
            jax.ShapeDtypeStruct((2 * capacity, LANES), jnp.int32),
        ),
        in_specs=[SMEM] * 2 + [VMEM] * 6,
        out_specs=(VMEM,) * 3,
        compiler_params=pltpu.CompilerParams(vmem_limit_bytes=32 << 20),
        name="fine_dft",
    )(
        band_edges,
        owner_counts,
        arrived,
        jnp.asarray(turns),
        jnp.asarray(matrix),
        jnp.asarray(sum_table(profiles)),
        dynamics.reshape(NCLASS * STATES, STATES),
        state,
    )
    return out.reshape(groups * profiles, KINDS, LANES), moved, band


def fine_step_general(arrived, owner_counts, capacity):
    groups, rows = arrived.shape[0], arrived.shape[1] // 2
    coarse = 2 * rows * groups
    fine_length = groups * LANES
    own = lax.axis_index("bins")
    real, imag = arrived[:, :rows], arrived[:, rows:]
    points = jnp.arange(fine_length, dtype=jnp.int32).reshape(groups, 1, LANES)
    k_index = own * rows + jnp.arange(rows, dtype=jnp.int32)[None, :, None]
    cosine, sine = unit_turn(points * k_index & (coarse * fine_length - 1), coarse * fine_length)
    packed = (own == 0) & (jnp.arange(rows)[None, :, None] == 0)
    middle = jnp.where(own == 0, imag[:, :1], 0.0)
    imag = jnp.where(packed, 0.0, imag)
    real, imag = real * cosine + imag * sine, imag * cosine - real * sine
    cosine, sine = unit_turn(points * (coarse // 2), coarse * fine_length)
    real = jnp.concatenate([real, middle * cosine], axis=1)
    imag = jnp.concatenate([imag, -middle * sine], axis=1)

    def turned(pattern, root, parts):
        cosine, sine = (jnp.asarray(part.astype(np.float32)) for part in root)
        mul = functools.partial(jnp.einsum, pattern, precision=HIGHEST)
        return (
            mul(cosine, parts[0]) - mul(sine, parts[1]),
            mul(cosine, parts[1]) + mul(sine, parts[0]),
        )

    group_index, lane_index = np.arange(groups), np.arange(LANES)
    parts = turned(
        "cu,crj->urj", unit_root(groups, group_index[:, None] * group_index), (real, imag)
    )
    parts = turned(
        "uj,urj->urj", unit_root(fine_length, group_index[:, None] * lane_index), parts
    )
    real, imag = (
        part.reshape(fine_length, rows + 1)
        for part in turned(
            "jv,urj->vur", unit_root(LANES, lane_index[:, None] * lane_index), parts
        )
    )
    half, tiles = fine_length // 2, fine_length // 4
    kept = jnp.concatenate([~packed[0, :, 0], jnp.zeros((1,), bool)])

    def sides(part, sign):
        low = part[:half].reshape(tiles, 2, rows + 1)
        high = sign * jnp.where(kept, part[half:][::-1], 0.0).reshape(tiles, 2, rows + 1)
        return low, high

    low_real, high_real = sides(real, 1.0)
    low_imag, high_imag = sides(imag, -1.0)
    power = sum(
        jnp.sum(part * part, axis=(1, 2)) for part in (low_real, high_real, low_imag, high_imag)
    )
    starts = jnp.cumsum(owner_counts) - owner_counts
    slot_index = jnp.arange(capacity, dtype=jnp.int32)
    filled = slot_index[None, :] < owner_counts[:, None]
    chosen = jnp.clip(starts[:, None] + slot_index[None, :], 0, tiles - 1)

    def kinds(low, high):
        low_sums = jnp.sum(low[:, :, :rows], axis=2)
        high_sums = jnp.sum(high[:, :, 1:rows], axis=2)
        rest = high[:, :, 0] + low[:, :, rows]
        last = jnp.stack([power, jnp.zeros_like(power)], axis=1)
        values = jnp.concatenate([low_sums, high_sums, rest, last], axis=1)
        return jnp.where(filled[:, :, None], values[chosen], 0.0).transpose(0, 2, 1)

    return jnp.concatenate([kinds(low_real, high_real), kinds(low_imag, high_imag)], axis=2)


def pool_table(shares, coarse):
    pool = np.zeros((shares, KINDS, 6, STATES), np.float32)
    wide = TILE // STATES
    rows = coarse // 2 // shares
    for share in range(shares):
        first = rows * share
        rest = coarse - first if share else coarse // 2
        for kind, at in ((0, first), (2, coarse - first - 1), (4, rest)):
            for h in range(2):
                for band in range(NCLASS):
                    pool[share, kind + h, band, (at + coarse * h) // wide >> band] = 1.0
        pool[share, 6, NCLASS, :] = 1.0
    return pool.reshape(shares * KINDS, 6 * STATES).astype(BF16)


def state_kernel(edges_ref, counts_ref, dynamics_ref, state_ref, moved_ref, band_ref):
    own = lax.axis_index("bins")
    groups = counts_ref.shape[0]
    capacity = state_ref.shape[0]
    wide = NCLASS * STATES

    def before(owner, start):
        return start + jnp.where(owner < own, counts_ref[owner], 0)

    start = lax.fori_loop(0, groups, before, jnp.int32(0))
    slot = lax.broadcasted_iota(jnp.int32, (2 * capacity, LANES), 0) & (capacity - 1)
    band = jnp.zeros_like(slot)
    for edge in range(1, NCLASS):
        band = band + jnp.where(slot + start >= edges_ref[edge], 1, 0)
    band = jnp.where(slot < counts_ref[own], band, -1)
    band_ref[...] = band
    state = state_ref[...]
    state = jnp.concatenate([state[:, :STATES], state[:, STATES:]], axis=0)
    row = lax.broadcasted_iota(jnp.int32, (wide, STATES), 0)
    column = lax.broadcasted_iota(jnp.int32, (wide, STATES), 1)
    limit = STATES >> (row >> 6)
    inside = ((row & (STATES - 1)) < limit) & (column < limit)
    dynamics = jnp.where(inside, dynamics_ref[...], 0.0)
    moved = lax.dot_general(
        state, dynamics, (((1,), (1,)), ((), ())), precision=HIGHEST, preferred_element_type=F32
    )
    moved = jnp.concatenate([moved, jnp.zeros((2 * capacity, STATES), F32)], axis=1)
    moved_ref[...] = of_band(moved, band)


def of_band(values, band):
    lane = lax.broadcasted_iota(jnp.int32, band.shape, 1) >> 6
    folded = jnp.zeros(band.shape, F32)
    for pair in range((NCLASS + 1) // 2):
        piece = values[:, pair * LANES : (pair + 1) * LANES]
        folded = folded + jnp.where(lane + 2 * pair == band, piece, 0.0)
    return folded[:, :STATES] + folded[:, STATES:]


def update_kernel(count, x_ref, pool_ref, moved_ref, band_ref, out_ref):
    capacity = out_ref.shape[0]
    band = band_ref[...]
    sums = lax.dot_general(
        jnp.concatenate(split_two(x_ref[...]), axis=1),
        pool_ref[...],
        (((0,), (0,)), ((), ())),
        preferred_element_type=F32,
    )
    sums = sums[: 2 * capacity] + sums[2 * capacity :]
    power = sums[:, NCLASS * STATES :] * (1.0 / count)
    span = jnp.left_shift(TILE // STATES, jnp.maximum(band[:, :STATES], 0)).astype(F32)
    scaling = 1.0 / jnp.sqrt(span * (power + EPSILON))
    result = moved_ref[...] + of_band(sums, band) * scaling
    out_ref[...] = jnp.concatenate([result[:capacity], result[capacity:]], axis=1)


def state_step(band_edges, owner_counts, dynamics, state):
    rows = 2 * state.shape[0]
    return pl.pallas_call(
        state_kernel,
        out_shape=(
            jax.ShapeDtypeStruct((rows, STATES), F32),
            jax.ShapeDtypeStruct((rows, LANES), jnp.int32),
        ),
        in_specs=[SMEM, SMEM, VMEM, VMEM],
        out_specs=(VMEM, VMEM),
        compiler_params=pltpu.CompilerParams(vmem_limit_bytes=32 << 20),
        cost_estimate=pl.CostEstimate(flops=1 << 25, bytes_accessed=1 << 19, transcendentals=0),
        name="state_step",
    )(band_edges, owner_counts, dynamics.reshape(NCLASS * STATES, STATES), state)


def update_step(arrived, moved, band, coarse, count):
    shares = arrived.shape[0]
    return pl.pallas_call(
        functools.partial(update_kernel, count),
        out_shape=jax.ShapeDtypeStruct((moved.shape[0] // 2, 2 * STATES), F32),
        in_specs=[VMEM] * 4,
        out_specs=VMEM,
        compiler_params=pltpu.CompilerParams(vmem_limit_bytes=32 << 20),
        name="state_update",
    )(arrived.reshape(shares * KINDS, LANES), jnp.asarray(pool_table(shares, coarse)), moved, band)


def exchanged(values, axes):
    return lax.all_to_all(values, axes, split_axis=0, concat_axis=0, tiled=True)


def body(profiles, band_edges, owner_counts, dynamics, prev_state):
    groups, scans = lax.axis_size("bins"), lax.axis_size("scans")
    prof_rows, length = profiles.shape
    capacity = prev_state.shape[0]
    coarse = length // LANES
    shares = groups * scans
    count = prof_rows * scans * TILE
    state = prev_state.reshape(capacity, 2 * STATES)
    columns = profiles.reshape(coarse // groups, groups, LANES).transpose(1, 0, 2)
    columns = exchanged(columns, "bins").reshape(coarse, LANES)
    if groups == 8 and scans == 4 and coarse == 8 * shares:
        blocks = exchanged(coarse_step(columns, shares), ("bins", "scans"))
        payload, moved, band = fine_step(
            blocks, band_edges, owner_counts, dynamics, state, scans, coarse
        )
        arrived = exchanged(payload, ("bins", "scans"))
    else:
        moved, band = state_step(band_edges, owner_counts, dynamics, state)
        blocks = exchanged(coarse_step(columns, groups), "bins")
        arrived = exchanged(fine_step_general(blocks, owner_counts, capacity), "bins")
        power = lax.psum(arrived[:, 6:7], "scans")
        arrived = jnp.concatenate([arrived[:, :6], power, arrived[:, 7:]], axis=1)
    updated = update_step(arrived, moved, band, coarse, count)
    return updated.reshape(prev_state.shape)


def solution(mesh):
    return jax.shard_map(
        body,
        mesh=mesh,
        in_specs=(P("scans", "bins"), P(), P(), P(), P("bins", "scans", None)),
        out_specs=P("bins", "scans", None),
        check_vma=False,
    )
```

```python
import functools
import math

import jax
import jax.numpy as jnp
import numpy as np
from jax import lax
from jax.experimental import pallas as pl
from jax.experimental.pallas import tpu as pltpu
from jax.sharding import PartitionSpec as P

TILE = 512
STATES = 64
NCLASS = 5
LANES = 128

EPSILON = 1e-05
HIGHEST = lax.Precision.HIGHEST
BF16 = jnp.bfloat16
F32 = jnp.float32


def unit_root(order, exponents):
    angles = 2.0 * np.pi * (np.asarray(exponents, dtype=np.int64) % order) / order
    return np.cos(angles), -np.sin(angles)


def two_terms(values):
    high = np.asarray(values, np.float32).astype(BF16)
    low = (np.asarray(values, np.float64) - high.astype(np.float64)).astype(BF16)
    return high, low


def split_two(values):
    high = values.astype(BF16)
    return high, (values - high.astype(F32)).astype(BF16)


def dot(left, right):
    return jnp.dot(left, right, preferred_element_type=F32)


VMEM = pl.BlockSpec(memory_space=pltpu.VMEM)
SMEM = pl.BlockSpec(memory_space=pltpu.SMEM)


KINDS = 4
HALF = LANES // 2


def columns_kernel(x_ref, out_ref):
    groups, rows, _ = out_ref.shape
    low_lanes = lax.broadcasted_iota(jnp.int32, (rows, LANES), 1) < HALF
    for pair in range(groups // 2):
        even = x_ref[pl.ds(pair, rows, stride=groups), :]
        odd = x_ref[pl.ds(groups // 2 + pair, rows, stride=groups), :]
        out_ref[2 * pair] = jnp.where(low_lanes, even, pltpu.roll(odd, HALF, 1))
        out_ref[2 * pair + 1] = jnp.where(low_lanes, pltpu.roll(even, HALF, 1), odd)


def columns_step(profile, groups):
    rows = profile.shape[0] // (groups * LANES)
    return pl.pallas_call(
        columns_kernel,
        out_shape=jax.ShapeDtypeStruct((groups, rows, LANES), F32),
        in_specs=[VMEM],
        out_specs=VMEM,
        compiler_params=pltpu.CompilerParams(vmem_limit_bytes=32 << 20),
        name="columns",
    )(profile.reshape(-1, LANES))


def coarse_table(coarse):
    half = coarse // 2
    real, imag = unit_root(half, np.arange(half)[:, None] * np.arange(half)[None, :])
    imag[0] = real[0]
    return np.concatenate(two_terms(np.concatenate([real, imag])), axis=1)


def coarse_kernel(x_ref, table_ref, out_ref):
    half = x_ref.shape[0]
    high, low = split_two(x_ref[...])
    both = dot(table_ref[:, :half], jnp.concatenate([high, low], axis=1))
    spectrum = both[:, :LANES] + both[:, LANES:] + dot(table_ref[:, half:], high)
    row = lax.broadcasted_iota(jnp.int32, (8, LANES), 0)
    low_lanes = lax.broadcasted_iota(jnp.int32, (8, LANES), 1) < HALF
    row_cosine, row_sine = unit_turn(row, 2 * half)
    side = jnp.where(low_lanes, 1.0, -1.0)
    for share in range(out_ref.shape[0]):
        real = spectrum[8 * share : 8 * (share + 1)]
        imag = spectrum[half + 8 * share : half + 8 * (share + 1)]
        even = jnp.where(low_lanes, real, pltpu.roll(imag, HALF, 1))
        odd = jnp.where(low_lanes, pltpu.roll(real, HALF, 1), imag)
        angle = math.pi * 8 * share / half
        cosine = row_cosine * math.cos(angle) - row_sine * math.sin(angle)
        sine = row_sine * math.cos(angle) + row_cosine * math.sin(angle)
        if share == 0:
            cosine = jnp.where((row == 0) & ~low_lanes, -1.0, cosine)
        out_ref[share] = even + odd * cosine + pltpu.roll(odd, HALF, 1) * (sine * side)


def coarse_step(columns):
    half = columns.shape[0]
    return pl.pallas_call(
        coarse_kernel,
        out_shape=jax.ShapeDtypeStruct((half // 8, 8, LANES), F32),
        in_specs=[VMEM] * 2,
        out_specs=VMEM,
        compiler_params=pltpu.CompilerParams(vmem_limit_bytes=32 << 20),
        name="coarse_dft",
    )(columns, jnp.asarray(coarse_table(2 * half)))


def coarse_step_general(columns, shares):
    coarse = columns.shape[0]
    half = coarse // 2
    real, imag = unit_root(coarse, np.arange(half)[:, None] * np.arange(coarse)[None, :])
    imag[0] = 1 - 2 * (np.arange(coarse) % 2)
    table = jnp.asarray(np.concatenate([real, imag]).astype(np.float32))
    spectrum = jnp.dot(table, columns, precision=HIGHEST)
    blocks = jnp.concatenate([spectrum[:half], spectrum[half:]], axis=1)
    return blocks.reshape(shares, half // shares, LANES)


def fine_tables(groups, profiles, coarse):
    fine_length = groups * HALF
    doubled = np.arange(LANES) % HALF
    turn = unit_root(fine_length, np.arange(groups)[:, None] * doubled[None, :])
    extra = unit_root(coarse * fine_length, np.arange(fine_length) * (coarse // 2))
    extra = np.concatenate([part.reshape(groups, HALF) for part in extra], axis=1)
    turns = np.concatenate([turn[0], turn[1], extra]).astype(np.float32)
    order = np.arange(HALF)
    order[HALF // 2 :] = order[HALF // 2 :][::-1]
    real, imag = unit_root(HALF, np.arange(HALF)[:, None] * order[None, :])
    sign = np.where(np.arange(HALF) < HALF // 2, 1, -1)
    matrix = np.block([[real, imag * sign], [-imag, real * sign]])
    sums = np.zeros((2, profiles, KINDS, 2, 6, 8), np.float32)
    for p in range(profiles):
        sums[0, p, 0, :, p, :] = 1
        sums[1, p, 1, :, p, 1:] = 1
        sums[1, p, 2, :, p, 0] = 1
        sums[0, p, 2, :, profiles, p] = 1
        sums[:, p, 3, :, profiles + 1, :] = 1
    sums = sums.reshape(2 * profiles * KINDS, -1)
    sums = np.pad(sums, [(0, 0), (0, 2 * LANES - sums.shape[1])]).astype(BF16)
    return turns, np.concatenate([np.concatenate(two_terms(matrix), axis=1), sums])


def unit_turn(phase, order):
    shifted = phase + order // 8
    quadrant = (shifted >> (order.bit_length() - 3)) & 3
    x = ((shifted & (order // 4 - 1)) - order // 8).astype(F32) * (2.0 * math.pi / order)
    y = x * x
    cosine = 1.0 + y * (-1 / 2 + y * (1 / 24 + y * (-1 / 720 + y * (1 / 40320))))
    sine = x * (1.0 + y * (-1 / 6 + y * (1 / 120 + y * (-1 / 5040 + y * (1 / 362880)))))
    odd = (quadrant & 1) == 1
    real, imag = jnp.where(odd, sine, cosine), jnp.where(odd, cosine, sine)
    real = jnp.where((quadrant == 1) | (quadrant == 2), -real, real)
    return real, jnp.where(quadrant >= 2, -imag, imag)


def eight_point(values, down):
    half = math.sqrt(0.5)

    def four(a, b, c, d):
        s0, s1, s2, s3 = a + c, a - c, b + d, down(b - d)
        return s0 + s2, s1 + s3, s0 - s2, s1 - s3

    even = four(values[0], values[2], values[4], values[6])
    odd = four(values[1], values[3], values[5], values[7])
    turned = [
        odd[0],
        (odd[1] + down(odd[1])) * half,
        down(odd[2]),
        (down(odd[3]) - odd[3]) * half,
    ]
    return [e + t for e, t in zip(even, turned)] + [e - t for e, t in zip(even, turned)]


def fine_kernel(
    profiles,
    order,
    edges_ref,
    counts_ref,
    x_ref,
    turns_ref,
    table_ref,
    dynamics_ref,
    state_ref,
    out_ref,
    moved_ref,
    band_ref,
):
    groups = counts_ref.shape[0]
    capacity = state_ref.shape[0]
    own = lax.axis_index("bins") * profiles + lax.axis_index("scans")
    row = lax.broadcasted_iota(jnp.int32, (8, LANES), 0)
    lane = lax.broadcasted_iota(jnp.int32, (8, LANES), 1)
    point = lane & (HALF - 1)
    low_side = point < HALF // 2
    first = own == 0
    side = jnp.where(lane < HALF, 1.0, -1.0)

    def swapped(values):
        return pltpu.roll(values, HALF, 1)

    def down(values):
        return swapped(values) * side

    columns = [[] for _ in range(profiles + 1)]
    for c in range(groups):
        cosine, sine = unit_turn(((c * HALF + point) * (8 * own + row)) & (order - 1), order)
        sine = sine * side
        middle = jnp.zeros((8, LANES), F32)
        for p in range(profiles):
            block = x_ref[c * profiles + p]
            middle = jnp.where(row == p, block[:1], middle)
            block = jnp.where(first & (row == 0) & (lane >= HALF), 0.0, block)
            columns[p].append(block * cosine + swapped(block) * sine)
        middle = jnp.where(lane < HALF, swapped(middle), middle)
        middle = middle * turns_ref[2 * groups + c : 2 * groups + c + 1, :]
        columns[profiles].append(jnp.where(first, middle, 0.0))
    transformed = [eight_point(column, down) for column in columns]
    blocks = []
    for u in range(groups):
        cosine, sine = turns_ref[u : u + 1, :], turns_ref[groups + u : groups + u + 1, :] * -side[:1]
        for column in transformed:
            block = column[u]
            blocks.append(block * cosine + swapped(block) * sine if u else block)
    high, low = split_two(jnp.concatenate(blocks, axis=0))
    product = dot(high, table_ref[:LANES, :])
    product = product[:, :LANES] + product[:, LANES:] + dot(low, table_ref[:LANES, :LANES])
    spectrum = []
    for at in range(len(blocks)):
        block = product[8 * at : 8 * (at + 1)]
        if at % (profiles + 1) < profiles:
            block = jnp.where(first & ~low_side & (row == 0), 0.0, block)
        else:
            block = jnp.where(low_side, block, 0.0)
        spectrum.append(block)
    spectrum = [spectrum[u * (profiles + 1) : (u + 1) * (profiles + 1)] for u in range(groups)]
    power = []
    for u in range(groups):
        squares = sum(block * block for block in spectrum[u])
        power.append(squares + swapped(squares))
    summands = []
    for u in range(groups):
        rows = [
            jnp.where(low_side, spectrum[u][p], spectrum[groups - 1 - u][p]) for p in range(profiles)
        ]
        rows.append(spectrum[u][profiles])
        rows.append(jnp.where(low_side, power[u], power[groups - 1 - u]))
        summands.append(jnp.concatenate(rows, axis=0))
    summands = jnp.concatenate(split_two(jnp.concatenate(summands, axis=1)), axis=0)
    summed = dot(table_ref[LANES:, : summands.shape[0]], summands)
    rows, quarter = summed.shape[0] // 2, HALF // 2
    lanes = lax.broadcasted_iota(jnp.int32, (rows, LANES), 1)
    left = [[], []]
    for part in range(2):
        for first_u in range(0, groups, 4):
            merged = None
            for u in range(first_u, first_u + 4):
                piece = summed[:rows, u * LANES : (u + 1) * LANES] + pltpu.roll(
                    summed[rows:, u * LANES : (u + 1) * LANES], LANES - quarter, 1
                )
                shift = ((u % 4) * quarter - part * HALF) % LANES
                piece = pltpu.roll(piece, shift, 1) if shift else piece
                here = lanes >= (u % 4) * quarter
                merged = piece if merged is None else jnp.where(here, piece, merged)
            left[part].append(merged)
    left = jnp.concatenate([jnp.concatenate(part, axis=1) for part in left], axis=0)
    owner_of = lax.broadcasted_iota(jnp.int32, (1, groups * capacity), 1)
    rank_of, owner_of = owner_of & (capacity - 1), owner_of >> (capacity.bit_length() - 1)
    wanted = jnp.full((1, groups * capacity), -1, jnp.int32)
    start = jnp.int32(0)
    for owner in range(groups):
        count = counts_ref[owner]
        wanted = jnp.where((owner_of == owner) & (rank_of < count), start + rank_of, wanted)
        start = start + count
    tile_of = lax.broadcasted_iota(jnp.int32, (groups * quarter, groups * capacity), 0)
    tile_of = (tile_of >> (quarter.bit_length() - 1)) + groups * (tile_of & (quarter - 1))
    chosen = jnp.where(tile_of == wanted, 1.0, 0.0).astype(BF16)
    routed = dot(jnp.concatenate(split_two(left), axis=0), chosen)
    routed = routed[: 2 * rows] + routed[2 * rows :]
    for owner in range(groups):
        piece = routed[:, owner * capacity : (owner + 1) * capacity]
        out_ref[owner] = jnp.concatenate([piece[:rows], piece[rows:]], axis=1)
    state_kernel(edges_ref, counts_ref, dynamics_ref, state_ref, moved_ref, band_ref)


def fine_step(arrived, band_edges, owner_counts, dynamics, state, profiles, coarse):
    groups, capacity = owner_counts.shape[0], state.shape[0]
    turns, table = fine_tables(groups, profiles, coarse)
    out, moved, band = pl.pallas_call(
        functools.partial(fine_kernel, profiles, coarse * groups * HALF),
        out_shape=(
            jax.ShapeDtypeStruct((groups, profiles * KINDS, LANES), F32),
            jax.ShapeDtypeStruct((2 * capacity, STATES), F32),
            jax.ShapeDtypeStruct((2 * capacity, LANES), jnp.int32),
        ),
        in_specs=[SMEM] * 2 + [VMEM] * 5,
        out_specs=(VMEM,) * 3,
        compiler_params=pltpu.CompilerParams(vmem_limit_bytes=32 << 20),
        name="fine_dft",
    )(
        band_edges,
        owner_counts,
        arrived,
        jnp.asarray(turns),
        jnp.asarray(table),
        dynamics.reshape(NCLASS * STATES, STATES),
        state,
    )
    return out.reshape(groups * profiles, KINDS, LANES), moved, band


def fine_step_general(arrived, owner_counts, capacity):
    groups, rows = arrived.shape[:2]
    coarse = 2 * rows * groups
    fine_length = groups * HALF
    order = coarse * fine_length
    own = lax.axis_index("bins")
    real, imag = arrived[:, :, :HALF], arrived[:, :, HALF:]
    points = jnp.arange(fine_length, dtype=jnp.int32).reshape(groups, 1, HALF)
    k_index = own * rows + jnp.arange(rows, dtype=jnp.int32)[None, :, None]
    cosine, sine = unit_turn(points * k_index & (order - 1), order)
    packed = (own == 0) & (jnp.arange(rows)[None, :, None] == 0)
    middle = jnp.where(own == 0, imag[:, :1], 0.0)
    imag = jnp.where(packed, 0.0, imag)
    real, imag = real * cosine + imag * sine, imag * cosine - real * sine
    cosine, sine = unit_turn(points * (coarse // 2), order)
    real = jnp.concatenate([real, middle * cosine], axis=1)
    imag = jnp.concatenate([imag, -middle * sine], axis=1)

    def turned(pattern, root, parts):
        cosine, sine = (jnp.asarray(part.astype(np.float32)) for part in root)
        mul = functools.partial(jnp.einsum, pattern, precision=HIGHEST)
        return (
            mul(cosine, parts[0]) - mul(sine, parts[1]),
            mul(cosine, parts[1]) + mul(sine, parts[0]),
        )

    group_index, point_index = np.arange(groups), np.arange(HALF)
    parts = turned(
        "cu,crj->urj", unit_root(groups, group_index[:, None] * group_index), (real, imag)
    )
    parts = turned(
        "uj,urj->urj", unit_root(fine_length, group_index[:, None] * point_index), parts
    )
    parts = turned(
        "jv,urj->vur", unit_root(HALF, point_index[:, None] * point_index), parts
    )
    tiles = fine_length // 2
    kept = jnp.concatenate([~packed[0, :, 0], jnp.zeros((1,), bool)])
    sides = []
    for part, sign in zip(parts, (1.0, -1.0)):
        part = part.reshape(fine_length, rows + 1)
        sides.append((part[:tiles], sign * jnp.where(kept, part[tiles:][::-1], 0.0)))
    power = sum(jnp.sum(part * part, axis=1) for pair in sides for part in pair)
    starts = jnp.cumsum(owner_counts) - owner_counts
    slot_index = jnp.arange(capacity, dtype=jnp.int32)
    filled = slot_index[None, :] < owner_counts[:, None]
    chosen = jnp.clip(starts[:, None] + slot_index[None, :], 0, tiles - 1)

    def kinds(low, high):
        low_sums, high_sums = jnp.sum(low[:, :rows], axis=1), jnp.sum(high[:, 1:rows], axis=1)
        values = jnp.stack([low_sums, high_sums, high[:, 0] + low[:, rows], power], axis=1)
        return jnp.where(filled[:, :, None], values[chosen], 0.0).transpose(0, 2, 1)

    return jnp.concatenate([kinds(*sides[0]), kinds(*sides[1])], axis=2)


def pool_table(shares, coarse):
    pool = np.zeros((shares, KINDS, 6, STATES), np.float32)
    wide = TILE // STATES
    rows = coarse // 2 // shares
    for share in range(shares):
        first = rows * share
        rest = coarse - first if share else coarse // 2
        for kind, at in enumerate((first, coarse - first - 1, rest)):
            for band in range(NCLASS):
                pool[share, kind, band, at // wide >> band] = 1.0
        pool[share, 3, NCLASS, :] = 1.0
    return pool.reshape(shares * KINDS, 6 * STATES).astype(BF16)


def state_kernel(edges_ref, counts_ref, dynamics_ref, state_ref, moved_ref, band_ref):
    own = lax.axis_index("bins")
    groups = counts_ref.shape[0]
    capacity = state_ref.shape[0]
    wide = NCLASS * STATES

    def before(owner, start):
        return start + jnp.where(owner < own, counts_ref[owner], 0)

    start = lax.fori_loop(0, groups, before, jnp.int32(0))
    slot = lax.broadcasted_iota(jnp.int32, (2 * capacity, LANES), 0) & (capacity - 1)
    band = jnp.zeros_like(slot)
    for edge in range(1, NCLASS):
        band = band + jnp.where(slot + start >= edges_ref[edge], 1, 0)
    band = jnp.where(slot < counts_ref[own], band, -1)
    band_ref[...] = band
    state = state_ref[...]
    state = jnp.concatenate([state[:, :STATES], state[:, STATES:]], axis=0)
    row = lax.broadcasted_iota(jnp.int32, (wide, STATES), 0)
    column = lax.broadcasted_iota(jnp.int32, (wide, STATES), 1)
    limit = STATES >> (row >> 6)
    inside = ((row & (STATES - 1)) < limit) & (column < limit)
    dynamics = jnp.where(inside, dynamics_ref[...], 0.0)
    state_high, state_low = split_two(state)
    high, low = split_two(dynamics)
    moved = lax.dot_general(
        jnp.concatenate([state_high, state_low, state_high], axis=1),
        jnp.concatenate([high, high, low], axis=1),
        (((1,), (1,)), ((), ())),
        preferred_element_type=F32,
    )
    moved = jnp.concatenate([moved, jnp.zeros((2 * capacity, STATES), F32)], axis=1)
    moved_ref[...] = of_band(moved, band)


def of_band(values, band):
    lane = lax.broadcasted_iota(jnp.int32, band.shape, 1) >> 6
    folded = jnp.zeros(band.shape, F32)
    for pair in range((NCLASS + 1) // 2):
        piece = values[:, pair * LANES : (pair + 1) * LANES]
        folded = folded + jnp.where(lane + 2 * pair == band, piece, 0.0)
    return folded[:, :STATES] + folded[:, STATES:]


def update_kernel(count, x_ref, pool_ref, moved_ref, band_ref, out_ref):
    capacity = out_ref.shape[0]
    band = band_ref[...]
    sums = lax.dot_general(
        jnp.concatenate(split_two(x_ref[...]), axis=1),
        pool_ref[...],
        (((0,), (0,)), ((), ())),
        preferred_element_type=F32,
    )
    sums = sums[: 2 * capacity] + sums[2 * capacity :]
    power = sums[:, NCLASS * STATES :] * (1.0 / count)
    span = jnp.left_shift(TILE // STATES, jnp.maximum(band[:, :STATES], 0)).astype(F32)
    scaling = 1.0 / jnp.sqrt(span * (power + EPSILON))
    result = moved_ref[...] + of_band(sums, band) * scaling
    out_ref[...] = jnp.concatenate([result[:capacity], result[capacity:]], axis=1)


def state_step(band_edges, owner_counts, dynamics, state):
    rows = 2 * state.shape[0]
    return pl.pallas_call(
        state_kernel,
        out_shape=(
            jax.ShapeDtypeStruct((rows, STATES), F32),
            jax.ShapeDtypeStruct((rows, LANES), jnp.int32),
        ),
        in_specs=[SMEM, SMEM, VMEM, VMEM],
        out_specs=(VMEM, VMEM),
        compiler_params=pltpu.CompilerParams(vmem_limit_bytes=32 << 20),
        cost_estimate=pl.CostEstimate(flops=1 << 25, bytes_accessed=1 << 19, transcendentals=0),
        name="state_step",
    )(band_edges, owner_counts, dynamics.reshape(NCLASS * STATES, STATES), state)


def update_step(arrived, moved, band, coarse, count):
    shares = arrived.shape[0]
    return pl.pallas_call(
        functools.partial(update_kernel, count),
        out_shape=jax.ShapeDtypeStruct((moved.shape[0] // 2, 2 * STATES), F32),
        in_specs=[VMEM] * 4,
        out_specs=VMEM,
        compiler_params=pltpu.CompilerParams(vmem_limit_bytes=32 << 20),
        name="state_update",
    )(arrived.reshape(shares * KINDS, LANES), jnp.asarray(pool_table(shares, coarse)), moved, band)


def exchanged(values, axes):
    return lax.all_to_all(values, axes, split_axis=0, concat_axis=0, tiled=True)


def body(profiles, band_edges, owner_counts, dynamics, prev_state):
    groups, scans = lax.axis_size("bins"), lax.axis_size("scans")
    prof_rows, length = profiles.shape
    capacity = prev_state.shape[0]
    coarse = length // HALF
    count = prof_rows * scans * TILE
    state = prev_state.reshape(capacity, 2 * STATES)
    if groups == 8 and scans == 4 and coarse == 16 * groups * scans:
        columns = exchanged(columns_step(profiles.reshape(length), groups), "bins")
        blocks = coarse_step(columns.reshape(coarse // 2, LANES))
        blocks = exchanged(blocks, ("bins", "scans"))
        payload, moved, band = fine_step(
            blocks, band_edges, owner_counts, dynamics, state, scans, coarse
        )
        arrived = exchanged(payload, ("bins", "scans"))
    else:
        moved, band = state_step(band_edges, owner_counts, dynamics, state)
        columns = profiles.reshape(coarse // groups, groups, HALF).transpose(1, 0, 2)
        columns = exchanged(columns, "bins").reshape(coarse, HALF)
        blocks = exchanged(coarse_step_general(columns, groups), "bins")
        arrived = exchanged(fine_step_general(blocks, owner_counts, capacity), "bins")
        power = lax.psum(arrived[:, 3:], "scans")
        arrived = jnp.concatenate([arrived[:, :3], power], axis=1)
    updated = update_step(arrived, moved, band, coarse, count)
    return updated.reshape(prev_state.shape)


def solution(mesh):
    return jax.shard_map(
        body,
        mesh=mesh,
        in_specs=(P("scans", "bins"), P(), P(), P(), P("bins", "scans", None)),
        out_specs=P("bins", "scans", None),
        check_vma=False,
    )
```

```python
import functools
import math

import jax
import jax.numpy as jnp
import numpy as np
from jax import lax
from jax.experimental import pallas as pl
from jax.experimental.pallas import tpu as pltpu
from jax.sharding import PartitionSpec as P

TILE = 512
STATES = 64
NCLASS = 5
LANES = 128

EPSILON = 1e-05
HIGHEST = lax.Precision.HIGHEST
BF16 = jnp.bfloat16
F32 = jnp.float32


def unit_root(order, exponents):
    angles = 2.0 * np.pi * (np.asarray(exponents, dtype=np.int64) % order) / order
    return np.cos(angles), -np.sin(angles)


def two_terms(values):
    high = np.asarray(values, np.float32).astype(BF16)
    low = (np.asarray(values, np.float64) - high.astype(np.float64)).astype(BF16)
    return high, low


def split_two(values):
    high = values.astype(BF16)
    return high, (values - high.astype(F32)).astype(BF16)


def dot(left, right):
    return jnp.dot(left, right, preferred_element_type=F32)


VMEM = pl.BlockSpec(memory_space=pltpu.VMEM)
PARAMS = pltpu.CompilerParams(vmem_limit_bytes=32 << 20)


KINDS = 4
HALF = LANES // 2


def unit_turn(phase, order):
    shifted = phase + order // 8
    quadrant = (shifted >> (order.bit_length() - 3)) & 3
    x = ((shifted & (order // 4 - 1)) - order // 8).astype(F32) * (2.0 * math.pi / order)
    y = x * x
    cosine = 1.0 + y * (-1 / 2 + y * (1 / 24 + y * (-1 / 720 + y * (1 / 40320))))
    sine = x * (1.0 + y * (-1 / 6 + y * (1 / 120 + y * (-1 / 5040 + y * (1 / 362880)))))
    odd = (quadrant & 1) == 1
    real, imag = jnp.where(odd, sine, cosine), jnp.where(odd, cosine, sine)
    real = jnp.where((quadrant == 1) | (quadrant == 2), -real, real)
    return real, jnp.where(quadrant >= 2, -imag, imag)


def iotas(shape):
    return [lax.broadcasted_iota(jnp.int32, shape, axis) for axis in range(len(shape))]


def columns_kernel(
    x_ref, edges_ref, counts_ref, out_ref, wanted_ref, lane_band_ref, row_band_ref
):
    groups, rows, _ = out_ref.shape
    capacity = row_band_ref.shape[0]
    low_lanes = iotas((rows, LANES))[1] < HALF
    for pair in range(groups // 2):
        even = x_ref[pl.ds(pair, rows, stride=groups), :]
        odd = x_ref[pl.ds(groups // 2 + pair, rows, stride=groups), :]
        out_ref[2 * pair] = jnp.where(low_lanes, even, pltpu.roll(odd, HALF, 1))
        out_ref[2 * pair + 1] = jnp.where(low_lanes, pltpu.roll(even, HALF, 1), odd)
    own = lax.axis_index("bins")
    counts = [
        jnp.broadcast_to(counts_ref[:, owner : owner + 1], (1, LANES)) for owner in range(groups)
    ]
    lane = iotas((1, LANES))[1]
    start = jnp.zeros((1, LANES), jnp.int32)
    own_start, own_count = start, start
    wanted = []
    for owner, count in enumerate(counts):
        rank = lane & (HALF - 1)
        wanted.append(jnp.where(rank < count, start + rank, -1))
        own_start = jnp.where(own == owner, start, own_start)
        own_count = jnp.where(own == owner, count, own_count)
        start = start + count
    for pair in range(groups // 2):
        wanted_ref[:, pair * LANES : (pair + 1) * LANES] = jnp.where(
            lane < HALF, wanted[2 * pair], wanted[2 * pair + 1]
        )
    edges = [jnp.broadcast_to(edges_ref[:, at : at + 1], (1, LANES)) for at in range(1, NCLASS)]
    for ref, slot in (
        (lane_band_ref, lane & (capacity - 1)),
        (row_band_ref, iotas((capacity, LANES))[0]),
    ):
        band = jnp.zeros_like(slot)
        for edge in edges:
            band = band + jnp.where(slot + own_start >= edge, 1, 0)
        ref[...] = jnp.where(slot < own_count, band, -1)


def columns_step(profile, band_edges, owner_counts, capacity):
    groups = owner_counts.shape[0]
    rows = profile.shape[0] // (groups * LANES)
    return pl.pallas_call(
        columns_kernel,
        out_shape=(
            jax.ShapeDtypeStruct((groups, rows, LANES), F32),
            jax.ShapeDtypeStruct((1, groups * capacity), jnp.int32),
            jax.ShapeDtypeStruct((1, LANES), jnp.int32),
            jax.ShapeDtypeStruct((capacity, LANES), jnp.int32),
        ),
        in_specs=[VMEM] * 3,
        out_specs=(VMEM,) * 4,
        compiler_params=PARAMS,
        name="columns",
    )(profile.reshape(-1, LANES), band_edges.reshape(1, -1), owner_counts.reshape(1, -1))


def coarse_table(coarse):
    half, quarter = coarse // 2, coarse // 4
    k_index = np.arange(quarter)
    a_index = np.concatenate([np.arange(0, half, 2), np.arange(1, half, 2)])
    real, imag = unit_root(half, k_index[:, None] * a_index[None, :])
    imag[0] = 1
    parts = [part.reshape(quarter // 16, 2, 2, 1, 4, half) for part in (real, imag)]
    parts = np.concatenate(parts, axis=3).transpose(0, 2, 3, 1, 4, 5)
    return np.concatenate(two_terms(parts.reshape(half, half)), axis=1)


def coarse_kernel(groups, shares, x_ref, table_ref, out_ref, turn_ref):
    half = x_ref.shape[0]
    quarter = half // 2
    row, lane = iotas((8, LANES))
    low_lanes = lane < HALF
    sums = []
    for parity in range(2):
        high, low = split_two(x_ref[pl.ds(parity, quarter, stride=2), :])
        at = parity * quarter
        both = dot(table_ref[:, at : at + quarter], jnp.concatenate([high, low], axis=1))
        rest = dot(table_ref[:, half + at : half + at + quarter], high)
        sums.append(both[:, :LANES] + both[:, LANES:] + rest)
    base = 8 * (row >> 2) + 4 * (lane >> 6) + (row & 3)
    base_cosine, base_sine = unit_turn(base, 2 * half)
    packed = low_lanes & (row == 0)
    for sign, block in [(sign, block) for block in range(half // 32) for sign in (1, -1)]:
        pieces = []
        for at in range(32 * block, 32 * (block + 1), 8):
            even, odd = sums[0][at : at + 8], sums[1][at : at + 8]
            pieces.append(even + odd if sign > 0 else even - odd)
        real_low, imag_low, real_high, imag_high = pieces
        if block == 0 and sign < 0:
            imag_low = jnp.where(row == 0, 0.0, imag_low)
        even_real = jnp.where(low_lanes, real_low, pltpu.roll(real_high, HALF, 1))
        even_imag = jnp.where(low_lanes, imag_low, pltpu.roll(imag_high, HALF, 1))
        odd_real = jnp.where(low_lanes, pltpu.roll(real_low, HALF, 1), real_high)
        odd_imag = jnp.where(low_lanes, pltpu.roll(imag_low, HALF, 1), imag_high)
        first = 2 * block + (0 if sign > 0 else shares // 2)
        angle = math.pi * 8 * first / half
        cosine = base_cosine * math.cos(angle) - base_sine * math.sin(angle)
        sine = base_sine * math.cos(angle) + base_cosine * math.sin(angle)
        real = even_real + odd_real * cosine + odd_imag * sine
        if first == 0:
            cosine = jnp.where(packed, -1.0, cosine)
        imag = even_imag + odd_imag * cosine - odd_real * sine
        out_ref[pl.ds(8 * first, 8, stride=2), :] = real
        out_ref[pl.ds(8 * first + 1, 8, stride=2), :] = imag
    own = lax.axis_index("bins") * lax.axis_size("scans") + lax.axis_index("scans")
    k_index = 8 * own + 4 * (lane >> 6) + (row & 3)
    order = 2 * half * groups * HALF
    for c in range(groups):
        phase = ((c * HALF + (lane & (HALF - 1))) * k_index) & (order - 1)
        turn_ref[2 * c], turn_ref[2 * c + 1] = unit_turn(phase, order)


def coarse_step(columns, groups, shares):
    half = columns.shape[0]
    return pl.pallas_call(
        functools.partial(coarse_kernel, groups, shares),
        out_shape=(
            jax.ShapeDtypeStruct((half, LANES), F32),
            jax.ShapeDtypeStruct((2 * groups, 8, LANES), F32),
        ),
        in_specs=[VMEM] * 2,
        out_specs=(VMEM,) * 2,
        compiler_params=PARAMS,
        name="coarse_dft",
    )(columns, jnp.asarray(coarse_table(2 * half)))


def coarse_step_general(columns, shares):
    coarse = columns.shape[0]
    half = coarse // 2
    real, imag = unit_root(coarse, np.arange(half)[:, None] * np.arange(coarse)[None, :])
    imag[0] = 1 - 2 * (np.arange(coarse) % 2)
    table = jnp.asarray(np.concatenate([real, imag]).astype(np.float32))
    spectrum = jnp.dot(table, columns, precision=HIGHEST)
    blocks = jnp.concatenate([spectrum[:half], spectrum[half:]], axis=1)
    return blocks.reshape(shares, half // shares, LANES)


def fine_tables(groups, profiles, coarse):
    fine_length = groups * HALF
    doubled = np.arange(LANES) % HALF
    turn = unit_root(fine_length, np.arange(groups)[:, None] * doubled[None, :])
    middle = (np.arange(groups)[:, None] * HALF + doubled[None, :]) * (coarse // 2)
    middle = unit_root(coarse * fine_length, middle)
    turns = np.concatenate(turn + middle).astype(np.float32)
    order = np.arange(HALF)
    order[HALF // 2 :] = order[HALF // 2 :][::-1]
    real, imag = unit_root(HALF, np.arange(HALF)[:, None] * order[None, :])
    sign = np.where(np.arange(HALF) < HALF // 2, 1, -1)
    both = np.eye(2)
    matrix = np.block(
        [
            [np.kron(both, real), np.kron(both, imag * sign)],
            [np.kron(both, -imag), np.kron(both, real * sign)],
        ]
    )
    sums = np.zeros((3, profiles, KINDS, 2, profiles // 2 + 2, 2, 4), np.float32)
    for p in range(profiles):
        pair, which = divmod(p, 2)
        sums[0, p, 0, :, pair, which, :] = 1
        sums[1, p, 1, :, pair, which, 1:] = 1
        sums[2, p, 1, :, pair, which, :] = 1
        sums[1, p, 2, :, pair, which, 0] = 1
        sums[0, p, 2, :, profiles // 2, which, pair] = 1
        sums[:, p, 3, :, profiles // 2 + 1] = 1
    sums = sums.reshape(3 * profiles * KINDS, -1)
    sums = np.pad(sums, [(0, 0), (0, 4 * LANES - sums.shape[1])]).astype(BF16)
    return turns, np.concatenate([np.concatenate(two_terms(matrix), axis=1), sums])


def add(p, q):
    return (p[0] + q[0], p[1] + q[1])


def sub(p, q):
    return (p[0] - q[0], p[1] - q[1])


def times(p, cosine, sine):
    return (p[0] * cosine + p[1] * sine, p[1] * cosine - p[0] * sine)


def eight_point(values):
    half = math.sqrt(0.5)

    def down(p):
        return (p[1], -p[0])

    def four(a, b, c, d):
        s0, s1, s2, s3 = add(a, c), sub(a, c), add(b, d), sub(b, d)
        turned = (s1[0] + s3[1], s1[1] - s3[0]), (s1[0] - s3[1], s1[1] + s3[0])
        return add(s0, s2), turned[0], sub(s0, s2), turned[1]

    even = four(values[0], values[2], values[4], values[6])
    odd = four(values[1], values[3], values[5], values[7])
    turned = [
        odd[0],
        ((odd[1][0] + odd[1][1]) * half, (odd[1][1] - odd[1][0]) * half),
        down(odd[2]),
        ((odd[3][1] - odd[3][0]) * half, (odd[3][0] + odd[3][1]) * -half),
    ]
    return [add(e, t) for e, t in zip(even, turned)] + [sub(e, t) for e, t in zip(even, turned)]


def fine_kernel(
    profiles,
    x_ref,
    turn_ref,
    wanted_ref,
    band_ref,
    turns_ref,
    table_ref,
    dynamics_ref,
    state_ref,
    out_ref,
    moved_ref,
):
    groups = out_ref.shape[0]
    first = (lax.axis_index("bins") == 0) & (lax.axis_index("scans") == 0)
    row, lane = iotas((8, LANES))
    low_lanes = lane < HALF
    low_side = (lane & (HALF - 1)) < HALF // 2
    packed = first & low_lanes & ((row & 3) == 0)
    shifted = first & low_lanes & ((row & 3) == 1)
    pairs = profiles // 2
    columns = [[] for _ in range(pairs + 1)]
    for c in range(groups):
        cosine, sine = turn_ref[2 * c], turn_ref[2 * c + 1]
        at = c * 8 * profiles
        for pair in range(pairs):
            real = x_ref[pl.ds(at + 16 * pair, 8, stride=2), :]
            imag = x_ref[pl.ds(at + 16 * pair + 1, 8, stride=2), :]
            if pair == 0:
                middle = jnp.where(packed, imag, 0.0)
            imag = jnp.where(packed, 0.0, imag)
            columns[pair].append(times((real, imag), cosine, sine))
        middle = jnp.where(shifted, x_ref[pl.ds(at + 15, 8, stride=2), :], middle)
        middle_real = turns_ref[2 * groups + c : 2 * groups + c + 1, :]
        middle_imag = turns_ref[3 * groups + c : 3 * groups + c + 1, :]
        columns[pairs].append((middle * middle_real, middle * middle_imag))
    transformed = [eight_point(column) for column in columns]
    blocks = []
    for u in range(groups):
        cosine, sine = turns_ref[u : u + 1, :], -turns_ref[groups + u : groups + u + 1, :]
        for column in transformed:
            blocks.append(times(column[u], cosine, sine) if u else column[u])
    wide = 2 * LANES
    size = wide
    left = jnp.concatenate(
        [jnp.concatenate([block[part] for block in blocks], axis=0) for part in range(2)], axis=1
    )
    high, low = split_two(left)
    product = dot(high, table_ref[:size, :])
    product = product[:, :wide] + product[:, wide:] + dot(low, table_ref[:size, :wide])
    spectrum = []
    for u in range(groups):
        spectrum.append([])
        for at in range(pairs + 1):
            start = 8 * (u * (pairs + 1) + at)
            block = (product[start : start + 8, :LANES], product[start : start + 8, LANES:])
            dropped = ~low_side & packed if at < pairs else ~low_side
            spectrum[u].append(tuple(jnp.where(dropped, 0.0, part) for part in block))
    power = [
        sum(block[0] * block[0] + block[1] * block[1] for block in spectrum[u])
        for u in range(groups)
    ]
    summands = []
    for part in range(2):
        for u in range(groups):
            mirror = groups - 1 - u
            rows = [
                jnp.where(low_side, spectrum[u][pair][part], spectrum[mirror][pair][part])
                for pair in range(pairs)
            ]
            rows.append(spectrum[u][pairs][part])
            rows.append(jnp.where(low_side, power[u], power[mirror]))
            summands.append(jnp.concatenate(rows, axis=0))
    summands = jnp.concatenate(split_two(jnp.concatenate(summands, axis=1)), axis=0)
    summed = dot(table_ref[size:, : summands.shape[0]], summands)
    rows = summed.shape[0] // 3
    _, lanes = iotas((rows, LANES))
    side, early = (lanes & (HALF - 1)) < HALF // 2, lanes < HALF
    left = []
    for part in range(2):
        pieces = []
        for at in range(part * groups, (part + 1) * groups):
            piece = summed[:, at * LANES : (at + 1) * LANES]
            piece = jnp.where(
                side,
                piece[:rows],
                jnp.where(early, piece[rows : 2 * rows], piece[2 * rows :]),
            )
            pieces.append(piece)
        left.append(jnp.concatenate(pieces, axis=1))
    left = jnp.concatenate(split_two(jnp.concatenate(left, axis=0)), axis=0)
    wanted = wanted_ref[...]
    chosen = []
    for u in range(groups):
        tile = u + groups * iotas((HALF // 2, wanted.shape[1]))[0]
        chosen += [jnp.where(tile == wanted, 1.0, 0.0).astype(BF16)] * 4
    routed = dot(left, jnp.concatenate(chosen, axis=0))
    routed = routed[: 2 * rows] + routed[2 * rows :]
    for pair in range(groups // 2):
        real = routed[:rows, pair * LANES : (pair + 1) * LANES]
        imag = routed[rows:, pair * LANES : (pair + 1) * LANES]
        out_ref[2 * pair] = jnp.where(early, real, pltpu.roll(imag, HALF, 1))
        out_ref[2 * pair + 1] = jnp.where(early, pltpu.roll(real, HALF, 1), imag)
    moved_ref[...] = state_product(dynamics_ref[...], state_ref[...], band_ref[...])


def state_product(dynamics, state, band):
    row, column = iotas((NCLASS * STATES, STATES))
    limit = STATES >> (row >> 6)
    inside = ((row & (STATES - 1)) < limit) & (column < limit)
    dynamics = jnp.where(inside, dynamics, 0.0)
    empty = jnp.zeros_like(dynamics)
    halves = [
        jnp.concatenate([dynamics, empty], axis=1),
        jnp.concatenate([empty, dynamics], axis=1),
    ]
    matrix = jnp.concatenate(
        [half[k * STATES : (k + 1) * STATES] for k in range(NCLASS) for half in halves], axis=0
    )
    state_high, state_low = split_two(state)
    high, low = split_two(matrix)
    moved = lax.dot_general(
        jnp.concatenate([state_high, state_low, state_high], axis=1),
        jnp.concatenate([high, high, low], axis=1),
        (((1,), (1,)), ((), ())),
        preferred_element_type=F32,
    )
    result = jnp.zeros(state.shape, F32)
    for k in range(NCLASS):
        result = jnp.where(band == k, moved[:, k * LANES : (k + 1) * LANES], result)
    return result


def fine_step(arrived, turn, wanted, band, dynamics, state, profiles, coarse):
    groups = turn.shape[0] // 2
    turns, table = fine_tables(groups, profiles, coarse)
    out, moved = pl.pallas_call(
        functools.partial(fine_kernel, profiles),
        out_shape=(
            jax.ShapeDtypeStruct((groups, profiles * KINDS, LANES), F32),
            jax.ShapeDtypeStruct(state.shape, F32),
        ),
        in_specs=[VMEM] * 8,
        out_specs=(VMEM,) * 2,
        compiler_params=PARAMS,
        name="fine_dft",
    )(
        arrived,
        turn,
        wanted,
        band,
        jnp.asarray(turns),
        jnp.asarray(table),
        dynamics.reshape(NCLASS * STATES, STATES),
        state,
    )
    return out.reshape(groups * profiles, KINDS, LANES), moved


def fine_step_general(arrived, owner_counts, capacity):
    groups, rows = arrived.shape[:2]
    coarse = 2 * rows * groups
    fine_length = groups * HALF
    order = coarse * fine_length
    own = lax.axis_index("bins")
    real, imag = arrived[:, :, :HALF], arrived[:, :, HALF:]
    points = jnp.arange(fine_length, dtype=jnp.int32).reshape(groups, 1, HALF)
    k_index = own * rows + jnp.arange(rows, dtype=jnp.int32)[None, :, None]
    cosine, sine = unit_turn(points * k_index & (order - 1), order)
    packed = (own == 0) & (jnp.arange(rows)[None, :, None] == 0)
    middle = jnp.where(own == 0, imag[:, :1], 0.0)
    imag = jnp.where(packed, 0.0, imag)
    real, imag = real * cosine + imag * sine, imag * cosine - real * sine
    cosine, sine = unit_turn(points * (coarse // 2), order)
    real = jnp.concatenate([real, middle * cosine], axis=1)
    imag = jnp.concatenate([imag, -middle * sine], axis=1)

    def turned(pattern, root, parts):
        cosine, sine = (jnp.asarray(part.astype(np.float32)) for part in root)
        mul = functools.partial(jnp.einsum, pattern, precision=HIGHEST)
        return (
            mul(cosine, parts[0]) - mul(sine, parts[1]),
            mul(cosine, parts[1]) + mul(sine, parts[0]),
        )

    group_index, point_index = np.arange(groups), np.arange(HALF)
    parts = turned(
        "cu,crj->urj", unit_root(groups, group_index[:, None] * group_index), (real, imag)
    )
    parts = turned(
        "uj,urj->urj", unit_root(fine_length, group_index[:, None] * point_index), parts
    )
    parts = turned(
        "jv,urj->vur", unit_root(HALF, point_index[:, None] * point_index), parts
    )
    tiles = fine_length // 2
    kept = jnp.concatenate([~packed[0, :, 0], jnp.zeros((1,), bool)])
    sides = []
    for part, sign in zip(parts, (1.0, -1.0)):
        part = part.reshape(fine_length, rows + 1)
        sides.append((part[:tiles], sign * jnp.where(kept, part[tiles:][::-1], 0.0)))
    power = sum(jnp.sum(part * part, axis=1) for pair in sides for part in pair)
    starts = jnp.cumsum(owner_counts) - owner_counts
    slot_index = jnp.arange(capacity, dtype=jnp.int32)
    filled = slot_index[None, :] < owner_counts[:, None]
    chosen = jnp.clip(starts[:, None] + slot_index[None, :], 0, tiles - 1)

    def kinds(low, high):
        low_sums, high_sums = jnp.sum(low[:, :rows], axis=1), jnp.sum(high[:, 1:rows], axis=1)
        values = jnp.stack([low_sums, high_sums, high[:, 0] + low[:, rows], power], axis=1)
        return jnp.where(filled[:, :, None], values[chosen], 0.0).transpose(0, 2, 1)

    return jnp.concatenate([kinds(*sides[0]), kinds(*sides[1])], axis=2)


def pool_table(shares, coarse):
    pool = np.zeros((21, 16, shares, KINDS), np.float32)
    sums = pool[:20].reshape(NCLASS, STATES, shares, KINDS)
    wide = TILE // STATES
    rows = coarse // 2 // shares
    for share in range(shares):
        first = rows * share
        rest = coarse - first if share else coarse // 2
        for kind, at in enumerate((first, coarse - first - 1, rest)):
            for band in range(NCLASS):
                sums[band, at // wide >> band, share, kind] = 1.0
    pool[20, :, :, 3] = 1.0
    return pool.reshape(-1, shares * KINDS).astype(BF16)


def update_kernel(count, x_ref, pool_ref, moved_ref, band_ref, out_ref):
    band = band_ref[...]
    sums = dot(pool_ref[...], jnp.concatenate(split_two(x_ref[...]), axis=1))
    sums = sums[:, :LANES] + sums[:, LANES:]
    power = sums[NCLASS * STATES : NCLASS * STATES + 1] * (1.0 / count)
    span = jnp.left_shift(TILE // STATES, jnp.maximum(band, 0)).astype(F32)
    scaling = 1.0 / jnp.sqrt(span * (power + EPSILON))
    scaling = jnp.where(band < 0, 0.0, scaling)
    chosen = sums[:STATES]
    for k in range(1, NCLASS):
        chosen = jnp.where(band == k, sums[k * STATES : (k + 1) * STATES], chosen)
    chosen = chosen * scaling
    turned = jnp.transpose(jnp.concatenate([chosen, chosen], axis=0))
    half = turned.shape[0] // 2
    measured = jnp.where(iotas((half, LANES))[1] < STATES, turned[:half], turned[half:])
    out_ref[...] = moved_ref[...] + measured


def update_step(arrived, moved, band, coarse, count):
    shares = arrived.shape[0]
    return pl.pallas_call(
        functools.partial(update_kernel, count),
        out_shape=jax.ShapeDtypeStruct(moved.shape, F32),
        in_specs=[VMEM] * 4,
        out_specs=VMEM,
        compiler_params=PARAMS,
        name="state_update",
    )(arrived.reshape(shares * KINDS, LANES), jnp.asarray(pool_table(shares, coarse)), moved, band)


def state_step_general(band_edges, owner_counts, dynamics, state):
    own = lax.axis_index("bins")
    capacity = state.shape[0]
    slot = jnp.arange(capacity, dtype=jnp.int32)
    start = jnp.cumsum(owner_counts)[own] - owner_counts[own]
    band = jnp.sum((slot + start)[:, None] >= band_edges[None, 1:NCLASS], axis=1)
    band = jnp.where(slot < owner_counts[own], band, -1).astype(jnp.int32)
    limit = STATES >> jnp.arange(NCLASS)[:, None, None]
    index = jnp.arange(STATES)
    inside = (index[:, None] < limit) & (index[None, :] < limit)
    chosen = (band[:, None] == jnp.arange(NCLASS)[None, :]).astype(F32)
    picked = jnp.einsum(
        "rk,kij->rij", chosen, jnp.where(inside, dynamics, 0.0), precision=HIGHEST
    )
    parts = state.reshape(capacity, 2, STATES)
    moved = jnp.einsum("rij,rcj->rci", picked, parts, precision=HIGHEST)
    return moved.reshape(state.shape), jnp.tile(band, 2)[None, :]


def exchanged(values, axes):
    return lax.all_to_all(values, axes, split_axis=0, concat_axis=0, tiled=True)


def body(profiles, band_edges, owner_counts, dynamics, prev_state):
    groups, scans = lax.axis_size("bins"), lax.axis_size("scans")
    prof_rows, length = profiles.shape
    capacity = prev_state.shape[0]
    coarse = length // HALF
    shares = groups * scans
    count = prof_rows * scans * TILE
    state = prev_state.reshape(capacity, 2 * STATES)
    if groups == 8 and scans == 4 and coarse == 16 * shares and capacity == HALF:
        columns, wanted, lane_band, row_band = columns_step(
            profiles.reshape(length), band_edges, owner_counts, capacity
        )
        columns = exchanged(columns, "bins").reshape(coarse // 2, LANES)
        blocks, turn = coarse_step(columns, groups, shares)
        blocks = exchanged(blocks.reshape(shares, 8, LANES), ("bins", "scans"))
        payload, moved = fine_step(
            blocks.reshape(8 * shares, LANES),
            turn,
            wanted,
            row_band,
            dynamics,
            state,
            scans,
            coarse,
        )
        arrived = exchanged(payload, ("bins", "scans"))
    else:
        moved, lane_band = state_step_general(band_edges, owner_counts, dynamics, state)
        columns = profiles.reshape(coarse // groups, groups, HALF).transpose(1, 0, 2)
        columns = exchanged(columns, "bins").reshape(coarse, HALF)
        blocks = exchanged(coarse_step_general(columns, groups), "bins")
        arrived = exchanged(fine_step_general(blocks, owner_counts, capacity), "bins")
        power = lax.psum(arrived[:, 3:], "scans")
        arrived = jnp.concatenate([arrived[:, :3], power], axis=1)
    updated = update_step(arrived, moved, lane_band, coarse, count)
    return updated.reshape(prev_state.shape)


def solution(mesh):
    return jax.shard_map(
        body,
        mesh=mesh,
        in_specs=(P("scans", "bins"), P(), P(), P(), P("bins", "scans", None)),
        out_specs=P("bins", "scans", None),
        check_vma=False,
    )
```

```python
import functools
import math

import jax
import jax.numpy as jnp
import numpy as np
from jax import lax
from jax.experimental import pallas as pl
from jax.experimental.pallas import tpu as pltpu
from jax.sharding import PartitionSpec as P

TILE = 512
STATES = 64
NCLASS = 5
LANES = 128

EPSILON = 1e-05
HIGHEST = lax.Precision.HIGHEST
BF16 = jnp.bfloat16
F32 = jnp.float32


def unit_root(order, exponents):
    angles = 2.0 * np.pi * (np.asarray(exponents, dtype=np.int64) % order) / order
    return np.cos(angles), -np.sin(angles)


def two_terms(values):
    high = np.asarray(values, np.float32).astype(BF16)
    low = (np.asarray(values, np.float64) - high.astype(np.float64)).astype(BF16)
    return high, low


def split_two(values):
    high = values.astype(BF16)
    return high, (values - high.astype(F32)).astype(BF16)


def dot(left, right):
    return jnp.dot(left, right, preferred_element_type=F32)


VMEM = pl.BlockSpec(memory_space=pltpu.VMEM)
PARAMS = pltpu.CompilerParams(vmem_limit_bytes=32 << 20)


KINDS = 4
HALF = LANES // 2


def unit_turn(phase, order):
    shifted = phase + order // 8
    quadrant = (shifted >> (order.bit_length() - 3)) & 3
    x = ((shifted & (order // 4 - 1)) - order // 8).astype(F32) * (2.0 * math.pi / order)
    y = x * x
    cosine = 1.0 + y * (-1 / 2 + y * (1 / 24 + y * (-1 / 720 + y * (1 / 40320))))
    sine = x * (1.0 + y * (-1 / 6 + y * (1 / 120 + y * (-1 / 5040 + y * (1 / 362880)))))
    odd = (quadrant & 1) == 1
    real, imag = jnp.where(odd, sine, cosine), jnp.where(odd, cosine, sine)
    real = jnp.where((quadrant == 1) | (quadrant == 2), -real, real)
    return real, jnp.where(quadrant >= 2, -imag, imag)


def iotas(shape):
    return [lax.broadcasted_iota(jnp.int32, shape, axis) for axis in range(len(shape))]


def columns_kernel(
    order,
    x_hbm,
    edges_hbm,
    counts_hbm,
    out_ref,
    turn_ref,
    wanted_ref,
    lane_band_ref,
    row_band_ref,
    x_ref,
    edges_ref,
    counts_ref,
    copied,
):
    groups, rows, _ = out_ref.shape
    capacity = row_band_ref.shape[0]
    copies = [
        pltpu.make_async_copy(source, target, copied.at[at])
        for at, (source, target) in enumerate(
            ((x_hbm, x_ref), (edges_hbm, edges_ref), (counts_hbm, counts_ref))
        )
    ]
    for copy in copies:
        copy.start()
    row, lane = iotas((8, LANES))
    own = lax.axis_index("bins")
    own_share = own * lax.axis_size("scans") + lax.axis_index("scans")
    k_index = 8 * own_share + 4 * (lane >> 6) + (row & 3)
    for c in range(groups):
        phase = ((c * HALF + (lane & (HALF - 1))) * k_index) & (order - 1)
        turn_ref[2 * c], turn_ref[2 * c + 1] = unit_turn(phase, order)
    for copy in copies:
        copy.wait()
    low_lanes = iotas((rows, LANES))[1] < HALF
    for pair in range(groups // 2):
        even = x_ref[pl.ds(pair, rows, stride=groups), :]
        odd = x_ref[pl.ds(groups // 2 + pair, rows, stride=groups), :]
        out_ref[2 * pair] = jnp.where(low_lanes, even, pltpu.roll(odd, HALF, 1))
        out_ref[2 * pair + 1] = jnp.where(low_lanes, pltpu.roll(even, HALF, 1), odd)
    lane = iotas((1, LANES))[1]
    rank = lane & (HALF - 1)
    start, own_start, own_count = jnp.int32(0), jnp.int32(0), jnp.int32(0)
    wanted = []
    for owner in range(groups):
        count = counts_ref[owner]
        wanted.append(jnp.where(rank < count, start + rank, -1))
        own_start = jnp.where(own == owner, start, own_start)
        own_count = jnp.where(own == owner, count, own_count)
        start = start + count
    for pair in range(groups // 2):
        wanted_ref[:, pair * LANES : (pair + 1) * LANES] = jnp.where(
            lane < HALF, wanted[2 * pair], wanted[2 * pair + 1]
        )
    for ref, slot in (
        (lane_band_ref, lane & (capacity - 1)),
        (row_band_ref, iotas((capacity, LANES))[0]),
    ):
        band = jnp.zeros_like(slot)
        for at in range(1, NCLASS):
            band = band + jnp.where(slot >= edges_ref[at] - own_start, 1, 0)
        ref[...] = jnp.where(slot < own_count, band, -1)


def columns_step(profile, band_edges, owner_counts, capacity, order):
    groups = owner_counts.shape[0]
    rows = profile.shape[0] // (groups * LANES)
    return pl.pallas_call(
        functools.partial(columns_kernel, order),
        out_shape=(
            jax.ShapeDtypeStruct((groups, rows, LANES), F32),
            jax.ShapeDtypeStruct((2 * groups, 8, LANES), F32),
            jax.ShapeDtypeStruct((1, groups * capacity), jnp.int32),
            jax.ShapeDtypeStruct((1, LANES), jnp.int32),
            jax.ShapeDtypeStruct((capacity, LANES), jnp.int32),
        ),
        in_specs=[pl.BlockSpec(memory_space=pltpu.HBM)] * 3,
        out_specs=(VMEM,) * 5,
        scratch_shapes=[
            pltpu.VMEM((groups * rows, LANES), F32),
            pltpu.SMEM(band_edges.shape, jnp.int32),
            pltpu.SMEM(owner_counts.shape, jnp.int32),
            pltpu.SemaphoreType.DMA((3,)),
        ],
        compiler_params=PARAMS,
        name="columns",
    )(profile.reshape(-1, LANES), band_edges, owner_counts)


def coarse_table(coarse):
    half, quarter = coarse // 2, coarse // 4
    k_index = np.arange(quarter)
    a_index = np.concatenate([np.arange(0, half, 2), np.arange(1, half, 2)])
    real, imag = unit_root(half, k_index[:, None] * a_index[None, :])
    imag[0] = 1
    parts = [part.reshape(quarter // 16, 2, 2, 1, 4, half) for part in (real, imag)]
    parts = np.concatenate(parts, axis=3).transpose(0, 2, 3, 1, 4, 5)
    return np.concatenate(two_terms(parts.reshape(half, half)), axis=1)


def coarse_kernel(shares, x_ref, table_ref, out_ref):
    half = x_ref.shape[0]
    quarter = half // 2
    row, lane = iotas((8, LANES))
    low_lanes = lane < HALF
    sums = []
    for parity in range(2):
        high, low = split_two(x_ref[pl.ds(parity, quarter, stride=2), :])
        at = parity * quarter
        both = dot(table_ref[:, at : at + quarter], jnp.concatenate([high, low], axis=1))
        rest = dot(table_ref[:, half + at : half + at + quarter], high)
        sums.append(both[:, :LANES] + both[:, LANES:] + rest)
    base = 8 * (row >> 2) + 4 * (lane >> 6) + (row & 3)
    base_cosine, base_sine = unit_turn(base, 2 * half)
    packed = low_lanes & (row == 0)
    for sign, block in [(sign, block) for block in range(half // 32) for sign in (1, -1)]:
        pieces = []
        for at in range(32 * block, 32 * (block + 1), 8):
            even, odd = sums[0][at : at + 8], sums[1][at : at + 8]
            pieces.append(even + odd if sign > 0 else even - odd)
        real_low, imag_low, real_high, imag_high = pieces
        if block == 0 and sign < 0:
            imag_low = jnp.where(row == 0, 0.0, imag_low)
        even_real = jnp.where(low_lanes, real_low, pltpu.roll(real_high, HALF, 1))
        even_imag = jnp.where(low_lanes, imag_low, pltpu.roll(imag_high, HALF, 1))
        odd_real = jnp.where(low_lanes, pltpu.roll(real_low, HALF, 1), real_high)
        odd_imag = jnp.where(low_lanes, pltpu.roll(imag_low, HALF, 1), imag_high)
        first = 2 * block + (0 if sign > 0 else shares // 2)
        angle = math.pi * 8 * first / half
        cosine = base_cosine * math.cos(angle) - base_sine * math.sin(angle)
        sine = base_sine * math.cos(angle) + base_cosine * math.sin(angle)
        real = even_real + odd_real * cosine + odd_imag * sine
        if first == 0:
            cosine = jnp.where(packed, -1.0, cosine)
        imag = even_imag + odd_imag * cosine - odd_real * sine
        out_ref[pl.ds(8 * first, 8, stride=2), :] = real
        out_ref[pl.ds(8 * first + 1, 8, stride=2), :] = imag


def coarse_step(columns, shares):
    half = columns.shape[0]
    return pl.pallas_call(
        functools.partial(coarse_kernel, shares),
        out_shape=jax.ShapeDtypeStruct((half, LANES), F32),
        in_specs=[VMEM] * 2,
        out_specs=VMEM,
        compiler_params=PARAMS,
        name="coarse_dft",
    )(columns, jnp.asarray(coarse_table(2 * half)))


def coarse_step_general(columns, shares):
    coarse = columns.shape[0]
    half = coarse // 2
    real, imag = unit_root(coarse, np.arange(half)[:, None] * np.arange(coarse)[None, :])
    imag[0] = 1 - 2 * (np.arange(coarse) % 2)
    table = jnp.asarray(np.concatenate([real, imag]).astype(np.float32))
    spectrum = jnp.dot(table, columns, precision=HIGHEST)
    blocks = jnp.concatenate([spectrum[:half], spectrum[half:]], axis=1)
    return blocks.reshape(shares, half // shares, LANES)


def fine_tables(groups, profiles, coarse):
    fine_length = groups * HALF
    doubled = np.arange(LANES) % HALF
    turn = unit_root(fine_length, np.arange(groups)[:, None] * doubled[None, :])
    middle = (np.arange(groups)[:, None] * HALF + doubled[None, :]) * (coarse // 2)
    middle = unit_root(coarse * fine_length, middle)
    turns = np.concatenate(turn + middle).astype(np.float32)
    order = np.arange(HALF)
    order[HALF // 2 :] = order[HALF // 2 :][::-1]
    real, imag = unit_root(HALF, np.arange(HALF)[:, None] * order[None, :])
    sign = np.where(np.arange(HALF) < HALF // 2, 1, -1)
    both = np.eye(2)
    matrix = np.block(
        [
            [np.kron(both, real), np.kron(both, imag * sign)],
            [np.kron(both, -imag), np.kron(both, real * sign)],
        ]
    )
    sums = np.zeros((3, profiles, KINDS, 2, profiles // 2 + 2, 2, 4), np.float32)
    for p in range(profiles):
        pair, which = divmod(p, 2)
        sums[0, p, 0, :, pair, which, :] = 1
        sums[1, p, 1, :, pair, which, 1:] = 1
        sums[2, p, 1, :, pair, which, :] = 1
        sums[1, p, 2, :, pair, which, 0] = 1
        sums[0, p, 2, :, profiles // 2, which, pair] = 1
        sums[:, p, 3, :, profiles // 2 + 1] = 1
    sums = sums.reshape(3 * profiles * KINDS, -1)
    sums = np.pad(sums, [(0, 0), (0, 4 * LANES - sums.shape[1])]).astype(BF16)
    return turns, np.concatenate([np.concatenate(two_terms(matrix), axis=1), sums])


def add(p, q):
    return (p[0] + q[0], p[1] + q[1])


def sub(p, q):
    return (p[0] - q[0], p[1] - q[1])


def times(p, cosine, sine):
    return (p[0] * cosine + p[1] * sine, p[1] * cosine - p[0] * sine)


def eight_point(values):
    half = math.sqrt(0.5)

    def down(p):
        return (p[1], -p[0])

    def four(a, b, c, d):
        s0, s1, s2, s3 = add(a, c), sub(a, c), add(b, d), sub(b, d)
        turned = (s1[0] + s3[1], s1[1] - s3[0]), (s1[0] - s3[1], s1[1] + s3[0])
        return add(s0, s2), turned[0], sub(s0, s2), turned[1]

    even = four(values[0], values[2], values[4], values[6])
    odd = four(values[1], values[3], values[5], values[7])
    turned = [
        odd[0],
        ((odd[1][0] + odd[1][1]) * half, (odd[1][1] - odd[1][0]) * half),
        down(odd[2]),
        ((odd[3][1] - odd[3][0]) * half, (odd[3][0] + odd[3][1]) * -half),
    ]
    return [add(e, t) for e, t in zip(even, turned)] + [sub(e, t) for e, t in zip(even, turned)]


def fine_kernel(
    profiles,
    x_ref,
    turn_ref,
    wanted_ref,
    band_ref,
    turns_ref,
    table_ref,
    dynamics_ref,
    state_ref,
    out_ref,
    moved_ref,
):
    groups = out_ref.shape[0]
    first = (lax.axis_index("bins") == 0) & (lax.axis_index("scans") == 0)
    row, lane = iotas((8, LANES))
    low_lanes = lane < HALF
    low_side = (lane & (HALF - 1)) < HALF // 2
    packed = first & low_lanes & ((row & 3) == 0)
    shifted = first & low_lanes & ((row & 3) == 1)
    pairs = profiles // 2
    columns = [[] for _ in range(pairs + 1)]
    for c in range(groups):
        cosine, sine = turn_ref[2 * c], turn_ref[2 * c + 1]
        at = c * 8 * profiles
        for pair in range(pairs):
            real = x_ref[pl.ds(at + 16 * pair, 8, stride=2), :]
            imag = x_ref[pl.ds(at + 16 * pair + 1, 8, stride=2), :]
            if pair == 0:
                middle = jnp.where(packed, imag, 0.0)
            imag = jnp.where(packed, 0.0, imag)
            columns[pair].append(times((real, imag), cosine, sine))
        middle = jnp.where(shifted, x_ref[pl.ds(at + 15, 8, stride=2), :], middle)
        middle_real = turns_ref[2 * groups + c : 2 * groups + c + 1, :]
        middle_imag = turns_ref[3 * groups + c : 3 * groups + c + 1, :]
        columns[pairs].append((middle * middle_real, middle * middle_imag))
    transformed = [eight_point(column) for column in columns]
    blocks = []
    for u in range(groups):
        cosine, sine = turns_ref[u : u + 1, :], -turns_ref[groups + u : groups + u + 1, :]
        for column in transformed:
            blocks.append(times(column[u], cosine, sine) if u else column[u])
    wide = 2 * LANES
    size = wide
    left = jnp.concatenate(
        [jnp.concatenate([block[part] for block in blocks], axis=0) for part in range(2)], axis=1
    )
    high, low = split_two(left)
    product = dot(high, table_ref[:size, :])
    product = product[:, :wide] + product[:, wide:] + dot(low, table_ref[:size, :wide])
    spectrum = []
    for u in range(groups):
        spectrum.append([])
        for at in range(pairs + 1):
            start = 8 * (u * (pairs + 1) + at)
            block = (product[start : start + 8, :LANES], product[start : start + 8, LANES:])
            dropped = ~low_side & packed if at < pairs else ~low_side
            spectrum[u].append(tuple(jnp.where(dropped, 0.0, part) for part in block))
    power = [
        sum(block[0] * block[0] + block[1] * block[1] for block in spectrum[u])
        for u in range(groups)
    ]
    summands = []
    for part in range(2):
        for u in range(groups):
            mirror = groups - 1 - u
            rows = [
                jnp.where(low_side, spectrum[u][pair][part], spectrum[mirror][pair][part])
                for pair in range(pairs)
            ]
            rows.append(spectrum[u][pairs][part])
            rows.append(jnp.where(low_side, power[u], power[mirror]))
            summands.append(jnp.concatenate(rows, axis=0))
    summands = jnp.concatenate(split_two(jnp.concatenate(summands, axis=1)), axis=0)
    summed = dot(table_ref[size:, : summands.shape[0]], summands)
    rows = summed.shape[0] // 3
    _, lanes = iotas((rows, LANES))
    side, early = (lanes & (HALF - 1)) < HALF // 2, lanes < HALF
    left = []
    for part in range(2):
        pieces = []
        for at in range(part * groups, (part + 1) * groups):
            piece = summed[:, at * LANES : (at + 1) * LANES]
            piece = jnp.where(
                side,
                piece[:rows],
                jnp.where(early, piece[rows : 2 * rows], piece[2 * rows :]),
            )
            pieces.append(piece)
        left.append(jnp.concatenate(pieces, axis=1))
    left = jnp.concatenate(split_two(jnp.concatenate(left, axis=0)), axis=0)
    wanted = wanted_ref[...]
    chosen = []
    for u in range(groups):
        tile = u + groups * iotas((HALF // 2, wanted.shape[1]))[0]
        chosen += [jnp.where(tile == wanted, 1.0, 0.0).astype(BF16)] * 4
    routed = dot(left, jnp.concatenate(chosen, axis=0))
    routed = routed[: 2 * rows] + routed[2 * rows :]
    for pair in range(groups // 2):
        real = routed[:rows, pair * LANES : (pair + 1) * LANES]
        imag = routed[rows:, pair * LANES : (pair + 1) * LANES]
        out_ref[2 * pair] = jnp.where(early, real, pltpu.roll(imag, HALF, 1))
        out_ref[2 * pair + 1] = jnp.where(early, pltpu.roll(real, HALF, 1), imag)
    moved_ref[...] = state_product(dynamics_ref[...], state_ref[...], band_ref[...])


def state_product(dynamics, state, band):
    row, column = iotas((NCLASS * STATES, STATES))
    limit = STATES >> (row >> 6)
    inside = ((row & (STATES - 1)) < limit) & (column < limit)
    dynamics = jnp.where(inside, dynamics, 0.0)
    empty = jnp.zeros_like(dynamics)
    halves = [
        jnp.concatenate([dynamics, empty], axis=1),
        jnp.concatenate([empty, dynamics], axis=1),
    ]
    matrix = jnp.concatenate(
        [half[k * STATES : (k + 1) * STATES] for k in range(NCLASS) for half in halves], axis=0
    )
    state_high, state_low = split_two(state)
    high, low = split_two(matrix)
    moved = lax.dot_general(
        jnp.concatenate([state_high, state_low, state_high], axis=1),
        jnp.concatenate([high, high, low], axis=1),
        (((1,), (1,)), ((), ())),
        preferred_element_type=F32,
    )
    result = jnp.zeros(state.shape, F32)
    for k in range(NCLASS):
        result = jnp.where(band == k, moved[:, k * LANES : (k + 1) * LANES], result)
    return result


def fine_step(arrived, turn, wanted, band, dynamics, state, profiles, coarse):
    groups = turn.shape[0] // 2
    turns, table = fine_tables(groups, profiles, coarse)
    out, moved = pl.pallas_call(
        functools.partial(fine_kernel, profiles),
        out_shape=(
            jax.ShapeDtypeStruct((groups, profiles * KINDS, LANES), F32),
            jax.ShapeDtypeStruct(state.shape, F32),
        ),
        in_specs=[VMEM] * 8,
        out_specs=(VMEM,) * 2,
        compiler_params=PARAMS,
        name="fine_dft",
    )(
        arrived,
        turn,
        wanted,
        band,
        jnp.asarray(turns),
        jnp.asarray(table),
        dynamics.reshape(NCLASS * STATES, STATES),
        state,
    )
    return out.reshape(groups * profiles, KINDS, LANES), moved


def fine_step_general(arrived, owner_counts, capacity):
    groups, rows = arrived.shape[:2]
    coarse = 2 * rows * groups
    fine_length = groups * HALF
    order = coarse * fine_length
    own = lax.axis_index("bins")
    real, imag = arrived[:, :, :HALF], arrived[:, :, HALF:]
    points = jnp.arange(fine_length, dtype=jnp.int32).reshape(groups, 1, HALF)
    k_index = own * rows + jnp.arange(rows, dtype=jnp.int32)[None, :, None]
    cosine, sine = unit_turn(points * k_index & (order - 1), order)
    packed = (own == 0) & (jnp.arange(rows)[None, :, None] == 0)
    middle = jnp.where(own == 0, imag[:, :1], 0.0)
    imag = jnp.where(packed, 0.0, imag)
    real, imag = real * cosine + imag * sine, imag * cosine - real * sine
    cosine, sine = unit_turn(points * (coarse // 2), order)
    real = jnp.concatenate([real, middle * cosine], axis=1)
    imag = jnp.concatenate([imag, -middle * sine], axis=1)

    def turned(pattern, root, parts):
        cosine, sine = (jnp.asarray(part.astype(np.float32)) for part in root)
        mul = functools.partial(jnp.einsum, pattern, precision=HIGHEST)
        return (
            mul(cosine, parts[0]) - mul(sine, parts[1]),
            mul(cosine, parts[1]) + mul(sine, parts[0]),
        )

    group_index, point_index = np.arange(groups), np.arange(HALF)
    parts = turned(
        "cu,crj->urj", unit_root(groups, group_index[:, None] * group_index), (real, imag)
    )
    parts = turned(
        "uj,urj->urj", unit_root(fine_length, group_index[:, None] * point_index), parts
    )
    parts = turned(
        "jv,urj->vur", unit_root(HALF, point_index[:, None] * point_index), parts
    )
    tiles = fine_length // 2
    kept = jnp.concatenate([~packed[0, :, 0], jnp.zeros((1,), bool)])
    sides = []
    for part, sign in zip(parts, (1.0, -1.0)):
        part = part.reshape(fine_length, rows + 1)
        sides.append((part[:tiles], sign * jnp.where(kept, part[tiles:][::-1], 0.0)))
    power = sum(jnp.sum(part * part, axis=1) for pair in sides for part in pair)
    starts = jnp.cumsum(owner_counts) - owner_counts
    slot_index = jnp.arange(capacity, dtype=jnp.int32)
    filled = slot_index[None, :] < owner_counts[:, None]
    chosen = jnp.clip(starts[:, None] + slot_index[None, :], 0, tiles - 1)

    def kinds(low, high):
        low_sums, high_sums = jnp.sum(low[:, :rows], axis=1), jnp.sum(high[:, 1:rows], axis=1)
        values = jnp.stack([low_sums, high_sums, high[:, 0] + low[:, rows], power], axis=1)
        return jnp.where(filled[:, :, None], values[chosen], 0.0).transpose(0, 2, 1)

    return jnp.concatenate([kinds(*sides[0]), kinds(*sides[1])], axis=2)


def pool_table(shares, coarse):
    pool = np.zeros((21, 16, shares, KINDS), np.float32)
    sums = pool[:20].reshape(NCLASS, STATES, shares, KINDS)
    wide = TILE // STATES
    rows = coarse // 2 // shares
    for share in range(shares):
        first = rows * share
        rest = coarse - first if share else coarse // 2
        for kind, at in enumerate((first, coarse - first - 1, rest)):
            for band in range(NCLASS):
                sums[band, at // wide >> band, share, kind] = 1.0
    pool[20, :, :, 3] = 1.0
    return pool.reshape(-1, shares * KINDS).astype(BF16)


def update_kernel(count, x_ref, pool_ref, moved_ref, band_ref, out_ref):
    band = band_ref[...]
    sums = dot(pool_ref[...], jnp.concatenate(split_two(x_ref[...]), axis=1))
    sums = sums[:, :LANES] + sums[:, LANES:]
    power = sums[NCLASS * STATES : NCLASS * STATES + 1] * (1.0 / count)
    span = jnp.left_shift(TILE // STATES, jnp.maximum(band, 0)).astype(F32)
    scaling = 1.0 / jnp.sqrt(span * (power + EPSILON))
    scaling = jnp.where(band < 0, 0.0, scaling)
    chosen = sums[:STATES]
    for k in range(1, NCLASS):
        chosen = jnp.where(band == k, sums[k * STATES : (k + 1) * STATES], chosen)
    chosen = chosen * scaling
    turned = jnp.transpose(jnp.concatenate([chosen, chosen], axis=0))
    half = turned.shape[0] // 2
    measured = jnp.where(iotas((half, LANES))[1] < STATES, turned[:half], turned[half:])
    out_ref[...] = moved_ref[...] + measured


def update_step(arrived, moved, band, coarse, count):
    shares = arrived.shape[0]
    return pl.pallas_call(
        functools.partial(update_kernel, count),
        out_shape=jax.ShapeDtypeStruct(moved.shape, F32),
        in_specs=[VMEM] * 4,
        out_specs=VMEM,
        compiler_params=PARAMS,
        name="state_update",
    )(arrived.reshape(shares * KINDS, LANES), jnp.asarray(pool_table(shares, coarse)), moved, band)


def state_step_general(band_edges, owner_counts, dynamics, state):
    own = lax.axis_index("bins")
    capacity = state.shape[0]
    slot = jnp.arange(capacity, dtype=jnp.int32)
    start = jnp.cumsum(owner_counts)[own] - owner_counts[own]
    band = jnp.sum((slot + start)[:, None] >= band_edges[None, 1:NCLASS], axis=1)
    band = jnp.where(slot < owner_counts[own], band, -1).astype(jnp.int32)
    limit = STATES >> jnp.arange(NCLASS)[:, None, None]
    index = jnp.arange(STATES)
    inside = (index[:, None] < limit) & (index[None, :] < limit)
    chosen = (band[:, None] == jnp.arange(NCLASS)[None, :]).astype(F32)
    picked = jnp.einsum(
        "rk,kij->rij", chosen, jnp.where(inside, dynamics, 0.0), precision=HIGHEST
    )
    parts = state.reshape(capacity, 2, STATES)
    moved = jnp.einsum("rij,rcj->rci", picked, parts, precision=HIGHEST)
    return moved.reshape(state.shape), jnp.tile(band, 2)[None, :]


def exchanged(values, axes):
    return lax.all_to_all(values, axes, split_axis=0, concat_axis=0, tiled=True)


def body(profiles, band_edges, owner_counts, dynamics, prev_state):
    groups, scans = lax.axis_size("bins"), lax.axis_size("scans")
    prof_rows, length = profiles.shape
    capacity = prev_state.shape[0]
    coarse = length // HALF
    shares = groups * scans
    count = prof_rows * scans * TILE
    state = prev_state.reshape(capacity, 2 * STATES)
    if groups == 8 and scans == 4 and coarse == 16 * shares and capacity == HALF:
        columns, turn, wanted, lane_band, row_band = columns_step(
            profiles.reshape(length), band_edges, owner_counts, capacity, length * groups
        )
        columns = exchanged(columns, "bins").reshape(coarse // 2, LANES)
        blocks = coarse_step(columns, shares)
        blocks = exchanged(blocks.reshape(shares, 8, LANES), ("bins", "scans"))
        payload, moved = fine_step(
            blocks.reshape(8 * shares, LANES),
            turn,
            wanted,
            row_band,
            dynamics,
            state,
            scans,
            coarse,
        )
        arrived = exchanged(payload, ("bins", "scans"))
    else:
        moved, lane_band = state_step_general(band_edges, owner_counts, dynamics, state)
        columns = profiles.reshape(coarse // groups, groups, HALF).transpose(1, 0, 2)
        columns = exchanged(columns, "bins").reshape(coarse, HALF)
        blocks = exchanged(coarse_step_general(columns, groups), "bins")
        arrived = exchanged(fine_step_general(blocks, owner_counts, capacity), "bins")
        power = lax.psum(arrived[:, 3:], "scans")
        arrived = jnp.concatenate([arrived[:, :3], power], axis=1)
    updated = update_step(arrived, moved, lane_band, coarse, count)
    return updated.reshape(prev_state.shape)


def solution(mesh):
    return jax.shard_map(
        body,
        mesh=mesh,
        in_specs=(P("scans", "bins"), P(), P(), P(), P("bins", "scans", None)),
        out_specs=P("bins", "scans", None),
        check_vma=False,
    )
```

```python
import functools
import math

import jax
import jax.numpy as jnp
import numpy as np
from jax import lax
from jax.experimental import pallas as pl
from jax.experimental.pallas import tpu as pltpu
from jax.sharding import PartitionSpec as P

TILE = 512
STATES = 64
NCLASS = 5
LANES = 128

EPSILON = 1e-05
HIGHEST = lax.Precision.HIGHEST
BF16 = jnp.bfloat16
F32 = jnp.float32


def unit_root(order, exponents):
    angles = 2.0 * np.pi * (np.asarray(exponents, dtype=np.int64) % order) / order
    return np.cos(angles), -np.sin(angles)


def two_terms(values):
    high = np.asarray(values, np.float32).astype(BF16)
    low = (np.asarray(values, np.float64) - high.astype(np.float64)).astype(BF16)
    return high, low


def split_two(values):
    high = values.astype(BF16)
    return high, (values - high.astype(F32)).astype(BF16)


def dot(left, right):
    return jnp.dot(left, right, preferred_element_type=F32)


VMEM = pl.BlockSpec(memory_space=pltpu.VMEM)
PARAMS = pltpu.CompilerParams(vmem_limit_bytes=32 << 20)
COST = pl.CostEstimate(flops=1 << 30, bytes_accessed=1 << 24, transcendentals=0)


KINDS = 4
HALF = LANES // 2


def unit_turn(phase, order):
    shifted = phase + order // 8
    quadrant = (shifted >> (order.bit_length() - 3)) & 3
    x = ((shifted & (order // 4 - 1)) - order // 8).astype(F32) * (2.0 * math.pi / order)
    y = x * x
    cosine = 1.0 + y * (-1 / 2 + y * (1 / 24 + y * (-1 / 720 + y * (1 / 40320))))
    sine = x * (1.0 + y * (-1 / 6 + y * (1 / 120 + y * (-1 / 5040 + y * (1 / 362880)))))
    odd = (quadrant & 1) == 1
    real, imag = jnp.where(odd, sine, cosine), jnp.where(odd, cosine, sine)
    real = jnp.where((quadrant == 1) | (quadrant == 2), -real, real)
    return real, jnp.where(quadrant >= 2, -imag, imag)


def iotas(shape):
    return [lax.broadcasted_iota(jnp.int32, shape, axis) for axis in range(len(shape))]


def columns_kernel(x_ref, out_ref):
    groups, rows, _ = out_ref.shape
    low_lanes = iotas((rows, LANES))[1] < HALF
    for pair in range(groups // 2):
        even = x_ref[pl.ds(pair, rows, stride=groups), :]
        odd = x_ref[pl.ds(groups // 2 + pair, rows, stride=groups), :]
        out_ref[2 * pair] = jnp.where(low_lanes, even, pltpu.roll(odd, HALF, 1))
        out_ref[2 * pair + 1] = jnp.where(low_lanes, pltpu.roll(even, HALF, 1), odd)


def columns_step(profile, groups):
    rows = profile.shape[0] // (groups * LANES)
    return pl.pallas_call(
        columns_kernel,
        out_shape=jax.ShapeDtypeStruct((groups, rows, LANES), F32),
        in_specs=[VMEM],
        out_specs=VMEM,
        compiler_params=PARAMS,
        cost_estimate=COST,
        name="columns",
    )(profile.reshape(-1, LANES))


def coarse_table(coarse):
    half, quarter = coarse // 2, coarse // 4
    k_index = np.arange(quarter)
    a_index = np.concatenate([np.arange(0, half, 2), np.arange(1, half, 2)])
    real, imag = unit_root(half, k_index[:, None] * a_index[None, :])
    imag[0] = 1
    parts = [part.reshape(quarter // 16, 2, 2, 1, 4, half) for part in (real, imag)]
    parts = np.concatenate(parts, axis=3).transpose(0, 2, 3, 1, 4, 5)
    return np.concatenate(two_terms(parts.reshape(half, half)), axis=1)


def slot_bands(edges_ref, counts_ref, wanted_ref, lane_band_ref, row_band_ref):
    groups, capacity = counts_ref.shape[1], row_band_ref.shape[0]
    own = lax.axis_index("bins")
    counts = [
        jnp.broadcast_to(counts_ref[:, owner : owner + 1], (1, LANES)) for owner in range(groups)
    ]
    lane = iotas((1, LANES))[1]
    rank = lane & (capacity - 1)
    start = jnp.zeros((1, LANES), jnp.int32)
    own_start, own_count = start, start
    wanted = []
    for owner, count in enumerate(counts):
        wanted.append(jnp.where(rank < count, start + rank, -1))
        own_start = jnp.where(own == owner, start, own_start)
        own_count = jnp.where(own == owner, count, own_count)
        start = start + count
    for pair in range(groups // 2):
        wanted_ref[:, pair * LANES : (pair + 1) * LANES] = jnp.where(
            lane < HALF, wanted[2 * pair], wanted[2 * pair + 1]
        )
    edges = [jnp.broadcast_to(edges_ref[:, at : at + 1], (1, LANES)) for at in range(1, NCLASS)]
    for ref, slot in ((lane_band_ref, rank), (row_band_ref, iotas((capacity, LANES))[0])):
        band = jnp.zeros_like(slot)
        for edge in edges:
            band = band + jnp.where(slot + own_start >= edge, 1, 0)
        ref[...] = jnp.where(slot < own_count, band, -1)


def coarse_kernel(
    groups,
    shares,
    x_ref,
    table_ref,
    edges_ref,
    counts_ref,
    out_ref,
    turn_ref,
    wanted_ref,
    lane_band_ref,
    row_band_ref,
):
    half = x_ref.shape[0]
    quarter = half // 2
    row, lane = iotas((8, LANES))
    low_lanes = lane < HALF
    sums = []
    for parity in range(2):
        high, low = split_two(x_ref[pl.ds(parity, quarter, stride=2), :])
        at = parity * quarter
        both = dot(table_ref[:, at : at + quarter], jnp.concatenate([high, low], axis=1))
        rest = dot(table_ref[:, half + at : half + at + quarter], high)
        sums.append(both[:, :LANES] + both[:, LANES:] + rest)
    base = 8 * (row >> 2) + 4 * (lane >> 6) + (row & 3)
    base_cosine, base_sine = unit_turn(base, 2 * half)
    packed = low_lanes & (row == 0)
    for sign, block in [(sign, block) for block in range(half // 32) for sign in (1, -1)]:
        pieces = []
        for at in range(32 * block, 32 * (block + 1), 8):
            even, odd = sums[0][at : at + 8], sums[1][at : at + 8]
            pieces.append(even + odd if sign > 0 else even - odd)
        real_low, imag_low, real_high, imag_high = pieces
        if block == 0 and sign < 0:
            imag_low = jnp.where(row == 0, 0.0, imag_low)
        even_real = jnp.where(low_lanes, real_low, pltpu.roll(real_high, HALF, 1))
        even_imag = jnp.where(low_lanes, imag_low, pltpu.roll(imag_high, HALF, 1))
        odd_real = jnp.where(low_lanes, pltpu.roll(real_low, HALF, 1), real_high)
        odd_imag = jnp.where(low_lanes, pltpu.roll(imag_low, HALF, 1), imag_high)
        first = 2 * block + (0 if sign > 0 else shares // 2)
        angle = math.pi * 8 * first / half
        cosine = base_cosine * math.cos(angle) - base_sine * math.sin(angle)
        sine = base_sine * math.cos(angle) + base_cosine * math.sin(angle)
        real = even_real + odd_real * cosine + odd_imag * sine
        if first == 0:
            cosine = jnp.where(packed, -1.0, cosine)
        imag = even_imag + odd_imag * cosine - odd_real * sine
        out_ref[pl.ds(8 * first, 8, stride=2), :] = real
        out_ref[pl.ds(8 * first + 1, 8, stride=2), :] = imag
    own = lax.axis_index("bins") * lax.axis_size("scans") + lax.axis_index("scans")
    k_index = 8 * own + 4 * (lane >> 6) + (row & 3)
    order = 2 * half * groups * HALF
    for c in range(groups):
        phase = ((c * HALF + (lane & (HALF - 1))) * k_index) & (order - 1)
        turn_ref[2 * c], turn_ref[2 * c + 1] = unit_turn(phase, order)
    slot_bands(edges_ref, counts_ref, wanted_ref, lane_band_ref, row_band_ref)


def coarse_step(columns, band_edges, owner_counts, shares, capacity):
    half, groups = columns.shape[0], owner_counts.shape[0]
    return pl.pallas_call(
        functools.partial(coarse_kernel, groups, shares),
        out_shape=(
            jax.ShapeDtypeStruct((half, LANES), F32),
            jax.ShapeDtypeStruct((2 * groups, 8, LANES), F32),
            jax.ShapeDtypeStruct((1, groups * capacity), jnp.int32),
            jax.ShapeDtypeStruct((1, LANES), jnp.int32),
            jax.ShapeDtypeStruct((capacity, LANES), jnp.int32),
        ),
        in_specs=[VMEM] * 4,
        out_specs=(VMEM,) * 5,
        compiler_params=PARAMS,
        cost_estimate=COST,
        name="coarse_dft",
    )(
        columns,
        jnp.asarray(coarse_table(2 * half)),
        band_edges.reshape(1, -1),
        owner_counts.reshape(1, -1),
    )


def coarse_step_general(columns, shares):
    coarse = columns.shape[0]
    half = coarse // 2
    real, imag = unit_root(coarse, np.arange(half)[:, None] * np.arange(coarse)[None, :])
    imag[0] = 1 - 2 * (np.arange(coarse) % 2)
    table = jnp.asarray(np.concatenate([real, imag]).astype(np.float32))
    spectrum = jnp.dot(table, columns, precision=HIGHEST)
    blocks = jnp.concatenate([spectrum[:half], spectrum[half:]], axis=1)
    return blocks.reshape(shares, half // shares, LANES)


def fine_tables(groups, profiles, coarse):
    fine_length = groups * HALF
    doubled = np.arange(LANES) % HALF
    turn = unit_root(fine_length, np.arange(groups)[:, None] * doubled[None, :])
    middle = (np.arange(groups)[:, None] * HALF + doubled[None, :]) * (coarse // 2)
    middle = unit_root(coarse * fine_length, middle)
    turns = np.concatenate(turn + middle).astype(np.float32)
    order = np.arange(HALF)
    order[HALF // 2 :] = order[HALF // 2 :][::-1]
    real, imag = unit_root(HALF, np.arange(HALF)[:, None] * order[None, :])
    sign = np.where(np.arange(HALF) < HALF // 2, 1, -1)
    both = np.eye(2)
    matrix = np.block(
        [
            [np.kron(both, real), np.kron(both, imag * sign)],
            [np.kron(both, -imag), np.kron(both, real * sign)],
        ]
    )
    sums = np.zeros((3, profiles, KINDS, 2, profiles // 2 + 2, 2, 4), np.float32)
    for p in range(profiles):
        pair, which = divmod(p, 2)
        sums[0, p, 0, :, pair, which, :] = 1
        sums[1, p, 1, :, pair, which, 1:] = 1
        sums[2, p, 1, :, pair, which, :] = 1
        sums[1, p, 2, :, pair, which, 0] = 1
        sums[0, p, 2, :, profiles // 2, which, pair] = 1
        sums[:, p, 3, :, profiles // 2 + 1] = 1
    sums = sums.reshape(3 * profiles * KINDS, -1)
    sums = np.pad(sums, [(0, 0), (0, 4 * LANES - sums.shape[1])]).astype(BF16)
    return turns, np.concatenate([np.concatenate(two_terms(matrix), axis=1), sums])


def add(p, q):
    return (p[0] + q[0], p[1] + q[1])


def sub(p, q):
    return (p[0] - q[0], p[1] - q[1])


def times(p, cosine, sine):
    return (p[0] * cosine + p[1] * sine, p[1] * cosine - p[0] * sine)


def eight_point(values):
    half = math.sqrt(0.5)

    def down(p):
        return (p[1], -p[0])

    def four(a, b, c, d):
        s0, s1, s2, s3 = add(a, c), sub(a, c), add(b, d), sub(b, d)
        turned = (s1[0] + s3[1], s1[1] - s3[0]), (s1[0] - s3[1], s1[1] + s3[0])
        return add(s0, s2), turned[0], sub(s0, s2), turned[1]

    even = four(values[0], values[2], values[4], values[6])
    odd = four(values[1], values[3], values[5], values[7])
    turned = [
        odd[0],
        ((odd[1][0] + odd[1][1]) * half, (odd[1][1] - odd[1][0]) * half),
        down(odd[2]),
        ((odd[3][1] - odd[3][0]) * half, (odd[3][0] + odd[3][1]) * -half),
    ]
    return [add(e, t) for e, t in zip(even, turned)] + [sub(e, t) for e, t in zip(even, turned)]


def fine_kernel(
    profiles,
    x_ref,
    turn_ref,
    wanted_ref,
    band_ref,
    turns_ref,
    table_ref,
    dynamics_ref,
    state_ref,
    out_ref,
    moved_ref,
):
    groups = out_ref.shape[0]
    first = (lax.axis_index("bins") == 0) & (lax.axis_index("scans") == 0)
    row, lane = iotas((8, LANES))
    low_lanes = lane < HALF
    low_side = (lane & (HALF - 1)) < HALF // 2
    packed = first & low_lanes & ((row & 3) == 0)
    shifted = first & low_lanes & ((row & 3) == 1)
    pairs = profiles // 2
    columns = [[] for _ in range(pairs + 1)]
    for c in range(groups):
        cosine, sine = turn_ref[2 * c], turn_ref[2 * c + 1]
        at = c * 8 * profiles
        for pair in range(pairs):
            real = x_ref[pl.ds(at + 16 * pair, 8, stride=2), :]
            imag = x_ref[pl.ds(at + 16 * pair + 1, 8, stride=2), :]
            if pair == 0:
                middle = jnp.where(packed, imag, 0.0)
            imag = jnp.where(packed, 0.0, imag)
            columns[pair].append(times((real, imag), cosine, sine))
        middle = jnp.where(shifted, x_ref[pl.ds(at + 15, 8, stride=2), :], middle)
        middle_real = turns_ref[2 * groups + c : 2 * groups + c + 1, :]
        middle_imag = turns_ref[3 * groups + c : 3 * groups + c + 1, :]
        columns[pairs].append((middle * middle_real, middle * middle_imag))
    transformed = [eight_point(column) for column in columns]
    blocks = []
    for u in range(groups):
        cosine, sine = turns_ref[u : u + 1, :], -turns_ref[groups + u : groups + u + 1, :]
        for column in transformed:
            blocks.append(times(column[u], cosine, sine) if u else column[u])
    wide = 2 * LANES
    size = wide
    left = jnp.concatenate(
        [jnp.concatenate([block[part] for block in blocks], axis=0) for part in range(2)], axis=1
    )
    high, low = split_two(left)
    product = dot(high, table_ref[:size, :])
    product = product[:, :wide] + product[:, wide:] + dot(low, table_ref[:size, :wide])
    spectrum = []
    for u in range(groups):
        spectrum.append([])
        for at in range(pairs + 1):
            start = 8 * (u * (pairs + 1) + at)
            block = (product[start : start + 8, :LANES], product[start : start + 8, LANES:])
            dropped = ~low_side & packed if at < pairs else ~low_side
            spectrum[u].append(tuple(jnp.where(dropped, 0.0, part) for part in block))
    power = [
        sum(block[0] * block[0] + block[1] * block[1] for block in spectrum[u])
        for u in range(groups)
    ]
    summands = []
    for part in range(2):
        for u in range(groups):
            mirror = groups - 1 - u
            rows = [
                jnp.where(low_side, spectrum[u][pair][part], spectrum[mirror][pair][part])
                for pair in range(pairs)
            ]
            rows.append(spectrum[u][pairs][part])
            rows.append(jnp.where(low_side, power[u], power[mirror]))
            summands.append(jnp.concatenate(rows, axis=0))
    summands = jnp.concatenate(split_two(jnp.concatenate(summands, axis=1)), axis=0)
    summed = dot(table_ref[size:, : summands.shape[0]], summands)
    rows = summed.shape[0] // 3
    _, lanes = iotas((rows, LANES))
    side, early = (lanes & (HALF - 1)) < HALF // 2, lanes < HALF
    left = []
    for part in range(2):
        pieces = []
        for at in range(part * groups, (part + 1) * groups):
            piece = summed[:, at * LANES : (at + 1) * LANES]
            piece = jnp.where(
                side,
                piece[:rows],
                jnp.where(early, piece[rows : 2 * rows], piece[2 * rows :]),
            )
            pieces.append(piece)
        left.append(jnp.concatenate(pieces, axis=1))
    left = jnp.concatenate(split_two(jnp.concatenate(left, axis=0)), axis=0)
    wanted = wanted_ref[...]
    chosen = []
    for u in range(groups):
        tile = u + groups * iotas((HALF // 2, wanted.shape[1]))[0]
        chosen += [jnp.where(tile == wanted, 1.0, 0.0).astype(BF16)] * 4
    routed = dot(left, jnp.concatenate(chosen, axis=0))
    routed = routed[: 2 * rows] + routed[2 * rows :]
    for pair in range(groups // 2):
        real = routed[:rows, pair * LANES : (pair + 1) * LANES]
        imag = routed[rows:, pair * LANES : (pair + 1) * LANES]
        out_ref[2 * pair] = jnp.where(early, real, pltpu.roll(imag, HALF, 1))
        out_ref[2 * pair + 1] = jnp.where(early, pltpu.roll(real, HALF, 1), imag)
    moved_ref[...] = state_product(dynamics_ref[...], state_ref[...], band_ref[...])


def state_product(dynamics, state, band):
    row, column = iotas((NCLASS * STATES, STATES))
    limit = STATES >> (row >> 6)
    inside = ((row & (STATES - 1)) < limit) & (column < limit)
    dynamics = jnp.where(inside, dynamics, 0.0)
    empty = jnp.zeros_like(dynamics)
    halves = [
        jnp.concatenate([dynamics, empty], axis=1),
        jnp.concatenate([empty, dynamics], axis=1),
    ]
    matrix = jnp.concatenate(
        [half[k * STATES : (k + 1) * STATES] for k in range(NCLASS) for half in halves], axis=0
    )
    state_high, state_low = split_two(state)
    high, low = split_two(matrix)
    moved = lax.dot_general(
        jnp.concatenate([state_high, state_low, state_high], axis=1),
        jnp.concatenate([high, high, low], axis=1),
        (((1,), (1,)), ((), ())),
        preferred_element_type=F32,
    )
    result = jnp.zeros(state.shape, F32)
    for k in range(NCLASS):
        result = jnp.where(band == k, moved[:, k * LANES : (k + 1) * LANES], result)
    return result


def fine_step(arrived, turn, wanted, band, dynamics, state, profiles, coarse):
    groups = turn.shape[0] // 2
    turns, table = fine_tables(groups, profiles, coarse)
    out, moved = pl.pallas_call(
        functools.partial(fine_kernel, profiles),
        out_shape=(
            jax.ShapeDtypeStruct((groups, profiles * KINDS, LANES), F32),
            jax.ShapeDtypeStruct(state.shape, F32),
        ),
        in_specs=[VMEM] * 8,
        out_specs=(VMEM,) * 2,
        compiler_params=PARAMS,
        cost_estimate=COST,
        name="fine_dft",
    )(
        arrived,
        turn,
        wanted,
        band,
        jnp.asarray(turns),
        jnp.asarray(table),
        dynamics.reshape(NCLASS * STATES, STATES),
        state,
    )
    return out.reshape(groups * profiles, KINDS, LANES), moved


def fine_step_general(arrived, owner_counts, capacity):
    groups, rows = arrived.shape[:2]
    coarse = 2 * rows * groups
    fine_length = groups * HALF
    order = coarse * fine_length
    own = lax.axis_index("bins")
    real, imag = arrived[:, :, :HALF], arrived[:, :, HALF:]
    points = jnp.arange(fine_length, dtype=jnp.int32).reshape(groups, 1, HALF)
    k_index = own * rows + jnp.arange(rows, dtype=jnp.int32)[None, :, None]
    cosine, sine = unit_turn(points * k_index & (order - 1), order)
    packed = (own == 0) & (jnp.arange(rows)[None, :, None] == 0)
    middle = jnp.where(own == 0, imag[:, :1], 0.0)
    imag = jnp.where(packed, 0.0, imag)
    real, imag = real * cosine + imag * sine, imag * cosine - real * sine
    cosine, sine = unit_turn(points * (coarse // 2), order)
    real = jnp.concatenate([real, middle * cosine], axis=1)
    imag = jnp.concatenate([imag, -middle * sine], axis=1)

    def turned(pattern, root, parts):
        cosine, sine = (jnp.asarray(part.astype(np.float32)) for part in root)
        mul = functools.partial(jnp.einsum, pattern, precision=HIGHEST)
        return (
            mul(cosine, parts[0]) - mul(sine, parts[1]),
            mul(cosine, parts[1]) + mul(sine, parts[0]),
        )

    group_index, point_index = np.arange(groups), np.arange(HALF)
    parts = turned(
        "cu,crj->urj", unit_root(groups, group_index[:, None] * group_index), (real, imag)
    )
    parts = turned(
        "uj,urj->urj", unit_root(fine_length, group_index[:, None] * point_index), parts
    )
    parts = turned(
        "jv,urj->vur", unit_root(HALF, point_index[:, None] * point_index), parts
    )
    tiles = fine_length // 2
    kept = jnp.concatenate([~packed[0, :, 0], jnp.zeros((1,), bool)])
    sides = []
    for part, sign in zip(parts, (1.0, -1.0)):
        part = part.reshape(fine_length, rows + 1)
        sides.append((part[:tiles], sign * jnp.where(kept, part[tiles:][::-1], 0.0)))
    power = sum(jnp.sum(part * part, axis=1) for pair in sides for part in pair)
    starts = jnp.cumsum(owner_counts) - owner_counts
    slot_index = jnp.arange(capacity, dtype=jnp.int32)
    filled = slot_index[None, :] < owner_counts[:, None]
    chosen = jnp.clip(starts[:, None] + slot_index[None, :], 0, tiles - 1)

    def kinds(low, high):
        low_sums, high_sums = jnp.sum(low[:, :rows], axis=1), jnp.sum(high[:, 1:rows], axis=1)
        values = jnp.stack([low_sums, high_sums, high[:, 0] + low[:, rows], power], axis=1)
        return jnp.where(filled[:, :, None], values[chosen], 0.0).transpose(0, 2, 1)

    return jnp.concatenate([kinds(*sides[0]), kinds(*sides[1])], axis=2)


def pool_table(shares, coarse):
    pool = np.zeros((21, 16, shares, KINDS), np.float32)
    sums = pool[:20].reshape(NCLASS, STATES, shares, KINDS)
    wide = TILE // STATES
    rows = coarse // 2 // shares
    for share in range(shares):
        first = rows * share
        rest = coarse - first if share else coarse // 2
        for kind, at in enumerate((first, coarse - first - 1, rest)):
            for band in range(NCLASS):
                sums[band, at // wide >> band, share, kind] = 1.0
    pool[20, :, :, 3] = 1.0
    return pool.reshape(-1, shares * KINDS).astype(BF16)


def update_kernel(count, x_ref, pool_ref, moved_ref, band_ref, out_ref):
    band = band_ref[...]
    sums = dot(pool_ref[...], jnp.concatenate(split_two(x_ref[...]), axis=1))
    sums = sums[:, :LANES] + sums[:, LANES:]
    power = sums[NCLASS * STATES : NCLASS * STATES + 1] * (1.0 / count)
    span = jnp.left_shift(TILE // STATES, jnp.maximum(band, 0)).astype(F32)
    scaling = 1.0 / jnp.sqrt(span * (power + EPSILON))
    scaling = jnp.where(band < 0, 0.0, scaling)
    chosen = sums[:STATES]
    for k in range(1, NCLASS):
        chosen = jnp.where(band == k, sums[k * STATES : (k + 1) * STATES], chosen)
    chosen = chosen * scaling
    turned = jnp.transpose(jnp.concatenate([chosen, chosen], axis=0))
    half = turned.shape[0] // 2
    measured = jnp.where(iotas((half, LANES))[1] < STATES, turned[:half], turned[half:])
    out_ref[...] = moved_ref[...] + measured


def update_step(arrived, moved, band, coarse, count):
    shares = arrived.shape[0]
    return pl.pallas_call(
        functools.partial(update_kernel, count),
        out_shape=jax.ShapeDtypeStruct(moved.shape, F32),
        in_specs=[VMEM] * 4,
        out_specs=VMEM,
        compiler_params=PARAMS,
        name="state_update",
    )(arrived.reshape(shares * KINDS, LANES), jnp.asarray(pool_table(shares, coarse)), moved, band)


def state_step_general(band_edges, owner_counts, dynamics, state):
    own = lax.axis_index("bins")
    capacity = state.shape[0]
    slot = jnp.arange(capacity, dtype=jnp.int32)
    start = jnp.cumsum(owner_counts)[own] - owner_counts[own]
    band = jnp.sum((slot + start)[:, None] >= band_edges[None, 1:NCLASS], axis=1)
    band = jnp.where(slot < owner_counts[own], band, -1).astype(jnp.int32)
    limit = STATES >> jnp.arange(NCLASS)[:, None, None]
    index = jnp.arange(STATES)
    inside = (index[:, None] < limit) & (index[None, :] < limit)
    chosen = (band[:, None] == jnp.arange(NCLASS)[None, :]).astype(F32)
    picked = jnp.einsum(
        "rk,kij->rij", chosen, jnp.where(inside, dynamics, 0.0), precision=HIGHEST
    )
    parts = state.reshape(capacity, 2, STATES)
    moved = jnp.einsum("rij,rcj->rci", picked, parts, precision=HIGHEST)
    return moved.reshape(state.shape), jnp.tile(band, 2)[None, :]


def exchanged(values, axes):
    return lax.all_to_all(values, axes, split_axis=0, concat_axis=0, tiled=True)


def body(profiles, band_edges, owner_counts, dynamics, prev_state):
    groups, scans = lax.axis_size("bins"), lax.axis_size("scans")
    prof_rows, length = profiles.shape
    capacity = prev_state.shape[0]
    coarse = length // HALF
    shares = groups * scans
    count = prof_rows * scans * TILE
    state = prev_state.reshape(capacity, 2 * STATES)
    if groups == 8 and scans == 4 and coarse == 16 * shares and capacity == HALF:
        columns = exchanged(columns_step(profiles.reshape(length), groups), "bins")
        blocks, turn, wanted, lane_band, row_band = coarse_step(
            columns.reshape(coarse // 2, LANES), band_edges, owner_counts, shares, capacity
        )
        blocks = exchanged(blocks.reshape(shares, 8, LANES), ("bins", "scans"))
        payload, moved = fine_step(
            blocks.reshape(8 * shares, LANES),
            turn,
            wanted,
            row_band,
            dynamics,
            state,
            scans,
            coarse,
        )
        arrived = exchanged(payload, ("bins", "scans"))
    else:
        moved, lane_band = state_step_general(band_edges, owner_counts, dynamics, state)
        columns = profiles.reshape(coarse // groups, groups, HALF).transpose(1, 0, 2)
        columns = exchanged(columns, "bins").reshape(coarse, HALF)
        blocks = exchanged(coarse_step_general(columns, groups), "bins")
        arrived = exchanged(fine_step_general(blocks, owner_counts, capacity), "bins")
        power = lax.psum(arrived[:, 3:], "scans")
        arrived = jnp.concatenate([arrived[:, :3], power], axis=1)
    updated = update_step(arrived, moved, lane_band, coarse, count)
    return updated.reshape(prev_state.shape)


def solution(mesh):
    return jax.shard_map(
        body,
        mesh=mesh,
        in_specs=(P("scans", "bins"), P(), P(), P(), P("bins", "scans", None)),
        out_specs=P("bins", "scans", None),
        check_vma=False,
    )
```

```python
import functools
import math

import jax
import jax.numpy as jnp
import numpy as np
from jax import lax
from jax.experimental import pallas as pl
from jax.experimental.pallas import tpu as pltpu
from jax.sharding import PartitionSpec as P

TILE = 512
STATES = 64
NCLASS = 5
LANES = 128

EPSILON = 1e-05
HIGHEST = lax.Precision.HIGHEST
BF16 = jnp.bfloat16
F32 = jnp.float32


def unit_root(order, exponents):
    angles = 2.0 * np.pi * (np.asarray(exponents, dtype=np.int64) % order) / order
    return np.cos(angles), -np.sin(angles)


def two_terms(values):
    high = np.asarray(values, np.float32).astype(BF16)
    low = (np.asarray(values, np.float64) - high.astype(np.float64)).astype(BF16)
    return high, low


def split_two(values):
    high = values.astype(BF16)
    return high, (values - high.astype(F32)).astype(BF16)


def dot(left, right):
    return jnp.dot(left, right, preferred_element_type=F32)


VMEM = pl.BlockSpec(memory_space=pltpu.VMEM)
PARAMS = pltpu.CompilerParams(vmem_limit_bytes=32 << 20)
COST = pl.CostEstimate(flops=1 << 30, bytes_accessed=1 << 24, transcendentals=0)


KINDS = 4
HALF = LANES // 2


def unit_turn(phase, order):
    shifted = phase + order // 8
    quadrant = (shifted >> (order.bit_length() - 3)) & 3
    x = ((shifted & (order // 4 - 1)) - order // 8).astype(F32) * (2.0 * math.pi / order)
    y = x * x
    cosine = 1.0 + y * (-1 / 2 + y * (1 / 24 + y * (-1 / 720 + y * (1 / 40320))))
    sine = x * (1.0 + y * (-1 / 6 + y * (1 / 120 + y * (-1 / 5040 + y * (1 / 362880)))))
    odd = (quadrant & 1) == 1
    real, imag = jnp.where(odd, sine, cosine), jnp.where(odd, cosine, sine)
    real = jnp.where((quadrant == 1) | (quadrant == 2), -real, real)
    return real, jnp.where(quadrant >= 2, -imag, imag)


def iotas(shape):
    return [lax.broadcasted_iota(jnp.int32, shape, axis) for axis in range(len(shape))]


def columns_kernel(x_ref, out_ref):
    groups, rows, _ = out_ref.shape
    low_lanes = iotas((rows, LANES))[1] < HALF
    for pair in range(groups // 2):
        even = x_ref[pl.ds(pair, rows, stride=groups), :]
        odd = x_ref[pl.ds(groups // 2 + pair, rows, stride=groups), :]
        out_ref[2 * pair] = jnp.where(low_lanes, even, pltpu.roll(odd, HALF, 1))
        out_ref[2 * pair + 1] = jnp.where(low_lanes, pltpu.roll(even, HALF, 1), odd)


def columns_step(profile, groups):
    rows = profile.shape[0] // (groups * LANES)
    return pl.pallas_call(
        columns_kernel,
        out_shape=jax.ShapeDtypeStruct((groups, rows, LANES), F32),
        in_specs=[VMEM],
        out_specs=VMEM,
        compiler_params=PARAMS,
        cost_estimate=COST,
        name="columns",
    )(profile.reshape(-1, LANES))


def coarse_table(coarse):
    half, quarter = coarse // 2, coarse // 4
    k_index = np.arange(quarter)
    a_index = np.concatenate([np.arange(0, half, 2), np.arange(1, half, 2)])
    real, imag = unit_root(half, k_index[:, None] * a_index[None, :])
    imag[0] = 1
    parts = [part.reshape(quarter // 16, 2, 2, 1, 4, half) for part in (real, imag)]
    parts = np.concatenate(parts, axis=3).transpose(0, 2, 3, 1, 4, 5)
    return np.concatenate(two_terms(parts.reshape(half, half)), axis=1)


def slot_tiles(counts_ref):
    groups = counts_ref.shape[1]
    own = lax.axis_index("bins")
    lane = iotas((1, LANES))[1]
    rank = lane & (HALF - 1)
    start = jnp.zeros((1, LANES), jnp.int32)
    own_start, own_count = start, start
    wanted = []
    for owner in range(groups):
        count = jnp.broadcast_to(counts_ref[:, owner : owner + 1], (1, LANES))
        wanted.append(jnp.where(rank < count, start + rank, -1))
        own_start = jnp.where(own == owner, start, own_start)
        own_count = jnp.where(own == owner, count, own_count)
        start = start + count
    wanted = [
        jnp.where(lane < HALF, wanted[2 * pair], wanted[2 * pair + 1]) for pair in range(groups // 2)
    ]
    return jnp.concatenate(wanted, axis=1), own_start, own_count


def bands(slot, start, count, edges_ref):
    band = jnp.zeros_like(slot)
    for at in range(1, NCLASS):
        edge = jnp.broadcast_to(edges_ref[:, at : at + 1], (1, LANES))
        band = band + jnp.where(slot + start >= edge, 1, 0)
    return jnp.where(slot < count, band, -1)


def coarse_kernel(
    groups,
    shares,
    x_ref,
    table_ref,
    edges_ref,
    counts_ref,
    out_ref,
    turn_ref,
    wanted_ref,
    band_ref,
):
    half = x_ref.shape[0]
    quarter = half // 2
    row, lane = iotas((8, LANES))
    low_lanes = lane < HALF
    sums = []
    for parity in range(2):
        high, low = split_two(x_ref[pl.ds(parity, quarter, stride=2), :])
        at = parity * quarter
        both = dot(table_ref[:, at : at + quarter], jnp.concatenate([high, low], axis=1))
        rest = dot(table_ref[:, half + at : half + at + quarter], high)
        sums.append(both[:, :LANES] + both[:, LANES:] + rest)
    base = 8 * (row >> 2) + 4 * (lane >> 6) + (row & 3)
    base_cosine, base_sine = unit_turn(base, 2 * half)
    packed = low_lanes & (row == 0)
    for sign, block in [(sign, block) for block in range(half // 32) for sign in (1, -1)]:
        pieces = []
        for at in range(32 * block, 32 * (block + 1), 8):
            even, odd = sums[0][at : at + 8], sums[1][at : at + 8]
            pieces.append(even + odd if sign > 0 else even - odd)
        real_low, imag_low, real_high, imag_high = pieces
        if block == 0 and sign < 0:
            imag_low = jnp.where(row == 0, 0.0, imag_low)
        even_real = jnp.where(low_lanes, real_low, pltpu.roll(real_high, HALF, 1))
        even_imag = jnp.where(low_lanes, imag_low, pltpu.roll(imag_high, HALF, 1))
        odd_real = jnp.where(low_lanes, pltpu.roll(real_low, HALF, 1), real_high)
        odd_imag = jnp.where(low_lanes, pltpu.roll(imag_low, HALF, 1), imag_high)
        first = 2 * block + (0 if sign > 0 else shares // 2)
        angle = math.pi * 8 * first / half
        cosine = base_cosine * math.cos(angle) - base_sine * math.sin(angle)
        sine = base_sine * math.cos(angle) + base_cosine * math.sin(angle)
        real = even_real + odd_real * cosine + odd_imag * sine
        if first == 0:
            cosine = jnp.where(packed, -1.0, cosine)
        imag = even_imag + odd_imag * cosine - odd_real * sine
        out_ref[pl.ds(8 * first, 8, stride=2), :] = real
        out_ref[pl.ds(8 * first + 1, 8, stride=2), :] = imag
    own = lax.axis_index("bins") * lax.axis_size("scans") + lax.axis_index("scans")
    k_index = 8 * own + 4 * (lane >> 6) + (row & 3)
    order = 2 * half * groups * HALF
    for c in range(groups):
        phase = ((c * HALF + (lane & (HALF - 1))) * k_index) & (order - 1)
        turn_ref[2 * c], turn_ref[2 * c + 1] = unit_turn(phase, order)
    wanted_ref[...], start, count = slot_tiles(counts_ref)
    band_ref[...] = bands(iotas(band_ref.shape)[0], start, count, edges_ref)


def coarse_step(columns, band_edges, owner_counts, shares, capacity):
    half, groups = columns.shape[0], owner_counts.shape[0]
    return pl.pallas_call(
        functools.partial(coarse_kernel, groups, shares),
        out_shape=(
            jax.ShapeDtypeStruct((half, LANES), F32),
            jax.ShapeDtypeStruct((2 * groups, 8, LANES), F32),
            jax.ShapeDtypeStruct((1, groups * capacity), jnp.int32),
            jax.ShapeDtypeStruct((capacity, LANES), jnp.int32),
        ),
        in_specs=[VMEM] * 4,
        out_specs=(VMEM,) * 4,
        compiler_params=PARAMS,
        cost_estimate=COST,
        name="coarse_dft",
    )(
        columns,
        jnp.asarray(coarse_table(2 * half)),
        band_edges.reshape(1, -1),
        owner_counts.reshape(1, -1),
    )


def coarse_step_general(columns, shares):
    coarse = columns.shape[0]
    half = coarse // 2
    real, imag = unit_root(coarse, np.arange(half)[:, None] * np.arange(coarse)[None, :])
    imag[0] = 1 - 2 * (np.arange(coarse) % 2)
    table = jnp.asarray(np.concatenate([real, imag]).astype(np.float32))
    spectrum = jnp.dot(table, columns, precision=HIGHEST)
    blocks = jnp.concatenate([spectrum[:half], spectrum[half:]], axis=1)
    return blocks.reshape(shares, half // shares, LANES)


def fine_tables(groups, profiles, coarse):
    fine_length = groups * HALF
    doubled = np.arange(LANES) % HALF
    turn = unit_root(fine_length, np.arange(groups)[:, None] * doubled[None, :])
    middle = (np.arange(groups)[:, None] * HALF + doubled[None, :]) * (coarse // 2)
    middle = unit_root(coarse * fine_length, middle)
    turns = np.concatenate(turn + middle).astype(np.float32)
    order = np.arange(HALF)
    order[HALF // 2 :] = order[HALF // 2 :][::-1]
    real, imag = unit_root(HALF, np.arange(HALF)[:, None] * order[None, :])
    sign = np.where(np.arange(HALF) < HALF // 2, 1, -1)
    both = np.eye(2)
    matrix = np.block(
        [
            [np.kron(both, real), np.kron(both, imag * sign)],
            [np.kron(both, -imag), np.kron(both, real * sign)],
        ]
    )
    sums = np.zeros((3, profiles, KINDS, 2, profiles // 2 + 2, 2, 4), np.float32)
    for p in range(profiles):
        pair, which = divmod(p, 2)
        sums[0, p, 0, :, pair, which, :] = 1
        sums[1, p, 1, :, pair, which, 1:] = 1
        sums[2, p, 1, :, pair, which, :] = 1
        sums[1, p, 2, :, pair, which, 0] = 1
        sums[0, p, 2, :, profiles // 2, which, pair] = 1
        sums[:, p, 3, :, profiles // 2 + 1] = 1
    sums = sums.reshape(3 * profiles * KINDS, -1)
    sums = np.pad(sums, [(0, 0), (0, 4 * LANES - sums.shape[1])]).astype(BF16)
    return turns, np.concatenate([np.concatenate(two_terms(matrix), axis=1), sums])


def add(p, q):
    return (p[0] + q[0], p[1] + q[1])


def sub(p, q):
    return (p[0] - q[0], p[1] - q[1])


def times(p, cosine, sine):
    return (p[0] * cosine + p[1] * sine, p[1] * cosine - p[0] * sine)


def eight_point(values):
    half = math.sqrt(0.5)

    def down(p):
        return (p[1], -p[0])

    def four(a, b, c, d):
        s0, s1, s2, s3 = add(a, c), sub(a, c), add(b, d), sub(b, d)
        turned = (s1[0] + s3[1], s1[1] - s3[0]), (s1[0] - s3[1], s1[1] + s3[0])
        return add(s0, s2), turned[0], sub(s0, s2), turned[1]

    even = four(values[0], values[2], values[4], values[6])
    odd = four(values[1], values[3], values[5], values[7])
    turned = [
        odd[0],
        ((odd[1][0] + odd[1][1]) * half, (odd[1][1] - odd[1][0]) * half),
        down(odd[2]),
        ((odd[3][1] - odd[3][0]) * half, (odd[3][0] + odd[3][1]) * -half),
    ]
    return [add(e, t) for e, t in zip(even, turned)] + [sub(e, t) for e, t in zip(even, turned)]


def fine_kernel(
    profiles,
    x_ref,
    turn_ref,
    wanted_ref,
    band_ref,
    turns_ref,
    table_ref,
    dynamics_ref,
    state_ref,
    out_ref,
    moved_ref,
):
    groups = out_ref.shape[0]
    first = (lax.axis_index("bins") == 0) & (lax.axis_index("scans") == 0)
    row, lane = iotas((8, LANES))
    low_lanes = lane < HALF
    low_side = (lane & (HALF - 1)) < HALF // 2
    packed = first & low_lanes & ((row & 3) == 0)
    shifted = first & low_lanes & ((row & 3) == 1)
    pairs = profiles // 2
    columns = [[] for _ in range(pairs + 1)]
    for c in range(groups):
        cosine, sine = turn_ref[2 * c], turn_ref[2 * c + 1]
        at = c * 8 * profiles
        for pair in range(pairs):
            real = x_ref[pl.ds(at + 16 * pair, 8, stride=2), :]
            imag = x_ref[pl.ds(at + 16 * pair + 1, 8, stride=2), :]
            if pair == 0:
                middle = jnp.where(packed, imag, 0.0)
            imag = jnp.where(packed, 0.0, imag)
            columns[pair].append(times((real, imag), cosine, sine))
        middle = jnp.where(shifted, x_ref[pl.ds(at + 15, 8, stride=2), :], middle)
        middle_real = turns_ref[2 * groups + c : 2 * groups + c + 1, :]
        middle_imag = turns_ref[3 * groups + c : 3 * groups + c + 1, :]
        columns[pairs].append((middle * middle_real, middle * middle_imag))
    transformed = [eight_point(column) for column in columns]
    blocks = []
    for u in range(groups):
        cosine, sine = turns_ref[u : u + 1, :], -turns_ref[groups + u : groups + u + 1, :]
        for column in transformed:
            blocks.append(times(column[u], cosine, sine) if u else column[u])
    wide = 2 * LANES
    size = wide
    left = jnp.concatenate(
        [jnp.concatenate([block[part] for block in blocks], axis=0) for part in range(2)], axis=1
    )
    high, low = split_two(left)
    product = dot(high, table_ref[:size, :])
    product = product[:, :wide] + product[:, wide:] + dot(low, table_ref[:size, :wide])
    spectrum = []
    for u in range(groups):
        spectrum.append([])
        for at in range(pairs + 1):
            start = 8 * (u * (pairs + 1) + at)
            block = (product[start : start + 8, :LANES], product[start : start + 8, LANES:])
            dropped = ~low_side & packed if at < pairs else ~low_side
            spectrum[u].append(tuple(jnp.where(dropped, 0.0, part) for part in block))
    power = [
        sum(block[0] * block[0] + block[1] * block[1] for block in spectrum[u])
        for u in range(groups)
    ]
    summands = []
    for part in range(2):
        for u in range(groups):
            mirror = groups - 1 - u
            rows = [
                jnp.where(low_side, spectrum[u][pair][part], spectrum[mirror][pair][part])
                for pair in range(pairs)
            ]
            rows.append(spectrum[u][pairs][part])
            rows.append(jnp.where(low_side, power[u], power[mirror]))
            summands.append(jnp.concatenate(rows, axis=0))
    summands = jnp.concatenate(split_two(jnp.concatenate(summands, axis=1)), axis=0)
    summed = dot(table_ref[size:, : summands.shape[0]], summands)
    rows = summed.shape[0] // 3
    _, lanes = iotas((rows, LANES))
    side, early = (lanes & (HALF - 1)) < HALF // 2, lanes < HALF
    left = []
    for part in range(2):
        pieces = []
        for at in range(part * groups, (part + 1) * groups):
            piece = summed[:, at * LANES : (at + 1) * LANES]
            piece = jnp.where(
                side,
                piece[:rows],
                jnp.where(early, piece[rows : 2 * rows], piece[2 * rows :]),
            )
            pieces.append(piece)
        left.append(jnp.concatenate(pieces, axis=1))
    left = jnp.concatenate(split_two(jnp.concatenate(left, axis=0)), axis=0)
    wanted = wanted_ref[...]
    chosen = []
    for u in range(groups):
        tile = u + groups * iotas((HALF // 2, wanted.shape[1]))[0]
        chosen += [jnp.where(tile == wanted, 1.0, 0.0).astype(BF16)] * 4
    routed = dot(left, jnp.concatenate(chosen, axis=0))
    routed = routed[: 2 * rows] + routed[2 * rows :]
    for pair in range(groups // 2):
        real = routed[:rows, pair * LANES : (pair + 1) * LANES]
        imag = routed[rows:, pair * LANES : (pair + 1) * LANES]
        out_ref[2 * pair] = jnp.where(early, real, pltpu.roll(imag, HALF, 1))
        out_ref[2 * pair + 1] = jnp.where(early, pltpu.roll(real, HALF, 1), imag)
    moved_ref[...] = state_product(dynamics_ref[...], state_ref[...], band_ref[...])


def state_product(dynamics, state, band):
    row, column = iotas((NCLASS * STATES, STATES))
    limit = STATES >> (row >> 6)
    inside = ((row & (STATES - 1)) < limit) & (column < limit)
    dynamics = jnp.where(inside, dynamics, 0.0)
    empty = jnp.zeros_like(dynamics)
    halves = [
        jnp.concatenate([dynamics, empty], axis=1),
        jnp.concatenate([empty, dynamics], axis=1),
    ]
    matrix = jnp.concatenate(
        [half[k * STATES : (k + 1) * STATES] for k in range(NCLASS) for half in halves], axis=0
    )
    state_high, state_low = split_two(state)
    high, low = split_two(matrix)
    moved = lax.dot_general(
        jnp.concatenate([state_high, state_low, state_high], axis=1),
        jnp.concatenate([high, high, low], axis=1),
        (((1,), (1,)), ((), ())),
        preferred_element_type=F32,
    )
    result = jnp.zeros(state.shape, F32)
    for k in range(NCLASS):
        result = jnp.where(band == k, moved[:, k * LANES : (k + 1) * LANES], result)
    return result


def fine_step(arrived, turn, wanted, band, dynamics, state, profiles, coarse):
    groups = turn.shape[0] // 2
    turns, table = fine_tables(groups, profiles, coarse)
    out, moved = pl.pallas_call(
        functools.partial(fine_kernel, profiles),
        out_shape=(
            jax.ShapeDtypeStruct((groups, profiles * KINDS, LANES), F32),
            jax.ShapeDtypeStruct(state.shape, F32),
        ),
        in_specs=[VMEM] * 8,
        out_specs=(VMEM,) * 2,
        compiler_params=PARAMS,
        cost_estimate=COST,
        name="fine_dft",
    )(
        arrived,
        turn,
        wanted,
        band,
        jnp.asarray(turns),
        jnp.asarray(table),
        dynamics.reshape(NCLASS * STATES, STATES),
        state,
    )
    return out.reshape(groups * profiles, KINDS, LANES), moved


def fine_step_general(arrived, owner_counts, capacity):
    groups, rows = arrived.shape[:2]
    coarse = 2 * rows * groups
    fine_length = groups * HALF
    order = coarse * fine_length
    own = lax.axis_index("bins")
    real, imag = arrived[:, :, :HALF], arrived[:, :, HALF:]
    points = jnp.arange(fine_length, dtype=jnp.int32).reshape(groups, 1, HALF)
    k_index = own * rows + jnp.arange(rows, dtype=jnp.int32)[None, :, None]
    cosine, sine = unit_turn(points * k_index & (order - 1), order)
    packed = (own == 0) & (jnp.arange(rows)[None, :, None] == 0)
    middle = jnp.where(own == 0, imag[:, :1], 0.0)
    imag = jnp.where(packed, 0.0, imag)
    real, imag = real * cosine + imag * sine, imag * cosine - real * sine
    cosine, sine = unit_turn(points * (coarse // 2), order)
    real = jnp.concatenate([real, middle * cosine], axis=1)
    imag = jnp.concatenate([imag, -middle * sine], axis=1)

    def turned(pattern, root, parts):
        cosine, sine = (jnp.asarray(part.astype(np.float32)) for part in root)
        mul = functools.partial(jnp.einsum, pattern, precision=HIGHEST)
        return (
            mul(cosine, parts[0]) - mul(sine, parts[1]),
            mul(cosine, parts[1]) + mul(sine, parts[0]),
        )

    group_index, point_index = np.arange(groups), np.arange(HALF)
    parts = turned(
        "cu,crj->urj", unit_root(groups, group_index[:, None] * group_index), (real, imag)
    )
    parts = turned(
        "uj,urj->urj", unit_root(fine_length, group_index[:, None] * point_index), parts
    )
    parts = turned(
        "jv,urj->vur", unit_root(HALF, point_index[:, None] * point_index), parts
    )
    tiles = fine_length // 2
    kept = jnp.concatenate([~packed[0, :, 0], jnp.zeros((1,), bool)])
    sides = []
    for part, sign in zip(parts, (1.0, -1.0)):
        part = part.reshape(fine_length, rows + 1)
        sides.append((part[:tiles], sign * jnp.where(kept, part[tiles:][::-1], 0.0)))
    power = sum(jnp.sum(part * part, axis=1) for pair in sides for part in pair)
    starts = jnp.cumsum(owner_counts) - owner_counts
    slot_index = jnp.arange(capacity, dtype=jnp.int32)
    filled = slot_index[None, :] < owner_counts[:, None]
    chosen = jnp.clip(starts[:, None] + slot_index[None, :], 0, tiles - 1)

    def kinds(low, high):
        low_sums, high_sums = jnp.sum(low[:, :rows], axis=1), jnp.sum(high[:, 1:rows], axis=1)
        values = jnp.stack([low_sums, high_sums, high[:, 0] + low[:, rows], power], axis=1)
        return jnp.where(filled[:, :, None], values[chosen], 0.0).transpose(0, 2, 1)

    return jnp.concatenate([kinds(*sides[0]), kinds(*sides[1])], axis=2)


def pool_table(shares, coarse):
    pool = np.zeros((21, 16, shares, KINDS), np.float32)
    sums = pool[:20].reshape(NCLASS, STATES, shares, KINDS)
    wide = TILE // STATES
    rows = coarse // 2 // shares
    for share in range(shares):
        first = rows * share
        rest = coarse - first if share else coarse // 2
        for kind, at in enumerate((first, coarse - first - 1, rest)):
            for band in range(NCLASS):
                sums[band, at // wide >> band, share, kind] = 1.0
    pool[20, :, :, 3] = 1.0
    return pool.reshape(-1, shares * KINDS).astype(BF16)


def update_kernel(count, x_ref, pool_ref, moved_ref, edges_ref, counts_ref, out_ref):
    _, own_start, own_count = slot_tiles(counts_ref)
    band = bands(iotas((1, LANES))[1] & (HALF - 1), own_start, own_count, edges_ref)
    sums = dot(pool_ref[...], jnp.concatenate(split_two(x_ref[...]), axis=1))
    sums = sums[:, :LANES] + sums[:, LANES:]
    power = sums[NCLASS * STATES : NCLASS * STATES + 1] * (1.0 / count)
    span = jnp.left_shift(TILE // STATES, jnp.maximum(band, 0)).astype(F32)
    scaling = 1.0 / jnp.sqrt(span * (power + EPSILON))
    scaling = jnp.where(band < 0, 0.0, scaling)
    chosen = sums[:STATES]
    for k in range(1, NCLASS):
        chosen = jnp.where(band == k, sums[k * STATES : (k + 1) * STATES], chosen)
    chosen = chosen * scaling
    turned = jnp.transpose(jnp.concatenate([chosen, chosen], axis=0))
    half = turned.shape[0] // 2
    measured = jnp.where(iotas((half, LANES))[1] < STATES, turned[:half], turned[half:])
    out_ref[...] = moved_ref[...] + measured


def update_step(arrived, moved, band_edges, owner_counts, coarse, count):
    shares = arrived.shape[0]
    return pl.pallas_call(
        functools.partial(update_kernel, count),
        out_shape=jax.ShapeDtypeStruct(moved.shape, F32),
        in_specs=[VMEM] * 5,
        out_specs=VMEM,
        compiler_params=PARAMS,
        name="state_update",
    )(
        arrived.reshape(shares * KINDS, LANES),
        jnp.asarray(pool_table(shares, coarse)),
        moved,
        band_edges.reshape(1, -1),
        owner_counts.reshape(1, -1),
    )


def state_step_general(band_edges, owner_counts, dynamics, state):
    own = lax.axis_index("bins")
    capacity = state.shape[0]
    slot = jnp.arange(capacity, dtype=jnp.int32)
    start = jnp.cumsum(owner_counts)[own] - owner_counts[own]
    band = jnp.sum((slot + start)[:, None] >= band_edges[None, 1:NCLASS], axis=1)
    band = jnp.where(slot < owner_counts[own], band, -1).astype(jnp.int32)
    limit = STATES >> jnp.arange(NCLASS)[:, None, None]
    index = jnp.arange(STATES)
    inside = (index[:, None] < limit) & (index[None, :] < limit)
    chosen = (band[:, None] == jnp.arange(NCLASS)[None, :]).astype(F32)
    picked = jnp.einsum(
        "rk,kij->rij", chosen, jnp.where(inside, dynamics, 0.0), precision=HIGHEST
    )
    parts = state.reshape(capacity, 2, STATES)
    moved = jnp.einsum("rij,rcj->rci", picked, parts, precision=HIGHEST)
    return moved.reshape(state.shape)


def exchanged(values, axes):
    return lax.all_to_all(values, axes, split_axis=0, concat_axis=0, tiled=True)


def body(profiles, band_edges, owner_counts, dynamics, prev_state):
    groups, scans = lax.axis_size("bins"), lax.axis_size("scans")
    prof_rows, length = profiles.shape
    capacity = prev_state.shape[0]
    coarse = length // HALF
    shares = groups * scans
    count = prof_rows * scans * TILE
    state = prev_state.reshape(capacity, 2 * STATES)
    if groups == 8 and scans == 4 and coarse == 16 * shares and capacity == HALF:
        columns = exchanged(columns_step(profiles.reshape(length), groups), "bins")
        blocks, turn, wanted, band = coarse_step(
            columns.reshape(coarse // 2, LANES), band_edges, owner_counts, shares, capacity
        )
        blocks = exchanged(blocks.reshape(shares, 8, LANES), ("bins", "scans"))
        payload, moved = fine_step(
            blocks.reshape(8 * shares, LANES),
            turn,
            wanted,
            band,
            dynamics,
            state,
            scans,
            coarse,
        )
        arrived = exchanged(payload, ("bins", "scans"))
    else:
        moved = state_step_general(band_edges, owner_counts, dynamics, state)
        columns = profiles.reshape(coarse // groups, groups, HALF).transpose(1, 0, 2)
        columns = exchanged(columns, "bins").reshape(coarse, HALF)
        blocks = exchanged(coarse_step_general(columns, groups), "bins")
        arrived = exchanged(fine_step_general(blocks, owner_counts, capacity), "bins")
        power = lax.psum(arrived[:, 3:], "scans")
        arrived = jnp.concatenate([arrived[:, :3], power], axis=1)
    updated = update_step(arrived, moved, band_edges, owner_counts, coarse, count)
    return updated.reshape(prev_state.shape)


def solution(mesh):
    return jax.shard_map(
        body,
        mesh=mesh,
        in_specs=(P("scans", "bins"), P(), P(), P(), P("bins", "scans", None)),
        out_specs=P("bins", "scans", None),
        check_vma=False,
    )
```

```python
import functools
import math

import jax
import jax.numpy as jnp
import numpy as np
from jax import lax
from jax.experimental import pallas as pl
from jax.experimental.pallas import tpu as pltpu
from jax.sharding import PartitionSpec as P

TILE = 512
STATES = 64
NCLASS = 5
LANES = 128

EPSILON = 1e-05
HIGHEST = lax.Precision.HIGHEST
BF16 = jnp.bfloat16
F32 = jnp.float32


def unit_root(order, exponents):
    angles = 2.0 * np.pi * (np.asarray(exponents, dtype=np.int64) % order) / order
    return np.cos(angles), -np.sin(angles)


def two_terms(values):
    high = np.asarray(values, np.float32).astype(BF16)
    low = (np.asarray(values, np.float64) - high.astype(np.float64)).astype(BF16)
    return high, low


def split_two(values):
    high = values.astype(BF16)
    return high, (values - high.astype(F32)).astype(BF16)


def dot(left, right):
    return jnp.dot(left, right, preferred_element_type=F32)


VMEM = pl.BlockSpec(memory_space=pltpu.VMEM)
PARAMS = pltpu.CompilerParams(vmem_limit_bytes=32 << 20)
COST = pl.CostEstimate(flops=1 << 30, bytes_accessed=1 << 24, transcendentals=0)


KINDS = 4
HALF = LANES // 2


def unit_turn(phase, order):
    shifted = phase + order // 8
    quadrant = (shifted >> (order.bit_length() - 3)) & 3
    x = ((shifted & (order // 4 - 1)) - order // 8).astype(F32) * (2.0 * math.pi / order)
    y = x * x
    cosine = 1.0 + y * (-1 / 2 + y * (1 / 24 + y * (-1 / 720 + y * (1 / 40320))))
    sine = x * (1.0 + y * (-1 / 6 + y * (1 / 120 + y * (-1 / 5040 + y * (1 / 362880)))))
    odd = (quadrant & 1) == 1
    real, imag = jnp.where(odd, sine, cosine), jnp.where(odd, cosine, sine)
    real = jnp.where((quadrant == 1) | (quadrant == 2), -real, real)
    return real, jnp.where(quadrant >= 2, -imag, imag)


def iotas(shape):
    return [lax.broadcasted_iota(jnp.int32, shape, axis) for axis in range(len(shape))]


def turns_kernel(order, turn_ref):
    row, lane = iotas((8, LANES))
    own = lax.axis_index("bins") * lax.axis_size("scans") + lax.axis_index("scans")
    k_index = 8 * own + 4 * (lane >> 6) + (row & 3)
    for c in range(turn_ref.shape[0] // 2):
        phase = ((c * HALF + (lane & (HALF - 1))) * k_index) & (order - 1)
        turn_ref[2 * c], turn_ref[2 * c + 1] = unit_turn(phase, order)


def turns_step(groups, order):
    return pl.pallas_call(
        functools.partial(turns_kernel, order),
        out_shape=jax.ShapeDtypeStruct((2 * groups, 8, LANES), F32),
        out_specs=VMEM,
        compiler_params=PARAMS,
        cost_estimate=COST,
        name="turns",
    )()


def columns_kernel(
    x_ref, turn_ref, edges_ref, counts_ref, out_ref, wanted_ref, lane_band_ref, row_band_ref
):
    groups, rows, _ = out_ref.shape
    capacity = row_band_ref.shape[0]
    low_lanes = iotas((rows, LANES))[1] < HALF
    for pair in range(groups // 2):
        even = x_ref[pl.ds(pair, rows, stride=groups), :]
        odd = x_ref[pl.ds(groups // 2 + pair, rows, stride=groups), :]
        out_ref[2 * pair] = jnp.where(low_lanes, even, pltpu.roll(odd, HALF, 1))
        out_ref[2 * pair + 1] = jnp.where(low_lanes, pltpu.roll(even, HALF, 1), odd)
    own = lax.axis_index("bins")
    counts = [
        jnp.broadcast_to(counts_ref[:, owner : owner + 1], (1, LANES)) for owner in range(groups)
    ]
    lane = iotas((1, LANES))[1]
    start = jnp.zeros((1, LANES), jnp.int32)
    own_start, own_count = start, start
    wanted = []
    for owner, count in enumerate(counts):
        rank = lane & (HALF - 1)
        wanted.append(jnp.where(rank < count, start + rank, -1))
        own_start = jnp.where(own == owner, start, own_start)
        own_count = jnp.where(own == owner, count, own_count)
        start = start + count
    for pair in range(groups // 2):
        wanted_ref[:, pair * LANES : (pair + 1) * LANES] = jnp.where(
            lane < HALF, wanted[2 * pair], wanted[2 * pair + 1]
        )
    edges = [jnp.broadcast_to(edges_ref[:, at : at + 1], (1, LANES)) for at in range(1, NCLASS)]
    for ref, slot in (
        (lane_band_ref, lane & (capacity - 1)),
        (row_band_ref, iotas((capacity, LANES))[0]),
    ):
        band = jnp.zeros_like(slot)
        for edge in edges:
            band = band + jnp.where(slot + own_start >= edge, 1, 0)
        ref[...] = jnp.where(slot < own_count, band, -1)


def columns_step(profile, turn, band_edges, owner_counts, capacity):
    groups = owner_counts.shape[0]
    rows = profile.shape[0] // (groups * LANES)
    return pl.pallas_call(
        columns_kernel,
        out_shape=(
            jax.ShapeDtypeStruct((groups, rows, LANES), F32),
            jax.ShapeDtypeStruct((1, groups * capacity), jnp.int32),
            jax.ShapeDtypeStruct((1, LANES), jnp.int32),
            jax.ShapeDtypeStruct((capacity, LANES), jnp.int32),
        ),
        in_specs=[VMEM] * 4,
        out_specs=(VMEM,) * 4,
        compiler_params=PARAMS,
        name="columns",
    )(profile.reshape(-1, LANES), turn, band_edges.reshape(1, -1), owner_counts.reshape(1, -1))


def coarse_table(coarse):
    half, quarter = coarse // 2, coarse // 4
    k_index = np.arange(quarter)
    a_index = np.concatenate([np.arange(0, half, 2), np.arange(1, half, 2)])
    real, imag = unit_root(half, k_index[:, None] * a_index[None, :])
    imag[0] = 1
    parts = [part.reshape(quarter // 16, 2, 2, 1, 4, half) for part in (real, imag)]
    parts = np.concatenate(parts, axis=3).transpose(0, 2, 3, 1, 4, 5)
    return np.concatenate(two_terms(parts.reshape(half, half)), axis=1)


def coarse_kernel(shares, x_ref, table_ref, out_ref):
    half = x_ref.shape[0]
    quarter = half // 2
    row, lane = iotas((8, LANES))
    low_lanes = lane < HALF
    sums = []
    for parity in range(2):
        high, low = split_two(x_ref[pl.ds(parity, quarter, stride=2), :])
        at = parity * quarter
        both = dot(table_ref[:, at : at + quarter], jnp.concatenate([high, low], axis=1))
        rest = dot(table_ref[:, half + at : half + at + quarter], high)
        sums.append(both[:, :LANES] + both[:, LANES:] + rest)
    base = 8 * (row >> 2) + 4 * (lane >> 6) + (row & 3)
    base_cosine, base_sine = unit_turn(base, 2 * half)
    packed = low_lanes & (row == 0)
    for sign, block in [(sign, block) for block in range(half // 32) for sign in (1, -1)]:
        pieces = []
        for at in range(32 * block, 32 * (block + 1), 8):
            even, odd = sums[0][at : at + 8], sums[1][at : at + 8]
            pieces.append(even + odd if sign > 0 else even - odd)
        real_low, imag_low, real_high, imag_high = pieces
        if block == 0 and sign < 0:
            imag_low = jnp.where(row == 0, 0.0, imag_low)
        even_real = jnp.where(low_lanes, real_low, pltpu.roll(real_high, HALF, 1))
        even_imag = jnp.where(low_lanes, imag_low, pltpu.roll(imag_high, HALF, 1))
        odd_real = jnp.where(low_lanes, pltpu.roll(real_low, HALF, 1), real_high)
        odd_imag = jnp.where(low_lanes, pltpu.roll(imag_low, HALF, 1), imag_high)
        first = 2 * block + (0 if sign > 0 else shares // 2)
        angle = math.pi * 8 * first / half
        cosine = base_cosine * math.cos(angle) - base_sine * math.sin(angle)
        sine = base_sine * math.cos(angle) + base_cosine * math.sin(angle)
        real = even_real + odd_real * cosine + odd_imag * sine
        if first == 0:
            cosine = jnp.where(packed, -1.0, cosine)
        imag = even_imag + odd_imag * cosine - odd_real * sine
        out_ref[pl.ds(8 * first, 8, stride=2), :] = real
        out_ref[pl.ds(8 * first + 1, 8, stride=2), :] = imag


def coarse_step(columns, shares):
    half = columns.shape[0]
    return pl.pallas_call(
        functools.partial(coarse_kernel, shares),
        out_shape=jax.ShapeDtypeStruct((half, LANES), F32),
        in_specs=[VMEM] * 2,
        out_specs=VMEM,
        compiler_params=PARAMS,
        name="coarse_dft",
    )(columns, jnp.asarray(coarse_table(2 * half)))


def coarse_step_general(columns, shares):
    coarse = columns.shape[0]
    half = coarse // 2
    real, imag = unit_root(coarse, np.arange(half)[:, None] * np.arange(coarse)[None, :])
    imag[0] = 1 - 2 * (np.arange(coarse) % 2)
    table = jnp.asarray(np.concatenate([real, imag]).astype(np.float32))
    spectrum = jnp.dot(table, columns, precision=HIGHEST)
    blocks = jnp.concatenate([spectrum[:half], spectrum[half:]], axis=1)
    return blocks.reshape(shares, half // shares, LANES)


def fine_tables(groups, profiles, coarse):
    fine_length = groups * HALF
    doubled = np.arange(LANES) % HALF
    turn = unit_root(fine_length, np.arange(groups)[:, None] * doubled[None, :])
    middle = (np.arange(groups)[:, None] * HALF + doubled[None, :]) * (coarse // 2)
    middle = unit_root(coarse * fine_length, middle)
    turns = np.concatenate(turn + middle).astype(np.float32)
    order = np.arange(HALF)
    order[HALF // 2 :] = order[HALF // 2 :][::-1]
    real, imag = unit_root(HALF, np.arange(HALF)[:, None] * order[None, :])
    sign = np.where(np.arange(HALF) < HALF // 2, 1, -1)
    both = np.eye(2)
    matrix = np.block(
        [
            [np.kron(both, real), np.kron(both, imag * sign)],
            [np.kron(both, -imag), np.kron(both, real * sign)],
        ]
    )
    sums = np.zeros((3, profiles, KINDS, 2, profiles // 2 + 2, 2, 4), np.float32)
    for p in range(profiles):
        pair, which = divmod(p, 2)
        sums[0, p, 0, :, pair, which, :] = 1
        sums[1, p, 1, :, pair, which, 1:] = 1
        sums[2, p, 1, :, pair, which, :] = 1
        sums[1, p, 2, :, pair, which, 0] = 1
        sums[0, p, 2, :, profiles // 2, which, pair] = 1
        sums[:, p, 3, :, profiles // 2 + 1] = 1
    sums = sums.reshape(3 * profiles * KINDS, -1)
    sums = np.pad(sums, [(0, 0), (0, 4 * LANES - sums.shape[1])]).astype(BF16)
    return turns, np.concatenate([np.concatenate(two_terms(matrix), axis=1), sums])


def add(p, q):
    return (p[0] + q[0], p[1] + q[1])


def sub(p, q):
    return (p[0] - q[0], p[1] - q[1])


def times(p, cosine, sine):
    return (p[0] * cosine + p[1] * sine, p[1] * cosine - p[0] * sine)


def eight_point(values):
    half = math.sqrt(0.5)

    def down(p):
        return (p[1], -p[0])

    def four(a, b, c, d):
        s0, s1, s2, s3 = add(a, c), sub(a, c), add(b, d), sub(b, d)
        turned = (s1[0] + s3[1], s1[1] - s3[0]), (s1[0] - s3[1], s1[1] + s3[0])
        return add(s0, s2), turned[0], sub(s0, s2), turned[1]

    even = four(values[0], values[2], values[4], values[6])
    odd = four(values[1], values[3], values[5], values[7])
    turned = [
        odd[0],
        ((odd[1][0] + odd[1][1]) * half, (odd[1][1] - odd[1][0]) * half),
        down(odd[2]),
        ((odd[3][1] - odd[3][0]) * half, (odd[3][0] + odd[3][1]) * -half),
    ]
    return [add(e, t) for e, t in zip(even, turned)] + [sub(e, t) for e, t in zip(even, turned)]


def fine_kernel(
    profiles,
    x_ref,
    turn_ref,
    wanted_ref,
    band_ref,
    turns_ref,
    table_ref,
    dynamics_ref,
    state_ref,
    out_ref,
    moved_ref,
):
    groups = out_ref.shape[0]
    first = (lax.axis_index("bins") == 0) & (lax.axis_index("scans") == 0)
    row, lane = iotas((8, LANES))
    low_lanes = lane < HALF
    low_side = (lane & (HALF - 1)) < HALF // 2
    packed = first & low_lanes & ((row & 3) == 0)
    shifted = first & low_lanes & ((row & 3) == 1)
    pairs = profiles // 2
    columns = [[] for _ in range(pairs + 1)]
    for c in range(groups):
        cosine, sine = turn_ref[2 * c], turn_ref[2 * c + 1]
        at = c * 8 * profiles
        for pair in range(pairs):
            real = x_ref[pl.ds(at + 16 * pair, 8, stride=2), :]
            imag = x_ref[pl.ds(at + 16 * pair + 1, 8, stride=2), :]
            if pair == 0:
                middle = jnp.where(packed, imag, 0.0)
            imag = jnp.where(packed, 0.0, imag)
            columns[pair].append(times((real, imag), cosine, sine))
        middle = jnp.where(shifted, x_ref[pl.ds(at + 15, 8, stride=2), :], middle)
        middle_real = turns_ref[2 * groups + c : 2 * groups + c + 1, :]
        middle_imag = turns_ref[3 * groups + c : 3 * groups + c + 1, :]
        columns[pairs].append((middle * middle_real, middle * middle_imag))
    transformed = [eight_point(column) for column in columns]
    blocks = []
    for u in range(groups):
        cosine, sine = turns_ref[u : u + 1, :], -turns_ref[groups + u : groups + u + 1, :]
        for column in transformed:
            blocks.append(times(column[u], cosine, sine) if u else column[u])
    wide = 2 * LANES
    size = wide
    left = jnp.concatenate(
        [jnp.concatenate([block[part] for block in blocks], axis=0) for part in range(2)], axis=1
    )
    high, low = split_two(left)
    product = dot(high, table_ref[:size, :])
    product = product[:, :wide] + product[:, wide:] + dot(low, table_ref[:size, :wide])
    spectrum = []
    for u in range(groups):
        spectrum.append([])
        for at in range(pairs + 1):
            start = 8 * (u * (pairs + 1) + at)
            block = (product[start : start + 8, :LANES], product[start : start + 8, LANES:])
            dropped = ~low_side & packed if at < pairs else ~low_side
            spectrum[u].append(tuple(jnp.where(dropped, 0.0, part) for part in block))
    power = [
        sum(block[0] * block[0] + block[1] * block[1] for block in spectrum[u])
        for u in range(groups)
    ]
    summands = []
    for part in range(2):
        for u in range(groups):
            mirror = groups - 1 - u
            rows = [
                jnp.where(low_side, spectrum[u][pair][part], spectrum[mirror][pair][part])
                for pair in range(pairs)
            ]
            rows.append(spectrum[u][pairs][part])
            rows.append(jnp.where(low_side, power[u], power[mirror]))
            summands.append(jnp.concatenate(rows, axis=0))
    summands = jnp.concatenate(split_two(jnp.concatenate(summands, axis=1)), axis=0)
    summed = dot(table_ref[size:, : summands.shape[0]], summands)
    rows = summed.shape[0] // 3
    _, lanes = iotas((rows, LANES))
    side, early = (lanes & (HALF - 1)) < HALF // 2, lanes < HALF
    left = []
    for part in range(2):
        pieces = []
        for at in range(part * groups, (part + 1) * groups):
            piece = summed[:, at * LANES : (at + 1) * LANES]
            piece = jnp.where(
                side,
                piece[:rows],
                jnp.where(early, piece[rows : 2 * rows], piece[2 * rows :]),
            )
            pieces.append(piece)
        left.append(jnp.concatenate(pieces, axis=1))
    left = jnp.concatenate(split_two(jnp.concatenate(left, axis=0)), axis=0)
    wanted = wanted_ref[...]
    chosen = []
    for u in range(groups):
        tile = u + groups * iotas((HALF // 2, wanted.shape[1]))[0]
        chosen += [jnp.where(tile == wanted, 1.0, 0.0).astype(BF16)] * 4
    routed = dot(left, jnp.concatenate(chosen, axis=0))
    routed = routed[: 2 * rows] + routed[2 * rows :]
    for pair in range(groups // 2):
        real = routed[:rows, pair * LANES : (pair + 1) * LANES]
        imag = routed[rows:, pair * LANES : (pair + 1) * LANES]
        out_ref[2 * pair] = jnp.where(early, real, pltpu.roll(imag, HALF, 1))
        out_ref[2 * pair + 1] = jnp.where(early, pltpu.roll(real, HALF, 1), imag)
    moved_ref[...] = state_product(dynamics_ref[...], state_ref[...], band_ref[...])


def state_product(dynamics, state, band):
    row, column = iotas((NCLASS * STATES, STATES))
    limit = STATES >> (row >> 6)
    inside = ((row & (STATES - 1)) < limit) & (column < limit)
    dynamics = jnp.where(inside, dynamics, 0.0)
    empty = jnp.zeros_like(dynamics)
    halves = [
        jnp.concatenate([dynamics, empty], axis=1),
        jnp.concatenate([empty, dynamics], axis=1),
    ]
    matrix = jnp.concatenate(
        [half[k * STATES : (k + 1) * STATES] for k in range(NCLASS) for half in halves], axis=0
    )
    state_high, state_low = split_two(state)
    high, low = split_two(matrix)
    moved = lax.dot_general(
        jnp.concatenate([state_high, state_low, state_high], axis=1),
        jnp.concatenate([high, high, low], axis=1),
        (((1,), (1,)), ((), ())),
        preferred_element_type=F32,
    )
    result = jnp.zeros(state.shape, F32)
    for k in range(NCLASS):
        result = jnp.where(band == k, moved[:, k * LANES : (k + 1) * LANES], result)
    return result


def fine_step(arrived, turn, wanted, band, dynamics, state, profiles, coarse):
    groups = turn.shape[0] // 2
    turns, table = fine_tables(groups, profiles, coarse)
    out, moved = pl.pallas_call(
        functools.partial(fine_kernel, profiles),
        out_shape=(
            jax.ShapeDtypeStruct((groups, profiles * KINDS, LANES), F32),
            jax.ShapeDtypeStruct(state.shape, F32),
        ),
        in_specs=[VMEM] * 8,
        out_specs=(VMEM,) * 2,
        compiler_params=PARAMS,
        name="fine_dft",
    )(
        arrived,
        turn,
        wanted,
        band,
        jnp.asarray(turns),
        jnp.asarray(table),
        dynamics.reshape(NCLASS * STATES, STATES),
        state,
    )
    return out.reshape(groups * profiles, KINDS, LANES), moved


def fine_step_general(arrived, owner_counts, capacity):
    groups, rows = arrived.shape[:2]
    coarse = 2 * rows * groups
    fine_length = groups * HALF
    order = coarse * fine_length
    own = lax.axis_index("bins")
    real, imag = arrived[:, :, :HALF], arrived[:, :, HALF:]
    points = jnp.arange(fine_length, dtype=jnp.int32).reshape(groups, 1, HALF)
    k_index = own * rows + jnp.arange(rows, dtype=jnp.int32)[None, :, None]
    cosine, sine = unit_turn(points * k_index & (order - 1), order)
    packed = (own == 0) & (jnp.arange(rows)[None, :, None] == 0)
    middle = jnp.where(own == 0, imag[:, :1], 0.0)
    imag = jnp.where(packed, 0.0, imag)
    real, imag = real * cosine + imag * sine, imag * cosine - real * sine
    cosine, sine = unit_turn(points * (coarse // 2), order)
    real = jnp.concatenate([real, middle * cosine], axis=1)
    imag = jnp.concatenate([imag, -middle * sine], axis=1)

    def turned(pattern, root, parts):
        cosine, sine = (jnp.asarray(part.astype(np.float32)) for part in root)
        mul = functools.partial(jnp.einsum, pattern, precision=HIGHEST)
        return (
            mul(cosine, parts[0]) - mul(sine, parts[1]),
            mul(cosine, parts[1]) + mul(sine, parts[0]),
        )

    group_index, point_index = np.arange(groups), np.arange(HALF)
    parts = turned(
        "cu,crj->urj", unit_root(groups, group_index[:, None] * group_index), (real, imag)
    )
    parts = turned(
        "uj,urj->urj", unit_root(fine_length, group_index[:, None] * point_index), parts
    )
    parts = turned(
        "jv,urj->vur", unit_root(HALF, point_index[:, None] * point_index), parts
    )
    tiles = fine_length // 2
    kept = jnp.concatenate([~packed[0, :, 0], jnp.zeros((1,), bool)])
    sides = []
    for part, sign in zip(parts, (1.0, -1.0)):
        part = part.reshape(fine_length, rows + 1)
        sides.append((part[:tiles], sign * jnp.where(kept, part[tiles:][::-1], 0.0)))
    power = sum(jnp.sum(part * part, axis=1) for pair in sides for part in pair)
    starts = jnp.cumsum(owner_counts) - owner_counts
    slot_index = jnp.arange(capacity, dtype=jnp.int32)
    filled = slot_index[None, :] < owner_counts[:, None]
    chosen = jnp.clip(starts[:, None] + slot_index[None, :], 0, tiles - 1)

    def kinds(low, high):
        low_sums, high_sums = jnp.sum(low[:, :rows], axis=1), jnp.sum(high[:, 1:rows], axis=1)
        values = jnp.stack([low_sums, high_sums, high[:, 0] + low[:, rows], power], axis=1)
        return jnp.where(filled[:, :, None], values[chosen], 0.0).transpose(0, 2, 1)

    return jnp.concatenate([kinds(*sides[0]), kinds(*sides[1])], axis=2)


def pool_table(shares, coarse):
    pool = np.zeros((21, 16, shares, KINDS), np.float32)
    sums = pool[:20].reshape(NCLASS, STATES, shares, KINDS)
    wide = TILE // STATES
    rows = coarse // 2 // shares
    for share in range(shares):
        first = rows * share
        rest = coarse - first if share else coarse // 2
        for kind, at in enumerate((first, coarse - first - 1, rest)):
            for band in range(NCLASS):
                sums[band, at // wide >> band, share, kind] = 1.0
    pool[20, :, :, 3] = 1.0
    return pool.reshape(-1, shares * KINDS).astype(BF16)


def update_kernel(count, x_ref, pool_ref, moved_ref, band_ref, out_ref):
    band = band_ref[...]
    sums = dot(pool_ref[...], jnp.concatenate(split_two(x_ref[...]), axis=1))
    sums = sums[:, :LANES] + sums[:, LANES:]
    power = sums[NCLASS * STATES : NCLASS * STATES + 1] * (1.0 / count)
    span = jnp.left_shift(TILE // STATES, jnp.maximum(band, 0)).astype(F32)
    scaling = 1.0 / jnp.sqrt(span * (power + EPSILON))
    scaling = jnp.where(band < 0, 0.0, scaling)
    chosen = sums[:STATES]
    for k in range(1, NCLASS):
        chosen = jnp.where(band == k, sums[k * STATES : (k + 1) * STATES], chosen)
    chosen = chosen * scaling
    turned = jnp.transpose(jnp.concatenate([chosen, chosen], axis=0))
    half = turned.shape[0] // 2
    measured = jnp.where(iotas((half, LANES))[1] < STATES, turned[:half], turned[half:])
    out_ref[...] = moved_ref[...] + measured


def update_step(arrived, moved, band, coarse, count):
    shares = arrived.shape[0]
    return pl.pallas_call(
        functools.partial(update_kernel, count),
        out_shape=jax.ShapeDtypeStruct(moved.shape, F32),
        in_specs=[VMEM] * 4,
        out_specs=VMEM,
        compiler_params=PARAMS,
        name="state_update",
    )(arrived.reshape(shares * KINDS, LANES), jnp.asarray(pool_table(shares, coarse)), moved, band)


def state_step_general(band_edges, owner_counts, dynamics, state):
    own = lax.axis_index("bins")
    capacity = state.shape[0]
    slot = jnp.arange(capacity, dtype=jnp.int32)
    start = jnp.cumsum(owner_counts)[own] - owner_counts[own]
    band = jnp.sum((slot + start)[:, None] >= band_edges[None, 1:NCLASS], axis=1)
    band = jnp.where(slot < owner_counts[own], band, -1).astype(jnp.int32)
    limit = STATES >> jnp.arange(NCLASS)[:, None, None]
    index = jnp.arange(STATES)
    inside = (index[:, None] < limit) & (index[None, :] < limit)
    chosen = (band[:, None] == jnp.arange(NCLASS)[None, :]).astype(F32)
    picked = jnp.einsum(
        "rk,kij->rij", chosen, jnp.where(inside, dynamics, 0.0), precision=HIGHEST
    )
    parts = state.reshape(capacity, 2, STATES)
    moved = jnp.einsum("rij,rcj->rci", picked, parts, precision=HIGHEST)
    return moved.reshape(state.shape), jnp.tile(band, 2)[None, :]


def exchanged(values, axes):
    return lax.all_to_all(values, axes, split_axis=0, concat_axis=0, tiled=True)


def body(profiles, band_edges, owner_counts, dynamics, prev_state):
    groups, scans = lax.axis_size("bins"), lax.axis_size("scans")
    prof_rows, length = profiles.shape
    capacity = prev_state.shape[0]
    coarse = length // HALF
    shares = groups * scans
    count = prof_rows * scans * TILE
    state = prev_state.reshape(capacity, 2 * STATES)
    if groups == 8 and scans == 4 and coarse == 16 * shares and capacity == HALF:
        turn = turns_step(groups, groups * length)
        columns, wanted, lane_band, row_band = columns_step(
            profiles.reshape(length), turn, band_edges, owner_counts, capacity
        )
        columns = exchanged(columns, "bins").reshape(coarse // 2, LANES)
        blocks = coarse_step(columns, shares)
        blocks = exchanged(blocks.reshape(shares, 8, LANES), ("bins", "scans"))
        payload, moved = fine_step(
            blocks.reshape(8 * shares, LANES),
            turn,
            wanted,
            row_band,
            dynamics,
            state,
            scans,
            coarse,
        )
        arrived = exchanged(payload, ("bins", "scans"))
    else:
        moved, lane_band = state_step_general(band_edges, owner_counts, dynamics, state)
        columns = profiles.reshape(coarse // groups, groups, HALF).transpose(1, 0, 2)
        columns = exchanged(columns, "bins").reshape(coarse, HALF)
        blocks = exchanged(coarse_step_general(columns, groups), "bins")
        arrived = exchanged(fine_step_general(blocks, owner_counts, capacity), "bins")
        power = lax.psum(arrived[:, 3:], "scans")
        arrived = jnp.concatenate([arrived[:, :3], power], axis=1)
    updated = update_step(arrived, moved, lane_band, coarse, count)
    return updated.reshape(prev_state.shape)


def solution(mesh):
    return jax.shard_map(
        body,
        mesh=mesh,
        in_specs=(P("scans", "bins"), P(), P(), P(), P("bins", "scans", None)),
        out_specs=P("bins", "scans", None),
        check_vma=False,
    )
```

```python
import functools
import math

import jax
import jax.numpy as jnp
import numpy as np
from jax import lax
from jax.experimental import pallas as pl
from jax.experimental.pallas import tpu as pltpu
from jax.sharding import PartitionSpec as P

TILE = 512
STATES = 64
NCLASS = 5
LANES = 128

EPSILON = 1e-05
HIGHEST = lax.Precision.HIGHEST
BF16 = jnp.bfloat16
F32 = jnp.float32


def unit_root(order, exponents):
    angles = 2.0 * np.pi * (np.asarray(exponents, dtype=np.int64) % order) / order
    return np.cos(angles), -np.sin(angles)


def two_terms(values):
    high = np.asarray(values, np.float32).astype(BF16)
    low = (np.asarray(values, np.float64) - high.astype(np.float64)).astype(BF16)
    return high, low


def split_two(values):
    high = values.astype(BF16)
    return high, (values - high.astype(F32)).astype(BF16)


def dot(left, right):
    return jnp.dot(left, right, preferred_element_type=F32)


VMEM = pl.BlockSpec(memory_space=pltpu.VMEM)
PARAMS = pltpu.CompilerParams(vmem_limit_bytes=32 << 20)
COST = pl.CostEstimate(flops=1 << 30, bytes_accessed=1 << 24, transcendentals=0)


KINDS = 4
HALF = LANES // 2


def unit_turn(phase, order):
    shifted = phase + order // 8
    quadrant = (shifted >> (order.bit_length() - 3)) & 3
    x = ((shifted & (order // 4 - 1)) - order // 8).astype(F32) * (2.0 * math.pi / order)
    y = x * x
    cosine = 1.0 + y * (-1 / 2 + y * (1 / 24 + y * (-1 / 720 + y * (1 / 40320))))
    sine = x * (1.0 + y * (-1 / 6 + y * (1 / 120 + y * (-1 / 5040 + y * (1 / 362880)))))
    odd = (quadrant & 1) == 1
    real, imag = jnp.where(odd, sine, cosine), jnp.where(odd, cosine, sine)
    real = jnp.where((quadrant == 1) | (quadrant == 2), -real, real)
    return real, jnp.where(quadrant >= 2, -imag, imag)


def iotas(shape):
    return [lax.broadcasted_iota(jnp.int32, shape, axis) for axis in range(len(shape))]


def turns_kernel(order, turn_ref):
    row, lane = iotas((8, LANES))
    own = lax.axis_index("bins") * lax.axis_size("scans") + lax.axis_index("scans")
    for at in range(turn_ref.shape[0] // 2):
        c, odd = divmod(at, 2)
        k_index = 8 * own + 4 * (lane >> 6) + 2 * (row & 1) + odd
        phase = ((c * HALF + (lane & (HALF - 1))) * k_index) & (order - 1)
        turn_ref[2 * at], turn_ref[2 * at + 1] = unit_turn(phase, order)


def turns_step(groups, order):
    return pl.pallas_call(
        functools.partial(turns_kernel, order),
        out_shape=jax.ShapeDtypeStruct((4 * groups, 8, LANES), F32),
        out_specs=VMEM,
        compiler_params=PARAMS,
        cost_estimate=COST,
        name="turns",
    )()


def slots_kernel(turn_ref, edges_ref, counts_ref, chosen_ref, lane_band_ref, row_band_ref):
    del turn_ref
    groups, capacity = counts_ref.shape[1], row_band_ref.shape[0]
    own = lax.axis_index("bins")
    counts = [
        jnp.broadcast_to(counts_ref[:, owner : owner + 1], (1, LANES)) for owner in range(groups)
    ]
    lane = iotas((1, LANES))[1]
    rank = lane & (capacity - 1)
    start = jnp.zeros((1, LANES), jnp.int32)
    own_start, own_count = start, start
    wanted = []
    for owner, count in enumerate(counts):
        wanted.append(jnp.where(rank < count, start + rank, -1))
        own_start = jnp.where(own == owner, start, own_start)
        own_count = jnp.where(own == owner, count, own_count)
        start = start + count
    quarter = HALF // 2
    tile = groups * iotas((quarter, LANES))[0]
    for pair in range(groups // 2):
        tiles = jnp.where(lane < HALF, wanted[2 * pair], wanted[2 * pair + 1])
        for u in range(groups):
            chosen_ref[u * quarter : (u + 1) * quarter, pair * LANES : (pair + 1) * LANES] = (
                jnp.where(tile + u == tiles, 1.0, 0.0).astype(BF16)
            )
    edges = [jnp.broadcast_to(edges_ref[:, at : at + 1], (1, LANES)) for at in range(1, NCLASS)]
    for ref, slot in ((lane_band_ref, rank), (row_band_ref, iotas((capacity, LANES))[0])):
        band = jnp.zeros_like(slot)
        for edge in edges:
            band = band + jnp.where(slot + own_start >= edge, 1, 0)
        ref[...] = jnp.where(slot < own_count, band, -1)


def slots_step(turn, band_edges, owner_counts, capacity):
    groups = owner_counts.shape[0]
    return pl.pallas_call(
        slots_kernel,
        out_shape=(
            jax.ShapeDtypeStruct((groups * HALF // 2, groups * capacity), BF16),
            jax.ShapeDtypeStruct((1, LANES), jnp.int32),
            jax.ShapeDtypeStruct((capacity, LANES), jnp.int32),
        ),
        in_specs=[VMEM] * 3,
        out_specs=(VMEM,) * 3,
        compiler_params=PARAMS,
        name="slots",
    )(turn, band_edges.reshape(1, -1), owner_counts.reshape(1, -1))


def columns_kernel(x_ref, band_ref, out_ref):
    del band_ref
    groups, rows, _ = out_ref.shape
    low_lanes = iotas((rows, LANES))[1] < HALF
    for pair in range(groups // 2):
        even = x_ref[pl.ds(pair, rows, stride=groups), :]
        odd = x_ref[pl.ds(groups // 2 + pair, rows, stride=groups), :]
        out_ref[2 * pair] = jnp.where(low_lanes, even, pltpu.roll(odd, HALF, 1))
        out_ref[2 * pair + 1] = jnp.where(low_lanes, pltpu.roll(even, HALF, 1), odd)


def columns_step(profile, band, groups):
    rows = profile.shape[0] // (groups * LANES)
    return pl.pallas_call(
        columns_kernel,
        out_shape=jax.ShapeDtypeStruct((groups, rows, LANES), F32),
        in_specs=[VMEM] * 2,
        out_specs=VMEM,
        compiler_params=PARAMS,
        name="columns",
    )(profile.reshape(-1, LANES), band)


def coarse_table(coarse):
    half, quarter = coarse // 2, coarse // 4
    k_index = np.arange(quarter)
    a_index = np.concatenate([np.arange(0, half, 2), np.arange(1, half, 2)])
    real, imag = unit_root(half, k_index[:, None] * a_index[None, :])
    imag[0] = 1
    parts = [part.reshape(quarter // 16, 2, 2, 1, 4, half) for part in (real, imag)]
    parts = np.concatenate(parts, axis=3).transpose(0, 2, 3, 1, 4, 5)
    return np.concatenate(two_terms(parts.reshape(half, half)), axis=1)


def coarse_kernel(shares, x_ref, table_ref, out_ref):
    half = x_ref.shape[0]
    quarter = half // 2
    row, lane = iotas((8, LANES))
    low_lanes = lane < HALF
    sums = []
    for parity in range(2):
        high, low = split_two(x_ref[pl.ds(parity, quarter, stride=2), :])
        at = parity * quarter
        both = dot(table_ref[:, at : at + quarter], jnp.concatenate([high, low], axis=1))
        rest = dot(table_ref[:, half + at : half + at + quarter], high)
        sums.append(both[:, :LANES] + both[:, LANES:] + rest)
    base = 8 * (row >> 2) + 4 * (lane >> 6) + (row & 3)
    base_cosine, base_sine = unit_turn(base, 2 * half)
    packed = low_lanes & (row == 0)
    for sign, block in [(sign, block) for block in range(half // 32) for sign in (1, -1)]:
        pieces = []
        for at in range(32 * block, 32 * (block + 1), 8):
            even, odd = sums[0][at : at + 8], sums[1][at : at + 8]
            pieces.append(even + odd if sign > 0 else even - odd)
        real_low, imag_low, real_high, imag_high = pieces
        if block == 0 and sign < 0:
            imag_low = jnp.where(row == 0, 0.0, imag_low)
        even_real = jnp.where(low_lanes, real_low, pltpu.roll(real_high, HALF, 1))
        even_imag = jnp.where(low_lanes, imag_low, pltpu.roll(imag_high, HALF, 1))
        odd_real = jnp.where(low_lanes, pltpu.roll(real_low, HALF, 1), real_high)
        odd_imag = jnp.where(low_lanes, pltpu.roll(imag_low, HALF, 1), imag_high)
        first = 2 * block + (0 if sign > 0 else shares // 2)
        angle = math.pi * 8 * first / half
        cosine = base_cosine * math.cos(angle) - base_sine * math.sin(angle)
        sine = base_sine * math.cos(angle) + base_cosine * math.sin(angle)
        real = even_real + odd_real * cosine + odd_imag * sine
        if first == 0:
            cosine = jnp.where(packed, -1.0, cosine)
        imag = even_imag + odd_imag * cosine - odd_real * sine
        out_ref[pl.ds(8 * first, 8, stride=2), :] = real
        out_ref[pl.ds(8 * first + 1, 8, stride=2), :] = imag


def coarse_step(columns, shares):
    half = columns.shape[0]
    return pl.pallas_call(
        functools.partial(coarse_kernel, shares),
        out_shape=jax.ShapeDtypeStruct((half, LANES), F32),
        in_specs=[VMEM] * 2,
        out_specs=VMEM,
        compiler_params=PARAMS,
        name="coarse_dft",
    )(columns, jnp.asarray(coarse_table(2 * half)))


def coarse_step_general(columns, shares):
    coarse = columns.shape[0]
    half = coarse // 2
    real, imag = unit_root(coarse, np.arange(half)[:, None] * np.arange(coarse)[None, :])
    imag[0] = 1 - 2 * (np.arange(coarse) % 2)
    table = jnp.asarray(np.concatenate([real, imag]).astype(np.float32))
    spectrum = jnp.dot(table, columns, precision=HIGHEST)
    blocks = jnp.concatenate([spectrum[:half], spectrum[half:]], axis=1)
    return blocks.reshape(shares, half // shares, LANES)


def fine_tables(groups, coarse):
    fine_length = groups * HALF
    doubled = np.arange(LANES) % HALF
    turn = unit_root(fine_length, np.arange(groups)[:, None] * doubled[None, :])
    middle = (np.arange(groups)[:, None] * HALF + doubled[None, :]) * (coarse // 2)
    middle = unit_root(coarse * fine_length, middle)
    turns = np.concatenate(turn + middle).astype(np.float32)
    order = np.arange(HALF)
    order[HALF // 2 :] = order[HALF // 2 :][::-1]
    real, imag = unit_root(HALF, np.arange(HALF)[:, None] * order[None, :])
    sign = np.where(np.arange(HALF) < HALF // 2, 1, -1)
    both = np.eye(2)
    matrix = np.block(
        [
            [np.kron(both, real), np.kron(both, imag * sign)],
            [np.kron(both, -imag), np.kron(both, real * sign)],
        ]
    )
    return turns, np.concatenate(two_terms(matrix), axis=1)


def add(p, q):
    return (p[0] + q[0], p[1] + q[1])


def sub(p, q):
    return (p[0] - q[0], p[1] - q[1])


def times(p, cosine, sine):
    return (p[0] * cosine + p[1] * sine, p[1] * cosine - p[0] * sine)


def eight_point(values):
    half = math.sqrt(0.5)

    def down(p):
        return (p[1], -p[0])

    def four(a, b, c, d):
        s0, s1, s2, s3 = add(a, c), sub(a, c), add(b, d), sub(b, d)
        turned = (s1[0] + s3[1], s1[1] - s3[0]), (s1[0] - s3[1], s1[1] + s3[0])
        return add(s0, s2), turned[0], sub(s0, s2), turned[1]

    even = four(values[0], values[2], values[4], values[6])
    odd = four(values[1], values[3], values[5], values[7])
    turned = [
        odd[0],
        ((odd[1][0] + odd[1][1]) * half, (odd[1][1] - odd[1][0]) * half),
        down(odd[2]),
        ((odd[3][1] - odd[3][0]) * half, (odd[3][0] + odd[3][1]) * -half),
    ]
    return [add(e, t) for e, t in zip(even, turned)] + [sub(e, t) for e, t in zip(even, turned)]


def fine_kernel(profiles, x_ref, turn_ref, chosen_ref, turns_ref, table_ref, out_ref):
    groups = turn_ref.shape[0] // 4
    first = (lax.axis_index("bins") == 0) & (lax.axis_index("scans") == 0)
    row, lane = iotas((8, LANES))
    low_lanes = lane < HALF
    low_side = (lane & (HALF - 1)) < HALF // 2
    even = (row & 1) == 0
    packed = first & low_lanes & even
    blocks = [[None] * 3 for _ in range(groups)]
    for at in range(3):
        column = []
        for c in range(groups):
            start = c * 8 * profiles
            if at < 2:
                real = x_ref[pl.ds(start + 2 * at, 8, stride=4), :]
                imag = x_ref[pl.ds(start + 2 * at + 1, 8, stride=4), :]
                imag = imag if at else jnp.where(packed, 0.0, imag)
                turn = 4 * c + 2 * at
                column.append(times((real, imag), turn_ref[turn], turn_ref[turn + 1]))
            else:
                middle = jnp.where(packed, x_ref[pl.ds(start + 1, 8, stride=4), :], 0.0)
                middle_real = turns_ref[2 * groups + c : 2 * groups + c + 1, :]
                middle_imag = turns_ref[3 * groups + c : 3 * groups + c + 1, :]
                column.append((middle * middle_real, middle * middle_imag))
        for u, value in enumerate(eight_point(column)):
            cosine, sine = turns_ref[u : u + 1, :], -turns_ref[groups + u : groups + u + 1, :]
            blocks[u][at] = times(value, cosine, sine) if u else value
    rows = [block for blocks_u in blocks for block in blocks_u]
    left = jnp.concatenate(
        [jnp.concatenate([block[part] for block in rows], axis=0) for part in range(2)], axis=1
    )
    wide = 2 * LANES
    high, low = split_two(left)
    product = dot(high, table_ref[...])
    product = product[:, :wide] + product[:, wide:] + dot(low, table_ref[:, :wide])
    spectrum = []
    for u in range(groups):
        spectrum.append([])
        for at in range(3):
            start = 8 * (3 * u + at)
            block = (product[start : start + 8, :LANES], product[start : start + 8, LANES:])
            if at != 1:
                dropped = ~low_side & packed if at == 0 else ~low_side
                block = tuple(jnp.where(dropped, 0.0, part) for part in block)
            spectrum[u].append(block)
    squares = [
        sum(block[0] * block[0] + block[1] * block[1] for block in spectrum[u])
        for u in range(groups)
    ]
    rest_place = ~low_side & low_lanes & even
    left = [[], [], [], []]
    for u in range(groups):
        mirror = groups - 1 - u
        power = jnp.where(low_side, squares[u], squares[mirror])
        for shift in (4, 2, 1):
            power = power + pltpu.roll(power, shift, 0)
        for part in range(2):
            evens, odds = (
                jnp.where(low_side, spectrum[u][at][part], spectrum[mirror][at][part])
                for at in range(2)
            )
            sums = jnp.where(rest_place, 0.0, evens) + odds
            sums = sums + pltpu.roll(sums, 7, 0)
            left[2 * part].append(
                jnp.where(
                    even,
                    jnp.where(low_side, sums, 0.0),
                    jnp.where(low_side, 0.0, pltpu.roll(sums, 1, 0)),
                )
            )
            rest = jnp.where(rest_place, evens, spectrum[u][2][part])
            left[2 * part + 1].append(jnp.where(even, rest, power))
    left = jnp.concatenate([jnp.concatenate(pieces, axis=1) for pieces in left], axis=0)
    left = jnp.concatenate(split_two(left), axis=0)
    quarter = HALF // 2
    chosen = [chosen_ref[u * quarter : (u + 1) * quarter, :] for u in range(groups)]
    routed = dot(left, jnp.concatenate([piece for piece in chosen for _ in range(4)], axis=0))
    routed = routed[:32] + routed[32:]
    for pair in range(groups // 2):
        for at in range(2):
            real = routed[8 * at : 8 * (at + 1), pair * LANES : (pair + 1) * LANES]
            imag = routed[16 + 8 * at : 16 + 8 * (at + 1), pair * LANES : (pair + 1) * LANES]
            start = 2 * pair * profiles * KINDS + at
            out_ref[pl.ds(start, 8, stride=2), :] = jnp.where(
                low_lanes, real, pltpu.roll(imag, HALF, 1)
            )
            out_ref[pl.ds(start + profiles * KINDS, 8, stride=2), :] = jnp.where(
                low_lanes, pltpu.roll(real, HALF, 1), imag
            )


def fine_step(arrived, turn, chosen, profiles, coarse):
    groups = turn.shape[0] // 4
    turns, table = fine_tables(groups, coarse)
    out = pl.pallas_call(
        functools.partial(fine_kernel, profiles),
        out_shape=jax.ShapeDtypeStruct((groups * profiles * KINDS, LANES), F32),
        in_specs=[VMEM] * 5,
        out_specs=VMEM,
        compiler_params=PARAMS,
        name="fine_dft",
    )(arrived, turn, chosen, jnp.asarray(turns), jnp.asarray(table))
    return out.reshape(groups * profiles, KINDS, LANES)


def fine_step_general(arrived, owner_counts, capacity):
    groups, rows = arrived.shape[:2]
    coarse = 2 * rows * groups
    fine_length = groups * HALF
    order = coarse * fine_length
    own = lax.axis_index("bins")
    real, imag = arrived[:, :, :HALF], arrived[:, :, HALF:]
    points = jnp.arange(fine_length, dtype=jnp.int32).reshape(groups, 1, HALF)
    k_index = own * rows + jnp.arange(rows, dtype=jnp.int32)[None, :, None]
    cosine, sine = unit_turn(points * k_index & (order - 1), order)
    packed = (own == 0) & (jnp.arange(rows)[None, :, None] == 0)
    middle = jnp.where(own == 0, imag[:, :1], 0.0)
    imag = jnp.where(packed, 0.0, imag)
    real, imag = real * cosine + imag * sine, imag * cosine - real * sine
    cosine, sine = unit_turn(points * (coarse // 2), order)
    real = jnp.concatenate([real, middle * cosine], axis=1)
    imag = jnp.concatenate([imag, -middle * sine], axis=1)

    def turned(pattern, root, parts):
        cosine, sine = (jnp.asarray(part.astype(np.float32)) for part in root)
        mul = functools.partial(jnp.einsum, pattern, precision=HIGHEST)
        return (
            mul(cosine, parts[0]) - mul(sine, parts[1]),
            mul(cosine, parts[1]) + mul(sine, parts[0]),
        )

    group_index, point_index = np.arange(groups), np.arange(HALF)
    parts = turned(
        "cu,crj->urj", unit_root(groups, group_index[:, None] * group_index), (real, imag)
    )
    parts = turned(
        "uj,urj->urj", unit_root(fine_length, group_index[:, None] * point_index), parts
    )
    parts = turned(
        "jv,urj->vur", unit_root(HALF, point_index[:, None] * point_index), parts
    )
    tiles = fine_length // 2
    kept = jnp.concatenate([~packed[0, :, 0], jnp.zeros((1,), bool)])
    sides = []
    for part, sign in zip(parts, (1.0, -1.0)):
        part = part.reshape(fine_length, rows + 1)
        sides.append((part[:tiles], sign * jnp.where(kept, part[tiles:][::-1], 0.0)))
    power = sum(jnp.sum(part * part, axis=1) for pair in sides for part in pair)
    starts = jnp.cumsum(owner_counts) - owner_counts
    slot_index = jnp.arange(capacity, dtype=jnp.int32)
    filled = slot_index[None, :] < owner_counts[:, None]
    chosen = jnp.clip(starts[:, None] + slot_index[None, :], 0, tiles - 1)

    def kinds(low, high):
        low_sums, high_sums = jnp.sum(low[:, :rows], axis=1), jnp.sum(high[:, 1:rows], axis=1)
        values = jnp.stack([low_sums, high[:, 0] + low[:, rows], high_sums, power], axis=1)
        return jnp.where(filled[:, :, None], values[chosen], 0.0).transpose(0, 2, 1)

    return jnp.concatenate([kinds(*sides[0]), kinds(*sides[1])], axis=2)


def pool_table(shares, coarse):
    pool = np.zeros((21, 16, shares, KINDS), np.float32)
    sums = pool[:20].reshape(NCLASS, STATES, shares, KINDS)
    wide = TILE // STATES
    rows = coarse // 2 // shares
    for share in range(shares):
        first = rows * share
        rest = coarse - first if share else coarse // 2
        for kind, at in enumerate((first, rest, coarse - first - 1)):
            for band in range(NCLASS):
                sums[band, at // wide >> band, share, kind] = 1.0
    pool[20, :, :, 3] = 1.0
    return pool.reshape(-1, shares * KINDS).astype(BF16)


def state_product(dynamics, state, band):
    row, column = iotas((NCLASS * STATES, STATES))
    limit = STATES >> (row >> 6)
    inside = ((row & (STATES - 1)) < limit) & (column < limit)
    dynamics = jnp.where(inside, dynamics, 0.0)
    empty = jnp.zeros_like(dynamics)
    halves = [
        jnp.concatenate([dynamics, empty], axis=1),
        jnp.concatenate([empty, dynamics], axis=1),
    ]
    matrix = jnp.concatenate(
        [half[k * STATES : (k + 1) * STATES] for k in range(NCLASS) for half in halves], axis=0
    )
    state_high, state_low = split_two(state)
    high, low = split_two(matrix)
    moved = lax.dot_general(
        jnp.concatenate([state_high, state_low, state_high], axis=1),
        jnp.concatenate([high, high, low], axis=1),
        (((1,), (1,)), ((), ())),
        preferred_element_type=F32,
    )
    result = jnp.zeros(state.shape, F32)
    for k in range(NCLASS):
        result = jnp.where(band == k, moved[:, k * LANES : (k + 1) * LANES], result)
    return result


def update_kernel(
    count, x_ref, pool_ref, lane_band_ref, row_band_ref, dynamics_ref, state_ref, out_ref
):
    band = lane_band_ref[...]
    sums = dot(pool_ref[...], jnp.concatenate(split_two(x_ref[...]), axis=1))
    sums = sums[:, :LANES] + sums[:, LANES:]
    power = sums[NCLASS * STATES : NCLASS * STATES + 1] * (1.0 / count)
    span = jnp.left_shift(TILE // STATES, jnp.maximum(band, 0)).astype(F32)
    scaling = 1.0 / jnp.sqrt(span * (power + EPSILON))
    scaling = jnp.where(band < 0, 0.0, scaling)
    chosen = sums[:STATES]
    for k in range(1, NCLASS):
        chosen = jnp.where(band == k, sums[k * STATES : (k + 1) * STATES], chosen)
    chosen = chosen * scaling
    turned = jnp.transpose(jnp.concatenate([chosen, chosen], axis=0))
    half = turned.shape[0] // 2
    measured = jnp.where(iotas((half, LANES))[1] < STATES, turned[:half], turned[half:])
    out_ref[...] = measured + state_product(
        dynamics_ref[...], state_ref[...], row_band_ref[...]
    )


def update_step(arrived, lane_band, row_band, dynamics, state, coarse, count):
    shares = arrived.shape[0]
    return pl.pallas_call(
        functools.partial(update_kernel, count),
        out_shape=jax.ShapeDtypeStruct(state.shape, F32),
        in_specs=[VMEM] * 6,
        out_specs=VMEM,
        compiler_params=PARAMS,
        name="state_update",
    )(
        arrived.reshape(shares * KINDS, LANES),
        jnp.asarray(pool_table(shares, coarse)),
        lane_band,
        row_band,
        dynamics.reshape(NCLASS * STATES, STATES),
        state,
    )


def bands_general(band_edges, owner_counts, capacity):
    own = lax.axis_index("bins")
    slot = jnp.arange(capacity, dtype=jnp.int32)
    start = jnp.cumsum(owner_counts)[own] - owner_counts[own]
    band = jnp.sum((slot + start)[:, None] >= band_edges[None, 1:NCLASS], axis=1)
    band = jnp.where(slot < owner_counts[own], band, -1).astype(jnp.int32)
    return jnp.tile(band, 2)[None, :], jnp.broadcast_to(band[:, None], (capacity, LANES))


def exchanged(values, axes):
    return lax.all_to_all(values, axes, split_axis=0, concat_axis=0, tiled=True)


def body(profiles, band_edges, owner_counts, dynamics, prev_state):
    groups, scans = lax.axis_size("bins"), lax.axis_size("scans")
    prof_rows, length = profiles.shape
    capacity = prev_state.shape[0]
    coarse = length // HALF
    shares = groups * scans
    count = prof_rows * scans * TILE
    state = prev_state.reshape(capacity, 2 * STATES)
    if groups == 8 and scans == 4 and coarse == 16 * shares and capacity == HALF:
        turn = turns_step(groups, groups * length)
        chosen, lane_band, row_band = slots_step(turn, band_edges, owner_counts, capacity)
        columns = columns_step(profiles.reshape(length), row_band, groups)
        columns = exchanged(columns, "bins").reshape(coarse // 2, LANES)
        blocks = coarse_step(columns, shares)
        blocks = exchanged(blocks.reshape(shares, 8, LANES), ("bins", "scans"))
        payload = fine_step(blocks.reshape(8 * shares, LANES), turn, chosen, scans, coarse)
        arrived = exchanged(payload, ("bins", "scans"))
    else:
        lane_band, row_band = bands_general(band_edges, owner_counts, capacity)
        columns = profiles.reshape(coarse // groups, groups, HALF).transpose(1, 0, 2)
        columns = exchanged(columns, "bins").reshape(coarse, HALF)
        blocks = exchanged(coarse_step_general(columns, groups), "bins")
        arrived = exchanged(fine_step_general(blocks, owner_counts, capacity), "bins")
        power = lax.psum(arrived[:, 3:], "scans")
        arrived = jnp.concatenate([arrived[:, :3], power], axis=1)
    updated = update_step(arrived, lane_band, row_band, dynamics, state, coarse, count)
    return updated.reshape(prev_state.shape)


def solution(mesh):
    return jax.shard_map(
        body,
        mesh=mesh,
        in_specs=(P("scans", "bins"), P(), P(), P(), P("bins", "scans", None)),
        out_specs=P("bins", "scans", None),
        check_vma=False,
    )
```

```python
import functools
import math

import jax
import jax.numpy as jnp
import numpy as np
from jax import lax
from jax.experimental import pallas as pl
from jax.experimental.pallas import tpu as pltpu
from jax.sharding import PartitionSpec as P

TILE = 512
STATES = 64
NCLASS = 5
LANES = 128

EPSILON = 1e-05
HIGHEST = lax.Precision.HIGHEST
BF16 = jnp.bfloat16
F32 = jnp.float32


def unit_root(order, exponents):
    angles = 2.0 * np.pi * (np.asarray(exponents, dtype=np.int64) % order) / order
    return np.cos(angles), -np.sin(angles)


def two_terms(values):
    high = np.asarray(values, np.float32).astype(BF16)
    low = (np.asarray(values, np.float64) - high.astype(np.float64)).astype(BF16)
    return high, low


def split_two(values):
    high = values.astype(BF16)
    return high, (values - high.astype(F32)).astype(BF16)


def dot(left, right):
    return jnp.dot(left, right, preferred_element_type=F32)


VMEM = pl.BlockSpec(memory_space=pltpu.VMEM)
PARAMS = pltpu.CompilerParams(vmem_limit_bytes=32 << 20)
COST = pl.CostEstimate(flops=1 << 30, bytes_accessed=1 << 24, transcendentals=0)


KINDS = 4
HALF = LANES // 2


def unit_turn(phase, order):
    shifted = phase + order // 8
    quadrant = (shifted >> (order.bit_length() - 3)) & 3
    x = ((shifted & (order // 4 - 1)) - order // 8).astype(F32) * (2.0 * math.pi / order)
    y = x * x
    cosine = 1.0 + y * (-1 / 2 + y * (1 / 24 + y * (-1 / 720 + y * (1 / 40320))))
    sine = x * (1.0 + y * (-1 / 6 + y * (1 / 120 + y * (-1 / 5040 + y * (1 / 362880)))))
    odd = (quadrant & 1) == 1
    real, imag = jnp.where(odd, sine, cosine), jnp.where(odd, cosine, sine)
    real = jnp.where((quadrant == 1) | (quadrant == 2), -real, real)
    return real, jnp.where(quadrant >= 2, -imag, imag)


def iotas(shape):
    return [lax.broadcasted_iota(jnp.int32, shape, axis) for axis in range(len(shape))]


def turns_kernel(order, turn_ref):
    row, lane = iotas((8, LANES))
    own = lax.axis_index("bins") * lax.axis_size("scans") + lax.axis_index("scans")
    for at in range(turn_ref.shape[0] // 2):
        c, odd = divmod(at, 2)
        k_index = 8 * own + 4 * (lane >> 6) + 2 * (row & 1) + odd
        phase = ((c * HALF + (lane & (HALF - 1))) * k_index) & (order - 1)
        turn_ref[2 * at], turn_ref[2 * at + 1] = unit_turn(phase, order)


def turns_step(groups, order):
    return pl.pallas_call(
        functools.partial(turns_kernel, order),
        out_shape=jax.ShapeDtypeStruct((4 * groups, 8, LANES), F32),
        out_specs=VMEM,
        compiler_params=PARAMS,
        cost_estimate=COST,
        name="turns",
    )()


def columns_kernel(
    x_ref, turn_ref, edges_ref, counts_ref, out_ref, wanted_ref, lane_band_ref, row_band_ref
):
    del turn_ref
    groups, rows, _ = out_ref.shape
    capacity = row_band_ref.shape[0]
    low_lanes = iotas((rows, LANES))[1] < HALF
    for pair in range(groups // 2):
        even = x_ref[pl.ds(pair, rows, stride=groups), :]
        odd = x_ref[pl.ds(groups // 2 + pair, rows, stride=groups), :]
        out_ref[2 * pair] = jnp.where(low_lanes, even, pltpu.roll(odd, HALF, 1))
        out_ref[2 * pair + 1] = jnp.where(low_lanes, pltpu.roll(even, HALF, 1), odd)
    own = lax.axis_index("bins")
    counts = [
        jnp.broadcast_to(counts_ref[:, owner : owner + 1], (1, LANES)) for owner in range(groups)
    ]
    lane = iotas((1, LANES))[1]
    rank = lane & (capacity - 1)
    start = jnp.zeros((1, LANES), jnp.int32)
    own_start, own_count = start, start
    wanted = []
    for owner, count in enumerate(counts):
        wanted.append(jnp.where(rank < count, start + rank, -1))
        own_start = jnp.where(own == owner, start, own_start)
        own_count = jnp.where(own == owner, count, own_count)
        start = start + count
    for pair in range(groups // 2):
        wanted_ref[:, pair * LANES : (pair + 1) * LANES] = jnp.where(
            lane < HALF, wanted[2 * pair], wanted[2 * pair + 1]
        )
    edges = [jnp.broadcast_to(edges_ref[:, at : at + 1], (1, LANES)) for at in range(1, NCLASS)]
    for ref, slot in ((lane_band_ref, rank), (row_band_ref, iotas((capacity, LANES))[0])):
        band = jnp.zeros_like(slot)
        for edge in edges:
            band = band + jnp.where(slot + own_start >= edge, 1, 0)
        ref[...] = jnp.where(slot < own_count, band, -1)


def columns_step(profile, turn, band_edges, owner_counts, capacity):
    groups = owner_counts.shape[0]
    rows = profile.shape[0] // (groups * LANES)
    return pl.pallas_call(
        columns_kernel,
        out_shape=(
            jax.ShapeDtypeStruct((groups, rows, LANES), F32),
            jax.ShapeDtypeStruct((1, groups * capacity), jnp.int32),
            jax.ShapeDtypeStruct((1, LANES), jnp.int32),
            jax.ShapeDtypeStruct((capacity, LANES), jnp.int32),
        ),
        in_specs=[VMEM] * 4,
        out_specs=(VMEM,) * 4,
        compiler_params=PARAMS,
        name="columns",
    )(profile.reshape(-1, LANES), turn, band_edges.reshape(1, -1), owner_counts.reshape(1, -1))


def coarse_table(coarse):
    half, quarter = coarse // 2, coarse // 4
    k_index = np.arange(quarter)
    a_index = np.concatenate([np.arange(0, half, 2), np.arange(1, half, 2)])
    real, imag = unit_root(half, k_index[:, None] * a_index[None, :])
    imag[0] = 1
    parts = [part.reshape(quarter // 16, 2, 2, 1, 4, half) for part in (real, imag)]
    parts = np.concatenate(parts, axis=3).transpose(0, 2, 3, 1, 4, 5)
    high, low = two_terms(parts.reshape(half, half))
    terms = [term[:, at : at + quarter] for at in (0, quarter) for term in (high, low)]
    return np.concatenate(terms, axis=1)


def coarse_kernel(shares, x_ref, table_ref, out_ref):
    half = x_ref.shape[0]
    quarter = half // 2
    row, lane = iotas((8, LANES))
    low_lanes = lane < HALF
    sums = []
    for parity in range(2):
        high, low = split_two(x_ref[pl.ds(parity, quarter, stride=2), :])
        right = jnp.concatenate(
            [
                jnp.concatenate([high, low], axis=1),
                jnp.concatenate([high, jnp.zeros_like(low)], axis=1),
            ],
            axis=0,
        )
        both = dot(table_ref[:, parity * half : (parity + 1) * half], right)
        sums.append(both[:, :LANES] + both[:, LANES:])
    base = 8 * (row >> 2) + 4 * (lane >> 6) + (row & 3)
    base_cosine, base_sine = unit_turn(base, 2 * half)
    packed = low_lanes & (row == 0)
    for sign, block in [(sign, block) for block in range(half // 32) for sign in (1, -1)]:
        pieces = []
        for at in range(32 * block, 32 * (block + 1), 8):
            even, odd = sums[0][at : at + 8], sums[1][at : at + 8]
            pieces.append(even + odd if sign > 0 else even - odd)
        real_low, imag_low, real_high, imag_high = pieces
        if block == 0 and sign < 0:
            imag_low = jnp.where(row == 0, 0.0, imag_low)
        even_real = jnp.where(low_lanes, real_low, pltpu.roll(real_high, HALF, 1))
        even_imag = jnp.where(low_lanes, imag_low, pltpu.roll(imag_high, HALF, 1))
        odd_real = jnp.where(low_lanes, pltpu.roll(real_low, HALF, 1), real_high)
        odd_imag = jnp.where(low_lanes, pltpu.roll(imag_low, HALF, 1), imag_high)
        first = 2 * block + (0 if sign > 0 else shares // 2)
        angle = math.pi * 8 * first / half
        cosine = base_cosine * math.cos(angle) - base_sine * math.sin(angle)
        sine = base_sine * math.cos(angle) + base_cosine * math.sin(angle)
        real = even_real + odd_real * cosine + odd_imag * sine
        if first == 0:
            cosine = jnp.where(packed, -1.0, cosine)
        imag = even_imag + odd_imag * cosine - odd_real * sine
        out_ref[pl.ds(8 * first, 8, stride=2), :] = real
        out_ref[pl.ds(8 * first + 1, 8, stride=2), :] = imag


def coarse_step(columns, shares):
    half = columns.shape[0]
    return pl.pallas_call(
        functools.partial(coarse_kernel, shares),
        out_shape=jax.ShapeDtypeStruct((half, LANES), F32),
        in_specs=[VMEM] * 2,
        out_specs=VMEM,
        compiler_params=PARAMS,
        name="coarse_dft",
    )(columns, jnp.asarray(coarse_table(2 * half)))


def coarse_step_general(columns, shares):
    coarse = columns.shape[0]
    half = coarse // 2
    real, imag = unit_root(coarse, np.arange(half)[:, None] * np.arange(coarse)[None, :])
    imag[0] = 1 - 2 * (np.arange(coarse) % 2)
    table = jnp.asarray(np.concatenate([real, imag]).astype(np.float32))
    spectrum = jnp.dot(table, columns, precision=HIGHEST)
    blocks = jnp.concatenate([spectrum[:half], spectrum[half:]], axis=1)
    return blocks.reshape(shares, half // shares, LANES)


def fine_tables(groups, coarse):
    fine_length = groups * HALF
    doubled = np.arange(LANES) % HALF
    turn = unit_root(fine_length, np.arange(groups)[:, None] * doubled[None, :])
    middle = (np.arange(groups)[:, None] * HALF + doubled[None, :]) * (coarse // 2)
    middle = unit_root(coarse * fine_length, middle)
    turns = np.concatenate(turn + middle).astype(np.float32)
    order = np.arange(HALF)
    order[HALF // 2 :] = order[HALF // 2 :][::-1]
    real, imag = unit_root(HALF, np.arange(HALF)[:, None] * order[None, :])
    sign = np.where(np.arange(HALF) < HALF // 2, 1, -1)
    both = np.eye(2)
    matrix = np.block(
        [
            [np.kron(both, real), np.kron(both, imag * sign)],
            [np.kron(both, -imag), np.kron(both, real * sign)],
        ]
    )
    return turns, np.concatenate(two_terms(matrix), axis=1)


def add(p, q):
    return (p[0] + q[0], p[1] + q[1])


def sub(p, q):
    return (p[0] - q[0], p[1] - q[1])


def times(p, cosine, sine):
    return (p[0] * cosine + p[1] * sine, p[1] * cosine - p[0] * sine)


def eight_point(values):
    half = math.sqrt(0.5)

    def down(p):
        return (p[1], -p[0])

    def four(a, b, c, d):
        s0, s1, s2, s3 = add(a, c), sub(a, c), add(b, d), sub(b, d)
        turned = (s1[0] + s3[1], s1[1] - s3[0]), (s1[0] - s3[1], s1[1] + s3[0])
        return add(s0, s2), turned[0], sub(s0, s2), turned[1]

    even = four(values[0], values[2], values[4], values[6])
    odd = four(values[1], values[3], values[5], values[7])
    turned = [
        odd[0],
        ((odd[1][0] + odd[1][1]) * half, (odd[1][1] - odd[1][0]) * half),
        down(odd[2]),
        ((odd[3][1] - odd[3][0]) * half, (odd[3][0] + odd[3][1]) * -half),
    ]
    return [add(e, t) for e, t in zip(even, turned)] + [sub(e, t) for e, t in zip(even, turned)]


def fine_kernel(profiles, x_ref, turn_ref, wanted_ref, turns_ref, table_ref, out_ref):
    groups = turn_ref.shape[0] // 4
    first = (lax.axis_index("bins") == 0) & (lax.axis_index("scans") == 0)
    row, lane = iotas((8, LANES))
    low_lanes = lane < HALF
    low_side = (lane & (HALF - 1)) < HALF // 2
    even = (row & 1) == 0
    packed = first & low_lanes & even
    blocks = [[None] * 3 for _ in range(groups)]
    for at in range(3):
        column = []
        for c in range(groups):
            start = c * 8 * profiles
            if at < 2:
                real = x_ref[pl.ds(start + 2 * at, 8, stride=4), :]
                imag = x_ref[pl.ds(start + 2 * at + 1, 8, stride=4), :]
                imag = imag if at else jnp.where(packed, 0.0, imag)
                turn = 4 * c + 2 * at
                column.append(times((real, imag), turn_ref[turn], turn_ref[turn + 1]))
            else:
                middle = jnp.where(packed, x_ref[pl.ds(start + 1, 8, stride=4), :], 0.0)
                middle_real = turns_ref[2 * groups + c : 2 * groups + c + 1, :]
                middle_imag = turns_ref[3 * groups + c : 3 * groups + c + 1, :]
                column.append((middle * middle_real, middle * middle_imag))
        for u, value in enumerate(eight_point(column)):
            cosine, sine = turns_ref[u : u + 1, :], -turns_ref[groups + u : groups + u + 1, :]
            blocks[u][at] = times(value, cosine, sine) if u else value
    rows = [block for blocks_u in blocks for block in blocks_u]
    left = jnp.concatenate(
        [jnp.concatenate([block[part] for block in rows], axis=0) for part in range(2)], axis=1
    )
    wide = 2 * LANES
    high, low = split_two(left)
    product = dot(high, table_ref[...])
    product = product[:, :wide] + product[:, wide:] + dot(low, table_ref[:, :wide])
    spectrum = []
    for u in range(groups):
        spectrum.append([])
        for at in range(3):
            start = 8 * (3 * u + at)
            block = (product[start : start + 8, :LANES], product[start : start + 8, LANES:])
            if at != 1:
                dropped = ~low_side & packed if at == 0 else ~low_side
                block = tuple(jnp.where(dropped, 0.0, part) for part in block)
            spectrum[u].append(block)
    squares = [
        sum(block[0] * block[0] + block[1] * block[1] for block in spectrum[u])
        for u in range(groups)
    ]
    rest_place = ~low_side & low_lanes & even
    left = [[], [], [], []]
    for u in range(groups):
        mirror = groups - 1 - u
        power = jnp.where(low_side, squares[u], squares[mirror])
        for shift in (4, 2, 1):
            power = power + pltpu.roll(power, shift, 0)
        for part in range(2):
            evens, odds = (
                jnp.where(low_side, spectrum[u][at][part], spectrum[mirror][at][part])
                for at in range(2)
            )
            sums = jnp.where(rest_place, 0.0, evens) + odds
            sums = sums + pltpu.roll(sums, 7, 0)
            left[2 * part].append(
                jnp.where(
                    even,
                    jnp.where(low_side, sums, 0.0),
                    jnp.where(low_side, 0.0, pltpu.roll(sums, 1, 0)),
                )
            )
            rest = jnp.where(rest_place, evens, spectrum[u][2][part])
            left[2 * part + 1].append(jnp.where(even, rest, power))
    left = jnp.concatenate([jnp.concatenate(pieces, axis=1) for pieces in left], axis=0)
    left = jnp.concatenate(split_two(left), axis=0)
    wanted = wanted_ref[...]
    chosen = []
    for u in range(groups):
        tile = u + groups * iotas((HALF // 2, wanted.shape[1]))[0]
        chosen += [jnp.where(tile == wanted, 1.0, 0.0).astype(BF16)] * 4
    routed = dot(left, jnp.concatenate(chosen, axis=0))
    routed = routed[:32] + routed[32:]
    for pair in range(groups // 2):
        for at in range(2):
            real = routed[8 * at : 8 * (at + 1), pair * LANES : (pair + 1) * LANES]
            imag = routed[16 + 8 * at : 16 + 8 * (at + 1), pair * LANES : (pair + 1) * LANES]
            start = 2 * pair * profiles * KINDS + at
            out_ref[pl.ds(start, 8, stride=2), :] = jnp.where(
                low_lanes, real, pltpu.roll(imag, HALF, 1)
            )
            out_ref[pl.ds(start + profiles * KINDS, 8, stride=2), :] = jnp.where(
                low_lanes, pltpu.roll(real, HALF, 1), imag
            )


def fine_step(arrived, turn, wanted, profiles, coarse):
    groups = turn.shape[0] // 4
    turns, table = fine_tables(groups, coarse)
    out = pl.pallas_call(
        functools.partial(fine_kernel, profiles),
        out_shape=jax.ShapeDtypeStruct((groups * profiles * KINDS, LANES), F32),
        in_specs=[VMEM] * 5,
        out_specs=VMEM,
        compiler_params=PARAMS,
        name="fine_dft",
    )(arrived, turn, wanted, jnp.asarray(turns), jnp.asarray(table))
    return out.reshape(groups * profiles, KINDS, LANES)


def fine_step_general(arrived, owner_counts, capacity):
    groups, rows = arrived.shape[:2]
    coarse = 2 * rows * groups
    fine_length = groups * HALF
    order = coarse * fine_length
    own = lax.axis_index("bins")
    real, imag = arrived[:, :, :HALF], arrived[:, :, HALF:]
    points = jnp.arange(fine_length, dtype=jnp.int32).reshape(groups, 1, HALF)
    k_index = own * rows + jnp.arange(rows, dtype=jnp.int32)[None, :, None]
    cosine, sine = unit_turn(points * k_index & (order - 1), order)
    packed = (own == 0) & (jnp.arange(rows)[None, :, None] == 0)
    middle = jnp.where(own == 0, imag[:, :1], 0.0)
    imag = jnp.where(packed, 0.0, imag)
    real, imag = real * cosine + imag * sine, imag * cosine - real * sine
    cosine, sine = unit_turn(points * (coarse // 2), order)
    real = jnp.concatenate([real, middle * cosine], axis=1)
    imag = jnp.concatenate([imag, -middle * sine], axis=1)

    def turned(pattern, root, parts):
        cosine, sine = (jnp.asarray(part.astype(np.float32)) for part in root)
        mul = functools.partial(jnp.einsum, pattern, precision=HIGHEST)
        return (
            mul(cosine, parts[0]) - mul(sine, parts[1]),
            mul(cosine, parts[1]) + mul(sine, parts[0]),
        )

    group_index, point_index = np.arange(groups), np.arange(HALF)
    parts = turned(
        "cu,crj->urj", unit_root(groups, group_index[:, None] * group_index), (real, imag)
    )
    parts = turned(
        "uj,urj->urj", unit_root(fine_length, group_index[:, None] * point_index), parts
    )
    parts = turned(
        "jv,urj->vur", unit_root(HALF, point_index[:, None] * point_index), parts
    )
    tiles = fine_length // 2
    kept = jnp.concatenate([~packed[0, :, 0], jnp.zeros((1,), bool)])
    sides = []
    for part, sign in zip(parts, (1.0, -1.0)):
        part = part.reshape(fine_length, rows + 1)
        sides.append((part[:tiles], sign * jnp.where(kept, part[tiles:][::-1], 0.0)))
    power = sum(jnp.sum(part * part, axis=1) for pair in sides for part in pair)
    starts = jnp.cumsum(owner_counts) - owner_counts
    slot_index = jnp.arange(capacity, dtype=jnp.int32)
    filled = slot_index[None, :] < owner_counts[:, None]
    chosen = jnp.clip(starts[:, None] + slot_index[None, :], 0, tiles - 1)

    def kinds(low, high):
        low_sums, high_sums = jnp.sum(low[:, :rows], axis=1), jnp.sum(high[:, 1:rows], axis=1)
        values = jnp.stack([low_sums, high[:, 0] + low[:, rows], high_sums, power], axis=1)
        return jnp.where(filled[:, :, None], values[chosen], 0.0).transpose(0, 2, 1)

    return jnp.concatenate([kinds(*sides[0]), kinds(*sides[1])], axis=2)


def pool_table(shares, coarse):
    pool = np.zeros((21, 16, shares, KINDS), np.float32)
    sums = pool[:20].reshape(NCLASS, STATES, shares, KINDS)
    wide = TILE // STATES
    rows = coarse // 2 // shares
    for share in range(shares):
        first = rows * share
        rest = coarse - first if share else coarse // 2
        for kind, at in enumerate((first, rest, coarse - first - 1)):
            for band in range(NCLASS):
                sums[band, at // wide >> band, share, kind] = 1.0
    pool[20, :, :, 3] = 1.0
    return pool.reshape(-1, shares * KINDS).astype(BF16)


def state_product(dynamics, state, band):
    row, column = iotas((NCLASS * STATES, STATES))
    limit = STATES >> (row >> 6)
    inside = ((row & (STATES - 1)) < limit) & (column < limit)
    dynamics = jnp.where(inside, dynamics, 0.0)
    empty = jnp.zeros_like(dynamics)
    halves = [
        jnp.concatenate([dynamics, empty], axis=1),
        jnp.concatenate([empty, dynamics], axis=1),
    ]
    matrix = jnp.concatenate(
        [half[k * STATES : (k + 1) * STATES] for k in range(NCLASS) for half in halves], axis=0
    )
    state_high, state_low = split_two(state)
    high, low = split_two(matrix)
    moved = lax.dot_general(
        jnp.concatenate([state_high, state_low, state_high], axis=1),
        jnp.concatenate([high, high, low], axis=1),
        (((1,), (1,)), ((), ())),
        preferred_element_type=F32,
    )
    result = jnp.zeros(state.shape, F32)
    for k in range(NCLASS):
        result = jnp.where(band == k, moved[:, k * LANES : (k + 1) * LANES], result)
    return result


def update_kernel(
    count, x_ref, pool_ref, lane_band_ref, row_band_ref, dynamics_ref, state_ref, out_ref
):
    band = lane_band_ref[...]
    sums = dot(pool_ref[...], jnp.concatenate(split_two(x_ref[...]), axis=1))
    sums = sums[:, :LANES] + sums[:, LANES:]
    power = sums[NCLASS * STATES : NCLASS * STATES + 1] * (1.0 / count)
    span = jnp.left_shift(TILE // STATES, jnp.maximum(band, 0)).astype(F32)
    scaling = 1.0 / jnp.sqrt(span * (power + EPSILON))
    scaling = jnp.where(band < 0, 0.0, scaling)
    chosen = sums[:STATES]
    for k in range(1, NCLASS):
        chosen = jnp.where(band == k, sums[k * STATES : (k + 1) * STATES], chosen)
    chosen = chosen * scaling
    turned = jnp.transpose(jnp.concatenate([chosen, chosen], axis=0))
    half = turned.shape[0] // 2
    measured = jnp.where(iotas((half, LANES))[1] < STATES, turned[:half], turned[half:])
    out_ref[...] = measured + state_product(
        dynamics_ref[...], state_ref[...], row_band_ref[...]
    )


def update_step(arrived, lane_band, row_band, dynamics, state, coarse, count):
    shares = arrived.shape[0]
    return pl.pallas_call(
        functools.partial(update_kernel, count),
        out_shape=jax.ShapeDtypeStruct(state.shape, F32),
        in_specs=[VMEM] * 6,
        out_specs=VMEM,
        compiler_params=PARAMS,
        name="state_update",
    )(
        arrived.reshape(shares * KINDS, LANES),
        jnp.asarray(pool_table(shares, coarse)),
        lane_band,
        row_band,
        dynamics.reshape(NCLASS * STATES, STATES),
        state,
    )


def bands_general(band_edges, owner_counts, capacity):
    own = lax.axis_index("bins")
    slot = jnp.arange(capacity, dtype=jnp.int32)
    start = jnp.cumsum(owner_counts)[own] - owner_counts[own]
    band = jnp.sum((slot + start)[:, None] >= band_edges[None, 1:NCLASS], axis=1)
    band = jnp.where(slot < owner_counts[own], band, -1).astype(jnp.int32)
    return jnp.tile(band, 2)[None, :], jnp.broadcast_to(band[:, None], (capacity, LANES))


def exchanged(values, axes):
    return lax.all_to_all(values, axes, split_axis=0, concat_axis=0, tiled=True)


def body(profiles, band_edges, owner_counts, dynamics, prev_state):
    groups, scans = lax.axis_size("bins"), lax.axis_size("scans")
    prof_rows, length = profiles.shape
    capacity = prev_state.shape[0]
    coarse = length // HALF
    shares = groups * scans
    count = prof_rows * scans * TILE
    state = prev_state.reshape(capacity, 2 * STATES)
    if groups == 8 and scans == 4 and coarse == 16 * shares and capacity == HALF:
        turn = turns_step(groups, groups * length)
        columns, wanted, lane_band, row_band = columns_step(
            profiles.reshape(length), turn, band_edges, owner_counts, capacity
        )
        columns = exchanged(columns, "bins").reshape(coarse // 2, LANES)
        blocks = coarse_step(columns, shares)
        blocks = exchanged(blocks.reshape(shares, 8, LANES), ("bins", "scans"))
        payload = fine_step(blocks.reshape(8 * shares, LANES), turn, wanted, scans, coarse)
        arrived = exchanged(payload, ("bins", "scans"))
    else:
        lane_band, row_band = bands_general(band_edges, owner_counts, capacity)
        columns = profiles.reshape(coarse // groups, groups, HALF).transpose(1, 0, 2)
        columns = exchanged(columns, "bins").reshape(coarse, HALF)
        blocks = exchanged(coarse_step_general(columns, groups), "bins")
        arrived = exchanged(fine_step_general(blocks, owner_counts, capacity), "bins")
        power = lax.psum(arrived[:, 3:], "scans")
        arrived = jnp.concatenate([arrived[:, :3], power], axis=1)
    updated = update_step(arrived, lane_band, row_band, dynamics, state, coarse, count)
    return updated.reshape(prev_state.shape)


def solution(mesh):
    return jax.shard_map(
        body,
        mesh=mesh,
        in_specs=(P("scans", "bins"), P(), P(), P(), P("bins", "scans", None)),
        out_specs=P("bins", "scans", None),
        check_vma=False,
    )
```

```python
import functools
import math

import jax
import jax.numpy as jnp
import numpy as np
from jax import lax
from jax.experimental import pallas as pl
from jax.experimental.pallas import tpu as pltpu
from jax.sharding import PartitionSpec as P

TILE = 512
STATES = 64
NCLASS = 5
LANES = 128

EPSILON = 1e-05
HIGHEST = lax.Precision.HIGHEST
BF16 = jnp.bfloat16
F32 = jnp.float32


def unit_root(order, exponents):
    angles = 2.0 * np.pi * (np.asarray(exponents, dtype=np.int64) % order) / order
    return np.cos(angles), -np.sin(angles)


def two_terms(values):
    high = np.asarray(values, np.float32).astype(BF16)
    low = (np.asarray(values, np.float64) - high.astype(np.float64)).astype(BF16)
    return high, low


def three_terms(values):
    high, middle = two_terms(values)
    rest = np.asarray(values, np.float64) - high.astype(np.float64) - middle.astype(np.float64)
    return high, middle, rest.astype(BF16)


def split_two(values):
    high = values.astype(BF16)
    return high, (values - high.astype(F32)).astype(BF16)


def split_three(values):
    high = values.astype(BF16)
    rest = values - high.astype(F32)
    middle = rest.astype(BF16)
    return high, middle, (rest - middle.astype(F32)).astype(BF16)


def dot(left, right):
    return jnp.dot(left, right, preferred_element_type=F32)


VMEM = pl.BlockSpec(memory_space=pltpu.VMEM)
PARAMS = pltpu.CompilerParams(vmem_limit_bytes=32 << 20)
COST = pl.CostEstimate(flops=1 << 30, bytes_accessed=1 << 24, transcendentals=0)


KINDS = 4
HALF = LANES // 2


def unit_turn(phase, order):
    shifted = phase + order // 8
    quadrant = (shifted >> (order.bit_length() - 3)) & 3
    x = ((shifted & (order // 4 - 1)) - order // 8).astype(F32) * (2.0 * math.pi / order)
    y = x * x
    cosine = 1.0 + y * (-1 / 2 + y * (1 / 24 + y * (-1 / 720 + y * (1 / 40320))))
    sine = x * (1.0 + y * (-1 / 6 + y * (1 / 120 + y * (-1 / 5040 + y * (1 / 362880)))))
    odd = (quadrant & 1) == 1
    real, imag = jnp.where(odd, sine, cosine), jnp.where(odd, cosine, sine)
    real = jnp.where((quadrant == 1) | (quadrant == 2), -real, real)
    return real, jnp.where(quadrant >= 2, -imag, imag)


def iotas(shape):
    return [lax.broadcasted_iota(jnp.int32, shape, axis) for axis in range(len(shape))]


def turns_kernel(order, turn_ref):
    row, lane = iotas((8, LANES))
    own = lax.axis_index("bins") * lax.axis_size("scans") + lax.axis_index("scans")
    for at in range(turn_ref.shape[0] // 2):
        c, odd = divmod(at, 2)
        k_index = 8 * own + 4 * (lane >> 6) + 2 * (row & 1) + odd
        phase = ((c * HALF + (lane & (HALF - 1))) * k_index) & (order - 1)
        turn_ref[2 * at], turn_ref[2 * at + 1] = unit_turn(phase, order)


def turns_step(groups, order):
    return pl.pallas_call(
        functools.partial(turns_kernel, order),
        out_shape=jax.ShapeDtypeStruct((4 * groups, 8, LANES), F32),
        out_specs=VMEM,
        compiler_params=PARAMS,
        cost_estimate=COST,
        name="turns",
    )()


def columns_kernel(
    x_ref, turn_ref, edges_ref, counts_ref, out_ref, wanted_ref, lane_band_ref, row_band_ref
):
    del turn_ref
    groups, rows, _ = out_ref.shape
    capacity = row_band_ref.shape[0]
    low_lanes = iotas((rows, LANES))[1] < HALF
    for pair in range(groups // 2):
        even = x_ref[pl.ds(pair, rows, stride=groups), :]
        odd = x_ref[pl.ds(groups // 2 + pair, rows, stride=groups), :]
        out_ref[2 * pair] = jnp.where(low_lanes, even, pltpu.roll(odd, HALF, 1))
        out_ref[2 * pair + 1] = jnp.where(low_lanes, pltpu.roll(even, HALF, 1), odd)
    own = lax.axis_index("bins")
    counts = [
        jnp.broadcast_to(counts_ref[:, owner : owner + 1], (1, LANES)) for owner in range(groups)
    ]
    lane = iotas((1, LANES))[1]
    rank = lane & (capacity - 1)
    start = jnp.zeros((1, LANES), jnp.int32)
    own_start, own_count = start, start
    wanted = []
    for owner, count in enumerate(counts):
        wanted.append(jnp.where(rank < count, start + rank, -1))
        own_start = jnp.where(own == owner, start, own_start)
        own_count = jnp.where(own == owner, count, own_count)
        start = start + count
    for pair in range(groups // 2):
        wanted_ref[:, pair * LANES : (pair + 1) * LANES] = jnp.where(
            lane < HALF, wanted[2 * pair], wanted[2 * pair + 1]
        )
    edges = [jnp.broadcast_to(edges_ref[:, at : at + 1], (1, LANES)) for at in range(1, NCLASS)]
    for ref, slot in ((lane_band_ref, rank), (row_band_ref, iotas((capacity, LANES))[0])):
        band = jnp.zeros_like(slot)
        for edge in edges:
            band = band + jnp.where(slot + own_start >= edge, 1, 0)
        ref[...] = jnp.where(slot < own_count, band, -1)


def columns_step(profile, turn, band_edges, owner_counts, capacity):
    groups = owner_counts.shape[0]
    rows = profile.shape[0] // (groups * LANES)
    return pl.pallas_call(
        columns_kernel,
        out_shape=(
            jax.ShapeDtypeStruct((groups, rows, LANES), F32),
            jax.ShapeDtypeStruct((1, groups * capacity), jnp.int32),
            jax.ShapeDtypeStruct((1, LANES), jnp.int32),
            jax.ShapeDtypeStruct((capacity, LANES), jnp.int32),
        ),
        in_specs=[VMEM] * 4,
        out_specs=(VMEM,) * 4,
        compiler_params=PARAMS,
        name="columns",
    )(profile.reshape(-1, LANES), turn, band_edges.reshape(1, -1), owner_counts.reshape(1, -1))


def coarse_table(coarse):
    half, quarter = coarse // 2, coarse // 4
    k_index = np.arange(quarter)
    a_index = np.concatenate([np.arange(0, half, 2), np.arange(1, half, 2)])
    real, imag = unit_root(half, k_index[:, None] * a_index[None, :])
    imag[0] = 1
    parts = [part.reshape(quarter // 16, 2, 2, 1, 4, half) for part in (real, imag)]
    parts = np.concatenate(parts, axis=3).transpose(0, 2, 3, 1, 4, 5)
    high, middle, low = three_terms(parts.reshape(half, half))
    terms = [term[:, at : at + quarter] for at in (0, quarter) for term in (middle, high, low)]
    return np.concatenate(terms, axis=1)


def coarse_kernel(shares, x_ref, table_ref, out_ref):
    half = x_ref.shape[0]
    quarter = half // 2
    row, lane = iotas((8, LANES))
    low_lanes = lane < HALF
    sums = []
    for parity in range(2):
        high, middle, low = split_three(x_ref[pl.ds(parity, quarter, stride=2), :])
        main = jnp.concatenate([high, middle], axis=1)
        rest = [jnp.concatenate([term, jnp.zeros_like(term)], axis=1) for term in (low, high)]
        at = 3 * quarter * parity
        left = jnp.concatenate(
            [table_ref[:, at : at + 2 * quarter], table_ref[:, at + quarter : at + 3 * quarter]], axis=1
        )
        both = dot(left, jnp.concatenate([main, main] + rest, axis=0))
        sums.append(both[:, :LANES] + both[:, LANES:])
    base = 8 * (row >> 2) + 4 * (lane >> 6) + (row & 3)
    base_cosine, base_sine = unit_turn(base, 2 * half)
    packed = low_lanes & (row == 0)
    for sign, block in [(sign, block) for block in range(half // 32) for sign in (1, -1)]:
        pieces = []
        for at in range(32 * block, 32 * (block + 1), 8):
            even, odd = sums[0][at : at + 8], sums[1][at : at + 8]
            pieces.append(even + odd if sign > 0 else even - odd)
        real_low, imag_low, real_high, imag_high = pieces
        if block == 0 and sign < 0:
            imag_low = jnp.where(row == 0, 0.0, imag_low)
        even_real = jnp.where(low_lanes, real_low, pltpu.roll(real_high, HALF, 1))
        even_imag = jnp.where(low_lanes, imag_low, pltpu.roll(imag_high, HALF, 1))
        odd_real = jnp.where(low_lanes, pltpu.roll(real_low, HALF, 1), real_high)
        odd_imag = jnp.where(low_lanes, pltpu.roll(imag_low, HALF, 1), imag_high)
        first = 2 * block + (0 if sign > 0 else shares // 2)
        angle = math.pi * 8 * first / half
        cosine = base_cosine * math.cos(angle) - base_sine * math.sin(angle)
        sine = base_sine * math.cos(angle) + base_cosine * math.sin(angle)
        real = even_real + odd_real * cosine + odd_imag * sine
        if first == 0:
            cosine = jnp.where(packed, -1.0, cosine)
        imag = even_imag + odd_imag * cosine - odd_real * sine
        out_ref[pl.ds(8 * first, 8, stride=2), :] = real
        out_ref[pl.ds(8 * first + 1, 8, stride=2), :] = imag


def coarse_step(columns, shares):
    half = columns.shape[0]
    return pl.pallas_call(
        functools.partial(coarse_kernel, shares),
        out_shape=jax.ShapeDtypeStruct((half, LANES), F32),
        in_specs=[VMEM] * 2,
        out_specs=VMEM,
        compiler_params=PARAMS,
        name="coarse_dft",
    )(columns, jnp.asarray(coarse_table(2 * half)))


def coarse_step_general(columns, shares):
    coarse = columns.shape[0]
    half = coarse // 2
    real, imag = unit_root(coarse, np.arange(half)[:, None] * np.arange(coarse)[None, :])
    imag[0] = 1 - 2 * (np.arange(coarse) % 2)
    table = jnp.asarray(np.concatenate([real, imag]).astype(np.float32))
    spectrum = jnp.dot(table, columns, precision=HIGHEST)
    blocks = jnp.concatenate([spectrum[:half], spectrum[half:]], axis=1)
    return blocks.reshape(shares, half // shares, LANES)


def fine_tables(groups, coarse):
    fine_length = groups * HALF
    doubled = np.arange(LANES) % HALF
    turn = unit_root(fine_length, np.arange(groups)[:, None] * doubled[None, :])
    middle = (np.arange(groups)[:, None] * HALF + doubled[None, :]) * (coarse // 2)
    middle = unit_root(coarse * fine_length, middle)
    turns = np.concatenate(turn + middle).astype(np.float32)
    order = np.arange(HALF)
    order[HALF // 2 :] = order[HALF // 2 :][::-1]
    real, imag = unit_root(HALF, np.arange(HALF)[:, None] * order[None, :])
    sign = np.where(np.arange(HALF) < HALF // 2, 1, -1)
    matrix = np.block([[real, imag * sign], [-imag, real * sign]])
    high, middle, low = three_terms(matrix)
    both = np.concatenate([high, middle], axis=1)
    rest = [np.concatenate([term, np.zeros_like(term)], axis=1) for term in (low, high)]
    return turns, np.concatenate([both, both] + rest, axis=0)


def add(p, q):
    return (p[0] + q[0], p[1] + q[1])


def sub(p, q):
    return (p[0] - q[0], p[1] - q[1])


def times(p, cosine, sine):
    return (p[0] * cosine + p[1] * sine, p[1] * cosine - p[0] * sine)


def eight_point(values):
    half = math.sqrt(0.5)

    def down(p):
        return (p[1], -p[0])

    def four(a, b, c, d):
        s0, s1, s2, s3 = add(a, c), sub(a, c), add(b, d), sub(b, d)
        turned = (s1[0] + s3[1], s1[1] - s3[0]), (s1[0] - s3[1], s1[1] + s3[0])
        return add(s0, s2), turned[0], sub(s0, s2), turned[1]

    even = four(values[0], values[2], values[4], values[6])
    odd = four(values[1], values[3], values[5], values[7])
    turned = [
        odd[0],
        ((odd[1][0] + odd[1][1]) * half, (odd[1][1] - odd[1][0]) * half),
        down(odd[2]),
        ((odd[3][1] - odd[3][0]) * half, (odd[3][0] + odd[3][1]) * -half),
    ]
    return [add(e, t) for e, t in zip(even, turned)] + [sub(e, t) for e, t in zip(even, turned)]


def fine_kernel(profiles, x_ref, turn_ref, wanted_ref, turns_ref, table_ref, out_ref):
    groups = turn_ref.shape[0] // 4
    first = (lax.axis_index("bins") == 0) & (lax.axis_index("scans") == 0)
    row, lane = iotas((8, LANES))
    low_lanes = lane < HALF
    low_side = (lane & (HALF - 1)) < HALF // 2
    even = (row & 1) == 0
    packed = first & low_lanes & even
    blocks = [[None] * 3 for _ in range(groups)]
    for at in range(3):
        column = []
        for c in range(groups):
            start = c * 8 * profiles
            if at < 2:
                real = x_ref[pl.ds(start + 2 * at, 8, stride=4), :]
                imag = x_ref[pl.ds(start + 2 * at + 1, 8, stride=4), :]
                imag = imag if at else jnp.where(packed, 0.0, imag)
                turn = 4 * c + 2 * at
                column.append(times((real, imag), turn_ref[turn], turn_ref[turn + 1]))
            else:
                middle = jnp.where(packed, x_ref[pl.ds(start + 1, 8, stride=4), :], 0.0)
                middle_real = turns_ref[2 * groups + c : 2 * groups + c + 1, :]
                middle_imag = turns_ref[3 * groups + c : 3 * groups + c + 1, :]
                column.append((middle * middle_real, middle * middle_imag))
        for u, value in enumerate(eight_point(column)):
            cosine, sine = turns_ref[u : u + 1, :], -turns_ref[groups + u : groups + u + 1, :]
            blocks[u][at] = times(value, cosine, sine) if u else value
    rows = []
    for u in range(groups):
        for at in range(3):
            real, imag = blocks[u][at]
            rows.append(jnp.where(low_lanes, real, pltpu.roll(imag, HALF, 1)))
            if at < 2:
                rows.append(jnp.where(low_lanes, pltpu.roll(real, HALF, 1), imag))
    high, middle, low = split_three(jnp.concatenate(rows, axis=0))
    product = dot(jnp.concatenate([high, middle, high, low], axis=1), table_ref[...])
    product = product[:, :LANES] + product[:, LANES:]
    spectrum = []
    for u in range(groups):
        spectrum.append([product[8 * at : 8 * (at + 1)] for at in range(5 * u, 5 * (u + 1))])
        spectrum[u][0] = jnp.where(first & even & ~low_side, 0.0, spectrum[u][0])
        spectrum[u][4] = jnp.where(low_side, spectrum[u][4], 0.0)
    squares = [sum(block * block for block in spectrum[u]) for u in range(groups)]
    rest_place = ~low_side & even
    pieces = []
    for u in range(groups):
        mirror = groups - 1 - u
        power = jnp.where(low_side, squares[u], squares[mirror])
        for shift in (4, 2, 1):
            power = power + pltpu.roll(power, shift, 0)
        evens, *others = (
            jnp.where(low_side, spectrum[u][at], spectrum[mirror][at]) for at in range(4)
        )
        sums = jnp.where(rest_place, 0.0, evens) + sum(others)
        sums = sums + pltpu.roll(sums, 7, 0)
        lows = jnp.where(low_side, sums, 0.0)
        highs = jnp.where(low_side, 0.0, pltpu.roll(sums, 1, 0))
        rest = jnp.where(rest_place, evens, spectrum[u][4])
        pieces.append((jnp.where(even, lows, highs), jnp.where(even, rest, power)))
    left = [[], [], [], []]
    for u in range(0, groups, 2):
        for at in range(2):
            one, two = pieces[u][at], pieces[u + 1][at]
            real = jnp.where(low_lanes, one, pltpu.roll(two, HALF, 1))
            imag = jnp.where(low_lanes, pltpu.roll(one, HALF, 1), two)
            if at == 1:
                power = real + imag
                real, imag = jnp.where(even, real, power), jnp.where(even, imag, power)
            left[at].append(real)
            left[2 + at].append(imag)
    left = jnp.concatenate([jnp.concatenate(parts, axis=1) for parts in left], axis=0)
    left = jnp.concatenate(split_two(left), axis=0)
    wanted = wanted_ref[...]
    chosen = []
    for u in range(groups):
        tile = u + groups * iotas((HALF // 2, wanted.shape[1]))[0]
        chosen += [jnp.where(tile == wanted, 1.0, 0.0).astype(BF16)] * 2
    routed = dot(left, jnp.concatenate(chosen, axis=0))
    routed = routed[:32] + routed[32:]
    for pair in range(groups // 2):
        for at in range(2):
            real = routed[8 * at : 8 * (at + 1), pair * LANES : (pair + 1) * LANES]
            imag = routed[16 + 8 * at : 16 + 8 * (at + 1), pair * LANES : (pair + 1) * LANES]
            start = 2 * pair * profiles * KINDS + at
            out_ref[pl.ds(start, 8, stride=2), :] = jnp.where(
                low_lanes, real, pltpu.roll(imag, HALF, 1)
            )
            out_ref[pl.ds(start + profiles * KINDS, 8, stride=2), :] = jnp.where(
                low_lanes, pltpu.roll(real, HALF, 1), imag
            )


def fine_step(arrived, turn, wanted, profiles, coarse):
    groups = turn.shape[0] // 4
    turns, table = fine_tables(groups, coarse)
    out = pl.pallas_call(
        functools.partial(fine_kernel, profiles),
        out_shape=jax.ShapeDtypeStruct((groups * profiles * KINDS, LANES), F32),
        in_specs=[VMEM] * 5,
        out_specs=VMEM,
        compiler_params=PARAMS,
        name="fine_dft",
    )(arrived, turn, wanted, jnp.asarray(turns), jnp.asarray(table))
    return out.reshape(groups * profiles, KINDS, LANES)


def fine_step_general(arrived, owner_counts, capacity):
    groups, rows = arrived.shape[:2]
    coarse = 2 * rows * groups
    fine_length = groups * HALF
    order = coarse * fine_length
    own = lax.axis_index("bins")
    real, imag = arrived[:, :, :HALF], arrived[:, :, HALF:]
    points = jnp.arange(fine_length, dtype=jnp.int32).reshape(groups, 1, HALF)
    k_index = own * rows + jnp.arange(rows, dtype=jnp.int32)[None, :, None]
    cosine, sine = unit_turn(points * k_index & (order - 1), order)
    packed = (own == 0) & (jnp.arange(rows)[None, :, None] == 0)
    middle = jnp.where(own == 0, imag[:, :1], 0.0)
    imag = jnp.where(packed, 0.0, imag)
    real, imag = real * cosine + imag * sine, imag * cosine - real * sine
    cosine, sine = unit_turn(points * (coarse // 2), order)
    real = jnp.concatenate([real, middle * cosine], axis=1)
    imag = jnp.concatenate([imag, -middle * sine], axis=1)

    def turned(pattern, root, parts):
        cosine, sine = (jnp.asarray(part.astype(np.float32)) for part in root)
        mul = functools.partial(jnp.einsum, pattern, precision=HIGHEST)
        return (
            mul(cosine, parts[0]) - mul(sine, parts[1]),
            mul(cosine, parts[1]) + mul(sine, parts[0]),
        )

    group_index, point_index = np.arange(groups), np.arange(HALF)
    parts = turned(
        "cu,crj->urj", unit_root(groups, group_index[:, None] * group_index), (real, imag)
    )
    parts = turned(
        "uj,urj->urj", unit_root(fine_length, group_index[:, None] * point_index), parts
    )
    parts = turned(
        "jv,urj->vur", unit_root(HALF, point_index[:, None] * point_index), parts
    )
    tiles = fine_length // 2
    kept = jnp.concatenate([~packed[0, :, 0], jnp.zeros((1,), bool)])
    sides = []
    for part, sign in zip(parts, (1.0, -1.0)):
        part = part.reshape(fine_length, rows + 1)
        sides.append((part[:tiles], sign * jnp.where(kept, part[tiles:][::-1], 0.0)))
    power = sum(jnp.sum(part * part, axis=1) for pair in sides for part in pair)
    starts = jnp.cumsum(owner_counts) - owner_counts
    slot_index = jnp.arange(capacity, dtype=jnp.int32)
    filled = slot_index[None, :] < owner_counts[:, None]
    chosen = jnp.clip(starts[:, None] + slot_index[None, :], 0, tiles - 1)

    def kinds(low, high):
        low_sums, high_sums = jnp.sum(low[:, :rows], axis=1), jnp.sum(high[:, 1:rows], axis=1)
        values = jnp.stack([low_sums, high[:, 0] + low[:, rows], high_sums, power], axis=1)
        return jnp.where(filled[:, :, None], values[chosen], 0.0).transpose(0, 2, 1)

    return jnp.concatenate([kinds(*sides[0]), kinds(*sides[1])], axis=2)


def pool_table(shares, coarse):
    pool = np.zeros((21, 16, shares, KINDS), np.float32)
    sums = pool[:20].reshape(NCLASS, STATES, shares, KINDS)
    wide = TILE // STATES
    rows = coarse // 2 // shares
    for share in range(shares):
        first = rows * share
        rest = coarse - first if share else coarse // 2
        for kind, at in enumerate((first, rest, coarse - first - 1)):
            for band in range(NCLASS):
                sums[band, at // wide >> band, share, kind] = 1.0
    pool[20, :, :, 3] = 1.0
    return pool.reshape(-1, shares * KINDS).astype(BF16)


def state_product(dynamics, state, band):
    row, column = iotas((NCLASS * STATES, STATES))
    limit = STATES >> (row >> 6)
    inside = ((row & (STATES - 1)) < limit) & (column < limit)
    dynamics = jnp.where(inside, dynamics, 0.0)
    empty = jnp.zeros_like(dynamics)
    halves = [
        jnp.concatenate([dynamics, empty], axis=1),
        jnp.concatenate([empty, dynamics], axis=1),
    ]
    matrix = jnp.concatenate(
        [half[k * STATES : (k + 1) * STATES] for k in range(NCLASS) for half in halves], axis=0
    )
    state_high, state_low = split_two(state)
    high, low = split_two(matrix)
    moved = lax.dot_general(
        jnp.concatenate([state_high, state_low, state_high], axis=1),
        jnp.concatenate([high, high, low], axis=1),
        (((1,), (1,)), ((), ())),
        preferred_element_type=F32,
    )
    result = jnp.zeros(state.shape, F32)
    for k in range(NCLASS):
        result = jnp.where(band == k, moved[:, k * LANES : (k + 1) * LANES], result)
    return result


def update_kernel(
    count, x_ref, pool_ref, lane_band_ref, row_band_ref, dynamics_ref, state_ref, out_ref
):
    band = lane_band_ref[...]
    sums = dot(pool_ref[...], jnp.concatenate(split_two(x_ref[...]), axis=1))
    sums = sums[:, :LANES] + sums[:, LANES:]
    power = sums[NCLASS * STATES : NCLASS * STATES + 1] * (1.0 / count)
    span = jnp.left_shift(TILE // STATES, jnp.maximum(band, 0)).astype(F32)
    scaling = 1.0 / jnp.sqrt(span * (power + EPSILON))
    scaling = jnp.where(band < 0, 0.0, scaling)
    chosen = sums[:STATES]
    for k in range(1, NCLASS):
        chosen = jnp.where(band == k, sums[k * STATES : (k + 1) * STATES], chosen)
    chosen = chosen * scaling
    turned = jnp.transpose(jnp.concatenate([chosen, chosen], axis=0))
    half = turned.shape[0] // 2
    measured = jnp.where(iotas((half, LANES))[1] < STATES, turned[:half], turned[half:])
    out_ref[...] = measured + state_product(
        dynamics_ref[...], state_ref[...], row_band_ref[...]
    )


def update_step(arrived, lane_band, row_band, dynamics, state, coarse, count):
    shares = arrived.shape[0]
    return pl.pallas_call(
        functools.partial(update_kernel, count),
        out_shape=jax.ShapeDtypeStruct(state.shape, F32),
        in_specs=[VMEM] * 6,
        out_specs=VMEM,
        compiler_params=PARAMS,
        name="state_update",
    )(
        arrived.reshape(shares * KINDS, LANES),
        jnp.asarray(pool_table(shares, coarse)),
        lane_band,
        row_band,
        dynamics.reshape(NCLASS * STATES, STATES),
        state,
    )


def bands_general(band_edges, owner_counts, capacity):
    own = lax.axis_index("bins")
    slot = jnp.arange(capacity, dtype=jnp.int32)
    start = jnp.cumsum(owner_counts)[own] - owner_counts[own]
    band = jnp.sum((slot + start)[:, None] >= band_edges[None, 1:NCLASS], axis=1)
    band = jnp.where(slot < owner_counts[own], band, -1).astype(jnp.int32)
    return jnp.tile(band, 2)[None, :], jnp.broadcast_to(band[:, None], (capacity, LANES))


def exchanged(values, axes):
    return lax.all_to_all(values, axes, split_axis=0, concat_axis=0, tiled=True)


def body(profiles, band_edges, owner_counts, dynamics, prev_state):
    groups, scans = lax.axis_size("bins"), lax.axis_size("scans")
    prof_rows, length = profiles.shape
    capacity = prev_state.shape[0]
    coarse = length // HALF
    shares = groups * scans
    count = prof_rows * scans * TILE
    state = prev_state.reshape(capacity, 2 * STATES)
    if groups == 8 and scans == 4 and coarse == 16 * shares and capacity == HALF:
        turn = turns_step(groups, groups * length)
        columns, wanted, lane_band, row_band = columns_step(
            profiles.reshape(length), turn, band_edges, owner_counts, capacity
        )
        columns = exchanged(columns, "bins").reshape(coarse // 2, LANES)
        blocks = coarse_step(columns, shares)
        blocks = exchanged(blocks.reshape(shares, 8, LANES), ("bins", "scans"))
        payload = fine_step(blocks.reshape(8 * shares, LANES), turn, wanted, scans, coarse)
        arrived = exchanged(payload, ("bins", "scans"))
    else:
        lane_band, row_band = bands_general(band_edges, owner_counts, capacity)
        columns = profiles.reshape(coarse // groups, groups, HALF).transpose(1, 0, 2)
        columns = exchanged(columns, "bins").reshape(coarse, HALF)
        blocks = exchanged(coarse_step_general(columns, groups), "bins")
        arrived = exchanged(fine_step_general(blocks, owner_counts, capacity), "bins")
        power = lax.psum(arrived[:, 3:], "scans")
        arrived = jnp.concatenate([arrived[:, :3], power], axis=1)
    updated = update_step(arrived, lane_band, row_band, dynamics, state, coarse, count)
    return updated.reshape(prev_state.shape)


def solution(mesh):
    return jax.shard_map(
        body,
        mesh=mesh,
        in_specs=(P("scans", "bins"), P(), P(), P(), P("bins", "scans", None)),
        out_specs=P("bins", "scans", None),
        check_vma=False,
    )
```

```python
import functools
import math

import jax
import jax.numpy as jnp
import numpy as np
from jax import lax
from jax.experimental import pallas as pl
from jax.experimental.pallas import tpu as pltpu
from jax.sharding import PartitionSpec as P

TILE = 512
STATES = 64
NCLASS = 5
LANES = 128

EPSILON = 1e-05
HIGHEST = lax.Precision.HIGHEST
BF16 = jnp.bfloat16
F32 = jnp.float32


def unit_root(order, exponents):
    angles = 2.0 * np.pi * (np.asarray(exponents, dtype=np.int64) % order) / order
    return np.cos(angles), -np.sin(angles)


def two_terms(values):
    high = np.asarray(values, np.float32).astype(BF16)
    low = (np.asarray(values, np.float64) - high.astype(np.float64)).astype(BF16)
    return high, low


def three_terms(values):
    high, middle = two_terms(values)
    rest = np.asarray(values, np.float64) - high.astype(np.float64) - middle.astype(np.float64)
    return high, middle, rest.astype(BF16)


def split_two(values):
    high = values.astype(BF16)
    return high, (values - high.astype(F32)).astype(BF16)


def split_three(values):
    high = values.astype(BF16)
    rest = values - high.astype(F32)
    middle = rest.astype(BF16)
    return high, middle, (rest - middle.astype(F32)).astype(BF16)


def dot(left, right):
    return jnp.dot(left, right, preferred_element_type=F32)


VMEM = pl.BlockSpec(memory_space=pltpu.VMEM)
PARAMS = pltpu.CompilerParams(vmem_limit_bytes=32 << 20)
COST = pl.CostEstimate(flops=1 << 30, bytes_accessed=1 << 24, transcendentals=0)


KINDS = 4
HALF = LANES // 2


def unit_turn(phase, order):
    shifted = phase + order // 8
    quadrant = (shifted >> (order.bit_length() - 3)) & 3
    x = ((shifted & (order // 4 - 1)) - order // 8).astype(F32) * (2.0 * math.pi / order)
    y = x * x
    cosine = 1.0 + y * (-1 / 2 + y * (1 / 24 + y * (-1 / 720 + y * (1 / 40320))))
    sine = x * (1.0 + y * (-1 / 6 + y * (1 / 120 + y * (-1 / 5040 + y * (1 / 362880)))))
    odd = (quadrant & 1) == 1
    real, imag = jnp.where(odd, sine, cosine), jnp.where(odd, cosine, sine)
    real = jnp.where((quadrant == 1) | (quadrant == 2), -real, real)
    return real, jnp.where(quadrant >= 2, -imag, imag)


def iotas(shape):
    return [lax.broadcasted_iota(jnp.int32, shape, axis) for axis in range(len(shape))]


def turns_kernel(order, turn_ref):
    row, lane = iotas((8, LANES))
    own = lax.axis_index("bins") * lax.axis_size("scans") + lax.axis_index("scans")
    for at in range(turn_ref.shape[0] // 2):
        c, odd = divmod(at, 2)
        k_index = 8 * own + 4 * (lane >> 6) + 2 * (row & 1) + odd
        phase = ((c * HALF + (lane & (HALF - 1))) * k_index) & (order - 1)
        turn_ref[2 * at], turn_ref[2 * at + 1] = unit_turn(phase, order)


def turns_step(groups, order):
    return pl.pallas_call(
        functools.partial(turns_kernel, order),
        out_shape=jax.ShapeDtypeStruct((4 * groups, 8, LANES), F32),
        out_specs=VMEM,
        compiler_params=PARAMS,
        cost_estimate=COST,
        name="turns",
    )()


def columns_kernel(
    x_ref, turn_ref, edges_ref, counts_ref, out_ref, wanted_ref, lane_band_ref, row_band_ref
):
    del turn_ref
    groups, rows, _ = out_ref.shape
    capacity = row_band_ref.shape[0]
    low_lanes = iotas((rows, LANES))[1] < HALF
    for pair in range(groups // 2):
        even = x_ref[pl.ds(pair, rows, stride=groups), :]
        odd = x_ref[pl.ds(groups // 2 + pair, rows, stride=groups), :]
        out_ref[2 * pair] = jnp.where(low_lanes, even, pltpu.roll(odd, HALF, 1))
        out_ref[2 * pair + 1] = jnp.where(low_lanes, pltpu.roll(even, HALF, 1), odd)
    own = lax.axis_index("bins")
    counts = [
        jnp.broadcast_to(counts_ref[:, owner : owner + 1], (1, LANES)) for owner in range(groups)
    ]
    lane = iotas((1, LANES))[1]
    rank = lane & (capacity - 1)
    start = jnp.zeros((1, LANES), jnp.int32)
    own_start, own_count = start, start
    wanted = []
    for owner, count in enumerate(counts):
        wanted.append(jnp.where(rank < count, start + rank, -1))
        own_start = jnp.where(own == owner, start, own_start)
        own_count = jnp.where(own == owner, count, own_count)
        start = start + count
    for pair in range(groups // 2):
        wanted_ref[:, pair * LANES : (pair + 1) * LANES] = jnp.where(
            lane < HALF, wanted[2 * pair], wanted[2 * pair + 1]
        )
    edges = [jnp.broadcast_to(edges_ref[:, at : at + 1], (1, LANES)) for at in range(1, NCLASS)]
    for ref, slot in ((lane_band_ref, rank), (row_band_ref, iotas((capacity, LANES))[0])):
        band = jnp.zeros_like(slot)
        for edge in edges:
            band = band + jnp.where(slot + own_start >= edge, 1, 0)
        ref[...] = jnp.where(slot < own_count, band, -1)


def columns_step(profile, turn, band_edges, owner_counts, capacity):
    groups = owner_counts.shape[0]
    rows = profile.shape[0] // (groups * LANES)
    return pl.pallas_call(
        columns_kernel,
        out_shape=(
            jax.ShapeDtypeStruct((groups, rows, LANES), F32),
            jax.ShapeDtypeStruct((1, groups * capacity), jnp.int32),
            jax.ShapeDtypeStruct((1, LANES), jnp.int32),
            jax.ShapeDtypeStruct((capacity, LANES), jnp.int32),
        ),
        in_specs=[VMEM] * 4,
        out_specs=(VMEM,) * 4,
        compiler_params=PARAMS,
        name="columns",
    )(profile.reshape(-1, LANES), turn, band_edges.reshape(1, -1), owner_counts.reshape(1, -1))


def coarse_table(coarse):
    half, quarter = coarse // 2, coarse // 4
    k_index = np.arange(quarter)
    a_index = np.concatenate([np.arange(0, half, 2), np.arange(1, half, 2)])
    real, imag = unit_root(half, k_index[:, None] * a_index[None, :])
    imag[0] = 1
    parts = [part.reshape(quarter // 16, 2, 2, 1, 4, half) for part in (real, imag)]
    parts = np.concatenate(parts, axis=3).transpose(0, 2, 3, 1, 4, 5)
    high, middle, low = three_terms(parts.reshape(half, half))
    terms = [term[:, at : at + quarter] for at in (0, quarter) for term in (middle, high, low)]
    return np.concatenate(terms, axis=1)


def coarse_kernel(shares, x_ref, table_ref, out_ref):
    half = x_ref.shape[0]
    quarter = half // 2
    row, lane = iotas((8, LANES))
    low_lanes = lane < HALF
    sums = []
    for parity in range(2):
        high, middle, low = split_three(x_ref[pl.ds(parity, quarter, stride=2), :])
        main = jnp.concatenate([high, middle], axis=1)
        rest = [jnp.concatenate([term, jnp.zeros_like(term)], axis=1) for term in (low, high)]
        at = 3 * quarter * parity
        left = jnp.concatenate(
            [table_ref[:, at : at + 2 * quarter], table_ref[:, at + quarter : at + 3 * quarter]], axis=1
        )
        both = dot(left, jnp.concatenate([main, main] + rest, axis=0))
        sums.append(both[:, :LANES] + both[:, LANES:])
    base = 8 * (row >> 2) + 4 * (lane >> 6) + (row & 3)
    base_cosine, base_sine = unit_turn(base, 2 * half)
    packed = low_lanes & (row == 0)
    for sign, block in [(sign, block) for block in range(half // 32) for sign in (1, -1)]:
        pieces = []
        for at in range(32 * block, 32 * (block + 1), 8):
            even, odd = sums[0][at : at + 8], sums[1][at : at + 8]
            pieces.append(even + odd if sign > 0 else even - odd)
        real_low, imag_low, real_high, imag_high = pieces
        if block == 0 and sign < 0:
            imag_low = jnp.where(row == 0, 0.0, imag_low)
        even_real = jnp.where(low_lanes, real_low, pltpu.roll(real_high, HALF, 1))
        even_imag = jnp.where(low_lanes, imag_low, pltpu.roll(imag_high, HALF, 1))
        odd_real = jnp.where(low_lanes, pltpu.roll(real_low, HALF, 1), real_high)
        odd_imag = jnp.where(low_lanes, pltpu.roll(imag_low, HALF, 1), imag_high)
        first = 2 * block + (0 if sign > 0 else shares // 2)
        angle = math.pi * 8 * first / half
        cosine = base_cosine * math.cos(angle) - base_sine * math.sin(angle)
        sine = base_sine * math.cos(angle) + base_cosine * math.sin(angle)
        real = even_real + odd_real * cosine + odd_imag * sine
        if first == 0:
            cosine = jnp.where(packed, -1.0, cosine)
        imag = even_imag + odd_imag * cosine - odd_real * sine
        out_ref[pl.ds(8 * first, 8, stride=2), :] = real
        out_ref[pl.ds(8 * first + 1, 8, stride=2), :] = imag


def coarse_step(columns, shares):
    half = columns.shape[0]
    return pl.pallas_call(
        functools.partial(coarse_kernel, shares),
        out_shape=jax.ShapeDtypeStruct((half, LANES), F32),
        in_specs=[VMEM] * 2,
        out_specs=VMEM,
        compiler_params=PARAMS,
        name="coarse_dft",
    )(columns, jnp.asarray(coarse_table(2 * half)))


def coarse_step_general(columns, shares):
    coarse = columns.shape[0]
    half = coarse // 2
    real, imag = unit_root(coarse, np.arange(half)[:, None] * np.arange(coarse)[None, :])
    imag[0] = 1 - 2 * (np.arange(coarse) % 2)
    table = jnp.asarray(np.concatenate([real, imag]).astype(np.float32))
    spectrum = jnp.dot(table, columns, precision=HIGHEST)
    blocks = jnp.concatenate([spectrum[:half], spectrum[half:]], axis=1)
    return blocks.reshape(shares, half // shares, LANES)


def fine_tables(groups, coarse):
    fine_length = groups * HALF
    doubled = np.arange(LANES) % HALF
    turn = unit_root(fine_length, np.arange(groups)[:, None] * doubled[None, :])
    middle = (np.arange(groups)[:, None] * HALF + doubled[None, :]) * (coarse // 2)
    middle = unit_root(coarse * fine_length, middle)
    turns = np.concatenate(turn + middle).astype(np.float32)
    order = np.arange(HALF)
    order[HALF // 2 :] = order[HALF // 2 :][::-1]
    real, imag = unit_root(HALF, np.arange(HALF)[:, None] * order[None, :])
    sign = np.where(np.arange(HALF) < HALF // 2, 1, -1)
    matrix = np.block([[real, imag * sign], [-imag, real * sign]])
    high, middle, low = three_terms(matrix)
    both = np.concatenate([high, middle], axis=1)
    rest = [np.concatenate([term, np.zeros_like(term)], axis=1) for term in (low, high)]
    return turns, np.concatenate([both, both] + rest, axis=0)


def add(p, q):
    return (p[0] + q[0], p[1] + q[1])


def sub(p, q):
    return (p[0] - q[0], p[1] - q[1])


def times(p, cosine, sine):
    return (p[0] * cosine + p[1] * sine, p[1] * cosine - p[0] * sine)


def eight_point(values):
    half = math.sqrt(0.5)

    def down(p):
        return (p[1], -p[0])

    def four(a, b, c, d):
        s0, s1, s2, s3 = add(a, c), sub(a, c), add(b, d), sub(b, d)
        turned = (s1[0] + s3[1], s1[1] - s3[0]), (s1[0] - s3[1], s1[1] + s3[0])
        return add(s0, s2), turned[0], sub(s0, s2), turned[1]

    even = four(values[0], values[2], values[4], values[6])
    odd = four(values[1], values[3], values[5], values[7])
    turned = [
        odd[0],
        ((odd[1][0] + odd[1][1]) * half, (odd[1][1] - odd[1][0]) * half),
        down(odd[2]),
        ((odd[3][1] - odd[3][0]) * half, (odd[3][0] + odd[3][1]) * -half),
    ]
    return [add(e, t) for e, t in zip(even, turned)] + [sub(e, t) for e, t in zip(even, turned)]


def fine_kernel(profiles, x_ref, turn_ref, wanted_ref, turns_ref, table_ref, out_ref):
    groups = turn_ref.shape[0] // 4
    first = (lax.axis_index("bins") == 0) & (lax.axis_index("scans") == 0)
    row, lane = iotas((8, LANES))
    low_lanes = lane < HALF
    low_side = (lane & (HALF - 1)) < HALF // 2
    even = (row & 1) == 0
    packed = first & low_lanes & even
    blocks = [[None] * 3 for _ in range(groups)]
    for at in range(3):
        column = []
        for c in range(groups):
            start = c * 8 * profiles
            if at < 2:
                real = x_ref[pl.ds(start + 2 * at, 8, stride=4), :]
                imag = x_ref[pl.ds(start + 2 * at + 1, 8, stride=4), :]
                imag = imag if at else jnp.where(packed, 0.0, imag)
                turn = 4 * c + 2 * at
                column.append(times((real, imag), turn_ref[turn], turn_ref[turn + 1]))
            else:
                middle = jnp.where(packed, x_ref[pl.ds(start + 1, 8, stride=4), :], 0.0)
                middle_real = turns_ref[2 * groups + c : 2 * groups + c + 1, :]
                middle_imag = turns_ref[3 * groups + c : 3 * groups + c + 1, :]
                column.append((middle * middle_real, middle * middle_imag))
        for u, value in enumerate(eight_point(column)):
            cosine, sine = turns_ref[u : u + 1, :], -turns_ref[groups + u : groups + u + 1, :]
            blocks[u][at] = times(value, cosine, sine) if u else value
    rows = []
    for u in range(groups):
        for at in range(3):
            real, imag = blocks[u][at]
            rows.append(jnp.where(low_lanes, real, pltpu.roll(imag, HALF, 1)))
            if at < 2:
                rows.append(jnp.where(low_lanes, pltpu.roll(real, HALF, 1), imag))
    product = []
    for at in range(0, len(rows), len(rows) // 2):
        part = jnp.concatenate(rows[at : at + len(rows) // 2], axis=0)
        high, middle, low = split_three(part)
        both = dot(jnp.concatenate([high, middle, high, low], axis=1), table_ref[...])
        product.append(both[:, :LANES] + both[:, LANES:])
    product = jnp.concatenate(product, axis=0)
    spectrum = []
    for u in range(groups):
        spectrum.append([product[8 * at : 8 * (at + 1)] for at in range(5 * u, 5 * (u + 1))])
        spectrum[u][0] = jnp.where(first & even & ~low_side, 0.0, spectrum[u][0])
        spectrum[u][4] = jnp.where(low_side, spectrum[u][4], 0.0)
    squares = [sum(block * block for block in spectrum[u]) for u in range(groups)]
    rest_place = ~low_side & even
    pieces = []
    for u in range(groups):
        mirror = groups - 1 - u
        power = jnp.where(low_side, squares[u], squares[mirror])
        for shift in (4, 2, 1):
            power = power + pltpu.roll(power, shift, 0)
        evens, *others = (
            jnp.where(low_side, spectrum[u][at], spectrum[mirror][at]) for at in range(4)
        )
        sums = jnp.where(rest_place, 0.0, evens) + sum(others)
        sums = sums + pltpu.roll(sums, 7, 0)
        lows = jnp.where(low_side, sums, 0.0)
        highs = jnp.where(low_side, 0.0, pltpu.roll(sums, 1, 0))
        rest = jnp.where(rest_place, evens, spectrum[u][4])
        pieces.append((jnp.where(even, lows, highs), jnp.where(even, rest, power)))
    left = [[], [], [], []]
    for u in range(0, groups, 2):
        for at in range(2):
            one, two = pieces[u][at], pieces[u + 1][at]
            real = jnp.where(low_lanes, one, pltpu.roll(two, HALF, 1))
            imag = jnp.where(low_lanes, pltpu.roll(one, HALF, 1), two)
            if at == 1:
                power = real + imag
                real, imag = jnp.where(even, real, power), jnp.where(even, imag, power)
            left[at].append(real)
            left[2 + at].append(imag)
    left = jnp.concatenate([jnp.concatenate(parts, axis=1) for parts in left], axis=0)
    left = jnp.concatenate(split_two(left), axis=0)
    wanted = wanted_ref[...]
    chosen = []
    for u in range(groups):
        tile = u + groups * iotas((HALF // 2, wanted.shape[1]))[0]
        chosen += [jnp.where(tile == wanted, 1.0, 0.0).astype(BF16)] * 2
    routed = dot(left, jnp.concatenate(chosen, axis=0))
    routed = routed[:32] + routed[32:]
    for pair in range(groups // 2):
        for at in range(2):
            real = routed[8 * at : 8 * (at + 1), pair * LANES : (pair + 1) * LANES]
            imag = routed[16 + 8 * at : 16 + 8 * (at + 1), pair * LANES : (pair + 1) * LANES]
            start = 2 * pair * profiles * KINDS + at
            out_ref[pl.ds(start, 8, stride=2), :] = jnp.where(
                low_lanes, real, pltpu.roll(imag, HALF, 1)
            )
            out_ref[pl.ds(start + profiles * KINDS, 8, stride=2), :] = jnp.where(
                low_lanes, pltpu.roll(real, HALF, 1), imag
            )


def fine_step(arrived, turn, wanted, profiles, coarse):
    groups = turn.shape[0] // 4
    turns, table = fine_tables(groups, coarse)
    out = pl.pallas_call(
        functools.partial(fine_kernel, profiles),
        out_shape=jax.ShapeDtypeStruct((groups * profiles * KINDS, LANES), F32),
        in_specs=[VMEM] * 5,
        out_specs=VMEM,
        compiler_params=PARAMS,
        name="fine_dft",
    )(arrived, turn, wanted, jnp.asarray(turns), jnp.asarray(table))
    return out.reshape(groups * profiles, KINDS, LANES)


def fine_step_general(arrived, owner_counts, capacity):
    groups, rows = arrived.shape[:2]
    coarse = 2 * rows * groups
    fine_length = groups * HALF
    order = coarse * fine_length
    own = lax.axis_index("bins")
    real, imag = arrived[:, :, :HALF], arrived[:, :, HALF:]
    points = jnp.arange(fine_length, dtype=jnp.int32).reshape(groups, 1, HALF)
    k_index = own * rows + jnp.arange(rows, dtype=jnp.int32)[None, :, None]
    cosine, sine = unit_turn(points * k_index & (order - 1), order)
    packed = (own == 0) & (jnp.arange(rows)[None, :, None] == 0)
    middle = jnp.where(own == 0, imag[:, :1], 0.0)
    imag = jnp.where(packed, 0.0, imag)
    real, imag = real * cosine + imag * sine, imag * cosine - real * sine
    cosine, sine = unit_turn(points * (coarse // 2), order)
    real = jnp.concatenate([real, middle * cosine], axis=1)
    imag = jnp.concatenate([imag, -middle * sine], axis=1)

    def turned(pattern, root, parts):
        cosine, sine = (jnp.asarray(part.astype(np.float32)) for part in root)
        mul = functools.partial(jnp.einsum, pattern, precision=HIGHEST)
        return (
            mul(cosine, parts[0]) - mul(sine, parts[1]),
            mul(cosine, parts[1]) + mul(sine, parts[0]),
        )

    group_index, point_index = np.arange(groups), np.arange(HALF)
    parts = turned(
        "cu,crj->urj", unit_root(groups, group_index[:, None] * group_index), (real, imag)
    )
    parts = turned(
        "uj,urj->urj", unit_root(fine_length, group_index[:, None] * point_index), parts
    )
    parts = turned(
        "jv,urj->vur", unit_root(HALF, point_index[:, None] * point_index), parts
    )
    tiles = fine_length // 2
    kept = jnp.concatenate([~packed[0, :, 0], jnp.zeros((1,), bool)])
    sides = []
    for part, sign in zip(parts, (1.0, -1.0)):
        part = part.reshape(fine_length, rows + 1)
        sides.append((part[:tiles], sign * jnp.where(kept, part[tiles:][::-1], 0.0)))
    power = sum(jnp.sum(part * part, axis=1) for pair in sides for part in pair)
    starts = jnp.cumsum(owner_counts) - owner_counts
    slot_index = jnp.arange(capacity, dtype=jnp.int32)
    filled = slot_index[None, :] < owner_counts[:, None]
    chosen = jnp.clip(starts[:, None] + slot_index[None, :], 0, tiles - 1)

    def kinds(low, high):
        low_sums, high_sums = jnp.sum(low[:, :rows], axis=1), jnp.sum(high[:, 1:rows], axis=1)
        values = jnp.stack([low_sums, high[:, 0] + low[:, rows], high_sums, power], axis=1)
        return jnp.where(filled[:, :, None], values[chosen], 0.0).transpose(0, 2, 1)

    return jnp.concatenate([kinds(*sides[0]), kinds(*sides[1])], axis=2)


def pool_table(shares, coarse):
    pool = np.zeros((21, 16, shares, KINDS), np.float32)
    sums = pool[:20].reshape(NCLASS, STATES, shares, KINDS)
    wide = TILE // STATES
    rows = coarse // 2 // shares
    for share in range(shares):
        first = rows * share
        rest = coarse - first if share else coarse // 2
        for kind, at in enumerate((first, rest, coarse - first - 1)):
            for band in range(NCLASS):
                sums[band, at // wide >> band, share, kind] = 1.0
    pool[20, :, :, 3] = 1.0
    return pool.reshape(-1, shares * KINDS).astype(BF16)


def state_product(dynamics, state, band):
    row, column = iotas((NCLASS * STATES, STATES))
    limit = STATES >> (row >> 6)
    inside = ((row & (STATES - 1)) < limit) & (column < limit)
    dynamics = jnp.where(inside, dynamics, 0.0)
    empty = jnp.zeros_like(dynamics)
    halves = [
        jnp.concatenate([dynamics, empty], axis=1),
        jnp.concatenate([empty, dynamics], axis=1),
    ]
    matrix = jnp.concatenate(
        [half[k * STATES : (k + 1) * STATES] for k in range(NCLASS) for half in halves], axis=0
    )
    state_high, state_low = split_two(state)
    high, low = split_two(matrix)
    moved = lax.dot_general(
        jnp.concatenate([state_high, state_low, state_high], axis=1),
        jnp.concatenate([high, high, low], axis=1),
        (((1,), (1,)), ((), ())),
        preferred_element_type=F32,
    )
    result = jnp.zeros(state.shape, F32)
    for k in range(NCLASS):
        result = jnp.where(band == k, moved[:, k * LANES : (k + 1) * LANES], result)
    return result


def update_kernel(
    count, x_ref, pool_ref, lane_band_ref, row_band_ref, dynamics_ref, state_ref, out_ref
):
    band = lane_band_ref[...]
    right = jnp.concatenate(split_two(x_ref[...]), axis=1)
    sums = jnp.concatenate([dot(pool_ref[:160], right), dot(pool_ref[160:], right)], axis=0)
    sums = sums[:, :LANES] + sums[:, LANES:]
    power = sums[NCLASS * STATES : NCLASS * STATES + 1] * (1.0 / count)
    span = jnp.left_shift(TILE // STATES, jnp.maximum(band, 0)).astype(F32)
    scaling = 1.0 / jnp.sqrt(span * (power + EPSILON))
    scaling = jnp.where(band < 0, 0.0, scaling)
    chosen = sums[:STATES]
    for k in range(1, NCLASS):
        chosen = jnp.where(band == k, sums[k * STATES : (k + 1) * STATES], chosen)
    chosen = chosen * scaling
    turned = jnp.transpose(jnp.concatenate([chosen, chosen], axis=0))
    half = turned.shape[0] // 2
    measured = jnp.where(iotas((half, LANES))[1] < STATES, turned[:half], turned[half:])
    out_ref[...] = measured + state_product(
        dynamics_ref[...], state_ref[...], row_band_ref[...]
    )


def update_step(arrived, lane_band, row_band, dynamics, state, coarse, count):
    shares = arrived.shape[0]
    return pl.pallas_call(
        functools.partial(update_kernel, count),
        out_shape=jax.ShapeDtypeStruct(state.shape, F32),
        in_specs=[VMEM] * 6,
        out_specs=VMEM,
        compiler_params=PARAMS,
        name="state_update",
    )(
        arrived.reshape(shares * KINDS, LANES),
        jnp.asarray(pool_table(shares, coarse)),
        lane_band,
        row_band,
        dynamics.reshape(NCLASS * STATES, STATES),
        state,
    )


def bands_general(band_edges, owner_counts, capacity):
    own = lax.axis_index("bins")
    slot = jnp.arange(capacity, dtype=jnp.int32)
    start = jnp.cumsum(owner_counts)[own] - owner_counts[own]
    band = jnp.sum((slot + start)[:, None] >= band_edges[None, 1:NCLASS], axis=1)
    band = jnp.where(slot < owner_counts[own], band, -1).astype(jnp.int32)
    return jnp.tile(band, 2)[None, :], jnp.broadcast_to(band[:, None], (capacity, LANES))


def exchanged(values, axes):
    return lax.all_to_all(values, axes, split_axis=0, concat_axis=0, tiled=True)


def body(profiles, band_edges, owner_counts, dynamics, prev_state):
    groups, scans = lax.axis_size("bins"), lax.axis_size("scans")
    prof_rows, length = profiles.shape
    capacity = prev_state.shape[0]
    coarse = length // HALF
    shares = groups * scans
    count = prof_rows * scans * TILE
    state = prev_state.reshape(capacity, 2 * STATES)
    if groups == 8 and scans == 4 and coarse == 16 * shares and capacity == HALF:
        turn = turns_step(groups, groups * length)
        columns, wanted, lane_band, row_band = columns_step(
            profiles.reshape(length), turn, band_edges, owner_counts, capacity
        )
        columns = exchanged(columns, "bins").reshape(coarse // 2, LANES)
        blocks = coarse_step(columns, shares)
        blocks = exchanged(blocks.reshape(shares, 8, LANES), ("bins", "scans"))
        payload = fine_step(blocks.reshape(8 * shares, LANES), turn, wanted, scans, coarse)
        arrived = exchanged(payload, ("bins", "scans"))
    else:
        lane_band, row_band = bands_general(band_edges, owner_counts, capacity)
        columns = profiles.reshape(coarse // groups, groups, HALF).transpose(1, 0, 2)
        columns = exchanged(columns, "bins").reshape(coarse, HALF)
        blocks = exchanged(coarse_step_general(columns, groups), "bins")
        arrived = exchanged(fine_step_general(blocks, owner_counts, capacity), "bins")
        power = lax.psum(arrived[:, 3:], "scans")
        arrived = jnp.concatenate([arrived[:, :3], power], axis=1)
    updated = update_step(arrived, lane_band, row_band, dynamics, state, coarse, count)
    return updated.reshape(prev_state.shape)


def solution(mesh):
    return jax.shard_map(
        body,
        mesh=mesh,
        in_specs=(P("scans", "bins"), P(), P(), P(), P("bins", "scans", None)),
        out_specs=P("bins", "scans", None),
        check_vma=False,
    )
```

```python
import functools
import math

import jax
import jax.numpy as jnp
import numpy as np
from jax import lax
from jax.experimental import pallas as pl
from jax.experimental.pallas import tpu as pltpu
from jax.sharding import PartitionSpec as P

TILE = 512
STATES = 64
NCLASS = 5
LANES = 128

EPSILON = 1e-05
HIGHEST = lax.Precision.HIGHEST
BF16 = jnp.bfloat16
F32 = jnp.float32


def unit_root(order, exponents):
    angles = 2.0 * np.pi * (np.asarray(exponents, dtype=np.int64) % order) / order
    return np.cos(angles), -np.sin(angles)


def two_terms(values):
    high = np.asarray(values, np.float32).astype(BF16)
    low = (np.asarray(values, np.float64) - high.astype(np.float64)).astype(BF16)
    return high, low


def three_terms(values):
    high, middle = two_terms(values)
    rest = np.asarray(values, np.float64) - high.astype(np.float64) - middle.astype(np.float64)
    return high, middle, rest.astype(BF16)


def split_two(values):
    high = values.astype(BF16)
    return high, (values - high.astype(F32)).astype(BF16)


def split_three(values):
    high = values.astype(BF16)
    rest = values - high.astype(F32)
    middle = rest.astype(BF16)
    return high, middle, (rest - middle.astype(F32)).astype(BF16)


def dot(left, right):
    return jnp.dot(left, right, preferred_element_type=F32)


VMEM = pl.BlockSpec(memory_space=pltpu.VMEM)
PARAMS = pltpu.CompilerParams(vmem_limit_bytes=32 << 20)
COST = pl.CostEstimate(flops=1 << 30, bytes_accessed=1 << 24, transcendentals=0)


KINDS = 4
HALF = LANES // 2


def unit_turn(phase, order):
    shifted = phase + order // 8
    quadrant = (shifted >> (order.bit_length() - 3)) & 3
    x = ((shifted & (order // 4 - 1)) - order // 8).astype(F32) * (2.0 * math.pi / order)
    y = x * x
    cosine = 1.0 + y * (-1 / 2 + y * (1 / 24 + y * (-1 / 720 + y * (1 / 40320))))
    sine = x * (1.0 + y * (-1 / 6 + y * (1 / 120 + y * (-1 / 5040 + y * (1 / 362880)))))
    odd = (quadrant & 1) == 1
    real, imag = jnp.where(odd, sine, cosine), jnp.where(odd, cosine, sine)
    real = jnp.where((quadrant == 1) | (quadrant == 2), -real, real)
    return real, jnp.where(quadrant >= 2, -imag, imag)


def iotas(shape):
    return [lax.broadcasted_iota(jnp.int32, shape, axis) for axis in range(len(shape))]


def turns_kernel(order, turn_ref):
    row, lane = iotas((8, LANES))
    own = lax.axis_index("bins") * lax.axis_size("scans") + lax.axis_index("scans")
    for at in range(turn_ref.shape[0] // 2):
        c, odd = divmod(at, 2)
        k_index = 8 * own + 4 * (lane >> 6) + 2 * (row & 1) + odd
        phase = ((c * HALF + (lane & (HALF - 1))) * k_index) & (order - 1)
        turn_ref[2 * at], turn_ref[2 * at + 1] = unit_turn(phase, order)


def turns_step(groups, order):
    return pl.pallas_call(
        functools.partial(turns_kernel, order),
        out_shape=jax.ShapeDtypeStruct((4 * groups, 8, LANES), F32),
        out_specs=VMEM,
        compiler_params=PARAMS,
        cost_estimate=COST,
        name="turns",
    )()


def columns_kernel(
    x_ref, turn_ref, edges_ref, counts_ref, out_ref, wanted_ref, lane_band_ref, row_band_ref
):
    del turn_ref
    groups, rows, _ = out_ref.shape
    capacity = row_band_ref.shape[0]
    low_lanes = iotas((rows, LANES))[1] < HALF
    for pair in range(groups // 2):
        even = x_ref[pl.ds(pair, rows, stride=groups), :]
        odd = x_ref[pl.ds(groups // 2 + pair, rows, stride=groups), :]
        out_ref[2 * pair] = jnp.where(low_lanes, even, pltpu.roll(odd, HALF, 1))
        out_ref[2 * pair + 1] = jnp.where(low_lanes, pltpu.roll(even, HALF, 1), odd)
    own = lax.axis_index("bins")
    counts = [
        jnp.broadcast_to(counts_ref[:, owner : owner + 1], (1, LANES)) for owner in range(groups)
    ]
    lane = iotas((1, LANES))[1]
    rank = lane & (capacity - 1)
    start = jnp.zeros((1, LANES), jnp.int32)
    own_start, own_count = start, start
    wanted = []
    for owner, count in enumerate(counts):
        wanted.append(jnp.where(rank < count, start + rank, -1))
        own_start = jnp.where(own == owner, start, own_start)
        own_count = jnp.where(own == owner, count, own_count)
        start = start + count
    for pair in range(groups // 2):
        wanted_ref[:, pair * LANES : (pair + 1) * LANES] = jnp.where(
            lane < HALF, wanted[2 * pair], wanted[2 * pair + 1]
        )
    edges = [jnp.broadcast_to(edges_ref[:, at : at + 1], (1, LANES)) for at in range(1, NCLASS)]
    for ref, slot in ((lane_band_ref, rank), (row_band_ref, iotas((capacity, LANES))[0])):
        band = jnp.zeros_like(slot)
        for edge in edges:
            band = band + jnp.where(slot + own_start >= edge, 1, 0)
        ref[...] = jnp.where(slot < own_count, band, -1)


def columns_step(profile, turn, band_edges, owner_counts, capacity):
    groups = owner_counts.shape[0]
    rows = profile.shape[0] // (groups * LANES)
    return pl.pallas_call(
        columns_kernel,
        out_shape=(
            jax.ShapeDtypeStruct((groups, rows, LANES), F32),
            jax.ShapeDtypeStruct((1, groups * capacity), jnp.int32),
            jax.ShapeDtypeStruct((1, LANES), jnp.int32),
            jax.ShapeDtypeStruct((capacity, LANES), jnp.int32),
        ),
        in_specs=[VMEM] * 4,
        out_specs=(VMEM,) * 4,
        compiler_params=PARAMS,
        name="columns",
    )(profile.reshape(-1, LANES), turn, band_edges.reshape(1, -1), owner_counts.reshape(1, -1))


def coarse_table(coarse):
    half, quarter = coarse // 2, coarse // 4
    k_index = np.arange(quarter)
    a_index = np.concatenate([np.arange(0, half, 2), np.arange(1, half, 2)])
    real, imag = unit_root(half, k_index[:, None] * a_index[None, :])
    imag[0] = 1
    parts = [part.reshape(quarter // 16, 2, 2, 1, 4, half) for part in (real, imag)]
    parts = np.concatenate(parts, axis=3).transpose(0, 2, 3, 1, 4, 5)
    high, middle, low = three_terms(parts.reshape(half, half))
    terms = [term[:, at : at + quarter] for at in (0, quarter) for term in (middle, high, low)]
    return np.concatenate(terms, axis=1)


def coarse_kernel(
    shares, x_ref, table_ref, row_band_ref, dynamics_ref, state_ref, out_ref, moved_ref
):
    half = x_ref.shape[0]
    quarter = half // 2
    row, lane = iotas((8, LANES))
    low_lanes = lane < HALF
    sums = []
    for parity in range(2):
        high, middle, low = split_three(x_ref[pl.ds(parity, quarter, stride=2), :])
        main = jnp.concatenate([high, middle], axis=1)
        rest = [jnp.concatenate([term, jnp.zeros_like(term)], axis=1) for term in (low, high)]
        at = 3 * quarter * parity
        left = jnp.concatenate(
            [table_ref[:, at : at + 2 * quarter], table_ref[:, at + quarter : at + 3 * quarter]], axis=1
        )
        both = dot(left, jnp.concatenate([main, main] + rest, axis=0))
        sums.append(both[:, :LANES] + both[:, LANES:])
    base = 8 * (row >> 2) + 4 * (lane >> 6) + (row & 3)
    base_cosine, base_sine = unit_turn(base, 2 * half)
    packed = low_lanes & (row == 0)
    for sign, block in [(sign, block) for block in range(half // 32) for sign in (1, -1)]:
        pieces = []
        for at in range(32 * block, 32 * (block + 1), 8):
            even, odd = sums[0][at : at + 8], sums[1][at : at + 8]
            pieces.append(even + odd if sign > 0 else even - odd)
        real_low, imag_low, real_high, imag_high = pieces
        if block == 0 and sign < 0:
            imag_low = jnp.where(row == 0, 0.0, imag_low)
        even_real = jnp.where(low_lanes, real_low, pltpu.roll(real_high, HALF, 1))
        even_imag = jnp.where(low_lanes, imag_low, pltpu.roll(imag_high, HALF, 1))
        odd_real = jnp.where(low_lanes, pltpu.roll(real_low, HALF, 1), real_high)
        odd_imag = jnp.where(low_lanes, pltpu.roll(imag_low, HALF, 1), imag_high)
        first = 2 * block + (0 if sign > 0 else shares // 2)
        angle = math.pi * 8 * first / half
        cosine = base_cosine * math.cos(angle) - base_sine * math.sin(angle)
        sine = base_sine * math.cos(angle) + base_cosine * math.sin(angle)
        real = even_real + odd_real * cosine + odd_imag * sine
        if first == 0:
            cosine = jnp.where(packed, -1.0, cosine)
        imag = even_imag + odd_imag * cosine - odd_real * sine
        out_ref[pl.ds(8 * first, 8, stride=2), :] = real
        out_ref[pl.ds(8 * first + 1, 8, stride=2), :] = imag
    moved_ref[...] = state_product(dynamics_ref[...], state_ref[...], row_band_ref[...])


def coarse_step(columns, row_band, dynamics, state, shares):
    half = columns.shape[0]
    return pl.pallas_call(
        functools.partial(coarse_kernel, shares),
        out_shape=(
            jax.ShapeDtypeStruct((half, LANES), F32),
            jax.ShapeDtypeStruct(state.shape, F32),
        ),
        in_specs=[VMEM] * 5,
        out_specs=(VMEM,) * 2,
        compiler_params=PARAMS,
        name="coarse_dft",
    )(
        columns,
        jnp.asarray(coarse_table(2 * half)),
        row_band,
        dynamics.reshape(NCLASS * STATES, STATES),
        state,
    )


def coarse_step_general(columns, shares):
    coarse = columns.shape[0]
    half = coarse // 2
    real, imag = unit_root(coarse, np.arange(half)[:, None] * np.arange(coarse)[None, :])
    imag[0] = 1 - 2 * (np.arange(coarse) % 2)
    table = jnp.asarray(np.concatenate([real, imag]).astype(np.float32))
    spectrum = jnp.dot(table, columns, precision=HIGHEST)
    blocks = jnp.concatenate([spectrum[:half], spectrum[half:]], axis=1)
    return blocks.reshape(shares, half // shares, LANES)


def fine_tables(groups, coarse):
    fine_length = groups * HALF
    doubled = np.arange(LANES) % HALF
    turn = unit_root(fine_length, np.arange(groups)[:, None] * doubled[None, :])
    middle = (np.arange(groups)[:, None] * HALF + doubled[None, :]) * (coarse // 2)
    middle = unit_root(coarse * fine_length, middle)
    turns = np.concatenate(turn + middle).astype(np.float32)
    order = np.arange(HALF)
    order[HALF // 2 :] = order[HALF // 2 :][::-1]
    real, imag = unit_root(HALF, np.arange(HALF)[:, None] * order[None, :])
    sign = np.where(np.arange(HALF) < HALF // 2, 1, -1)
    matrix = np.block([[real, imag * sign], [-imag, real * sign]])
    high, middle, low = three_terms(matrix)
    both = np.concatenate([high, middle], axis=1)
    rest = [np.concatenate([term, np.zeros_like(term)], axis=1) for term in (low, high)]
    return turns, np.concatenate([both, both] + rest, axis=0)


def add(p, q):
    return (p[0] + q[0], p[1] + q[1])


def sub(p, q):
    return (p[0] - q[0], p[1] - q[1])


def times(p, cosine, sine):
    return (p[0] * cosine + p[1] * sine, p[1] * cosine - p[0] * sine)


def eight_point(values):
    half = math.sqrt(0.5)

    def down(p):
        return (p[1], -p[0])

    def four(a, b, c, d):
        s0, s1, s2, s3 = add(a, c), sub(a, c), add(b, d), sub(b, d)
        turned = (s1[0] + s3[1], s1[1] - s3[0]), (s1[0] - s3[1], s1[1] + s3[0])
        return add(s0, s2), turned[0], sub(s0, s2), turned[1]

    even = four(values[0], values[2], values[4], values[6])
    odd = four(values[1], values[3], values[5], values[7])
    turned = [
        odd[0],
        ((odd[1][0] + odd[1][1]) * half, (odd[1][1] - odd[1][0]) * half),
        down(odd[2]),
        ((odd[3][1] - odd[3][0]) * half, (odd[3][0] + odd[3][1]) * -half),
    ]
    return [add(e, t) for e, t in zip(even, turned)] + [sub(e, t) for e, t in zip(even, turned)]


def state_product(dynamics, state, band):
    row, column = iotas((NCLASS * STATES, STATES))
    limit = STATES >> (row >> 6)
    inside = ((row & (STATES - 1)) < limit) & (column < limit)
    dynamics = jnp.where(inside, dynamics, 0.0)
    empty = jnp.zeros_like(dynamics)
    halves = [
        jnp.concatenate([dynamics, empty], axis=1),
        jnp.concatenate([empty, dynamics], axis=1),
    ]
    matrix = jnp.concatenate(
        [half[k * STATES : (k + 1) * STATES] for k in range(NCLASS) for half in halves], axis=0
    )
    state_high, state_low = split_two(state)
    high, low = split_two(matrix)
    moved = lax.dot_general(
        jnp.concatenate([state_high, state_low, state_high], axis=1),
        jnp.concatenate([high, high, low], axis=1),
        (((1,), (1,)), ((), ())),
        preferred_element_type=F32,
    )
    result = jnp.zeros(state.shape, F32)
    for k in range(NCLASS):
        result = jnp.where(band == k, moved[:, k * LANES : (k + 1) * LANES], result)
    return result


def moved_kernel(row_band_ref, dynamics_ref, state_ref, out_ref):
    out_ref[...] = state_product(dynamics_ref[...], state_ref[...], row_band_ref[...])


def moved_step(row_band, dynamics, state):
    return pl.pallas_call(
        moved_kernel,
        out_shape=jax.ShapeDtypeStruct(state.shape, F32),
        in_specs=[VMEM] * 3,
        out_specs=VMEM,
        compiler_params=PARAMS,
        name="moved",
    )(row_band, dynamics.reshape(NCLASS * STATES, STATES), state)


def fine_kernel(
    profiles,
    x_ref,
    turn_ref,
    wanted_ref,
    turns_ref,
    table_ref,
    out_ref,
):
    groups = turn_ref.shape[0] // 4
    first = (lax.axis_index("bins") == 0) & (lax.axis_index("scans") == 0)
    row, lane = iotas((8, LANES))
    low_lanes = lane < HALF
    low_side = (lane & (HALF - 1)) < HALF // 2
    even = (row & 1) == 0
    packed = first & low_lanes & even
    blocks = [[None] * 3 for _ in range(groups)]
    for at in range(3):
        column = []
        for c in range(groups):
            start = c * 8 * profiles
            if at < 2:
                real = x_ref[pl.ds(start + 2 * at, 8, stride=4), :]
                imag = x_ref[pl.ds(start + 2 * at + 1, 8, stride=4), :]
                imag = imag if at else jnp.where(packed, 0.0, imag)
                turn = 4 * c + 2 * at
                column.append(times((real, imag), turn_ref[turn], turn_ref[turn + 1]))
            else:
                middle = jnp.where(packed, x_ref[pl.ds(start + 1, 8, stride=4), :], 0.0)
                middle_real = turns_ref[2 * groups + c : 2 * groups + c + 1, :]
                middle_imag = turns_ref[3 * groups + c : 3 * groups + c + 1, :]
                column.append((middle * middle_real, middle * middle_imag))
        for u, value in enumerate(eight_point(column)):
            cosine, sine = turns_ref[u : u + 1, :], -turns_ref[groups + u : groups + u + 1, :]
            blocks[u][at] = times(value, cosine, sine) if u else value
    rows = []
    for u in range(groups):
        for at in range(3):
            real, imag = blocks[u][at]
            rows.append(jnp.where(low_lanes, real, pltpu.roll(imag, HALF, 1)))
            if at < 2:
                rows.append(jnp.where(low_lanes, pltpu.roll(real, HALF, 1), imag))
    product = []
    for at in range(0, len(rows), len(rows) // 2):
        part = jnp.concatenate(rows[at : at + len(rows) // 2], axis=0)
        high, middle, low = split_three(part)
        both = dot(jnp.concatenate([high, middle, high, low], axis=1), table_ref[...])
        product.append(both[:, :LANES] + both[:, LANES:])
    product = jnp.concatenate(product, axis=0)
    spectrum = []
    for u in range(groups):
        spectrum.append([product[8 * at : 8 * (at + 1)] for at in range(5 * u, 5 * (u + 1))])
        spectrum[u][0] = jnp.where(first & even & ~low_side, 0.0, spectrum[u][0])
        spectrum[u][4] = jnp.where(low_side, spectrum[u][4], 0.0)
    squares = [sum(block * block for block in spectrum[u]) for u in range(groups)]
    rest_place = ~low_side & even
    pieces = []
    for u in range(groups):
        mirror = groups - 1 - u
        power = jnp.where(low_side, squares[u], squares[mirror])
        for shift in (4, 2, 1):
            power = power + pltpu.roll(power, shift, 0)
        evens, *others = (
            jnp.where(low_side, spectrum[u][at], spectrum[mirror][at]) for at in range(4)
        )
        sums = jnp.where(rest_place, 0.0, evens) + sum(others)
        sums = sums + pltpu.roll(sums, 7, 0)
        lows = jnp.where(low_side, sums, 0.0)
        highs = jnp.where(low_side, 0.0, pltpu.roll(sums, 1, 0))
        rest = jnp.where(rest_place, evens, spectrum[u][4])
        pieces.append((jnp.where(even, lows, highs), jnp.where(even, rest, power)))
    left = [[], [], [], []]
    for u in range(0, groups, 2):
        for at in range(2):
            one, two = pieces[u][at], pieces[u + 1][at]
            real = jnp.where(low_lanes, one, pltpu.roll(two, HALF, 1))
            imag = jnp.where(low_lanes, pltpu.roll(one, HALF, 1), two)
            if at == 1:
                power = real + imag
                real, imag = jnp.where(even, real, power), jnp.where(even, imag, power)
            left[at].append(real)
            left[2 + at].append(imag)
    left = jnp.concatenate([jnp.concatenate(parts, axis=1) for parts in left], axis=0)
    left = jnp.concatenate(split_two(left), axis=0)
    wanted = wanted_ref[...]
    chosen = []
    for u in range(groups):
        tile = u + groups * iotas((HALF // 2, wanted.shape[1]))[0]
        chosen += [jnp.where(tile == wanted, 1.0, 0.0).astype(BF16)] * 2
    routed = dot(left, jnp.concatenate(chosen, axis=0))
    routed = routed[:32] + routed[32:]
    for pair in range(groups // 2):
        for at in range(2):
            real = routed[8 * at : 8 * (at + 1), pair * LANES : (pair + 1) * LANES]
            imag = routed[16 + 8 * at : 16 + 8 * (at + 1), pair * LANES : (pair + 1) * LANES]
            start = 2 * pair * profiles * KINDS + at
            out_ref[pl.ds(start, 8, stride=2), :] = jnp.where(
                low_lanes, real, pltpu.roll(imag, HALF, 1)
            )
            out_ref[pl.ds(start + profiles * KINDS, 8, stride=2), :] = jnp.where(
                low_lanes, pltpu.roll(real, HALF, 1), imag
            )


def fine_step(arrived, turn, wanted, profiles, coarse):
    groups = turn.shape[0] // 4
    turns, table = fine_tables(groups, coarse)
    out = pl.pallas_call(
        functools.partial(fine_kernel, profiles),
        out_shape=jax.ShapeDtypeStruct((groups * profiles * KINDS, LANES), F32),
        in_specs=[VMEM] * 5,
        out_specs=VMEM,
        compiler_params=PARAMS,
        name="fine_dft",
    )(
        arrived,
        turn,
        wanted,
        jnp.asarray(turns),
        jnp.asarray(table),
    )
    return out.reshape(groups * profiles, KINDS, LANES)


def fine_step_general(arrived, owner_counts, capacity):
    groups, rows = arrived.shape[:2]
    coarse = 2 * rows * groups
    fine_length = groups * HALF
    order = coarse * fine_length
    own = lax.axis_index("bins")
    real, imag = arrived[:, :, :HALF], arrived[:, :, HALF:]
    points = jnp.arange(fine_length, dtype=jnp.int32).reshape(groups, 1, HALF)
    k_index = own * rows + jnp.arange(rows, dtype=jnp.int32)[None, :, None]
    cosine, sine = unit_turn(points * k_index & (order - 1), order)
    packed = (own == 0) & (jnp.arange(rows)[None, :, None] == 0)
    middle = jnp.where(own == 0, imag[:, :1], 0.0)
    imag = jnp.where(packed, 0.0, imag)
    real, imag = real * cosine + imag * sine, imag * cosine - real * sine
    cosine, sine = unit_turn(points * (coarse // 2), order)
    real = jnp.concatenate([real, middle * cosine], axis=1)
    imag = jnp.concatenate([imag, -middle * sine], axis=1)

    def turned(pattern, root, parts):
        cosine, sine = (jnp.asarray(part.astype(np.float32)) for part in root)
        mul = functools.partial(jnp.einsum, pattern, precision=HIGHEST)
        return (
            mul(cosine, parts[0]) - mul(sine, parts[1]),
            mul(cosine, parts[1]) + mul(sine, parts[0]),
        )

    group_index, point_index = np.arange(groups), np.arange(HALF)
    parts = turned(
        "cu,crj->urj", unit_root(groups, group_index[:, None] * group_index), (real, imag)
    )
    parts = turned(
        "uj,urj->urj", unit_root(fine_length, group_index[:, None] * point_index), parts
    )
    parts = turned(
        "jv,urj->vur", unit_root(HALF, point_index[:, None] * point_index), parts
    )
    tiles = fine_length // 2
    kept = jnp.concatenate([~packed[0, :, 0], jnp.zeros((1,), bool)])
    sides = []
    for part, sign in zip(parts, (1.0, -1.0)):
        part = part.reshape(fine_length, rows + 1)
        sides.append((part[:tiles], sign * jnp.where(kept, part[tiles:][::-1], 0.0)))
    power = sum(jnp.sum(part * part, axis=1) for pair in sides for part in pair)
    starts = jnp.cumsum(owner_counts) - owner_counts
    slot_index = jnp.arange(capacity, dtype=jnp.int32)
    filled = slot_index[None, :] < owner_counts[:, None]
    chosen = jnp.clip(starts[:, None] + slot_index[None, :], 0, tiles - 1)

    def kinds(low, high):
        low_sums, high_sums = jnp.sum(low[:, :rows], axis=1), jnp.sum(high[:, 1:rows], axis=1)
        values = jnp.stack([low_sums, high[:, 0] + low[:, rows], high_sums, power], axis=1)
        return jnp.where(filled[:, :, None], values[chosen], 0.0).transpose(0, 2, 1)

    return jnp.concatenate([kinds(*sides[0]), kinds(*sides[1])], axis=2)


def pool_table(shares, coarse):
    pool = np.zeros((21, 16, shares, KINDS), np.float32)
    sums = pool[:20].reshape(NCLASS, STATES, shares, KINDS)
    wide = TILE // STATES
    rows = coarse // 2 // shares
    for share in range(shares):
        first = rows * share
        rest = coarse - first if share else coarse // 2
        for kind, at in enumerate((first, rest, coarse - first - 1)):
            for band in range(NCLASS):
                sums[band, at // wide >> band, share, kind] = 1.0
    pool[20, :, :, 3] = 1.0
    return pool.reshape(-1, shares * KINDS).astype(BF16)


def update_kernel(
    count, x_ref, pool_ref, lane_band_ref, moved_ref, out_ref
):
    band = lane_band_ref[...]
    right = jnp.concatenate(split_two(x_ref[...]), axis=1)
    sums = jnp.concatenate([dot(pool_ref[:160], right), dot(pool_ref[160:], right)], axis=0)
    sums = sums[:, :LANES] + sums[:, LANES:]
    power = sums[NCLASS * STATES : NCLASS * STATES + 1] * (1.0 / count)
    span = jnp.left_shift(TILE // STATES, jnp.maximum(band, 0)).astype(F32)
    scaling = 1.0 / jnp.sqrt(span * (power + EPSILON))
    scaling = jnp.where(band < 0, 0.0, scaling)
    chosen = sums[:STATES]
    for k in range(1, NCLASS):
        chosen = jnp.where(band == k, sums[k * STATES : (k + 1) * STATES], chosen)
    chosen = chosen * scaling
    turned = jnp.transpose(jnp.concatenate([chosen, chosen], axis=0))
    half = turned.shape[0] // 2
    measured = jnp.where(iotas((half, LANES))[1] < STATES, turned[:half], turned[half:])
    out_ref[...] = measured + moved_ref[...]


def update_step(arrived, lane_band, moved, coarse, count):
    shares = arrived.shape[0]
    return pl.pallas_call(
        functools.partial(update_kernel, count),
        out_shape=jax.ShapeDtypeStruct(moved.shape, F32),
        in_specs=[VMEM] * 4,
        out_specs=VMEM,
        compiler_params=PARAMS,
        name="state_update",
    )(
        arrived.reshape(shares * KINDS, LANES),
        jnp.asarray(pool_table(shares, coarse)),
        lane_band,
        moved,
    )


def bands_general(band_edges, owner_counts, capacity):
    own = lax.axis_index("bins")
    slot = jnp.arange(capacity, dtype=jnp.int32)
    start = jnp.cumsum(owner_counts)[own] - owner_counts[own]
    band = jnp.sum((slot + start)[:, None] >= band_edges[None, 1:NCLASS], axis=1)
    band = jnp.where(slot < owner_counts[own], band, -1).astype(jnp.int32)
    return jnp.tile(band, 2)[None, :], jnp.broadcast_to(band[:, None], (capacity, LANES))


def exchanged(values, axes):
    return lax.all_to_all(values, axes, split_axis=0, concat_axis=0, tiled=True)


def body(profiles, band_edges, owner_counts, dynamics, prev_state):
    groups, scans = lax.axis_size("bins"), lax.axis_size("scans")
    prof_rows, length = profiles.shape
    capacity = prev_state.shape[0]
    coarse = length // HALF
    shares = groups * scans
    count = prof_rows * scans * TILE
    state = prev_state.reshape(capacity, 2 * STATES)
    if groups == 8 and scans == 4 and coarse == 16 * shares and capacity == HALF:
        turn = turns_step(groups, groups * length)
        columns, wanted, lane_band, row_band = columns_step(
            profiles.reshape(length), turn, band_edges, owner_counts, capacity
        )
        columns = exchanged(columns, "bins").reshape(coarse // 2, LANES)
        blocks, moved = coarse_step(columns, row_band, dynamics, state, shares)
        blocks = exchanged(blocks.reshape(shares, 8, LANES), ("bins", "scans"))
        blocks = blocks.reshape(8 * shares, LANES)
        payload = fine_step(blocks, turn, wanted, scans, coarse)
        arrived = exchanged(payload, ("bins", "scans"))
    else:
        lane_band, row_band = bands_general(band_edges, owner_counts, capacity)
        moved = moved_step(row_band, dynamics, state)
        columns = profiles.reshape(coarse // groups, groups, HALF).transpose(1, 0, 2)
        columns = exchanged(columns, "bins").reshape(coarse, HALF)
        blocks = exchanged(coarse_step_general(columns, groups), "bins")
        arrived = exchanged(fine_step_general(blocks, owner_counts, capacity), "bins")
        power = lax.psum(arrived[:, 3:], "scans")
        arrived = jnp.concatenate([arrived[:, :3], power], axis=1)
    updated = update_step(arrived, lane_band, moved, coarse, count)
    return updated.reshape(prev_state.shape)


def solution(mesh):
    return jax.shard_map(
        body,
        mesh=mesh,
        in_specs=(P("scans", "bins"), P(), P(), P(), P("bins", "scans", None)),
        out_specs=P("bins", "scans", None),
        check_vma=False,
    )
```

```python
import functools
import math

import jax
import jax.numpy as jnp
import numpy as np
from jax import lax
from jax.experimental import pallas as pl
from jax.experimental.pallas import tpu as pltpu
from jax.sharding import PartitionSpec as P

TILE = 512
STATES = 64
NCLASS = 5
LANES = 128

EPSILON = 1e-05
HIGHEST = lax.Precision.HIGHEST
BF16 = jnp.bfloat16
F32 = jnp.float32


def unit_root(order, exponents):
    angles = 2.0 * np.pi * (np.asarray(exponents, dtype=np.int64) % order) / order
    return np.cos(angles), -np.sin(angles)


def two_terms(values):
    high = np.asarray(values, np.float32).astype(BF16)
    low = (np.asarray(values, np.float64) - high.astype(np.float64)).astype(BF16)
    return high, low


def three_terms(values):
    high, middle = two_terms(values)
    rest = np.asarray(values, np.float64) - high.astype(np.float64) - middle.astype(np.float64)
    return high, middle, rest.astype(BF16)


def split_two(values):
    high = values.astype(BF16)
    return high, (values - high.astype(F32)).astype(BF16)


def split_three(values):
    high = values.astype(BF16)
    rest = values - high.astype(F32)
    middle = rest.astype(BF16)
    return high, middle, (rest - middle.astype(F32)).astype(BF16)


def dot(left, right):
    return jnp.dot(left, right, preferred_element_type=F32)


VMEM = pl.BlockSpec(memory_space=pltpu.VMEM)
PARAMS = pltpu.CompilerParams(vmem_limit_bytes=32 << 20)
COST = pl.CostEstimate(flops=1 << 30, bytes_accessed=1 << 24, transcendentals=0)


KINDS = 4
HALF = LANES // 2


def unit_turn(phase, order):
    shifted = phase + order // 8
    quadrant = (shifted >> (order.bit_length() - 3)) & 3
    x = ((shifted & (order // 4 - 1)) - order // 8).astype(F32) * (2.0 * math.pi / order)
    y = x * x
    cosine = 1.0 + y * (-1 / 2 + y * (1 / 24 + y * (-1 / 720 + y * (1 / 40320))))
    sine = x * (1.0 + y * (-1 / 6 + y * (1 / 120 + y * (-1 / 5040 + y * (1 / 362880)))))
    odd = (quadrant & 1) == 1
    real, imag = jnp.where(odd, sine, cosine), jnp.where(odd, cosine, sine)
    real = jnp.where((quadrant == 1) | (quadrant == 2), -real, real)
    return real, jnp.where(quadrant >= 2, -imag, imag)


def iotas(shape):
    return [lax.broadcasted_iota(jnp.int32, shape, axis) for axis in range(len(shape))]


def turns_kernel(order, turn_ref):
    row, lane = iotas((8, LANES))
    own = lax.axis_index("bins") * lax.axis_size("scans") + lax.axis_index("scans")
    for at in range(turn_ref.shape[0] // 2):
        c, odd = divmod(at, 2)
        k_index = 8 * own + 4 * (lane >> 6) + 2 * (row & 1) + odd
        phase = ((c * HALF + (lane & (HALF - 1))) * k_index) & (order - 1)
        turn_ref[2 * at], turn_ref[2 * at + 1] = unit_turn(phase, order)


def turns_step(groups, order):
    return pl.pallas_call(
        functools.partial(turns_kernel, order),
        out_shape=jax.ShapeDtypeStruct((4 * groups, 8, LANES), F32),
        out_specs=VMEM,
        compiler_params=PARAMS,
        cost_estimate=COST,
        name="turns",
    )()


def columns_kernel(x_ref, turn_ref, edges_ref, counts_ref, out_ref, whole_ref):
    del turn_ref
    groups, rows, _ = out_ref.shape
    low_lanes = iotas((rows, LANES))[1] < HALF
    for pair in range(groups // 2):
        even = x_ref[pl.ds(pair, rows, stride=groups), :]
        odd = x_ref[pl.ds(groups // 2 + pair, rows, stride=groups), :]
        out_ref[2 * pair] = jnp.where(low_lanes, even, pltpu.roll(odd, HALF, 1))
        out_ref[2 * pair + 1] = jnp.where(low_lanes, pltpu.roll(even, HALF, 1), odd)
    whole_ref[:, : NCLASS + 1] = edges_ref[...]
    whole_ref[:, 8 : 8 + groups] = counts_ref[...]


def columns_step(profile, turn, band_edges, owner_counts):
    groups = owner_counts.shape[0]
    rows = profile.shape[0] // (groups * LANES)
    return pl.pallas_call(
        columns_kernel,
        out_shape=(
            jax.ShapeDtypeStruct((groups, rows, LANES), F32),
            jax.ShapeDtypeStruct((1, LANES), jnp.int32),
        ),
        in_specs=[VMEM] * 4,
        out_specs=(VMEM,) * 2,
        compiler_params=PARAMS,
        name="columns",
    )(profile.reshape(-1, LANES), turn, band_edges.reshape(1, -1), owner_counts.reshape(1, -1))


def coarse_table(coarse):
    half, quarter = coarse // 2, coarse // 4
    k_index = np.arange(quarter)
    a_index = np.concatenate([np.arange(0, half, 2), np.arange(1, half, 2)])
    real, imag = unit_root(half, k_index[:, None] * a_index[None, :])
    imag[0] = 1
    parts = [part.reshape(quarter // 16, 2, 2, 1, 4, half) for part in (real, imag)]
    parts = np.concatenate(parts, axis=3).transpose(0, 2, 3, 1, 4, 5)
    high, middle, low = three_terms(parts.reshape(half, half))
    terms = [term[:, at : at + quarter] for at in (0, quarter) for term in (middle, high, low)]
    return np.concatenate(terms, axis=1)


def slot_bands(groups, whole_ref, wanted_ref, lane_band_ref, row_band_ref):
    capacity = row_band_ref.shape[0]
    own = lax.axis_index("bins")
    counts = [
        jnp.broadcast_to(whole_ref[:, 8 + owner : 9 + owner], (1, LANES)) for owner in range(groups)
    ]
    lane = iotas((1, LANES))[1]
    rank = lane & (capacity - 1)
    start = jnp.zeros((1, LANES), jnp.int32)
    own_start, own_count = start, start
    wanted = []
    for owner, count in enumerate(counts):
        wanted.append(jnp.where(rank < count, start + rank, -1))
        own_start = jnp.where(own == owner, start, own_start)
        own_count = jnp.where(own == owner, count, own_count)
        start = start + count
    for pair in range(groups // 2):
        wanted_ref[:, pair * LANES : (pair + 1) * LANES] = jnp.where(
            lane < HALF, wanted[2 * pair], wanted[2 * pair + 1]
        )
    edges = [jnp.broadcast_to(whole_ref[:, at : at + 1], (1, LANES)) for at in range(1, NCLASS)]
    for ref, slot in ((lane_band_ref, rank), (row_band_ref, iotas((capacity, LANES))[0])):
        band = jnp.zeros_like(slot)
        for edge in edges:
            band = band + jnp.where(slot + own_start >= edge, 1, 0)
        ref[...] = jnp.where(slot < own_count, band, -1)


def coarse_kernel(
    groups,
    shares,
    x_ref,
    table_ref,
    whole_ref,
    dynamics_ref,
    state_ref,
    out_ref,
    moved_ref,
    wanted_ref,
    lane_band_ref,
    row_band_ref,
):
    slot_bands(groups, whole_ref, wanted_ref, lane_band_ref, row_band_ref)
    half = x_ref.shape[0]
    quarter = half // 2
    row, lane = iotas((8, LANES))
    low_lanes = lane < HALF
    sums = []
    for parity in range(2):
        high, middle, low = split_three(x_ref[pl.ds(parity, quarter, stride=2), :])
        main = jnp.concatenate([high, middle], axis=1)
        rest = [jnp.concatenate([term, jnp.zeros_like(term)], axis=1) for term in (low, high)]
        at = 3 * quarter * parity
        left = jnp.concatenate(
            [table_ref[:, at : at + 2 * quarter], table_ref[:, at + quarter : at + 3 * quarter]], axis=1
        )
        both = dot(left, jnp.concatenate([main, main] + rest, axis=0))
        sums.append(both[:, :LANES] + both[:, LANES:])
    base = 8 * (row >> 2) + 4 * (lane >> 6) + (row & 3)
    base_cosine, base_sine = unit_turn(base, 2 * half)
    packed = low_lanes & (row == 0)
    for sign, block in [(sign, block) for block in range(half // 32) for sign in (1, -1)]:
        pieces = []
        for at in range(32 * block, 32 * (block + 1), 8):
            even, odd = sums[0][at : at + 8], sums[1][at : at + 8]
            pieces.append(even + odd if sign > 0 else even - odd)
        real_low, imag_low, real_high, imag_high = pieces
        if block == 0 and sign < 0:
            imag_low = jnp.where(row == 0, 0.0, imag_low)
        even_real = jnp.where(low_lanes, real_low, pltpu.roll(real_high, HALF, 1))
        even_imag = jnp.where(low_lanes, imag_low, pltpu.roll(imag_high, HALF, 1))
        odd_real = jnp.where(low_lanes, pltpu.roll(real_low, HALF, 1), real_high)
        odd_imag = jnp.where(low_lanes, pltpu.roll(imag_low, HALF, 1), imag_high)
        first = 2 * block + (0 if sign > 0 else shares // 2)
        angle = math.pi * 8 * first / half
        cosine = base_cosine * math.cos(angle) - base_sine * math.sin(angle)
        sine = base_sine * math.cos(angle) + base_cosine * math.sin(angle)
        real = even_real + odd_real * cosine + odd_imag * sine
        if first == 0:
            cosine = jnp.where(packed, -1.0, cosine)
        imag = even_imag + odd_imag * cosine - odd_real * sine
        out_ref[pl.ds(8 * first, 8, stride=2), :] = real
        out_ref[pl.ds(8 * first + 1, 8, stride=2), :] = imag
    moved_ref[...] = state_product(dynamics_ref[...], state_ref[...], row_band_ref[...])


def coarse_step(columns, whole, dynamics, state, groups, shares):
    capacity = state.shape[0]
    half = columns.shape[0]
    return pl.pallas_call(
        functools.partial(coarse_kernel, groups, shares),
        out_shape=(
            jax.ShapeDtypeStruct((half, LANES), F32),
            jax.ShapeDtypeStruct(state.shape, F32),
            jax.ShapeDtypeStruct((1, groups * capacity), jnp.int32),
            jax.ShapeDtypeStruct((1, LANES), jnp.int32),
        ),
        in_specs=[VMEM] * 5,
        out_specs=(VMEM,) * 4,
        scratch_shapes=[pltpu.VMEM((capacity, LANES), jnp.int32)],
        compiler_params=PARAMS,
        name="coarse_dft",
    )(
        columns,
        jnp.asarray(coarse_table(2 * half)),
        whole,
        dynamics.reshape(NCLASS * STATES, STATES),
        state,
    )


def coarse_step_general(columns, shares):
    coarse = columns.shape[0]
    half = coarse // 2
    real, imag = unit_root(coarse, np.arange(half)[:, None] * np.arange(coarse)[None, :])
    imag[0] = 1 - 2 * (np.arange(coarse) % 2)
    table = jnp.asarray(np.concatenate([real, imag]).astype(np.float32))
    spectrum = jnp.dot(table, columns, precision=HIGHEST)
    blocks = jnp.concatenate([spectrum[:half], spectrum[half:]], axis=1)
    return blocks.reshape(shares, half // shares, LANES)


def fine_tables(groups, coarse):
    fine_length = groups * HALF
    doubled = np.arange(LANES) % HALF
    turn = unit_root(fine_length, np.arange(groups)[:, None] * doubled[None, :])
    middle = (np.arange(groups)[:, None] * HALF + doubled[None, :]) * (coarse // 2)
    middle = unit_root(coarse * fine_length, middle)
    turns = np.concatenate(turn + middle).astype(np.float32)
    order = np.arange(HALF)
    order[HALF // 2 :] = order[HALF // 2 :][::-1]
    real, imag = unit_root(HALF, np.arange(HALF)[:, None] * order[None, :])
    sign = np.where(np.arange(HALF) < HALF // 2, 1, -1)
    matrix = np.block([[real, imag * sign], [-imag, real * sign]])
    high, middle, low = three_terms(matrix)
    both = np.concatenate([high, middle], axis=1)
    rest = [np.concatenate([term, np.zeros_like(term)], axis=1) for term in (low, high)]
    return turns, np.concatenate([both, both] + rest, axis=0)


def add(p, q):
    return (p[0] + q[0], p[1] + q[1])


def sub(p, q):
    return (p[0] - q[0], p[1] - q[1])


def times(p, cosine, sine):
    return (p[0] * cosine + p[1] * sine, p[1] * cosine - p[0] * sine)


def eight_point(values):
    half = math.sqrt(0.5)

    def down(p):
        return (p[1], -p[0])

    def four(a, b, c, d):
        s0, s1, s2, s3 = add(a, c), sub(a, c), add(b, d), sub(b, d)
        turned = (s1[0] + s3[1], s1[1] - s3[0]), (s1[0] - s3[1], s1[1] + s3[0])
        return add(s0, s2), turned[0], sub(s0, s2), turned[1]

    even = four(values[0], values[2], values[4], values[6])
    odd = four(values[1], values[3], values[5], values[7])
    turned = [
        odd[0],
        ((odd[1][0] + odd[1][1]) * half, (odd[1][1] - odd[1][0]) * half),
        down(odd[2]),
        ((odd[3][1] - odd[3][0]) * half, (odd[3][0] + odd[3][1]) * -half),
    ]
    return [add(e, t) for e, t in zip(even, turned)] + [sub(e, t) for e, t in zip(even, turned)]


def state_product(dynamics, state, band):
    row, column = iotas((NCLASS * STATES, STATES))
    limit = STATES >> (row >> 6)
    inside = ((row & (STATES - 1)) < limit) & (column < limit)
    dynamics = jnp.where(inside, dynamics, 0.0)
    empty = jnp.zeros_like(dynamics)
    halves = [
        jnp.concatenate([dynamics, empty], axis=1),
        jnp.concatenate([empty, dynamics], axis=1),
    ]
    matrix = jnp.concatenate(
        [half[k * STATES : (k + 1) * STATES] for k in range(NCLASS) for half in halves], axis=0
    )
    state_high, state_low = split_two(state)
    high, low = split_two(matrix)
    moved = lax.dot_general(
        jnp.concatenate([state_high, state_low, state_high], axis=1),
        jnp.concatenate([high, high, low], axis=1),
        (((1,), (1,)), ((), ())),
        preferred_element_type=F32,
    )
    result = jnp.zeros(state.shape, F32)
    for k in range(NCLASS):
        result = jnp.where(band == k, moved[:, k * LANES : (k + 1) * LANES], result)
    return result


def moved_kernel(row_band_ref, dynamics_ref, state_ref, out_ref):
    out_ref[...] = state_product(dynamics_ref[...], state_ref[...], row_band_ref[...])


def moved_step(row_band, dynamics, state):
    return pl.pallas_call(
        moved_kernel,
        out_shape=jax.ShapeDtypeStruct(state.shape, F32),
        in_specs=[VMEM] * 3,
        out_specs=VMEM,
        compiler_params=PARAMS,
        name="moved",
    )(row_band, dynamics.reshape(NCLASS * STATES, STATES), state)


def fine_kernel(
    profiles,
    x_ref,
    turn_ref,
    wanted_ref,
    turns_ref,
    table_ref,
    out_ref,
):
    groups = turn_ref.shape[0] // 4
    first = (lax.axis_index("bins") == 0) & (lax.axis_index("scans") == 0)
    row, lane = iotas((8, LANES))
    low_lanes = lane < HALF
    low_side = (lane & (HALF - 1)) < HALF // 2
    even = (row & 1) == 0
    packed = first & low_lanes & even
    blocks = [[None] * 3 for _ in range(groups)]
    for at in range(3):
        column = []
        for c in range(groups):
            start = c * 8 * profiles
            if at < 2:
                real = x_ref[pl.ds(start + 2 * at, 8, stride=4), :]
                imag = x_ref[pl.ds(start + 2 * at + 1, 8, stride=4), :]
                imag = imag if at else jnp.where(packed, 0.0, imag)
                turn = 4 * c + 2 * at
                column.append(times((real, imag), turn_ref[turn], turn_ref[turn + 1]))
            else:
                middle = jnp.where(packed, x_ref[pl.ds(start + 1, 8, stride=4), :], 0.0)
                middle_real = turns_ref[2 * groups + c : 2 * groups + c + 1, :]
                middle_imag = turns_ref[3 * groups + c : 3 * groups + c + 1, :]
                column.append((middle * middle_real, middle * middle_imag))
        for u, value in enumerate(eight_point(column)):
            cosine, sine = turns_ref[u : u + 1, :], -turns_ref[groups + u : groups + u + 1, :]
            blocks[u][at] = times(value, cosine, sine) if u else value
    rows = []
    for u in range(groups):
        for at in range(3):
            real, imag = blocks[u][at]
            rows.append(jnp.where(low_lanes, real, pltpu.roll(imag, HALF, 1)))
            if at < 2:
                rows.append(jnp.where(low_lanes, pltpu.roll(real, HALF, 1), imag))
    product = []
    for at in range(0, len(rows), len(rows) // 2):
        part = jnp.concatenate(rows[at : at + len(rows) // 2], axis=0)
        high, middle, low = split_three(part)
        both = dot(jnp.concatenate([high, middle, high, low], axis=1), table_ref[...])
        product.append(both[:, :LANES] + both[:, LANES:])
    product = jnp.concatenate(product, axis=0)
    spectrum = []
    for u in range(groups):
        spectrum.append([product[8 * at : 8 * (at + 1)] for at in range(5 * u, 5 * (u + 1))])
        spectrum[u][0] = jnp.where(first & even & ~low_side, 0.0, spectrum[u][0])
        spectrum[u][4] = jnp.where(low_side, spectrum[u][4], 0.0)
    squares = [sum(block * block for block in spectrum[u]) for u in range(groups)]
    rest_place = ~low_side & even
    pieces = []
    for u in range(groups):
        mirror = groups - 1 - u
        power = jnp.where(low_side, squares[u], squares[mirror])
        for shift in (4, 2, 1):
            power = power + pltpu.roll(power, shift, 0)
        evens, *others = (
            jnp.where(low_side, spectrum[u][at], spectrum[mirror][at]) for at in range(4)
        )
        sums = jnp.where(rest_place, 0.0, evens) + sum(others)
        sums = sums + pltpu.roll(sums, 7, 0)
        lows = jnp.where(low_side, sums, 0.0)
        highs = jnp.where(low_side, 0.0, pltpu.roll(sums, 1, 0))
        rest = jnp.where(rest_place, evens, spectrum[u][4])
        pieces.append((jnp.where(even, lows, highs), jnp.where(even, rest, power)))
    left = [[], [], [], []]
    for u in range(0, groups, 2):
        for at in range(2):
            one, two = pieces[u][at], pieces[u + 1][at]
            real = jnp.where(low_lanes, one, pltpu.roll(two, HALF, 1))
            imag = jnp.where(low_lanes, pltpu.roll(one, HALF, 1), two)
            if at == 1:
                power = real + imag
                real, imag = jnp.where(even, real, power), jnp.where(even, imag, power)
            left[at].append(real)
            left[2 + at].append(imag)
    left = jnp.concatenate([jnp.concatenate(parts, axis=1) for parts in left], axis=0)
    left = jnp.concatenate(split_two(left), axis=0)
    wanted = wanted_ref[...]
    chosen = []
    for u in range(groups):
        tile = u + groups * iotas((HALF // 2, wanted.shape[1]))[0]
        chosen += [jnp.where(tile == wanted, 1.0, 0.0).astype(BF16)] * 2
    routed = dot(left, jnp.concatenate(chosen, axis=0))
    routed = routed[:32] + routed[32:]
    for pair in range(groups // 2):
        for at in range(2):
            real = routed[8 * at : 8 * (at + 1), pair * LANES : (pair + 1) * LANES]
            imag = routed[16 + 8 * at : 16 + 8 * (at + 1), pair * LANES : (pair + 1) * LANES]
            start = 2 * pair * profiles * KINDS + at
            out_ref[pl.ds(start, 8, stride=2), :] = jnp.where(
                low_lanes, real, pltpu.roll(imag, HALF, 1)
            )
            out_ref[pl.ds(start + profiles * KINDS, 8, stride=2), :] = jnp.where(
                low_lanes, pltpu.roll(real, HALF, 1), imag
            )


def fine_step(arrived, turn, wanted, profiles, coarse):
    groups = turn.shape[0] // 4
    turns, table = fine_tables(groups, coarse)
    out = pl.pallas_call(
        functools.partial(fine_kernel, profiles),
        out_shape=jax.ShapeDtypeStruct((groups * profiles * KINDS, LANES), F32),
        in_specs=[VMEM] * 5,
        out_specs=VMEM,
        compiler_params=PARAMS,
        name="fine_dft",
    )(
        arrived,
        turn,
        wanted,
        jnp.asarray(turns),
        jnp.asarray(table),
    )
    return out.reshape(groups * profiles, KINDS, LANES)


def fine_step_general(arrived, owner_counts, capacity):
    groups, rows = arrived.shape[:2]
    coarse = 2 * rows * groups
    fine_length = groups * HALF
    order = coarse * fine_length
    own = lax.axis_index("bins")
    real, imag = arrived[:, :, :HALF], arrived[:, :, HALF:]
    points = jnp.arange(fine_length, dtype=jnp.int32).reshape(groups, 1, HALF)
    k_index = own * rows + jnp.arange(rows, dtype=jnp.int32)[None, :, None]
    cosine, sine = unit_turn(points * k_index & (order - 1), order)
    packed = (own == 0) & (jnp.arange(rows)[None, :, None] == 0)
    middle = jnp.where(own == 0, imag[:, :1], 0.0)
    imag = jnp.where(packed, 0.0, imag)
    real, imag = real * cosine + imag * sine, imag * cosine - real * sine
    cosine, sine = unit_turn(points * (coarse // 2), order)
    real = jnp.concatenate([real, middle * cosine], axis=1)
    imag = jnp.concatenate([imag, -middle * sine], axis=1)

    def turned(pattern, root, parts):
        cosine, sine = (jnp.asarray(part.astype(np.float32)) for part in root)
        mul = functools.partial(jnp.einsum, pattern, precision=HIGHEST)
        return (
            mul(cosine, parts[0]) - mul(sine, parts[1]),
            mul(cosine, parts[1]) + mul(sine, parts[0]),
        )

    group_index, point_index = np.arange(groups), np.arange(HALF)
    parts = turned(
        "cu,crj->urj", unit_root(groups, group_index[:, None] * group_index), (real, imag)
    )
    parts = turned(
        "uj,urj->urj", unit_root(fine_length, group_index[:, None] * point_index), parts
    )
    parts = turned(
        "jv,urj->vur", unit_root(HALF, point_index[:, None] * point_index), parts
    )
    tiles = fine_length // 2
    kept = jnp.concatenate([~packed[0, :, 0], jnp.zeros((1,), bool)])
    sides = []
    for part, sign in zip(parts, (1.0, -1.0)):
        part = part.reshape(fine_length, rows + 1)
        sides.append((part[:tiles], sign * jnp.where(kept, part[tiles:][::-1], 0.0)))
    power = sum(jnp.sum(part * part, axis=1) for pair in sides for part in pair)
    starts = jnp.cumsum(owner_counts) - owner_counts
    slot_index = jnp.arange(capacity, dtype=jnp.int32)
    filled = slot_index[None, :] < owner_counts[:, None]
    chosen = jnp.clip(starts[:, None] + slot_index[None, :], 0, tiles - 1)

    def kinds(low, high):
        low_sums, high_sums = jnp.sum(low[:, :rows], axis=1), jnp.sum(high[:, 1:rows], axis=1)
        values = jnp.stack([low_sums, high[:, 0] + low[:, rows], high_sums, power], axis=1)
        return jnp.where(filled[:, :, None], values[chosen], 0.0).transpose(0, 2, 1)

    return jnp.concatenate([kinds(*sides[0]), kinds(*sides[1])], axis=2)


def pool_table(shares, coarse):
    pool = np.zeros((21, 16, shares, KINDS), np.float32)
    sums = pool[1:].reshape(NCLASS, STATES, shares, KINDS)
    wide = TILE // STATES
    rows = coarse // 2 // shares
    for share in range(shares):
        first = rows * share
        rest = coarse - first if share else coarse // 2
        for kind, at in enumerate((first, rest, coarse - first - 1)):
            for band in range(NCLASS):
                sums[band, at // wide >> band, share, kind] = 1.0
    pool[0, :, :, 3] = 1.0
    return pool.reshape(-1, shares * KINDS).astype(BF16)


def update_kernel(
    count, x_ref, pool_ref, lane_band_ref, moved_ref, out_ref
):
    band = lane_band_ref[...]
    right = jnp.concatenate(split_two(x_ref[...]), axis=1)
    sums = jnp.concatenate([dot(pool_ref[:176], right), dot(pool_ref[176:], right)], axis=0)
    sums = sums[:, :LANES] + sums[:, LANES:]
    power = sums[:1] * (1.0 / count)
    sums = sums[16:]
    span = jnp.left_shift(TILE // STATES, jnp.maximum(band, 0)).astype(F32)
    scaling = lax.rsqrt(span * (power + EPSILON))
    scaling = jnp.where(band < 0, 0.0, scaling)
    chosen = sums[:STATES]
    for k in range(1, NCLASS):
        chosen = jnp.where(band == k, sums[k * STATES : (k + 1) * STATES], chosen)
    chosen = chosen * scaling
    turned = jnp.transpose(jnp.concatenate([chosen, chosen], axis=0))
    half = turned.shape[0] // 2
    measured = jnp.where(iotas((half, LANES))[1] < STATES, turned[:half], turned[half:])
    out_ref[...] = measured + moved_ref[...]


def update_step(arrived, lane_band, moved, coarse, count):
    shares = arrived.shape[0]
    return pl.pallas_call(
        functools.partial(update_kernel, count),
        out_shape=jax.ShapeDtypeStruct(moved.shape, F32),
        in_specs=[VMEM] * 4,
        out_specs=VMEM,
        compiler_params=PARAMS,
        name="state_update",
    )(
        arrived.reshape(shares * KINDS, LANES),
        jnp.asarray(pool_table(shares, coarse)),
        lane_band,
        moved,
    )


def bands_general(band_edges, owner_counts, capacity):
    own = lax.axis_index("bins")
    slot = jnp.arange(capacity, dtype=jnp.int32)
    start = jnp.cumsum(owner_counts)[own] - owner_counts[own]
    band = jnp.sum((slot + start)[:, None] >= band_edges[None, 1:NCLASS], axis=1)
    band = jnp.where(slot < owner_counts[own], band, -1).astype(jnp.int32)
    return jnp.tile(band, 2)[None, :], jnp.broadcast_to(band[:, None], (capacity, LANES))


def exchanged(values, axes):
    return lax.all_to_all(values, axes, split_axis=0, concat_axis=0, tiled=True)


def body(profiles, band_edges, owner_counts, dynamics, prev_state):
    groups, scans = lax.axis_size("bins"), lax.axis_size("scans")
    prof_rows, length = profiles.shape
    capacity = prev_state.shape[0]
    coarse = length // HALF
    shares = groups * scans
    count = prof_rows * scans * TILE
    state = prev_state.reshape(capacity, 2 * STATES)
    if groups == 8 and scans == 4 and coarse == 16 * shares and capacity == HALF:
        turn = turns_step(groups, groups * length)
        columns, whole = columns_step(profiles.reshape(length), turn, band_edges, owner_counts)
        columns = exchanged(columns, "bins").reshape(coarse // 2, LANES)
        blocks, moved, wanted, lane_band = coarse_step(
            columns, whole, dynamics, state, groups, shares
        )
        blocks = exchanged(blocks.reshape(shares, 8, LANES), ("bins", "scans"))
        blocks = blocks.reshape(8 * shares, LANES)
        payload = fine_step(blocks, turn, wanted, scans, coarse)
        arrived = exchanged(payload, ("bins", "scans"))
    else:
        lane_band, row_band = bands_general(band_edges, owner_counts, capacity)
        moved = moved_step(row_band, dynamics, state)
        columns = profiles.reshape(coarse // groups, groups, HALF).transpose(1, 0, 2)
        columns = exchanged(columns, "bins").reshape(coarse, HALF)
        blocks = exchanged(coarse_step_general(columns, groups), "bins")
        arrived = exchanged(fine_step_general(blocks, owner_counts, capacity), "bins")
        power = lax.psum(arrived[:, 3:], "scans")
        arrived = jnp.concatenate([arrived[:, :3], power], axis=1)
    updated = update_step(arrived, lane_band, moved, coarse, count)
    return updated.reshape(prev_state.shape)


def solution(mesh):
    return jax.shard_map(
        body,
        mesh=mesh,
        in_specs=(P("scans", "bins"), P(), P(), P(), P("bins", "scans", None)),
        out_specs=P("bins", "scans", None),
        check_vma=False,
    )
```

```python
import functools
import math

import jax
import jax.numpy as jnp
import numpy as np
from jax import lax
from jax.experimental import pallas as pl
from jax.experimental.pallas import tpu as pltpu
from jax.sharding import PartitionSpec as P

TILE = 512
STATES = 64
NCLASS = 5
LANES = 128

EPSILON = 1e-05
HIGHEST = lax.Precision.HIGHEST
BF16 = jnp.bfloat16
F32 = jnp.float32


def unit_root(order, exponents):
    angles = 2.0 * np.pi * (np.asarray(exponents, dtype=np.int64) % order) / order
    return np.cos(angles), -np.sin(angles)


def two_terms(values):
    high = np.asarray(values, np.float32).astype(BF16)
    low = (np.asarray(values, np.float64) - high.astype(np.float64)).astype(BF16)
    return high, low


def three_terms(values):
    high, middle = two_terms(values)
    rest = np.asarray(values, np.float64) - high.astype(np.float64) - middle.astype(np.float64)
    return high, middle, rest.astype(BF16)


def split_two(values):
    high = values.astype(BF16)
    return high, (values - high.astype(F32)).astype(BF16)


def split_three(values):
    high = values.astype(BF16)
    rest = values - high.astype(F32)
    middle = rest.astype(BF16)
    return high, middle, (rest - middle.astype(F32)).astype(BF16)


def dot(left, right):
    return jnp.dot(left, right, preferred_element_type=F32)


VMEM = pl.BlockSpec(memory_space=pltpu.VMEM)
PARAMS = pltpu.CompilerParams(vmem_limit_bytes=32 << 20)
COST = pl.CostEstimate(flops=1 << 30, bytes_accessed=1 << 24, transcendentals=0)


KINDS = 4
HALF = LANES // 2


def unit_turn(phase, order):
    shifted = phase + order // 8
    quadrant = (shifted >> (order.bit_length() - 3)) & 3
    x = ((shifted & (order // 4 - 1)) - order // 8).astype(F32) * (2.0 * math.pi / order)
    y = x * x
    cosine = 1.0 + y * (-1 / 2 + y * (1 / 24 + y * (-1 / 720 + y * (1 / 40320))))
    sine = x * (1.0 + y * (-1 / 6 + y * (1 / 120 + y * (-1 / 5040 + y * (1 / 362880)))))
    odd = (quadrant & 1) == 1
    real, imag = jnp.where(odd, sine, cosine), jnp.where(odd, cosine, sine)
    real = jnp.where((quadrant == 1) | (quadrant == 2), -real, real)
    return real, jnp.where(quadrant >= 2, -imag, imag)


def iotas(shape):
    return [lax.broadcasted_iota(jnp.int32, shape, axis) for axis in range(len(shape))]


def halves(one, two):
    low_lanes = iotas(one.shape)[1] < HALF
    crossed = pltpu.roll(jnp.where(low_lanes, two, one), HALF, 1)
    return jnp.where(low_lanes, one, crossed), jnp.where(low_lanes, crossed, two)


def turns_kernel(order, turn_ref):
    row, lane = iotas((8, LANES))
    own = lax.axis_index("bins") * lax.axis_size("scans") + lax.axis_index("scans")
    for at in range(turn_ref.shape[0] // 2):
        c, odd = divmod(at, 2)
        k_index = 8 * own + 4 * (lane >> 6) + 2 * (row & 1) + odd
        phase = ((c * HALF + (lane & (HALF - 1))) * k_index) & (order - 1)
        turn_ref[2 * at], turn_ref[2 * at + 1] = unit_turn(phase, order)


def turns_step(groups, order):
    return pl.pallas_call(
        functools.partial(turns_kernel, order),
        out_shape=jax.ShapeDtypeStruct((4 * groups, 8, LANES), F32),
        out_specs=VMEM,
        compiler_params=PARAMS,
        cost_estimate=COST,
        name="turns",
    )()


def columns_kernel(x_ref, turn_ref, edges_ref, counts_ref, out_ref, whole_ref):
    del turn_ref
    groups, rows, _ = out_ref.shape
    for pair in range(groups // 2):
        even = x_ref[pl.ds(pair, rows, stride=groups), :]
        odd = x_ref[pl.ds(groups // 2 + pair, rows, stride=groups), :]
        out_ref[2 * pair], out_ref[2 * pair + 1] = halves(even, odd)
    whole_ref[:, : NCLASS + 1] = edges_ref[...]
    whole_ref[:, 8 : 8 + groups] = counts_ref[...]


def columns_step(profile, turn, band_edges, owner_counts):
    groups = owner_counts.shape[0]
    rows = profile.shape[0] // (groups * LANES)
    return pl.pallas_call(
        columns_kernel,
        out_shape=(
            jax.ShapeDtypeStruct((groups, rows, LANES), F32),
            jax.ShapeDtypeStruct((1, LANES), jnp.int32),
        ),
        in_specs=[VMEM] * 4,
        out_specs=(VMEM,) * 2,
        compiler_params=PARAMS,
        name="columns",
    )(profile.reshape(-1, LANES), turn, band_edges.reshape(1, -1), owner_counts.reshape(1, -1))


def coarse_table(coarse):
    half, quarter = coarse // 2, coarse // 4
    k_index = np.arange(quarter)
    a_index = np.concatenate([np.arange(0, half, 2), np.arange(1, half, 2)])
    real, imag = unit_root(half, k_index[:, None] * a_index[None, :])
    imag[0] = 1
    parts = [part.reshape(quarter // 16, 2, 2, 1, 4, half) for part in (real, imag)]
    parts = np.concatenate(parts, axis=3).transpose(0, 2, 3, 1, 4, 5)
    high, middle, low = three_terms(parts.reshape(half, half))
    terms = [term[:, at : at + quarter] for at in (0, quarter) for term in (middle, high, low)]
    return np.concatenate(terms, axis=1)


def slot_bands(groups, whole_ref, wanted_ref, lane_band_ref, row_band_ref):
    capacity = row_band_ref.shape[0]
    own = lax.axis_index("bins")
    counts = [
        jnp.broadcast_to(whole_ref[:, 8 + owner : 9 + owner], (1, LANES)) for owner in range(groups)
    ]
    lane = iotas((1, LANES))[1]
    rank = lane & (capacity - 1)
    start = jnp.zeros((1, LANES), jnp.int32)
    own_start, own_count = start, start
    wanted = []
    for owner, count in enumerate(counts):
        wanted.append(jnp.where(rank < count, start + rank, -1))
        own_start = jnp.where(own == owner, start, own_start)
        own_count = jnp.where(own == owner, count, own_count)
        start = start + count
    for pair in range(groups // 2):
        wanted_ref[:, pair * LANES : (pair + 1) * LANES] = jnp.where(
            lane < HALF, wanted[2 * pair], wanted[2 * pair + 1]
        )
    edges = [jnp.broadcast_to(whole_ref[:, at : at + 1], (1, LANES)) for at in range(1, NCLASS)]
    for ref, slot in ((lane_band_ref, rank), (row_band_ref, iotas((capacity, LANES))[0])):
        band = jnp.zeros_like(slot)
        for edge in edges:
            band = band + jnp.where(slot + own_start >= edge, 1, 0)
        ref[...] = jnp.where(slot < own_count, band, -1)


def coarse_kernel(
    groups,
    shares,
    x_ref,
    table_ref,
    whole_ref,
    dynamics_ref,
    state_ref,
    out_ref,
    moved_ref,
    wanted_ref,
    lane_band_ref,
    row_band_ref,
):
    slot_bands(groups, whole_ref, wanted_ref, lane_band_ref, row_band_ref)
    half = x_ref.shape[0]
    quarter = half // 2
    row, lane = iotas((8, LANES))
    low_lanes = lane < HALF
    sums = []
    for parity in range(2):
        high, middle, low = split_three(x_ref[pl.ds(parity, quarter, stride=2), :])
        main = jnp.concatenate([high, middle], axis=1)
        rest = [jnp.concatenate([term, jnp.zeros_like(term)], axis=1) for term in (low, high)]
        at = 3 * quarter * parity
        left = jnp.concatenate(
            [table_ref[:, at : at + 2 * quarter], table_ref[:, at + quarter : at + 3 * quarter]], axis=1
        )
        both = dot(left, jnp.concatenate([main, main] + rest, axis=0))
        sums.append(both[:, :LANES] + both[:, LANES:])
    base = 8 * (row >> 2) + 4 * (lane >> 6) + (row & 3)
    base_cosine, base_sine = unit_turn(base, 2 * half)
    packed = low_lanes & (row == 0)
    for sign, block in [(sign, block) for block in range(half // 32) for sign in (1, -1)]:
        pieces = []
        for at in range(32 * block, 32 * (block + 1), 8):
            even, odd = sums[0][at : at + 8], sums[1][at : at + 8]
            pieces.append(even + odd if sign > 0 else even - odd)
        real_low, imag_low, real_high, imag_high = pieces
        if block == 0 and sign < 0:
            imag_low = jnp.where(row == 0, 0.0, imag_low)
        even_real, odd_real = halves(real_low, real_high)
        even_imag, odd_imag = halves(imag_low, imag_high)
        first = 2 * block + (0 if sign > 0 else shares // 2)
        angle = math.pi * 8 * first / half
        cosine = base_cosine * math.cos(angle) - base_sine * math.sin(angle)
        sine = base_sine * math.cos(angle) + base_cosine * math.sin(angle)
        real = even_real + odd_real * cosine + odd_imag * sine
        if first == 0:
            cosine = jnp.where(packed, -1.0, cosine)
        imag = even_imag + odd_imag * cosine - odd_real * sine
        out_ref[pl.ds(8 * first, 8, stride=2), :] = real
        out_ref[pl.ds(8 * first + 1, 8, stride=2), :] = imag
    moved_ref[...] = state_product(dynamics_ref[...], state_ref[...], row_band_ref[...])


def coarse_step(columns, whole, dynamics, state, groups, shares):
    capacity = state.shape[0]
    half = columns.shape[0]
    return pl.pallas_call(
        functools.partial(coarse_kernel, groups, shares),
        out_shape=(
            jax.ShapeDtypeStruct((half, LANES), F32),
            jax.ShapeDtypeStruct(state.shape, F32),
            jax.ShapeDtypeStruct((1, groups * capacity), jnp.int32),
            jax.ShapeDtypeStruct((1, LANES), jnp.int32),
        ),
        in_specs=[VMEM] * 5,
        out_specs=(VMEM,) * 4,
        scratch_shapes=[pltpu.VMEM((capacity, LANES), jnp.int32)],
        compiler_params=PARAMS,
        name="coarse_dft",
    )(
        columns,
        jnp.asarray(coarse_table(2 * half)),
        whole,
        dynamics.reshape(NCLASS * STATES, STATES),
        state,
    )


def coarse_step_general(columns, shares):
    coarse = columns.shape[0]
    half = coarse // 2
    real, imag = unit_root(coarse, np.arange(half)[:, None] * np.arange(coarse)[None, :])
    imag[0] = 1 - 2 * (np.arange(coarse) % 2)
    table = jnp.asarray(np.concatenate([real, imag]).astype(np.float32))
    spectrum = jnp.dot(table, columns, precision=HIGHEST)
    blocks = jnp.concatenate([spectrum[:half], spectrum[half:]], axis=1)
    return blocks.reshape(shares, half // shares, LANES)


def fine_tables(groups, coarse):
    fine_length = groups * HALF
    doubled = np.arange(LANES) % HALF
    turn = unit_root(fine_length, np.arange(groups)[:, None] * doubled[None, :])
    middle = (np.arange(groups)[:, None] * HALF + doubled[None, :]) * (coarse // 2)
    middle = unit_root(coarse * fine_length, middle)
    turns = np.concatenate(turn + middle).astype(np.float32)
    order = np.arange(HALF)
    order[HALF // 2 :] = order[HALF // 2 :][::-1]
    real, imag = unit_root(HALF, np.arange(HALF)[:, None] * order[None, :])
    sign = np.where(np.arange(HALF) < HALF // 2, 1, -1)
    matrix = np.block([[real, imag * sign], [-imag, real * sign]])
    high, middle, low = three_terms(matrix)
    both = np.concatenate([high, middle], axis=1)
    rest = [np.concatenate([term, np.zeros_like(term)], axis=1) for term in (low, high)]
    return turns, np.concatenate([both, both] + rest, axis=0)


def add(p, q):
    return (p[0] + q[0], p[1] + q[1])


def sub(p, q):
    return (p[0] - q[0], p[1] - q[1])


def times(p, cosine, sine):
    return (p[0] * cosine + p[1] * sine, p[1] * cosine - p[0] * sine)


def eight_point(values):
    half = math.sqrt(0.5)

    def down(p):
        return (p[1], -p[0])

    def four(a, b, c, d):
        s0, s1, s2, s3 = add(a, c), sub(a, c), add(b, d), sub(b, d)
        turned = (s1[0] + s3[1], s1[1] - s3[0]), (s1[0] - s3[1], s1[1] + s3[0])
        return add(s0, s2), turned[0], sub(s0, s2), turned[1]

    even = four(values[0], values[2], values[4], values[6])
    odd = four(values[1], values[3], values[5], values[7])
    turned = [
        odd[0],
        ((odd[1][0] + odd[1][1]) * half, (odd[1][1] - odd[1][0]) * half),
        down(odd[2]),
        ((odd[3][1] - odd[3][0]) * half, (odd[3][0] + odd[3][1]) * -half),
    ]
    return [add(e, t) for e, t in zip(even, turned)] + [sub(e, t) for e, t in zip(even, turned)]


def state_product(dynamics, state, band):
    row, column = iotas((NCLASS * STATES, STATES))
    limit = STATES >> (row >> 6)
    inside = ((row & (STATES - 1)) < limit) & (column < limit)
    dynamics = jnp.where(inside, dynamics, 0.0)
    empty = jnp.zeros_like(dynamics)
    halves = [
        jnp.concatenate([dynamics, empty], axis=1),
        jnp.concatenate([empty, dynamics], axis=1),
    ]
    matrix = jnp.concatenate(
        [half[k * STATES : (k + 1) * STATES] for k in range(NCLASS) for half in halves], axis=0
    )
    state_high, state_low = split_two(state)
    high, low = split_two(matrix)
    moved = lax.dot_general(
        jnp.concatenate([state_high, state_low, state_high], axis=1),
        jnp.concatenate([high, high, low], axis=1),
        (((1,), (1,)), ((), ())),
        preferred_element_type=F32,
    )
    result = jnp.zeros(state.shape, F32)
    for k in range(NCLASS):
        result = jnp.where(band == k, moved[:, k * LANES : (k + 1) * LANES], result)
    return result


def moved_kernel(row_band_ref, dynamics_ref, state_ref, out_ref):
    out_ref[...] = state_product(dynamics_ref[...], state_ref[...], row_band_ref[...])


def moved_step(row_band, dynamics, state):
    return pl.pallas_call(
        moved_kernel,
        out_shape=jax.ShapeDtypeStruct(state.shape, F32),
        in_specs=[VMEM] * 3,
        out_specs=VMEM,
        compiler_params=PARAMS,
        name="moved",
    )(row_band, dynamics.reshape(NCLASS * STATES, STATES), state)


def fine_kernel(
    profiles,
    x_ref,
    turn_ref,
    wanted_ref,
    turns_ref,
    table_ref,
    out_ref,
):
    groups = turn_ref.shape[0] // 4
    first = (lax.axis_index("bins") == 0) & (lax.axis_index("scans") == 0)
    row, lane = iotas((8, LANES))
    low_lanes = lane < HALF
    low_side = (lane & (HALF - 1)) < HALF // 2
    even = (row & 1) == 0
    packed = first & low_lanes & even
    blocks = [[None] * 3 for _ in range(groups)]
    for at in range(3):
        column = []
        for c in range(groups):
            start = c * 8 * profiles
            if at < 2:
                real = x_ref[pl.ds(start + 2 * at, 8, stride=4), :]
                imag = x_ref[pl.ds(start + 2 * at + 1, 8, stride=4), :]
                imag = imag if at else jnp.where(packed, 0.0, imag)
                turn = 4 * c + 2 * at
                column.append(times((real, imag), turn_ref[turn], turn_ref[turn + 1]))
            else:
                middle = jnp.where(packed, x_ref[pl.ds(start + 1, 8, stride=4), :], 0.0)
                middle_real = turns_ref[2 * groups + c : 2 * groups + c + 1, :]
                middle_imag = turns_ref[3 * groups + c : 3 * groups + c + 1, :]
                column.append((middle * middle_real, middle * middle_imag))
        for u, value in enumerate(eight_point(column)):
            cosine, sine = turns_ref[u : u + 1, :], -turns_ref[groups + u : groups + u + 1, :]
            blocks[u][at] = times(value, cosine, sine) if u else value
    rows = []
    for u in range(groups):
        for at in range(3):
            rows += halves(*blocks[u][at])[: 2 if at < 2 else 1]
    product = []
    for at in range(0, len(rows), len(rows) // 2):
        part = jnp.concatenate(rows[at : at + len(rows) // 2], axis=0)
        high, middle, low = split_three(part)
        both = dot(jnp.concatenate([high, middle, high, low], axis=1), table_ref[...])
        product.append(both[:, :LANES] + both[:, LANES:])
    product = jnp.concatenate(product, axis=0)
    spectrum = []
    for u in range(groups):
        spectrum.append([product[8 * at : 8 * (at + 1)] for at in range(5 * u, 5 * (u + 1))])
        spectrum[u][0] = jnp.where(first & even & ~low_side, 0.0, spectrum[u][0])
        spectrum[u][4] = jnp.where(low_side, spectrum[u][4], 0.0)
    squares = [sum(block * block for block in spectrum[u]) for u in range(groups)]
    rest_place = ~low_side & even
    pieces = []
    for u in range(groups):
        mirror = groups - 1 - u
        power = jnp.where(low_side, squares[u], squares[mirror])
        for shift in (4, 2, 1):
            power = power + pltpu.roll(power, shift, 0)
        evens, *others = (
            jnp.where(low_side, spectrum[u][at], spectrum[mirror][at]) for at in range(4)
        )
        sums = jnp.where(rest_place, 0.0, evens) + sum(others)
        sums = sums + pltpu.roll(sums, 7, 0)
        lows = jnp.where(low_side, sums, 0.0)
        highs = jnp.where(low_side, 0.0, pltpu.roll(sums, 1, 0))
        rest = jnp.where(rest_place, evens, spectrum[u][4])
        pieces.append((jnp.where(even, lows, highs), jnp.where(even, rest, power)))
    left = [[], [], [], []]
    for u in range(0, groups, 2):
        for at in range(2):
            one, two = pieces[u][at], pieces[u + 1][at]
            real, imag = halves(one, two)
            if at == 1:
                power = real + imag
                real, imag = jnp.where(even, real, power), jnp.where(even, imag, power)
            left[at].append(real)
            left[2 + at].append(imag)
    left = jnp.concatenate([jnp.concatenate(parts, axis=1) for parts in left], axis=0)
    left = jnp.concatenate(split_two(left), axis=0)
    wanted = wanted_ref[...]
    chosen = []
    for u in range(groups):
        tile = u + groups * iotas((HALF // 2, wanted.shape[1]))[0]
        chosen += [jnp.where(tile == wanted, 1.0, 0.0).astype(BF16)] * 2
    routed = dot(left, jnp.concatenate(chosen, axis=0))
    routed = routed[:32] + routed[32:]
    for pair in range(groups // 2):
        for at in range(2):
            real = routed[8 * at : 8 * (at + 1), pair * LANES : (pair + 1) * LANES]
            imag = routed[16 + 8 * at : 16 + 8 * (at + 1), pair * LANES : (pair + 1) * LANES]
            start = 2 * pair * profiles * KINDS + at
            one, two = halves(real, imag)
            out_ref[pl.ds(start, 8, stride=2), :] = one
            out_ref[pl.ds(start + profiles * KINDS, 8, stride=2), :] = two


def fine_step(arrived, turn, wanted, profiles, coarse):
    groups = turn.shape[0] // 4
    turns, table = fine_tables(groups, coarse)
    out = pl.pallas_call(
        functools.partial(fine_kernel, profiles),
        out_shape=jax.ShapeDtypeStruct((groups * profiles * KINDS, LANES), F32),
        in_specs=[VMEM] * 5,
        out_specs=VMEM,
        compiler_params=PARAMS,
        name="fine_dft",
    )(
        arrived,
        turn,
        wanted,
        jnp.asarray(turns),
        jnp.asarray(table),
    )
    return out.reshape(groups * profiles, KINDS, LANES)


def fine_step_general(arrived, owner_counts, capacity):
    groups, rows = arrived.shape[:2]
    coarse = 2 * rows * groups
    fine_length = groups * HALF
    order = coarse * fine_length
    own = lax.axis_index("bins")
    real, imag = arrived[:, :, :HALF], arrived[:, :, HALF:]
    points = jnp.arange(fine_length, dtype=jnp.int32).reshape(groups, 1, HALF)
    k_index = own * rows + jnp.arange(rows, dtype=jnp.int32)[None, :, None]
    cosine, sine = unit_turn(points * k_index & (order - 1), order)
    packed = (own == 0) & (jnp.arange(rows)[None, :, None] == 0)
    middle = jnp.where(own == 0, imag[:, :1], 0.0)
    imag = jnp.where(packed, 0.0, imag)
    real, imag = real * cosine + imag * sine, imag * cosine - real * sine
    cosine, sine = unit_turn(points * (coarse // 2), order)
    real = jnp.concatenate([real, middle * cosine], axis=1)
    imag = jnp.concatenate([imag, -middle * sine], axis=1)

    def turned(pattern, root, parts):
        cosine, sine = (jnp.asarray(part.astype(np.float32)) for part in root)
        mul = functools.partial(jnp.einsum, pattern, precision=HIGHEST)
        return (
            mul(cosine, parts[0]) - mul(sine, parts[1]),
            mul(cosine, parts[1]) + mul(sine, parts[0]),
        )

    group_index, point_index = np.arange(groups), np.arange(HALF)
    parts = turned(
        "cu,crj->urj", unit_root(groups, group_index[:, None] * group_index), (real, imag)
    )
    parts = turned(
        "uj,urj->urj", unit_root(fine_length, group_index[:, None] * point_index), parts
    )
    parts = turned(
        "jv,urj->vur", unit_root(HALF, point_index[:, None] * point_index), parts
    )
    tiles = fine_length // 2
    kept = jnp.concatenate([~packed[0, :, 0], jnp.zeros((1,), bool)])
    sides = []
    for part, sign in zip(parts, (1.0, -1.0)):
        part = part.reshape(fine_length, rows + 1)
        sides.append((part[:tiles], sign * jnp.where(kept, part[tiles:][::-1], 0.0)))
    power = sum(jnp.sum(part * part, axis=1) for pair in sides for part in pair)
    starts = jnp.cumsum(owner_counts) - owner_counts
    slot_index = jnp.arange(capacity, dtype=jnp.int32)
    filled = slot_index[None, :] < owner_counts[:, None]
    chosen = jnp.clip(starts[:, None] + slot_index[None, :], 0, tiles - 1)

    def kinds(low, high):
        low_sums, high_sums = jnp.sum(low[:, :rows], axis=1), jnp.sum(high[:, 1:rows], axis=1)
        values = jnp.stack([low_sums, high[:, 0] + low[:, rows], high_sums, power], axis=1)
        return jnp.where(filled[:, :, None], values[chosen], 0.0).transpose(0, 2, 1)

    return jnp.concatenate([kinds(*sides[0]), kinds(*sides[1])], axis=2)


def pool_table(shares, coarse):
    pool = np.zeros((21, 16, shares, KINDS), np.float32)
    sums = pool[1:].reshape(NCLASS, STATES, shares, KINDS)
    wide = TILE // STATES
    rows = coarse // 2 // shares
    for share in range(shares):
        first = rows * share
        rest = coarse - first if share else coarse // 2
        for kind, at in enumerate((first, rest, coarse - first - 1)):
            for band in range(NCLASS):
                sums[band, at // wide >> band, share, kind] = 1.0
    pool[0, :, :, 3] = 1.0
    return pool.reshape(-1, shares * KINDS).astype(BF16)


def update_kernel(
    count, x_ref, pool_ref, lane_band_ref, moved_ref, out_ref
):
    band = lane_band_ref[...]
    right = jnp.concatenate(split_two(x_ref[...]), axis=1)
    sums = jnp.concatenate([dot(pool_ref[:176], right), dot(pool_ref[176:], right)], axis=0)
    sums = sums[:, :LANES] + sums[:, LANES:]
    power = sums[:1] * (1.0 / count)
    sums = sums[16:]
    span = jnp.left_shift(TILE // STATES, jnp.maximum(band, 0)).astype(F32)
    scaling = lax.rsqrt(span * (power + EPSILON))
    scaling = jnp.where(band < 0, 0.0, scaling)
    chosen = sums[:STATES]
    for k in range(1, NCLASS):
        chosen = jnp.where(band == k, sums[k * STATES : (k + 1) * STATES], chosen)
    chosen = chosen * scaling
    turned = jnp.transpose(jnp.concatenate([chosen, chosen], axis=0))
    half = turned.shape[0] // 2
    measured = jnp.where(iotas((half, LANES))[1] < STATES, turned[:half], turned[half:])
    out_ref[...] = measured + moved_ref[...]


def update_step(arrived, lane_band, moved, coarse, count):
    shares = arrived.shape[0]
    return pl.pallas_call(
        functools.partial(update_kernel, count),
        out_shape=jax.ShapeDtypeStruct(moved.shape, F32),
        in_specs=[VMEM] * 4,
        out_specs=VMEM,
        compiler_params=PARAMS,
        name="state_update",
    )(
        arrived.reshape(shares * KINDS, LANES),
        jnp.asarray(pool_table(shares, coarse)),
        lane_band,
        moved,
    )


def bands_general(band_edges, owner_counts, capacity):
    own = lax.axis_index("bins")
    slot = jnp.arange(capacity, dtype=jnp.int32)
    start = jnp.cumsum(owner_counts)[own] - owner_counts[own]
    band = jnp.sum((slot + start)[:, None] >= band_edges[None, 1:NCLASS], axis=1)
    band = jnp.where(slot < owner_counts[own], band, -1).astype(jnp.int32)
    return jnp.tile(band, 2)[None, :], jnp.broadcast_to(band[:, None], (capacity, LANES))


def exchanged(values, axes):
    return lax.all_to_all(values, axes, split_axis=0, concat_axis=0, tiled=True)


def body(profiles, band_edges, owner_counts, dynamics, prev_state):
    groups, scans = lax.axis_size("bins"), lax.axis_size("scans")
    prof_rows, length = profiles.shape
    capacity = prev_state.shape[0]
    coarse = length // HALF
    shares = groups * scans
    count = prof_rows * scans * TILE
    state = prev_state.reshape(capacity, 2 * STATES)
    if groups == 8 and scans == 4 and coarse == 16 * shares and capacity == HALF:
        turn = turns_step(groups, groups * length)
        columns, whole = columns_step(profiles.reshape(length), turn, band_edges, owner_counts)
        columns = exchanged(columns, "bins").reshape(coarse // 2, LANES)
        blocks, moved, wanted, lane_band = coarse_step(
            columns, whole, dynamics, state, groups, shares
        )
        blocks = exchanged(blocks.reshape(shares, 8, LANES), ("bins", "scans"))
        blocks = blocks.reshape(8 * shares, LANES)
        payload = fine_step(blocks, turn, wanted, scans, coarse)
        arrived = exchanged(payload, ("bins", "scans"))
    else:
        lane_band, row_band = bands_general(band_edges, owner_counts, capacity)
        moved = moved_step(row_band, dynamics, state)
        columns = profiles.reshape(coarse // groups, groups, HALF).transpose(1, 0, 2)
        columns = exchanged(columns, "bins").reshape(coarse, HALF)
        blocks = exchanged(coarse_step_general(columns, groups), "bins")
        arrived = exchanged(fine_step_general(blocks, owner_counts, capacity), "bins")
        power = lax.psum(arrived[:, 3:], "scans")
        arrived = jnp.concatenate([arrived[:, :3], power], axis=1)
    updated = update_step(arrived, lane_band, moved, coarse, count)
    return updated.reshape(prev_state.shape)


def solution(mesh):
    return jax.shard_map(
        body,
        mesh=mesh,
        in_specs=(P("scans", "bins"), P(), P(), P(), P("bins", "scans", None)),
        out_specs=P("bins", "scans", None),
        check_vma=False,
    )
```

```python
import functools
import math

import jax
import jax.numpy as jnp
import numpy as np
from jax import lax
from jax.experimental import pallas as pl
from jax.experimental.pallas import tpu as pltpu
from jax.sharding import PartitionSpec as P

TILE = 512
STATES = 64
NCLASS = 5
LANES = 128

EPSILON = 1e-05
HIGHEST = lax.Precision.HIGHEST
BF16 = jnp.bfloat16
F32 = jnp.float32


def unit_root(order, exponents):
    angles = 2.0 * np.pi * (np.asarray(exponents, dtype=np.int64) % order) / order
    return np.cos(angles), -np.sin(angles)


def two_terms(values):
    high = np.asarray(values, np.float32).astype(BF16)
    low = (np.asarray(values, np.float64) - high.astype(np.float64)).astype(BF16)
    return high, low


def three_terms(values):
    high, middle = two_terms(values)
    rest = np.asarray(values, np.float64) - high.astype(np.float64) - middle.astype(np.float64)
    return high, middle, rest.astype(BF16)


def split_two(values):
    high = values.astype(BF16)
    return high, (values - high.astype(F32)).astype(BF16)


def split_three(values):
    high = values.astype(BF16)
    rest = values - high.astype(F32)
    middle = rest.astype(BF16)
    return high, middle, (rest - middle.astype(F32)).astype(BF16)


def dot(left, right):
    return jnp.dot(left, right, preferred_element_type=F32)


VMEM = pl.BlockSpec(memory_space=pltpu.VMEM)
PARAMS = pltpu.CompilerParams(vmem_limit_bytes=32 << 20)
COST = pl.CostEstimate(flops=1 << 30, bytes_accessed=1 << 24, transcendentals=0)


KINDS = 4
HALF = LANES // 2


def unit_turn(phase, order):
    shifted = phase + order // 8
    quadrant = (shifted >> (order.bit_length() - 3)) & 3
    x = ((shifted & (order // 4 - 1)) - order // 8).astype(F32) * (2.0 * math.pi / order)
    y = x * x
    cosine = 1.0 + y * (-1 / 2 + y * (1 / 24 + y * (-1 / 720 + y * (1 / 40320))))
    sine = x * (1.0 + y * (-1 / 6 + y * (1 / 120 + y * (-1 / 5040 + y * (1 / 362880)))))
    odd = (quadrant & 1) == 1
    real, imag = jnp.where(odd, sine, cosine), jnp.where(odd, cosine, sine)
    real = jnp.where((quadrant == 1) | (quadrant == 2), -real, real)
    return real, jnp.where(quadrant >= 2, -imag, imag)


def iotas(shape):
    return [lax.broadcasted_iota(jnp.int32, shape, axis) for axis in range(len(shape))]


def turns_kernel(order, turn_ref):
    row, lane = iotas((8, LANES))
    own = lax.axis_index("bins") * lax.axis_size("scans") + lax.axis_index("scans")
    for at in range(turn_ref.shape[0] // 2):
        c, odd = divmod(at, 2)
        k_index = 8 * own + 4 * (lane >> 6) + 2 * (row & 1) + odd
        phase = ((c * HALF + (lane & (HALF - 1))) * k_index) & (order - 1)
        turn_ref[2 * at], turn_ref[2 * at + 1] = unit_turn(phase, order)


def turns_step(groups, order):
    return pl.pallas_call(
        functools.partial(turns_kernel, order),
        out_shape=jax.ShapeDtypeStruct((4 * groups, 8, LANES), F32),
        out_specs=VMEM,
        compiler_params=PARAMS,
        cost_estimate=COST,
        name="turns",
    )()


def columns_kernel(x_ref, turn_ref, edges_ref, counts_ref, out_ref, whole_ref):
    del turn_ref
    groups, rows, _ = out_ref.shape
    low_lanes = iotas((rows, LANES))[1] < HALF
    for pair in range(groups // 2):
        even = x_ref[pl.ds(pair, rows, stride=groups), :]
        odd = x_ref[pl.ds(groups // 2 + pair, rows, stride=groups), :]
        crossed = pltpu.roll(jnp.where(low_lanes, odd, even), HALF, 1)
        out_ref[2 * pair] = jnp.where(low_lanes, even, crossed)
        out_ref[2 * pair + 1] = jnp.where(low_lanes, crossed, odd)
    whole_ref[:, : NCLASS + 1] = edges_ref[...]
    whole_ref[:, 8 : 8 + groups] = counts_ref[...]


def columns_step(profile, turn, band_edges, owner_counts):
    groups = owner_counts.shape[0]
    rows = profile.shape[0] // (groups * LANES)
    return pl.pallas_call(
        columns_kernel,
        out_shape=(
            jax.ShapeDtypeStruct((groups, rows, LANES), F32),
            jax.ShapeDtypeStruct((1, LANES), jnp.int32),
        ),
        in_specs=[VMEM] * 4,
        out_specs=(VMEM,) * 2,
        compiler_params=PARAMS,
        name="columns",
    )(profile.reshape(-1, LANES), turn, band_edges.reshape(1, -1), owner_counts.reshape(1, -1))


def coarse_table(coarse):
    half, quarter = coarse // 2, coarse // 4
    k_index = np.arange(quarter)
    a_index = np.concatenate([np.arange(0, half, 2), np.arange(1, half, 2)])
    real, imag = unit_root(half, k_index[:, None] * a_index[None, :])
    imag[0] = 1
    parts = [part.reshape(quarter // 16, 2, 2, 1, 4, half) for part in (real, imag)]
    parts = np.concatenate(parts, axis=3).transpose(0, 2, 3, 1, 4, 5)
    high, middle, low = three_terms(parts.reshape(half, half))
    terms = [term[:, at : at + quarter] for at in (0, quarter) for term in (middle, high, low)]
    return np.concatenate(terms, axis=1)


def slot_bands(groups, whole_ref, wanted_ref, lane_band_ref, row_band_ref):
    capacity = row_band_ref.shape[0]
    own = lax.axis_index("bins")
    counts = [
        jnp.broadcast_to(whole_ref[:, 8 + owner : 9 + owner], (1, LANES)) for owner in range(groups)
    ]
    lane = iotas((1, LANES))[1]
    rank = lane & (capacity - 1)
    start = jnp.zeros((1, LANES), jnp.int32)
    own_start, own_count = start, start
    wanted = []
    for owner, count in enumerate(counts):
        wanted.append(jnp.where(rank < count, start + rank, -1))
        own_start = jnp.where(own == owner, start, own_start)
        own_count = jnp.where(own == owner, count, own_count)
        start = start + count
    for pair in range(groups // 2):
        wanted_ref[:, pair * LANES : (pair + 1) * LANES] = jnp.where(
            lane < HALF, wanted[2 * pair], wanted[2 * pair + 1]
        )
    edges = [jnp.broadcast_to(whole_ref[:, at : at + 1], (1, LANES)) for at in range(1, NCLASS)]
    for ref, slot in ((lane_band_ref, rank), (row_band_ref, iotas((capacity, LANES))[0])):
        band = jnp.zeros_like(slot)
        for edge in edges:
            band = band + jnp.where(slot + own_start >= edge, 1, 0)
        ref[...] = jnp.where(slot < own_count, band, -1)


def coarse_kernel(
    groups,
    shares,
    x_ref,
    table_ref,
    whole_ref,
    dynamics_ref,
    state_ref,
    out_ref,
    moved_ref,
    wanted_ref,
    lane_band_ref,
    row_band_ref,
):
    slot_bands(groups, whole_ref, wanted_ref, lane_band_ref, row_band_ref)
    half = x_ref.shape[0]
    quarter = half // 2
    row, lane = iotas((8, LANES))
    low_lanes = lane < HALF
    sums = []
    for parity in range(2):
        high, middle, low = split_three(x_ref[pl.ds(parity, quarter, stride=2), :])
        main = jnp.concatenate([high, middle], axis=1)
        rest = [jnp.concatenate([term, jnp.zeros_like(term)], axis=1) for term in (low, high)]
        at = 3 * quarter * parity
        left = jnp.concatenate(
            [table_ref[:, at : at + 2 * quarter], table_ref[:, at + quarter : at + 3 * quarter]], axis=1
        )
        both = dot(left, jnp.concatenate([main, main] + rest, axis=0))
        sums.append(both[:, :LANES] + both[:, LANES:])
    base = 8 * (row >> 2) + 4 * (lane >> 6) + (row & 3)
    base_cosine, base_sine = unit_turn(base, 2 * half)
    packed = low_lanes & (row == 0)
    for sign, block in [(sign, block) for block in range(half // 32) for sign in (1, -1)]:
        pieces = []
        for at in range(32 * block, 32 * (block + 1), 8):
            even, odd = sums[0][at : at + 8], sums[1][at : at + 8]
            pieces.append(even + odd if sign > 0 else even - odd)
        real_low, imag_low, real_high, imag_high = pieces
        if block == 0 and sign < 0:
            imag_low = jnp.where(row == 0, 0.0, imag_low)
        even_real = jnp.where(low_lanes, real_low, pltpu.roll(real_high, HALF, 1))
        even_imag = jnp.where(low_lanes, imag_low, pltpu.roll(imag_high, HALF, 1))
        odd_real = jnp.where(low_lanes, pltpu.roll(real_low, HALF, 1), real_high)
        odd_imag = jnp.where(low_lanes, pltpu.roll(imag_low, HALF, 1), imag_high)
        first = 2 * block + (0 if sign > 0 else shares // 2)
        angle = math.pi * 8 * first / half
        cosine = base_cosine * math.cos(angle) - base_sine * math.sin(angle)
        sine = base_sine * math.cos(angle) + base_cosine * math.sin(angle)
        real = even_real + odd_real * cosine + odd_imag * sine
        if first == 0:
            cosine = jnp.where(packed, -1.0, cosine)
        imag = even_imag + odd_imag * cosine - odd_real * sine
        out_ref[pl.ds(8 * first, 8, stride=2), :] = real
        out_ref[pl.ds(8 * first + 1, 8, stride=2), :] = imag
    moved_ref[...] = state_product(dynamics_ref[...], state_ref[...], row_band_ref[...])


def coarse_step(columns, whole, dynamics, state, groups, shares):
    capacity = state.shape[0]
    half = columns.shape[0]
    return pl.pallas_call(
        functools.partial(coarse_kernel, groups, shares),
        out_shape=(
            jax.ShapeDtypeStruct((half, LANES), F32),
            jax.ShapeDtypeStruct(state.shape, F32),
            jax.ShapeDtypeStruct((1, groups * capacity), jnp.int32),
            jax.ShapeDtypeStruct((1, LANES), jnp.int32),
        ),
        in_specs=[VMEM] * 5,
        out_specs=(VMEM,) * 4,
        scratch_shapes=[pltpu.VMEM((capacity, LANES), jnp.int32)],
        compiler_params=PARAMS,
        name="coarse_dft",
    )(
        columns,
        jnp.asarray(coarse_table(2 * half)),
        whole,
        dynamics.reshape(NCLASS * STATES, STATES),
        state,
    )


def coarse_step_general(columns, shares):
    coarse = columns.shape[0]
    half = coarse // 2
    real, imag = unit_root(coarse, np.arange(half)[:, None] * np.arange(coarse)[None, :])
    imag[0] = 1 - 2 * (np.arange(coarse) % 2)
    table = jnp.asarray(np.concatenate([real, imag]).astype(np.float32))
    spectrum = jnp.dot(table, columns, precision=HIGHEST)
    blocks = jnp.concatenate([spectrum[:half], spectrum[half:]], axis=1)
    return blocks.reshape(shares, half // shares, LANES)


def fine_tables(groups, coarse):
    fine_length = groups * HALF
    doubled = np.arange(LANES) % HALF
    turn = unit_root(fine_length, np.arange(groups)[:, None] * doubled[None, :])
    middle = (np.arange(groups)[:, None] * HALF + doubled[None, :]) * (coarse // 2)
    middle = unit_root(coarse * fine_length, middle)
    turns = np.concatenate(turn + middle).astype(np.float32)
    order = np.arange(HALF)
    order[HALF // 2 :] = order[HALF // 2 :][::-1]
    real, imag = unit_root(HALF, np.arange(HALF)[:, None] * order[None, :])
    sign = np.where(np.arange(HALF) < HALF // 2, 1, -1)
    matrix = np.block([[real, imag * sign], [-imag, real * sign]])
    high, middle, low = three_terms(matrix)
    both = np.concatenate([high, middle], axis=1)
    rest = [np.concatenate([term, np.zeros_like(term)], axis=1) for term in (low, high)]
    return turns, np.concatenate([both, both] + rest, axis=0)


def add(p, q):
    return (p[0] + q[0], p[1] + q[1])


def sub(p, q):
    return (p[0] - q[0], p[1] - q[1])


def times(p, cosine, sine):
    return (p[0] * cosine + p[1] * sine, p[1] * cosine - p[0] * sine)


def eight_point(values):
    half = math.sqrt(0.5)

    def down(p):
        return (p[1], -p[0])

    def four(a, b, c, d):
        s0, s1, s2, s3 = add(a, c), sub(a, c), add(b, d), sub(b, d)
        turned = (s1[0] + s3[1], s1[1] - s3[0]), (s1[0] - s3[1], s1[1] + s3[0])
        return add(s0, s2), turned[0], sub(s0, s2), turned[1]

    even = four(values[0], values[2], values[4], values[6])
    odd = four(values[1], values[3], values[5], values[7])
    turned = [
        odd[0],
        ((odd[1][0] + odd[1][1]) * half, (odd[1][1] - odd[1][0]) * half),
        down(odd[2]),
        ((odd[3][1] - odd[3][0]) * half, (odd[3][0] + odd[3][1]) * -half),
    ]
    return [add(e, t) for e, t in zip(even, turned)] + [sub(e, t) for e, t in zip(even, turned)]


def state_product(dynamics, state, band):
    row, column = iotas((NCLASS * STATES, STATES))
    limit = STATES >> (row >> 6)
    inside = ((row & (STATES - 1)) < limit) & (column < limit)
    dynamics = jnp.where(inside, dynamics, 0.0)
    empty = jnp.zeros_like(dynamics)
    halves = [
        jnp.concatenate([dynamics, empty], axis=1),
        jnp.concatenate([empty, dynamics], axis=1),
    ]
    matrix = jnp.concatenate(
        [half[k * STATES : (k + 1) * STATES] for k in range(NCLASS) for half in halves], axis=0
    )
    state_high, state_low = split_two(state)
    high, low = split_two(matrix)
    moved = lax.dot_general(
        jnp.concatenate([state_high, state_low, state_high], axis=1),
        jnp.concatenate([high, high, low], axis=1),
        (((1,), (1,)), ((), ())),
        preferred_element_type=F32,
    )
    result = jnp.zeros(state.shape, F32)
    for k in range(NCLASS):
        result = jnp.where(band == k, moved[:, k * LANES : (k + 1) * LANES], result)
    return result


def moved_kernel(row_band_ref, dynamics_ref, state_ref, out_ref):
    out_ref[...] = state_product(dynamics_ref[...], state_ref[...], row_band_ref[...])


def moved_step(row_band, dynamics, state):
    return pl.pallas_call(
        moved_kernel,
        out_shape=jax.ShapeDtypeStruct(state.shape, F32),
        in_specs=[VMEM] * 3,
        out_specs=VMEM,
        compiler_params=PARAMS,
        name="moved",
    )(row_band, dynamics.reshape(NCLASS * STATES, STATES), state)


def fine_kernel(
    profiles,
    x_ref,
    turn_ref,
    wanted_ref,
    turns_ref,
    table_ref,
    out_ref,
):
    groups = turn_ref.shape[0] // 4
    first = (lax.axis_index("bins") == 0) & (lax.axis_index("scans") == 0)
    row, lane = iotas((8, LANES))
    low_lanes = lane < HALF
    low_side = (lane & (HALF - 1)) < HALF // 2
    even = (row & 1) == 0
    packed = first & low_lanes & even
    blocks = [[None] * 3 for _ in range(groups)]
    for at in range(3):
        column = []
        for c in range(groups):
            start = c * 8 * profiles
            if at < 2:
                real = x_ref[pl.ds(start + 2 * at, 8, stride=4), :]
                imag = x_ref[pl.ds(start + 2 * at + 1, 8, stride=4), :]
                imag = imag if at else jnp.where(packed, 0.0, imag)
                turn = 4 * c + 2 * at
                column.append(times((real, imag), turn_ref[turn], turn_ref[turn + 1]))
            else:
                middle = jnp.where(packed, x_ref[pl.ds(start + 1, 8, stride=4), :], 0.0)
                middle_real = turns_ref[2 * groups + c : 2 * groups + c + 1, :]
                middle_imag = turns_ref[3 * groups + c : 3 * groups + c + 1, :]
                column.append((middle * middle_real, middle * middle_imag))
        for u, value in enumerate(eight_point(column)):
            cosine, sine = turns_ref[u : u + 1, :], -turns_ref[groups + u : groups + u + 1, :]
            blocks[u][at] = times(value, cosine, sine) if u else value
    rows = []
    for u in range(groups):
        for at in range(3):
            real, imag = blocks[u][at]
            rows.append(jnp.where(low_lanes, real, pltpu.roll(imag, HALF, 1)))
            if at < 2:
                rows.append(jnp.where(low_lanes, pltpu.roll(real, HALF, 1), imag))
    product = []
    for at in range(0, len(rows), len(rows) // 2):
        part = jnp.concatenate(rows[at : at + len(rows) // 2], axis=0)
        high, middle, low = split_three(part)
        both = dot(jnp.concatenate([high, middle, high, low], axis=1), table_ref[...])
        product.append(both[:, :LANES] + both[:, LANES:])
    product = jnp.concatenate(product, axis=0)
    spectrum = []
    for u in range(groups):
        spectrum.append([product[8 * at : 8 * (at + 1)] for at in range(5 * u, 5 * (u + 1))])
        spectrum[u][0] = jnp.where(first & even & ~low_side, 0.0, spectrum[u][0])
        spectrum[u][4] = jnp.where(low_side, spectrum[u][4], 0.0)
    squares = [sum(block * block for block in spectrum[u]) for u in range(groups)]
    rest_place = ~low_side & even
    pieces = []
    for u in range(groups):
        mirror = groups - 1 - u
        power = jnp.where(low_side, squares[u], squares[mirror])
        for shift in (4, 2, 1):
            power = power + pltpu.roll(power, shift, 0)
        evens, *others = (
            jnp.where(low_side, spectrum[u][at], spectrum[mirror][at]) for at in range(4)
        )
        sums = jnp.where(rest_place, 0.0, evens) + sum(others)
        sums = sums + pltpu.roll(sums, 7, 0)
        lows = jnp.where(low_side, sums, 0.0)
        highs = jnp.where(low_side, 0.0, pltpu.roll(sums, 1, 0))
        rest = jnp.where(rest_place, evens, spectrum[u][4])
        pieces.append((jnp.where(even, lows, highs), jnp.where(even, rest, power)))
    left = [[], [], [], []]
    for u in range(0, groups, 2):
        for at in range(2):
            one, two = pieces[u][at], pieces[u + 1][at]
            real = jnp.where(low_lanes, one, pltpu.roll(two, HALF, 1))
            imag = jnp.where(low_lanes, pltpu.roll(one, HALF, 1), two)
            if at == 1:
                power = real + imag
                real, imag = jnp.where(even, real, power), jnp.where(even, imag, power)
            left[at].append(real)
            left[2 + at].append(imag)
    left = jnp.concatenate([jnp.concatenate(parts, axis=1) for parts in left], axis=0)
    left = jnp.concatenate(split_two(left), axis=0)
    wanted = wanted_ref[...]
    chosen = []
    for u in range(groups):
        tile = u + groups * iotas((HALF // 2, wanted.shape[1]))[0]
        chosen += [jnp.where(tile == wanted, 1.0, 0.0).astype(BF16)] * 2
    routed = dot(left, jnp.concatenate(chosen, axis=0))
    routed = routed[:32] + routed[32:]
    for pair in range(groups // 2):
        for at in range(2):
            real = routed[8 * at : 8 * (at + 1), pair * LANES : (pair + 1) * LANES]
            imag = routed[16 + 8 * at : 16 + 8 * (at + 1), pair * LANES : (pair + 1) * LANES]
            start = 2 * pair * profiles * KINDS + at
            out_ref[pl.ds(start, 8, stride=2), :] = jnp.where(
                low_lanes, real, pltpu.roll(imag, HALF, 1)
            )
            out_ref[pl.ds(start + profiles * KINDS, 8, stride=2), :] = jnp.where(
                low_lanes, pltpu.roll(real, HALF, 1), imag
            )


def fine_step(arrived, turn, wanted, profiles, coarse):
    groups = turn.shape[0] // 4
    turns, table = fine_tables(groups, coarse)
    out = pl.pallas_call(
        functools.partial(fine_kernel, profiles),
        out_shape=jax.ShapeDtypeStruct((groups * profiles * KINDS, LANES), F32),
        in_specs=[VMEM] * 5,
        out_specs=VMEM,
        compiler_params=PARAMS,
        name="fine_dft",
    )(
        arrived,
        turn,
        wanted,
        jnp.asarray(turns),
        jnp.asarray(table),
    )
    return out.reshape(groups * profiles, KINDS, LANES)


def fine_step_general(arrived, owner_counts, capacity):
    groups, rows = arrived.shape[:2]
    coarse = 2 * rows * groups
    fine_length = groups * HALF
    order = coarse * fine_length
    own = lax.axis_index("bins")
    real, imag = arrived[:, :, :HALF], arrived[:, :, HALF:]
    points = jnp.arange(fine_length, dtype=jnp.int32).reshape(groups, 1, HALF)
    k_index = own * rows + jnp.arange(rows, dtype=jnp.int32)[None, :, None]
    cosine, sine = unit_turn(points * k_index & (order - 1), order)
    packed = (own == 0) & (jnp.arange(rows)[None, :, None] == 0)
    middle = jnp.where(own == 0, imag[:, :1], 0.0)
    imag = jnp.where(packed, 0.0, imag)
    real, imag = real * cosine + imag * sine, imag * cosine - real * sine
    cosine, sine = unit_turn(points * (coarse // 2), order)
    real = jnp.concatenate([real, middle * cosine], axis=1)
    imag = jnp.concatenate([imag, -middle * sine], axis=1)

    def turned(pattern, root, parts):
        cosine, sine = (jnp.asarray(part.astype(np.float32)) for part in root)
        mul = functools.partial(jnp.einsum, pattern, precision=HIGHEST)
        return (
            mul(cosine, parts[0]) - mul(sine, parts[1]),
            mul(cosine, parts[1]) + mul(sine, parts[0]),
        )

    group_index, point_index = np.arange(groups), np.arange(HALF)
    parts = turned(
        "cu,crj->urj", unit_root(groups, group_index[:, None] * group_index), (real, imag)
    )
    parts = turned(
        "uj,urj->urj", unit_root(fine_length, group_index[:, None] * point_index), parts
    )
    parts = turned(
        "jv,urj->vur", unit_root(HALF, point_index[:, None] * point_index), parts
    )
    tiles = fine_length // 2
    kept = jnp.concatenate([~packed[0, :, 0], jnp.zeros((1,), bool)])
    sides = []
    for part, sign in zip(parts, (1.0, -1.0)):
        part = part.reshape(fine_length, rows + 1)
        sides.append((part[:tiles], sign * jnp.where(kept, part[tiles:][::-1], 0.0)))
    power = sum(jnp.sum(part * part, axis=1) for pair in sides for part in pair)
    starts = jnp.cumsum(owner_counts) - owner_counts
    slot_index = jnp.arange(capacity, dtype=jnp.int32)
    filled = slot_index[None, :] < owner_counts[:, None]
    chosen = jnp.clip(starts[:, None] + slot_index[None, :], 0, tiles - 1)

    def kinds(low, high):
        low_sums, high_sums = jnp.sum(low[:, :rows], axis=1), jnp.sum(high[:, 1:rows], axis=1)
        values = jnp.stack([low_sums, high[:, 0] + low[:, rows], high_sums, power], axis=1)
        return jnp.where(filled[:, :, None], values[chosen], 0.0).transpose(0, 2, 1)

    return jnp.concatenate([kinds(*sides[0]), kinds(*sides[1])], axis=2)


def pool_table(shares, coarse):
    pool = np.zeros((21, 16, shares, KINDS), np.float32)
    sums = pool[1:].reshape(NCLASS, STATES, shares, KINDS)
    wide = TILE // STATES
    rows = coarse // 2 // shares
    for share in range(shares):
        first = rows * share
        rest = coarse - first if share else coarse // 2
        for kind, at in enumerate((first, rest, coarse - first - 1)):
            for band in range(NCLASS):
                sums[band, at // wide >> band, share, kind] = 1.0
    pool[0, :, :, 3] = 1.0
    return pool.reshape(-1, shares * KINDS).astype(BF16)


def update_kernel(
    count, x_ref, pool_ref, lane_band_ref, moved_ref, out_ref
):
    band = lane_band_ref[...]
    right = jnp.concatenate(split_two(x_ref[...]), axis=1)
    sums = jnp.concatenate([dot(pool_ref[:176], right), dot(pool_ref[176:], right)], axis=0)
    sums = sums[:, :LANES] + sums[:, LANES:]
    power = sums[:1] * (1.0 / count)
    sums = sums[16:]
    span = jnp.left_shift(TILE // STATES, jnp.maximum(band, 0)).astype(F32)
    scaling = lax.rsqrt(span * (power + EPSILON))
    scaling = jnp.where(band < 0, 0.0, scaling)
    chosen = sums[:STATES]
    for k in range(1, NCLASS):
        chosen = jnp.where(band == k, sums[k * STATES : (k + 1) * STATES], chosen)
    chosen = chosen * scaling
    turned = jnp.transpose(jnp.concatenate([chosen, chosen], axis=0))
    half = turned.shape[0] // 2
    measured = jnp.where(iotas((half, LANES))[1] < STATES, turned[:half], turned[half:])
    out_ref[...] = measured + moved_ref[...]


def update_step(arrived, lane_band, moved, coarse, count):
    shares = arrived.shape[0]
    return pl.pallas_call(
        functools.partial(update_kernel, count),
        out_shape=jax.ShapeDtypeStruct(moved.shape, F32),
        in_specs=[VMEM] * 4,
        out_specs=VMEM,
        compiler_params=PARAMS,
        name="state_update",
    )(
        arrived.reshape(shares * KINDS, LANES),
        jnp.asarray(pool_table(shares, coarse)),
        lane_band,
        moved,
    )


def bands_general(band_edges, owner_counts, capacity):
    own = lax.axis_index("bins")
    slot = jnp.arange(capacity, dtype=jnp.int32)
    start = jnp.cumsum(owner_counts)[own] - owner_counts[own]
    band = jnp.sum((slot + start)[:, None] >= band_edges[None, 1:NCLASS], axis=1)
    band = jnp.where(slot < owner_counts[own], band, -1).astype(jnp.int32)
    return jnp.tile(band, 2)[None, :], jnp.broadcast_to(band[:, None], (capacity, LANES))


def exchanged(values, axes):
    return lax.all_to_all(values, axes, split_axis=0, concat_axis=0, tiled=True)


def body(profiles, band_edges, owner_counts, dynamics, prev_state):
    groups, scans = lax.axis_size("bins"), lax.axis_size("scans")
    prof_rows, length = profiles.shape
    capacity = prev_state.shape[0]
    coarse = length // HALF
    shares = groups * scans
    count = prof_rows * scans * TILE
    state = prev_state.reshape(capacity, 2 * STATES)
    if groups == 8 and scans == 4 and coarse == 16 * shares and capacity == HALF:
        turn = turns_step(groups, groups * length)
        columns, whole = columns_step(profiles.reshape(length), turn, band_edges, owner_counts)
        columns = exchanged(columns, "bins").reshape(coarse // 2, LANES)
        blocks, moved, wanted, lane_band = coarse_step(
            columns, whole, dynamics, state, groups, shares
        )
        blocks = exchanged(blocks.reshape(shares, 8, LANES), ("bins", "scans"))
        blocks = blocks.reshape(8 * shares, LANES)
        payload = fine_step(blocks, turn, wanted, scans, coarse)
        arrived = exchanged(payload, ("bins", "scans"))
    else:
        lane_band, row_band = bands_general(band_edges, owner_counts, capacity)
        moved = moved_step(row_band, dynamics, state)
        columns = profiles.reshape(coarse // groups, groups, HALF).transpose(1, 0, 2)
        columns = exchanged(columns, "bins").reshape(coarse, HALF)
        blocks = exchanged(coarse_step_general(columns, groups), "bins")
        arrived = exchanged(fine_step_general(blocks, owner_counts, capacity), "bins")
        power = lax.psum(arrived[:, 3:], "scans")
        arrived = jnp.concatenate([arrived[:, :3], power], axis=1)
    updated = update_step(arrived, lane_band, moved, coarse, count)
    return updated.reshape(prev_state.shape)


def solution(mesh):
    return jax.shard_map(
        body,
        mesh=mesh,
        in_specs=(P("scans", "bins"), P(), P(), P(), P("bins", "scans", None)),
        out_specs=P("bins", "scans", None),
        check_vma=False,
    )
```

```python
import functools
import math

import jax
import jax.numpy as jnp
import numpy as np
from jax import lax
from jax.experimental import pallas as pl
from jax.experimental.pallas import tpu as pltpu
from jax.sharding import PartitionSpec as P

TILE = 512
STATES = 64
NCLASS = 5
LANES = 128

EPSILON = 1e-05
HIGHEST = lax.Precision.HIGHEST
BF16 = jnp.bfloat16
F32 = jnp.float32


def unit_root(order, exponents):
    angles = 2.0 * np.pi * (np.asarray(exponents, dtype=np.int64) % order) / order
    return np.cos(angles), -np.sin(angles)


def two_terms(values):
    high = np.asarray(values, np.float32).astype(BF16)
    low = (np.asarray(values, np.float64) - high.astype(np.float64)).astype(BF16)
    return high, low


def three_terms(values):
    high, middle = two_terms(values)
    rest = np.asarray(values, np.float64) - high.astype(np.float64) - middle.astype(np.float64)
    return high, middle, rest.astype(BF16)


def split_two(values):
    high = values.astype(BF16)
    return high, (values - high.astype(F32)).astype(BF16)


def split_three(values):
    high = values.astype(BF16)
    rest = values - high.astype(F32)
    middle = rest.astype(BF16)
    return high, middle, (rest - middle.astype(F32)).astype(BF16)


def dot(left, right):
    return jnp.dot(left, right, preferred_element_type=F32)


VMEM = pl.BlockSpec(memory_space=pltpu.VMEM)
PARAMS = pltpu.CompilerParams(vmem_limit_bytes=32 << 20)
COST = pl.CostEstimate(flops=1 << 30, bytes_accessed=1 << 24, transcendentals=0)


KINDS = 4
HALF = LANES // 2


def unit_turn(phase, order):
    shifted = phase + order // 8
    quadrant = (shifted >> (order.bit_length() - 3)) & 3
    x = ((shifted & (order // 4 - 1)) - order // 8).astype(F32) * (2.0 * math.pi / order)
    y = x * x
    cosine = 1.0 + y * (-1 / 2 + y * (1 / 24 + y * (-1 / 720 + y * (1 / 40320))))
    sine = x * (1.0 + y * (-1 / 6 + y * (1 / 120 + y * (-1 / 5040 + y * (1 / 362880)))))
    odd = (quadrant & 1) == 1
    real, imag = jnp.where(odd, sine, cosine), jnp.where(odd, cosine, sine)
    real = jnp.where((quadrant == 1) | (quadrant == 2), -real, real)
    return real, jnp.where(quadrant >= 2, -imag, imag)


def iotas(shape):
    return [lax.broadcasted_iota(jnp.int32, shape, axis) for axis in range(len(shape))]


def turns_kernel(order, turn_ref):
    row, lane = iotas((8, LANES))
    own = lax.axis_index("bins") * lax.axis_size("scans") + lax.axis_index("scans")
    for at in range(turn_ref.shape[0] // 2):
        c, odd = divmod(at, 2)
        k_index = 8 * own + 4 * (lane >> 6) + 2 * (row & 1) + odd
        phase = ((c * HALF + (lane & (HALF - 1))) * k_index) & (order - 1)
        turn_ref[2 * at], turn_ref[2 * at + 1] = unit_turn(phase, order)


def turns_step(groups, order):
    return pl.pallas_call(
        functools.partial(turns_kernel, order),
        out_shape=jax.ShapeDtypeStruct((4 * groups, 8, LANES), F32),
        out_specs=VMEM,
        compiler_params=PARAMS,
        cost_estimate=COST,
        name="turns",
    )()


def columns_kernel(x_ref, turn_ref, edges_ref, counts_ref, out_ref, whole_ref):
    del turn_ref
    groups, rows, _ = out_ref.shape
    low_lanes = iotas((rows, LANES))[1] < HALF
    for pair in range(groups // 2):
        even = x_ref[pl.ds(pair, rows, stride=groups), :]
        odd = x_ref[pl.ds(groups // 2 + pair, rows, stride=groups), :]
        out_ref[2 * pair] = jnp.where(low_lanes, even, pltpu.roll(odd, HALF, 1))
        out_ref[2 * pair + 1] = jnp.where(low_lanes, pltpu.roll(even, HALF, 1), odd)
    whole_ref[:, : NCLASS + 1] = edges_ref[...]
    whole_ref[:, 8 : 8 + groups] = counts_ref[...]


def columns_step(profile, turn, band_edges, owner_counts):
    groups = owner_counts.shape[0]
    rows = profile.shape[0] // (groups * LANES)
    return pl.pallas_call(
        columns_kernel,
        out_shape=(
            jax.ShapeDtypeStruct((groups, rows, LANES), F32),
            jax.ShapeDtypeStruct((1, LANES), jnp.int32),
        ),
        in_specs=[VMEM] * 4,
        out_specs=(VMEM,) * 2,
        compiler_params=PARAMS,
        name="columns",
    )(profile.reshape(-1, LANES), turn, band_edges.reshape(1, -1), owner_counts.reshape(1, -1))


def coarse_table(coarse):
    half, quarter = coarse // 2, coarse // 4
    k_index = np.arange(quarter)
    a_index = np.concatenate([np.arange(0, half, 2), np.arange(1, half, 2)])
    real, imag = unit_root(half, k_index[:, None] * a_index[None, :])
    imag[0] = 1
    parts = [part.reshape(quarter // 16, 2, 2, 1, 4, half) for part in (real, imag)]
    parts = np.concatenate(parts, axis=3).transpose(0, 2, 3, 1, 4, 5)
    high, middle, low = three_terms(parts.reshape(half, half))
    terms = [term[:, at : at + quarter] for at in (0, quarter) for term in (middle, high, low)]
    return np.concatenate(terms, axis=1)


def slot_bands(groups, whole_ref, wanted_ref, lane_band_ref, row_band_ref):
    capacity = row_band_ref.shape[0]
    own = lax.axis_index("bins")
    counts = [
        jnp.broadcast_to(whole_ref[:, 8 + owner : 9 + owner], (1, LANES)) for owner in range(groups)
    ]
    lane = iotas((1, LANES))[1]
    rank = lane & (capacity - 1)
    start = jnp.zeros((1, LANES), jnp.int32)
    own_start, own_count = start, start
    wanted = []
    for owner, count in enumerate(counts):
        wanted.append(jnp.where(rank < count, start + rank, -1))
        own_start = jnp.where(own == owner, start, own_start)
        own_count = jnp.where(own == owner, count, own_count)
        start = start + count
    for pair in range(groups // 2):
        wanted_ref[:, pair * LANES : (pair + 1) * LANES] = jnp.where(
            lane < HALF, wanted[2 * pair], wanted[2 * pair + 1]
        )
    edges = [jnp.broadcast_to(whole_ref[:, at : at + 1], (1, LANES)) for at in range(1, NCLASS)]
    for ref, slot in ((lane_band_ref, rank), (row_band_ref, iotas((capacity, LANES))[0])):
        band = jnp.zeros_like(slot)
        for edge in edges:
            band = band + jnp.where(slot + own_start >= edge, 1, 0)
        ref[...] = jnp.where(slot < own_count, band, -1)


def coarse_kernel(
    groups,
    shares,
    x_ref,
    table_ref,
    whole_ref,
    dynamics_ref,
    state_ref,
    out_ref,
    moved_ref,
    wanted_ref,
    lane_band_ref,
    row_band_ref,
):
    slot_bands(groups, whole_ref, wanted_ref, lane_band_ref, row_band_ref)
    half = x_ref.shape[0]
    quarter = half // 2
    row, lane = iotas((8, LANES))
    low_lanes = lane < HALF
    sums = []
    for parity in range(2):
        high, middle, low = split_three(x_ref[pl.ds(parity, quarter, stride=2), :])
        main = jnp.concatenate([high, middle], axis=1)
        rest = [jnp.concatenate([term, jnp.zeros_like(term)], axis=1) for term in (low, high)]
        at = 3 * quarter * parity
        left = jnp.concatenate(
            [table_ref[:, at : at + 2 * quarter], table_ref[:, at + quarter : at + 3 * quarter]], axis=1
        )
        both = dot(left, jnp.concatenate([main, main] + rest, axis=0))
        sums.append(both[:, :LANES] + both[:, LANES:])
    base = 8 * (row >> 2) + 4 * (lane >> 6) + (row & 3)
    base_cosine, base_sine = unit_turn(base, 2 * half)
    packed = low_lanes & (row == 0)
    for sign, block in [(sign, block) for block in range(half // 32) for sign in (1, -1)]:
        pieces = []
        for at in range(32 * block, 32 * (block + 1), 8):
            even, odd = sums[0][at : at + 8], sums[1][at : at + 8]
            pieces.append(even + odd if sign > 0 else even - odd)
        real_low, imag_low, real_high, imag_high = pieces
        if block == 0 and sign < 0:
            imag_low = jnp.where(row == 0, 0.0, imag_low)
        crossed_real = pltpu.roll(jnp.where(low_lanes, real_high, real_low), HALF, 1)
        crossed_imag = pltpu.roll(jnp.where(low_lanes, imag_high, imag_low), HALF, 1)
        even_real = jnp.where(low_lanes, real_low, crossed_real)
        even_imag = jnp.where(low_lanes, imag_low, crossed_imag)
        odd_real = jnp.where(low_lanes, crossed_real, real_high)
        odd_imag = jnp.where(low_lanes, crossed_imag, imag_high)
        first = 2 * block + (0 if sign > 0 else shares // 2)
        angle = math.pi * 8 * first / half
        cosine = base_cosine * math.cos(angle) - base_sine * math.sin(angle)
        sine = base_sine * math.cos(angle) + base_cosine * math.sin(angle)
        real = even_real + odd_real * cosine + odd_imag * sine
        if first == 0:
            cosine = jnp.where(packed, -1.0, cosine)
        imag = even_imag + odd_imag * cosine - odd_real * sine
        out_ref[pl.ds(8 * first, 8, stride=2), :] = real
        out_ref[pl.ds(8 * first + 1, 8, stride=2), :] = imag
    moved_ref[...] = state_product(dynamics_ref[...], state_ref[...], row_band_ref[...])


def coarse_step(columns, whole, dynamics, state, groups, shares):
    capacity = state.shape[0]
    half = columns.shape[0]
    return pl.pallas_call(
        functools.partial(coarse_kernel, groups, shares),
        out_shape=(
            jax.ShapeDtypeStruct((half, LANES), F32),
            jax.ShapeDtypeStruct(state.shape, F32),
            jax.ShapeDtypeStruct((1, groups * capacity), jnp.int32),
            jax.ShapeDtypeStruct((1, LANES), jnp.int32),
        ),
        in_specs=[VMEM] * 5,
        out_specs=(VMEM,) * 4,
        scratch_shapes=[pltpu.VMEM((capacity, LANES), jnp.int32)],
        compiler_params=PARAMS,
        name="coarse_dft",
    )(
        columns,
        jnp.asarray(coarse_table(2 * half)),
        whole,
        dynamics.reshape(NCLASS * STATES, STATES),
        state,
    )


def coarse_step_general(columns, shares):
    coarse = columns.shape[0]
    half = coarse // 2
    real, imag = unit_root(coarse, np.arange(half)[:, None] * np.arange(coarse)[None, :])
    imag[0] = 1 - 2 * (np.arange(coarse) % 2)
    table = jnp.asarray(np.concatenate([real, imag]).astype(np.float32))
    spectrum = jnp.dot(table, columns, precision=HIGHEST)
    blocks = jnp.concatenate([spectrum[:half], spectrum[half:]], axis=1)
    return blocks.reshape(shares, half // shares, LANES)


def fine_tables(groups, coarse):
    fine_length = groups * HALF
    doubled = np.arange(LANES) % HALF
    turn = unit_root(fine_length, np.arange(groups)[:, None] * doubled[None, :])
    middle = (np.arange(groups)[:, None] * HALF + doubled[None, :]) * (coarse // 2)
    middle = unit_root(coarse * fine_length, middle)
    turns = np.concatenate(turn + middle).astype(np.float32)
    order = np.arange(HALF)
    order[HALF // 2 :] = order[HALF // 2 :][::-1]
    real, imag = unit_root(HALF, np.arange(HALF)[:, None] * order[None, :])
    sign = np.where(np.arange(HALF) < HALF // 2, 1, -1)
    matrix = np.block([[real, imag * sign], [-imag, real * sign]])
    high, middle, low = three_terms(matrix)
    both = np.concatenate([high, middle], axis=1)
    rest = [np.concatenate([term, np.zeros_like(term)], axis=1) for term in (low, high)]
    return turns, np.concatenate([both, both] + rest, axis=0)


def add(p, q):
    return (p[0] + q[0], p[1] + q[1])


def sub(p, q):
    return (p[0] - q[0], p[1] - q[1])


def times(p, cosine, sine):
    return (p[0] * cosine + p[1] * sine, p[1] * cosine - p[0] * sine)


def eight_point(values):
    half = math.sqrt(0.5)

    def down(p):
        return (p[1], -p[0])

    def four(a, b, c, d):
        s0, s1, s2, s3 = add(a, c), sub(a, c), add(b, d), sub(b, d)
        turned = (s1[0] + s3[1], s1[1] - s3[0]), (s1[0] - s3[1], s1[1] + s3[0])
        return add(s0, s2), turned[0], sub(s0, s2), turned[1]

    even = four(values[0], values[2], values[4], values[6])
    odd = four(values[1], values[3], values[5], values[7])
    turned = [
        odd[0],
        ((odd[1][0] + odd[1][1]) * half, (odd[1][1] - odd[1][0]) * half),
        down(odd[2]),
        ((odd[3][1] - odd[3][0]) * half, (odd[3][0] + odd[3][1]) * -half),
    ]
    return [add(e, t) for e, t in zip(even, turned)] + [sub(e, t) for e, t in zip(even, turned)]


def state_product(dynamics, state, band):
    row, column = iotas((NCLASS * STATES, STATES))
    limit = STATES >> (row >> 6)
    inside = ((row & (STATES - 1)) < limit) & (column < limit)
    dynamics = jnp.where(inside, dynamics, 0.0)
    empty = jnp.zeros_like(dynamics)
    halves = [
        jnp.concatenate([dynamics, empty], axis=1),
        jnp.concatenate([empty, dynamics], axis=1),
    ]
    matrix = jnp.concatenate(
        [half[k * STATES : (k + 1) * STATES] for k in range(NCLASS) for half in halves], axis=0
    )
    state_high, state_low = split_two(state)
    high, low = split_two(matrix)
    moved = lax.dot_general(
        jnp.concatenate([state_high, state_low, state_high], axis=1),
        jnp.concatenate([high, high, low], axis=1),
        (((1,), (1,)), ((), ())),
        preferred_element_type=F32,
    )
    result = jnp.zeros(state.shape, F32)
    for k in range(NCLASS):
        result = jnp.where(band == k, moved[:, k * LANES : (k + 1) * LANES], result)
    return result


def moved_kernel(row_band_ref, dynamics_ref, state_ref, out_ref):
    out_ref[...] = state_product(dynamics_ref[...], state_ref[...], row_band_ref[...])


def moved_step(row_band, dynamics, state):
    return pl.pallas_call(
        moved_kernel,
        out_shape=jax.ShapeDtypeStruct(state.shape, F32),
        in_specs=[VMEM] * 3,
        out_specs=VMEM,
        compiler_params=PARAMS,
        name="moved",
    )(row_band, dynamics.reshape(NCLASS * STATES, STATES), state)


def fine_kernel(
    profiles,
    x_ref,
    turn_ref,
    wanted_ref,
    turns_ref,
    table_ref,
    out_ref,
):
    groups = turn_ref.shape[0] // 4
    first = (lax.axis_index("bins") == 0) & (lax.axis_index("scans") == 0)
    row, lane = iotas((8, LANES))
    low_lanes = lane < HALF
    low_side = (lane & (HALF - 1)) < HALF // 2
    even = (row & 1) == 0
    packed = first & low_lanes & even
    blocks = [[None] * 3 for _ in range(groups)]
    for at in range(3):
        column = []
        for c in range(groups):
            start = c * 8 * profiles
            if at < 2:
                real = x_ref[pl.ds(start + 2 * at, 8, stride=4), :]
                imag = x_ref[pl.ds(start + 2 * at + 1, 8, stride=4), :]
                imag = imag if at else jnp.where(packed, 0.0, imag)
                turn = 4 * c + 2 * at
                column.append(times((real, imag), turn_ref[turn], turn_ref[turn + 1]))
            else:
                middle = jnp.where(packed, x_ref[pl.ds(start + 1, 8, stride=4), :], 0.0)
                middle_real = turns_ref[2 * groups + c : 2 * groups + c + 1, :]
                middle_imag = turns_ref[3 * groups + c : 3 * groups + c + 1, :]
                column.append((middle * middle_real, middle * middle_imag))
        for u, value in enumerate(eight_point(column)):
            cosine, sine = turns_ref[u : u + 1, :], -turns_ref[groups + u : groups + u + 1, :]
            blocks[u][at] = times(value, cosine, sine) if u else value
    rows = []
    for u in range(groups):
        for at in range(3):
            real, imag = blocks[u][at]
            rows.append(jnp.where(low_lanes, real, pltpu.roll(imag, HALF, 1)))
            if at < 2:
                rows.append(jnp.where(low_lanes, pltpu.roll(real, HALF, 1), imag))
    product = []
    for at in range(0, len(rows), len(rows) // 2):
        part = jnp.concatenate(rows[at : at + len(rows) // 2], axis=0)
        high, middle, low = split_three(part)
        both = dot(jnp.concatenate([high, middle, high, low], axis=1), table_ref[...])
        product.append(both[:, :LANES] + both[:, LANES:])
    product = jnp.concatenate(product, axis=0)
    spectrum = []
    for u in range(groups):
        spectrum.append([product[8 * at : 8 * (at + 1)] for at in range(5 * u, 5 * (u + 1))])
        spectrum[u][0] = jnp.where(first & even & ~low_side, 0.0, spectrum[u][0])
        spectrum[u][4] = jnp.where(low_side, spectrum[u][4], 0.0)
    squares = [sum(block * block for block in spectrum[u]) for u in range(groups)]
    rest_place = ~low_side & even
    pieces = []
    for u in range(groups):
        mirror = groups - 1 - u
        power = jnp.where(low_side, squares[u], squares[mirror])
        for shift in (4, 2, 1):
            power = power + pltpu.roll(power, shift, 0)
        evens, *others = (
            jnp.where(low_side, spectrum[u][at], spectrum[mirror][at]) for at in range(4)
        )
        sums = jnp.where(rest_place, 0.0, evens) + sum(others)
        sums = sums + pltpu.roll(sums, 7, 0)
        lows = jnp.where(low_side, sums, 0.0)
        highs = jnp.where(low_side, 0.0, pltpu.roll(sums, 1, 0))
        rest = jnp.where(rest_place, evens, spectrum[u][4])
        pieces.append((jnp.where(even, lows, highs), jnp.where(even, rest, power)))
    left = [[], [], [], []]
    for u in range(0, groups, 2):
        for at in range(2):
            one, two = pieces[u][at], pieces[u + 1][at]
            real = jnp.where(low_lanes, one, pltpu.roll(two, HALF, 1))
            imag = jnp.where(low_lanes, pltpu.roll(one, HALF, 1), two)
            if at == 1:
                power = real + imag
                real, imag = jnp.where(even, real, power), jnp.where(even, imag, power)
            left[at].append(real)
            left[2 + at].append(imag)
    left = jnp.concatenate([jnp.concatenate(parts, axis=1) for parts in left], axis=0)
    left = jnp.concatenate(split_two(left), axis=0)
    wanted = wanted_ref[...]
    chosen = []
    for u in range(groups):
        tile = u + groups * iotas((HALF // 2, wanted.shape[1]))[0]
        chosen += [jnp.where(tile == wanted, 1.0, 0.0).astype(BF16)] * 2
    routed = dot(left, jnp.concatenate(chosen, axis=0))
    routed = routed[:32] + routed[32:]
    for pair in range(groups // 2):
        for at in range(2):
            real = routed[8 * at : 8 * (at + 1), pair * LANES : (pair + 1) * LANES]
            imag = routed[16 + 8 * at : 16 + 8 * (at + 1), pair * LANES : (pair + 1) * LANES]
            start = 2 * pair * profiles * KINDS + at
            out_ref[pl.ds(start, 8, stride=2), :] = jnp.where(
                low_lanes, real, pltpu.roll(imag, HALF, 1)
            )
            out_ref[pl.ds(start + profiles * KINDS, 8, stride=2), :] = jnp.where(
                low_lanes, pltpu.roll(real, HALF, 1), imag
            )


def fine_step(arrived, turn, wanted, profiles, coarse):
    groups = turn.shape[0] // 4
    turns, table = fine_tables(groups, coarse)
    out = pl.pallas_call(
        functools.partial(fine_kernel, profiles),
        out_shape=jax.ShapeDtypeStruct((groups * profiles * KINDS, LANES), F32),
        in_specs=[VMEM] * 5,
        out_specs=VMEM,
        compiler_params=PARAMS,
        name="fine_dft",
    )(
        arrived,
        turn,
        wanted,
        jnp.asarray(turns),
        jnp.asarray(table),
    )
    return out.reshape(groups * profiles, KINDS, LANES)


def fine_step_general(arrived, owner_counts, capacity):
    groups, rows = arrived.shape[:2]
    coarse = 2 * rows * groups
    fine_length = groups * HALF
    order = coarse * fine_length
    own = lax.axis_index("bins")
    real, imag = arrived[:, :, :HALF], arrived[:, :, HALF:]
    points = jnp.arange(fine_length, dtype=jnp.int32).reshape(groups, 1, HALF)
    k_index = own * rows + jnp.arange(rows, dtype=jnp.int32)[None, :, None]
    cosine, sine = unit_turn(points * k_index & (order - 1), order)
    packed = (own == 0) & (jnp.arange(rows)[None, :, None] == 0)
    middle = jnp.where(own == 0, imag[:, :1], 0.0)
    imag = jnp.where(packed, 0.0, imag)
    real, imag = real * cosine + imag * sine, imag * cosine - real * sine
    cosine, sine = unit_turn(points * (coarse // 2), order)
    real = jnp.concatenate([real, middle * cosine], axis=1)
    imag = jnp.concatenate([imag, -middle * sine], axis=1)

    def turned(pattern, root, parts):
        cosine, sine = (jnp.asarray(part.astype(np.float32)) for part in root)
        mul = functools.partial(jnp.einsum, pattern, precision=HIGHEST)
        return (
            mul(cosine, parts[0]) - mul(sine, parts[1]),
            mul(cosine, parts[1]) + mul(sine, parts[0]),
        )

    group_index, point_index = np.arange(groups), np.arange(HALF)
    parts = turned(
        "cu,crj->urj", unit_root(groups, group_index[:, None] * group_index), (real, imag)
    )
    parts = turned(
        "uj,urj->urj", unit_root(fine_length, group_index[:, None] * point_index), parts
    )
    parts = turned(
        "jv,urj->vur", unit_root(HALF, point_index[:, None] * point_index), parts
    )
    tiles = fine_length // 2
    kept = jnp.concatenate([~packed[0, :, 0], jnp.zeros((1,), bool)])
    sides = []
    for part, sign in zip(parts, (1.0, -1.0)):
        part = part.reshape(fine_length, rows + 1)
        sides.append((part[:tiles], sign * jnp.where(kept, part[tiles:][::-1], 0.0)))
    power = sum(jnp.sum(part * part, axis=1) for pair in sides for part in pair)
    starts = jnp.cumsum(owner_counts) - owner_counts
    slot_index = jnp.arange(capacity, dtype=jnp.int32)
    filled = slot_index[None, :] < owner_counts[:, None]
    chosen = jnp.clip(starts[:, None] + slot_index[None, :], 0, tiles - 1)

    def kinds(low, high):
        low_sums, high_sums = jnp.sum(low[:, :rows], axis=1), jnp.sum(high[:, 1:rows], axis=1)
        values = jnp.stack([low_sums, high[:, 0] + low[:, rows], high_sums, power], axis=1)
        return jnp.where(filled[:, :, None], values[chosen], 0.0).transpose(0, 2, 1)

    return jnp.concatenate([kinds(*sides[0]), kinds(*sides[1])], axis=2)


def pool_table(shares, coarse):
    pool = np.zeros((21, 16, shares, KINDS), np.float32)
    sums = pool[1:].reshape(NCLASS, STATES, shares, KINDS)
    wide = TILE // STATES
    rows = coarse // 2 // shares
    for share in range(shares):
        first = rows * share
        rest = coarse - first if share else coarse // 2
        for kind, at in enumerate((first, rest, coarse - first - 1)):
            for band in range(NCLASS):
                sums[band, at // wide >> band, share, kind] = 1.0
    pool[0, :, :, 3] = 1.0
    return pool.reshape(-1, shares * KINDS).astype(BF16)


def update_kernel(
    count, x_ref, pool_ref, lane_band_ref, moved_ref, out_ref
):
    band = lane_band_ref[...]
    right = jnp.concatenate(split_two(x_ref[...]), axis=1)
    sums = jnp.concatenate([dot(pool_ref[:176], right), dot(pool_ref[176:], right)], axis=0)
    sums = sums[:, :LANES] + sums[:, LANES:]
    power = sums[:1] * (1.0 / count)
    sums = sums[16:]
    span = jnp.left_shift(TILE // STATES, jnp.maximum(band, 0)).astype(F32)
    scaling = lax.rsqrt(span * (power + EPSILON))
    scaling = jnp.where(band < 0, 0.0, scaling)
    chosen = sums[:STATES]
    for k in range(1, NCLASS):
        chosen = jnp.where(band == k, sums[k * STATES : (k + 1) * STATES], chosen)
    chosen = chosen * scaling
    turned = jnp.transpose(jnp.concatenate([chosen, chosen], axis=0))
    half = turned.shape[0] // 2
    measured = jnp.where(iotas((half, LANES))[1] < STATES, turned[:half], turned[half:])
    out_ref[...] = measured + moved_ref[...]


def update_step(arrived, lane_band, moved, coarse, count):
    shares = arrived.shape[0]
    return pl.pallas_call(
        functools.partial(update_kernel, count),
        out_shape=jax.ShapeDtypeStruct(moved.shape, F32),
        in_specs=[VMEM] * 4,
        out_specs=VMEM,
        compiler_params=PARAMS,
        name="state_update",
    )(
        arrived.reshape(shares * KINDS, LANES),
        jnp.asarray(pool_table(shares, coarse)),
        lane_band,
        moved,
    )


def bands_general(band_edges, owner_counts, capacity):
    own = lax.axis_index("bins")
    slot = jnp.arange(capacity, dtype=jnp.int32)
    start = jnp.cumsum(owner_counts)[own] - owner_counts[own]
    band = jnp.sum((slot + start)[:, None] >= band_edges[None, 1:NCLASS], axis=1)
    band = jnp.where(slot < owner_counts[own], band, -1).astype(jnp.int32)
    return jnp.tile(band, 2)[None, :], jnp.broadcast_to(band[:, None], (capacity, LANES))


def exchanged(values, axes):
    return lax.all_to_all(values, axes, split_axis=0, concat_axis=0, tiled=True)


def body(profiles, band_edges, owner_counts, dynamics, prev_state):
    groups, scans = lax.axis_size("bins"), lax.axis_size("scans")
    prof_rows, length = profiles.shape
    capacity = prev_state.shape[0]
    coarse = length // HALF
    shares = groups * scans
    count = prof_rows * scans * TILE
    state = prev_state.reshape(capacity, 2 * STATES)
    if groups == 8 and scans == 4 and coarse == 16 * shares and capacity == HALF:
        turn = turns_step(groups, groups * length)
        columns, whole = columns_step(profiles.reshape(length), turn, band_edges, owner_counts)
        columns = exchanged(columns, "bins").reshape(coarse // 2, LANES)
        blocks, moved, wanted, lane_band = coarse_step(
            columns, whole, dynamics, state, groups, shares
        )
        blocks = exchanged(blocks.reshape(shares, 8, LANES), ("bins", "scans"))
        blocks = blocks.reshape(8 * shares, LANES)
        payload = fine_step(blocks, turn, wanted, scans, coarse)
        arrived = exchanged(payload, ("bins", "scans"))
    else:
        lane_band, row_band = bands_general(band_edges, owner_counts, capacity)
        moved = moved_step(row_band, dynamics, state)
        columns = profiles.reshape(coarse // groups, groups, HALF).transpose(1, 0, 2)
        columns = exchanged(columns, "bins").reshape(coarse, HALF)
        blocks = exchanged(coarse_step_general(columns, groups), "bins")
        arrived = exchanged(fine_step_general(blocks, owner_counts, capacity), "bins")
        power = lax.psum(arrived[:, 3:], "scans")
        arrived = jnp.concatenate([arrived[:, :3], power], axis=1)
    updated = update_step(arrived, lane_band, moved, coarse, count)
    return updated.reshape(prev_state.shape)


def solution(mesh):
    return jax.shard_map(
        body,
        mesh=mesh,
        in_specs=(P("scans", "bins"), P(), P(), P(), P("bins", "scans", None)),
        out_specs=P("bins", "scans", None),
        check_vma=False,
    )
```

```python
import functools
import math

import jax
import jax.numpy as jnp
import numpy as np
from jax import lax
from jax.experimental import pallas as pl
from jax.experimental.pallas import tpu as pltpu
from jax.sharding import PartitionSpec as P

TILE = 512
STATES = 64
NCLASS = 5
LANES = 128

EPSILON = 1e-05
HIGHEST = lax.Precision.HIGHEST
BF16 = jnp.bfloat16
F32 = jnp.float32


def unit_root(order, exponents):
    angles = 2.0 * np.pi * (np.asarray(exponents, dtype=np.int64) % order) / order
    return np.cos(angles), -np.sin(angles)


def two_terms(values):
    high = np.asarray(values, np.float32).astype(BF16)
    low = (np.asarray(values, np.float64) - high.astype(np.float64)).astype(BF16)
    return high, low


def three_terms(values):
    high, middle = two_terms(values)
    rest = np.asarray(values, np.float64) - high.astype(np.float64) - middle.astype(np.float64)
    return high, middle, rest.astype(BF16)


def split_two(values):
    high = values.astype(BF16)
    return high, (values - high.astype(F32)).astype(BF16)


def split_three(values):
    high = values.astype(BF16)
    rest = values - high.astype(F32)
    middle = rest.astype(BF16)
    return high, middle, (rest - middle.astype(F32)).astype(BF16)


def dot(left, right):
    return jnp.dot(left, right, preferred_element_type=F32)


VMEM = pl.BlockSpec(memory_space=pltpu.VMEM)
PARAMS = pltpu.CompilerParams(vmem_limit_bytes=32 << 20)
COST = pl.CostEstimate(flops=1 << 30, bytes_accessed=1 << 24, transcendentals=0)


KINDS = 4
HALF = LANES // 2


def unit_turn(phase, order):
    shifted = phase + order // 8
    quadrant = (shifted >> (order.bit_length() - 3)) & 3
    x = ((shifted & (order // 4 - 1)) - order // 8).astype(F32) * (2.0 * math.pi / order)
    y = x * x
    cosine = 1.0 + y * (-1 / 2 + y * (1 / 24 + y * (-1 / 720 + y * (1 / 40320))))
    sine = x * (1.0 + y * (-1 / 6 + y * (1 / 120 + y * (-1 / 5040 + y * (1 / 362880)))))
    odd = (quadrant & 1) == 1
    real, imag = jnp.where(odd, sine, cosine), jnp.where(odd, cosine, sine)
    real = jnp.where((quadrant == 1) | (quadrant == 2), -real, real)
    return real, jnp.where(quadrant >= 2, -imag, imag)


def iotas(shape):
    return [lax.broadcasted_iota(jnp.int32, shape, axis) for axis in range(len(shape))]


def turns_kernel(order, turn_ref):
    row, lane = iotas((8, LANES))
    own = lax.axis_index("bins") * lax.axis_size("scans") + lax.axis_index("scans")
    for at in range(turn_ref.shape[0] // 2):
        c, odd = divmod(at, 2)
        k_index = 8 * own + 4 * (lane >> 6) + 2 * (row & 1) + odd
        phase = ((c * HALF + (lane & (HALF - 1))) * k_index) & (order - 1)
        turn_ref[2 * at], turn_ref[2 * at + 1] = unit_turn(phase, order)


def turns_step(groups, order):
    return pl.pallas_call(
        functools.partial(turns_kernel, order),
        out_shape=jax.ShapeDtypeStruct((4 * groups, 8, LANES), F32),
        out_specs=VMEM,
        compiler_params=PARAMS,
        cost_estimate=COST,
        name="turns",
    )()


def columns_kernel(x_ref, turn_ref, edges_ref, counts_ref, out_ref, whole_ref):
    del turn_ref
    groups, rows, _ = out_ref.shape
    low_lanes = iotas((rows, LANES))[1] < HALF
    for pair in range(groups // 2):
        even = x_ref[pl.ds(pair, rows, stride=groups), :]
        odd = x_ref[pl.ds(groups // 2 + pair, rows, stride=groups), :]
        out_ref[2 * pair] = jnp.where(low_lanes, even, pltpu.roll(odd, HALF, 1))
        out_ref[2 * pair + 1] = jnp.where(low_lanes, pltpu.roll(even, HALF, 1), odd)
    whole_ref[:, : NCLASS + 1] = edges_ref[...]
    whole_ref[:, 8 : 8 + groups] = counts_ref[...]


def columns_step(profile, turn, band_edges, owner_counts):
    groups = owner_counts.shape[0]
    rows = profile.shape[0] // (groups * LANES)
    return pl.pallas_call(
        columns_kernel,
        out_shape=(
            jax.ShapeDtypeStruct((groups, rows, LANES), F32),
            jax.ShapeDtypeStruct((1, LANES), jnp.int32),
        ),
        in_specs=[VMEM] * 4,
        out_specs=(VMEM,) * 2,
        compiler_params=PARAMS,
        name="columns",
    )(profile.reshape(-1, LANES), turn, band_edges.reshape(1, -1), owner_counts.reshape(1, -1))


def coarse_table(coarse):
    half, quarter = coarse // 2, coarse // 4
    k_index = np.arange(quarter)
    a_index = np.concatenate([np.arange(0, half, 2), np.arange(1, half, 2)])
    real, imag = unit_root(half, k_index[:, None] * a_index[None, :])
    imag[0] = 1
    parts = [part.reshape(quarter // 16, 2, 2, 1, 4, half) for part in (real, imag)]
    parts = np.concatenate(parts, axis=3).transpose(0, 2, 3, 1, 4, 5)
    high, middle, low = three_terms(parts.reshape(half, half))
    terms = [term[:, at : at + quarter] for at in (0, quarter) for term in (middle, high, low)]
    return np.concatenate(terms, axis=1)


def slot_bands(groups, whole_ref, wanted_ref, lane_band_ref, row_band_ref):
    capacity = row_band_ref.shape[0]
    own = lax.axis_index("bins")
    counts = [
        jnp.broadcast_to(whole_ref[:, 8 + owner : 9 + owner], (1, LANES)) for owner in range(groups)
    ]
    lane = iotas((1, LANES))[1]
    rank = lane & (capacity - 1)
    start = jnp.zeros((1, LANES), jnp.int32)
    own_start, own_count = start, start
    wanted = []
    for owner, count in enumerate(counts):
        wanted.append(jnp.where(rank < count, start + rank, -1))
        own_start = jnp.where(own == owner, start, own_start)
        own_count = jnp.where(own == owner, count, own_count)
        start = start + count
    for pair in range(groups // 2):
        wanted_ref[:, pair * LANES : (pair + 1) * LANES] = jnp.where(
            lane < HALF, wanted[2 * pair], wanted[2 * pair + 1]
        )
    edges = [jnp.broadcast_to(whole_ref[:, at : at + 1], (1, LANES)) for at in range(1, NCLASS)]
    for ref, slot in ((lane_band_ref, rank), (row_band_ref, iotas((capacity, LANES))[0])):
        band = jnp.zeros_like(slot)
        for edge in edges:
            band = band + jnp.where(slot + own_start >= edge, 1, 0)
        ref[...] = jnp.where(slot < own_count, band, -1)


def coarse_kernel(
    groups,
    shares,
    x_ref,
    table_ref,
    whole_ref,
    dynamics_ref,
    state_ref,
    out_ref,
    moved_ref,
    wanted_ref,
    lane_band_ref,
    row_band_ref,
):
    slot_bands(groups, whole_ref, wanted_ref, lane_band_ref, row_band_ref)
    half = x_ref.shape[0]
    quarter = half // 2
    row, lane = iotas((8, LANES))
    low_lanes = lane < HALF
    sums = []
    for parity in range(2):
        high, middle, low = split_three(x_ref[pl.ds(parity, quarter, stride=2), :])
        main = jnp.concatenate([high, middle], axis=1)
        rest = [jnp.concatenate([term, jnp.zeros_like(term)], axis=1) for term in (low, high)]
        at = 3 * quarter * parity
        left = jnp.concatenate(
            [table_ref[:, at : at + 2 * quarter], table_ref[:, at + quarter : at + 3 * quarter]], axis=1
        )
        both = dot(left, jnp.concatenate([main, main] + rest, axis=0))
        sums.append(both[:, :LANES] + both[:, LANES:])
    base = 8 * (row >> 2) + 4 * (lane >> 6) + (row & 3)
    base_cosine, base_sine = unit_turn(base, 2 * half)
    packed = low_lanes & (row == 0)
    for sign, block in [(sign, block) for block in range(half // 32) for sign in (1, -1)]:
        pieces = []
        for at in range(32 * block, 32 * (block + 1), 8):
            even, odd = sums[0][at : at + 8], sums[1][at : at + 8]
            pieces.append(even + odd if sign > 0 else even - odd)
        real_low, imag_low, real_high, imag_high = pieces
        if block == 0 and sign < 0:
            imag_low = jnp.where(row == 0, 0.0, imag_low)
        even_real = jnp.where(low_lanes, real_low, pltpu.roll(real_high, HALF, 1))
        even_imag = jnp.where(low_lanes, imag_low, pltpu.roll(imag_high, HALF, 1))
        odd_real = jnp.where(low_lanes, pltpu.roll(real_low, HALF, 1), real_high)
        odd_imag = jnp.where(low_lanes, pltpu.roll(imag_low, HALF, 1), imag_high)
        first = 2 * block + (0 if sign > 0 else shares // 2)
        angle = math.pi * 8 * first / half
        cosine = base_cosine * math.cos(angle) - base_sine * math.sin(angle)
        sine = base_sine * math.cos(angle) + base_cosine * math.sin(angle)
        real = even_real + odd_real * cosine + odd_imag * sine
        if first == 0:
            cosine = jnp.where(packed, -1.0, cosine)
        imag = even_imag + odd_imag * cosine - odd_real * sine
        out_ref[pl.ds(8 * first, 8, stride=2), :] = real
        out_ref[pl.ds(8 * first + 1, 8, stride=2), :] = imag
    moved_ref[...] = state_product(dynamics_ref[...], state_ref[...], row_band_ref[...])


def coarse_step(columns, whole, dynamics, state, groups, shares):
    capacity = state.shape[0]
    half = columns.shape[0]
    return pl.pallas_call(
        functools.partial(coarse_kernel, groups, shares),
        out_shape=(
            jax.ShapeDtypeStruct((half, LANES), F32),
            jax.ShapeDtypeStruct(state.shape, F32),
            jax.ShapeDtypeStruct((1, groups * capacity), jnp.int32),
            jax.ShapeDtypeStruct((1, LANES), jnp.int32),
        ),
        in_specs=[VMEM] * 5,
        out_specs=(VMEM,) * 4,
        scratch_shapes=[pltpu.VMEM((capacity, LANES), jnp.int32)],
        compiler_params=PARAMS,
        name="coarse_dft",
    )(
        columns,
        jnp.asarray(coarse_table(2 * half)),
        whole,
        dynamics.reshape(NCLASS * STATES, STATES),
        state,
    )


def coarse_step_general(columns, shares):
    coarse = columns.shape[0]
    half = coarse // 2
    real, imag = unit_root(coarse, np.arange(half)[:, None] * np.arange(coarse)[None, :])
    imag[0] = 1 - 2 * (np.arange(coarse) % 2)
    table = jnp.asarray(np.concatenate([real, imag]).astype(np.float32))
    spectrum = jnp.dot(table, columns, precision=HIGHEST)
    blocks = jnp.concatenate([spectrum[:half], spectrum[half:]], axis=1)
    return blocks.reshape(shares, half // shares, LANES)


def fine_tables(groups, coarse):
    fine_length = groups * HALF
    doubled = np.arange(LANES) % HALF
    turn = unit_root(fine_length, np.arange(groups)[:, None] * doubled[None, :])
    middle = (np.arange(groups)[:, None] * HALF + doubled[None, :]) * (coarse // 2)
    middle = unit_root(coarse * fine_length, middle)
    turns = np.concatenate(turn + middle).astype(np.float32)
    order = np.arange(HALF)
    order[HALF // 2 :] = order[HALF // 2 :][::-1]
    real, imag = unit_root(HALF, np.arange(HALF)[:, None] * order[None, :])
    sign = np.where(np.arange(HALF) < HALF // 2, 1, -1)
    matrix = np.block([[real, imag * sign], [-imag, real * sign]])
    high, middle, low = three_terms(matrix)
    both = np.concatenate([high, middle], axis=1)
    rest = [np.concatenate([term, np.zeros_like(term)], axis=1) for term in (low, high)]
    return turns, np.concatenate([both, both] + rest, axis=0)


def add(p, q):
    return (p[0] + q[0], p[1] + q[1])


def sub(p, q):
    return (p[0] - q[0], p[1] - q[1])


def times(p, cosine, sine):
    return (p[0] * cosine + p[1] * sine, p[1] * cosine - p[0] * sine)


def eight_point(values):
    half = math.sqrt(0.5)

    def down(p):
        return (p[1], -p[0])

    def four(a, b, c, d):
        s0, s1, s2, s3 = add(a, c), sub(a, c), add(b, d), sub(b, d)
        turned = (s1[0] + s3[1], s1[1] - s3[0]), (s1[0] - s3[1], s1[1] + s3[0])
        return add(s0, s2), turned[0], sub(s0, s2), turned[1]

    even = four(values[0], values[2], values[4], values[6])
    odd = four(values[1], values[3], values[5], values[7])
    turned = [
        odd[0],
        ((odd[1][0] + odd[1][1]) * half, (odd[1][1] - odd[1][0]) * half),
        down(odd[2]),
        ((odd[3][1] - odd[3][0]) * half, (odd[3][0] + odd[3][1]) * -half),
    ]
    return [add(e, t) for e, t in zip(even, turned)] + [sub(e, t) for e, t in zip(even, turned)]


def state_product(dynamics, state, band):
    row, column = iotas((NCLASS * STATES, STATES))
    limit = STATES >> (row >> 6)
    inside = ((row & (STATES - 1)) < limit) & (column < limit)
    dynamics = jnp.where(inside, dynamics, 0.0)
    empty = jnp.zeros_like(dynamics)
    halves = [
        jnp.concatenate([dynamics, empty], axis=1),
        jnp.concatenate([empty, dynamics], axis=1),
    ]
    matrix = jnp.concatenate(
        [half[k * STATES : (k + 1) * STATES] for k in range(NCLASS) for half in halves], axis=0
    )
    state_high, state_low = split_two(state)
    high, low = split_two(matrix)
    moved = lax.dot_general(
        jnp.concatenate([state_high, state_low, state_high], axis=1),
        jnp.concatenate([high, high, low], axis=1),
        (((1,), (1,)), ((), ())),
        preferred_element_type=F32,
    )
    result = jnp.zeros(state.shape, F32)
    for k in range(NCLASS):
        result = jnp.where(band == k, moved[:, k * LANES : (k + 1) * LANES], result)
    return result


def moved_kernel(row_band_ref, dynamics_ref, state_ref, out_ref):
    out_ref[...] = state_product(dynamics_ref[...], state_ref[...], row_band_ref[...])


def moved_step(row_band, dynamics, state):
    return pl.pallas_call(
        moved_kernel,
        out_shape=jax.ShapeDtypeStruct(state.shape, F32),
        in_specs=[VMEM] * 3,
        out_specs=VMEM,
        compiler_params=PARAMS,
        name="moved",
    )(row_band, dynamics.reshape(NCLASS * STATES, STATES), state)


def fine_kernel(
    profiles,
    x_ref,
    turn_ref,
    wanted_ref,
    turns_ref,
    table_ref,
    out_ref,
):
    groups = turn_ref.shape[0] // 4
    first = (lax.axis_index("bins") == 0) & (lax.axis_index("scans") == 0)
    row, lane = iotas((8, LANES))
    low_lanes = lane < HALF
    low_side = (lane & (HALF - 1)) < HALF // 2
    even = (row & 1) == 0
    packed = first & low_lanes & even
    blocks = [[None] * 3 for _ in range(groups)]
    for at in range(3):
        column = []
        for c in range(groups):
            start = c * 8 * profiles
            if at < 2:
                real = x_ref[pl.ds(start + 2 * at, 8, stride=4), :]
                imag = x_ref[pl.ds(start + 2 * at + 1, 8, stride=4), :]
                imag = imag if at else jnp.where(packed, 0.0, imag)
                turn = 4 * c + 2 * at
                column.append(times((real, imag), turn_ref[turn], turn_ref[turn + 1]))
            else:
                middle = jnp.where(packed, x_ref[pl.ds(start + 1, 8, stride=4), :], 0.0)
                middle_real = turns_ref[2 * groups + c : 2 * groups + c + 1, :]
                middle_imag = turns_ref[3 * groups + c : 3 * groups + c + 1, :]
                column.append((middle * middle_real, middle * middle_imag))
        for u, value in enumerate(eight_point(column)):
            cosine, sine = turns_ref[u : u + 1, :], -turns_ref[groups + u : groups + u + 1, :]
            blocks[u][at] = times(value, cosine, sine) if u else value
    rows = []
    for u in range(groups):
        for at in range(3):
            real, imag = blocks[u][at]
            rows.append(jnp.where(low_lanes, real, pltpu.roll(imag, HALF, 1)))
            if at < 2:
                rows.append(jnp.where(low_lanes, pltpu.roll(real, HALF, 1), imag))
    product = []
    for at in range(0, len(rows), len(rows) // 2):
        part = jnp.concatenate(rows[at : at + len(rows) // 2], axis=0)
        high, middle, low = split_three(part)
        both = dot(jnp.concatenate([high, middle, high, low], axis=1), table_ref[...])
        product.append(both[:, :LANES] + both[:, LANES:])
    product = jnp.concatenate(product, axis=0)
    spectrum = []
    for u in range(groups):
        spectrum.append([product[8 * at : 8 * (at + 1)] for at in range(5 * u, 5 * (u + 1))])
        spectrum[u][0] = jnp.where(first & even & ~low_side, 0.0, spectrum[u][0])
        spectrum[u][4] = jnp.where(low_side, spectrum[u][4], 0.0)
    squares = [sum(block * block for block in spectrum[u]) for u in range(groups)]
    rest_place = ~low_side & even
    pieces = []
    for u in range(groups):
        mirror = groups - 1 - u
        power = jnp.where(low_side, squares[u], squares[mirror])
        for shift in (4, 2, 1):
            power = power + pltpu.roll(power, shift, 0)
        evens, *others = (
            jnp.where(low_side, spectrum[u][at], spectrum[mirror][at]) for at in range(4)
        )
        sums = jnp.where(rest_place, 0.0, evens) + sum(others)
        sums = sums + pltpu.roll(sums, 7, 0)
        lows = jnp.where(low_side, sums, 0.0)
        highs = jnp.where(low_side, 0.0, pltpu.roll(sums, 1, 0))
        rest = jnp.where(rest_place, evens, spectrum[u][4])
        pieces.append((jnp.where(even, lows, highs), jnp.where(even, rest, power)))
    left = [[], [], [], []]
    for u in range(0, groups, 2):
        for at in range(2):
            one, two = pieces[u][at], pieces[u + 1][at]
            real = jnp.where(low_lanes, one, pltpu.roll(two, HALF, 1))
            imag = jnp.where(low_lanes, pltpu.roll(one, HALF, 1), two)
            if at == 1:
                power = real + imag
                real, imag = jnp.where(even, real, power), jnp.where(even, imag, power)
            left[at].append(real)
            left[2 + at].append(imag)
    left = jnp.concatenate([jnp.concatenate(parts, axis=1) for parts in left], axis=0)
    left = jnp.concatenate(split_two(left), axis=0)
    wanted = wanted_ref[...]
    chosen = []
    for u in range(groups):
        tile = u + groups * iotas((HALF // 2, wanted.shape[1]))[0]
        chosen += [jnp.where(tile == wanted, 1.0, 0.0).astype(BF16)] * 2
    routed = dot(left, jnp.concatenate(chosen, axis=0))
    routed = routed[:32] + routed[32:]
    for pair in range(groups // 2):
        for at in range(2):
            real = routed[8 * at : 8 * (at + 1), pair * LANES : (pair + 1) * LANES]
            imag = routed[16 + 8 * at : 16 + 8 * (at + 1), pair * LANES : (pair + 1) * LANES]
            start = 2 * pair * profiles * KINDS + at
            crossed = pltpu.roll(jnp.where(low_lanes, imag, real), HALF, 1)
            out_ref[pl.ds(start, 8, stride=2), :] = jnp.where(low_lanes, real, crossed)
            out_ref[pl.ds(start + profiles * KINDS, 8, stride=2), :] = jnp.where(
                low_lanes, crossed, imag
            )


def fine_step(arrived, turn, wanted, profiles, coarse):
    groups = turn.shape[0] // 4
    turns, table = fine_tables(groups, coarse)
    out = pl.pallas_call(
        functools.partial(fine_kernel, profiles),
        out_shape=jax.ShapeDtypeStruct((groups * profiles * KINDS, LANES), F32),
        in_specs=[VMEM] * 5,
        out_specs=VMEM,
        compiler_params=PARAMS,
        name="fine_dft",
    )(
        arrived,
        turn,
        wanted,
        jnp.asarray(turns),
        jnp.asarray(table),
    )
    return out.reshape(groups * profiles, KINDS, LANES)


def fine_step_general(arrived, owner_counts, capacity):
    groups, rows = arrived.shape[:2]
    coarse = 2 * rows * groups
    fine_length = groups * HALF
    order = coarse * fine_length
    own = lax.axis_index("bins")
    real, imag = arrived[:, :, :HALF], arrived[:, :, HALF:]
    points = jnp.arange(fine_length, dtype=jnp.int32).reshape(groups, 1, HALF)
    k_index = own * rows + jnp.arange(rows, dtype=jnp.int32)[None, :, None]
    cosine, sine = unit_turn(points * k_index & (order - 1), order)
    packed = (own == 0) & (jnp.arange(rows)[None, :, None] == 0)
    middle = jnp.where(own == 0, imag[:, :1], 0.0)
    imag = jnp.where(packed, 0.0, imag)
    real, imag = real * cosine + imag * sine, imag * cosine - real * sine
    cosine, sine = unit_turn(points * (coarse // 2), order)
    real = jnp.concatenate([real, middle * cosine], axis=1)
    imag = jnp.concatenate([imag, -middle * sine], axis=1)

    def turned(pattern, root, parts):
        cosine, sine = (jnp.asarray(part.astype(np.float32)) for part in root)
        mul = functools.partial(jnp.einsum, pattern, precision=HIGHEST)
        return (
            mul(cosine, parts[0]) - mul(sine, parts[1]),
            mul(cosine, parts[1]) + mul(sine, parts[0]),
        )

    group_index, point_index = np.arange(groups), np.arange(HALF)
    parts = turned(
        "cu,crj->urj", unit_root(groups, group_index[:, None] * group_index), (real, imag)
    )
    parts = turned(
        "uj,urj->urj", unit_root(fine_length, group_index[:, None] * point_index), parts
    )
    parts = turned(
        "jv,urj->vur", unit_root(HALF, point_index[:, None] * point_index), parts
    )
    tiles = fine_length // 2
    kept = jnp.concatenate([~packed[0, :, 0], jnp.zeros((1,), bool)])
    sides = []
    for part, sign in zip(parts, (1.0, -1.0)):
        part = part.reshape(fine_length, rows + 1)
        sides.append((part[:tiles], sign * jnp.where(kept, part[tiles:][::-1], 0.0)))
    power = sum(jnp.sum(part * part, axis=1) for pair in sides for part in pair)
    starts = jnp.cumsum(owner_counts) - owner_counts
    slot_index = jnp.arange(capacity, dtype=jnp.int32)
    filled = slot_index[None, :] < owner_counts[:, None]
    chosen = jnp.clip(starts[:, None] + slot_index[None, :], 0, tiles - 1)

    def kinds(low, high):
        low_sums, high_sums = jnp.sum(low[:, :rows], axis=1), jnp.sum(high[:, 1:rows], axis=1)
        values = jnp.stack([low_sums, high[:, 0] + low[:, rows], high_sums, power], axis=1)
        return jnp.where(filled[:, :, None], values[chosen], 0.0).transpose(0, 2, 1)

    return jnp.concatenate([kinds(*sides[0]), kinds(*sides[1])], axis=2)


def pool_table(shares, coarse):
    pool = np.zeros((21, 16, shares, KINDS), np.float32)
    sums = pool[1:].reshape(NCLASS, STATES, shares, KINDS)
    wide = TILE // STATES
    rows = coarse // 2 // shares
    for share in range(shares):
        first = rows * share
        rest = coarse - first if share else coarse // 2
        for kind, at in enumerate((first, rest, coarse - first - 1)):
            for band in range(NCLASS):
                sums[band, at // wide >> band, share, kind] = 1.0
    pool[0, :, :, 3] = 1.0
    return pool.reshape(-1, shares * KINDS).astype(BF16)


def update_kernel(
    count, x_ref, pool_ref, lane_band_ref, moved_ref, out_ref
):
    band = lane_band_ref[...]
    right = jnp.concatenate(split_two(x_ref[...]), axis=1)
    sums = jnp.concatenate([dot(pool_ref[:176], right), dot(pool_ref[176:], right)], axis=0)
    sums = sums[:, :LANES] + sums[:, LANES:]
    power = sums[:1] * (1.0 / count)
    sums = sums[16:]
    span = jnp.left_shift(TILE // STATES, jnp.maximum(band, 0)).astype(F32)
    scaling = lax.rsqrt(span * (power + EPSILON))
    scaling = jnp.where(band < 0, 0.0, scaling)
    chosen = sums[:STATES]
    for k in range(1, NCLASS):
        chosen = jnp.where(band == k, sums[k * STATES : (k + 1) * STATES], chosen)
    chosen = chosen * scaling
    turned = jnp.transpose(jnp.concatenate([chosen, chosen], axis=0))
    half = turned.shape[0] // 2
    measured = jnp.where(iotas((half, LANES))[1] < STATES, turned[:half], turned[half:])
    out_ref[...] = measured + moved_ref[...]


def update_step(arrived, lane_band, moved, coarse, count):
    shares = arrived.shape[0]
    return pl.pallas_call(
        functools.partial(update_kernel, count),
        out_shape=jax.ShapeDtypeStruct(moved.shape, F32),
        in_specs=[VMEM] * 4,
        out_specs=VMEM,
        compiler_params=PARAMS,
        name="state_update",
    )(
        arrived.reshape(shares * KINDS, LANES),
        jnp.asarray(pool_table(shares, coarse)),
        lane_band,
        moved,
    )


def bands_general(band_edges, owner_counts, capacity):
    own = lax.axis_index("bins")
    slot = jnp.arange(capacity, dtype=jnp.int32)
    start = jnp.cumsum(owner_counts)[own] - owner_counts[own]
    band = jnp.sum((slot + start)[:, None] >= band_edges[None, 1:NCLASS], axis=1)
    band = jnp.where(slot < owner_counts[own], band, -1).astype(jnp.int32)
    return jnp.tile(band, 2)[None, :], jnp.broadcast_to(band[:, None], (capacity, LANES))


def exchanged(values, axes):
    return lax.all_to_all(values, axes, split_axis=0, concat_axis=0, tiled=True)


def body(profiles, band_edges, owner_counts, dynamics, prev_state):
    groups, scans = lax.axis_size("bins"), lax.axis_size("scans")
    prof_rows, length = profiles.shape
    capacity = prev_state.shape[0]
    coarse = length // HALF
    shares = groups * scans
    count = prof_rows * scans * TILE
    state = prev_state.reshape(capacity, 2 * STATES)
    if groups == 8 and scans == 4 and coarse == 16 * shares and capacity == HALF:
        turn = turns_step(groups, groups * length)
        columns, whole = columns_step(profiles.reshape(length), turn, band_edges, owner_counts)
        columns = exchanged(columns, "bins").reshape(coarse // 2, LANES)
        blocks, moved, wanted, lane_band = coarse_step(
            columns, whole, dynamics, state, groups, shares
        )
        blocks = exchanged(blocks.reshape(shares, 8, LANES), ("bins", "scans"))
        blocks = blocks.reshape(8 * shares, LANES)
        payload = fine_step(blocks, turn, wanted, scans, coarse)
        arrived = exchanged(payload, ("bins", "scans"))
    else:
        lane_band, row_band = bands_general(band_edges, owner_counts, capacity)
        moved = moved_step(row_band, dynamics, state)
        columns = profiles.reshape(coarse // groups, groups, HALF).transpose(1, 0, 2)
        columns = exchanged(columns, "bins").reshape(coarse, HALF)
        blocks = exchanged(coarse_step_general(columns, groups), "bins")
        arrived = exchanged(fine_step_general(blocks, owner_counts, capacity), "bins")
        power = lax.psum(arrived[:, 3:], "scans")
        arrived = jnp.concatenate([arrived[:, :3], power], axis=1)
    updated = update_step(arrived, lane_band, moved, coarse, count)
    return updated.reshape(prev_state.shape)


def solution(mesh):
    return jax.shard_map(
        body,
        mesh=mesh,
        in_specs=(P("scans", "bins"), P(), P(), P(), P("bins", "scans", None)),
        out_specs=P("bins", "scans", None),
        check_vma=False,
    )
```
